32 devices in a mesh: depth: 8 (over y, x, core), seq: 4 (over z).
Axes of the slice: x: 2, y: 2, z: 4, core: 2. Of those that a mesh axis runs over, the one named last changes fastest.
Arguments:
- interfaces: bfloat16 [8, 1, 2048, 1024], P('depth', None, 'seq'), may hold values from -6 to 6
- doc_ids: int32 [1, 2048], replicated, may hold values from 0 to 3, never falling along the last dimension, each value on 1 to 1024 neighbouring positions
- w_attn: bfloat16 [8, 1, 4, 1024, 1024], P('depth'), may hold values from -0.1875 to 0.1875
- w_up: bfloat16 [8, 1, 1024, 4096], P('depth'), may hold values from -0.1875 to 0.1875
- w_down: bfloat16 [8, 1, 4096, 1024], P('depth'), may hold values from -0.09375 to 0.09375
- norm_gains: float32 [8, 1, 2, 1024], P('depth'), may hold values from 0.25 to 1.75
- coarse_gain: float32 [8, 1024], P('depth'), may hold values from 0 to 1
Outputs:
- relaxed: bfloat16 [8, 1, 2048, 1024], P('depth', None, 'seq')
The draws below stay inside these ranges and needn't reach their ends.
Inputs may be any that keep to these rules, and one draw needn't show every extreme that they name: doc_ids never fall along a sequence and number the documents packed into it.
All inputs are finite; a program needn't handle non-finite values.
Results may differ from the reference program's by a relative error of at most 0.025.
Values may be sent and summed in bfloat16 or wider, within the bound.
No kernel may reach another device: no remote copies, remote signals or barrier semaphores. Data moves between devices by JAX's collectives and lax.ppermute only.
A program may use at most 192 MiB of HBM per device.

```python
import math
import jax
import jax.numpy as jnp
import numpy as np
from jax import lax

D = 1024
FF = 4096
HEADS = 16
SEC_LAYERS = 1
LEN = 2048
SEQS = 1
LAYER_SPANS = 8


def draw_coarse_gain(key, part):
    first_key = jax.random.fold_in(key, 11)
    second_key = jax.random.fold_in(key, 12)
    lookup_slice_final = jax.random.fold_in(key, 13)
    decay_rate = jnp.exp(jax.random.uniform(first_key, (D,), jnp.float32, math.log(0.3 / LAYER_SPANS), math.log(3.0)))
    dispersion = jax.random.uniform(second_key, (LAYER_SPANS, D), jnp.float32, 0.5, 2.0)
    packet_clusters = jax.random.bernoulli(lookup_slice_final, 2.0 / LAYER_SPANS, (LAYER_SPANS, 1))
    multiplier_coefficient = jnp.where(packet_clusters, 0.6, 1.0).astype(jnp.float32)
    return (jnp.exp(-decay_rate[None, :] * dispersion) * multiplier_coefficient).astype(jnp.float32)


def shard_levels(key, extent, cuts, low, largest):
    def one(dim, blocks):
        draws = jax.random.uniform(jax.random.fold_in(jax.random.fold_in(key, 6), dim), (blocks,), jnp.float32, low / len(cuts), largest / len(cuts))
        return jnp.repeat(jnp.exp(draws), extent[dim] // blocks).reshape((-1,) + (1,) * (len(extent) - dim - 1))

    level = one(*cuts[0])
    for cut in cuts[1:]:
        level = level * one(*cut)
    return level


def split_up(amount, total, limit, skew):
    loads = [(1 << 20) // math.isqrt(rank ** skew) + 1 for rank in range(2, amount + 1)]
    spare, given = total - limit - (amount - 1), [1] * (amount - 1)
    while spare > 0:
        movable = [i for i in range(amount - 1) if given[i] < limit]
        whole, remaining = sum([loads[i] for i in movable]), spare
        for i in movable:
            extra = min(limit - given[i], max(1, remaining * loads[i] // whole), spare)
            given[i] = given[i] + extra
            spare = spare - extra
    return np.array([limit] + given)


def uneven(rng, amount, total, bound, lean):
    if amount == 2:
        one = jax.random.randint(rng, (), max(1, total - bound), min(bound, total - 1) + 1)
        return jnp.stack([one, total - one])
    sizes = jnp.asarray(split_up(amount, total, bound, lean), jnp.int32)
    twos = (amount - 1) // 2
    giver, receiver = sizes[1:1 + 2 * twos:2], sizes[2:2 + 2 * twos:2]
    margin = jnp.minimum(giver - 1, bound - receiver)
    shifted = jax.random.randint(jax.random.fold_in(rng, 1), (twos,), 0, 1 << 20) % (margin + 1)
    sizes = sizes.at[1:1 + 2 * twos:2].set(giver - shifted).at[2:2 + 2 * twos:2].set(receiver + shifted)
    return sizes[jax.random.permutation(jax.random.fold_in(rng, 2), amount)]


def bell_draw(rng, extent, spread, bound, pieces=(), kind=jnp.bfloat16):
    level = shard_levels(rng, extent, pieces, -0.22, 0.18) if pieces else 1.0
    values = jax.random.normal(rng, extent, jnp.float32) * spread * level
    return jnp.minimum(jnp.maximum(values, -bound), bound).astype(kind)


def setup_inputs(seed: int = 0) -> dict:
    arg_keys = jax.random.split(jax.random.key(seed), 8)
    return {
        "interfaces": bell_draw(arg_keys[0], (LAYER_SPANS, SEQS, LEN, D), 1.0, 6.0, ((0, 8), (2, 4))),
        "doc_ids": jax.vmap(lambda own: jnp.searchsorted(jnp.cumsum(uneven(own, 4, LEN, LEN // 2, 1)), jnp.arange(LEN), side="right"))(jax.random.split(arg_keys[1], SEQS)).reshape((SEQS, LEN)).astype(jnp.int32),
        "w_attn": bell_draw(arg_keys[2], (LAYER_SPANS, SEC_LAYERS, 4, D, D), D ** -0.5, 0.1875, ((0, 8),)),
        "w_up": bell_draw(arg_keys[3], (LAYER_SPANS, SEC_LAYERS, D, FF), D ** -0.5, 0.1875, ((0, 8),)),
        "w_down": bell_draw(arg_keys[4], (LAYER_SPANS, SEC_LAYERS, FF, D), FF ** -0.5, 0.09375, ((0, 8),)),
        "norm_gains": jnp.clip(1.0 + 0.15 * jax.random.normal(arg_keys[5], (LAYER_SPANS, SEC_LAYERS, 2, D), jnp.float32), 0.25, 1.75),
        "coarse_gain": draw_coarse_gain(jax.random.fold_in(arg_keys[7], 71), 0),
    }


def rms_norm(value_tensor, gain):
    return value_tensor * lax.rsqrt(lax.optimization_barrier(jnp.mean(value_tensor * value_tensor, axis=-1, keepdims=True)) + 1e-05) * gain

def one_layer(states, attn_w, up_w, lowering_matrix, gain_pair, doc_ids):
    batch, rows, width = states.shape
    head_dim = width // HEADS
    normed = rms_norm(states.astype(jnp.float32), gain_pair[0]).astype(jnp.bfloat16)
    flat = normed.reshape(-1, width)
    queries = jnp.dot(flat, attn_w[0], preferred_element_type=jnp.float32).astype(jnp.bfloat16).reshape(batch, rows, HEADS, head_dim)
    keys_all = jnp.dot(flat, attn_w[1], preferred_element_type=jnp.float32).astype(jnp.bfloat16).reshape(batch, rows, HEADS, head_dim)
    values_all = jnp.dot(flat, attn_w[2], preferred_element_type=jnp.float32).astype(jnp.bfloat16).reshape(batch, rows, HEADS, head_dim)
    scores = jnp.einsum('sqhd,skhd->shqk', queries.astype(jnp.float32), keys_all.astype(jnp.float32)) * head_dim ** (-0.5)
    position = jnp.arange(rows)
    causal = position[None, :] <= position[:, None]
    same_doc = doc_ids[:, :, None] == doc_ids[:, None, :]
    allowed = (causal[None] & same_doc)[:, None]
    weights = jnp.where(allowed, jnp.exp(scores), jnp.zeros_like(scores))
    denominator = lax.optimization_barrier(jnp.sum(weights, axis=-1))
    numerator = jnp.einsum('shqk,skhd->shqd', weights.astype(jnp.bfloat16).astype(jnp.float32), values_all.astype(jnp.float32))
    attended = (numerator / denominator[..., None]).transpose(0, 2, 1, 3).reshape(batch * rows, width).astype(jnp.bfloat16)
    mixed = states.astype(jnp.float32) + jnp.dot(attended, attn_w[3], preferred_element_type=jnp.float32).reshape(batch, rows, width)
    second = rms_norm(mixed, gain_pair[1]).astype(jnp.bfloat16).reshape(-1, width)
    expanded = jax.nn.gelu(jnp.dot(second, up_w, preferred_element_type=jnp.float32)).astype(jnp.bfloat16)
    result = mixed + jnp.dot(expanded, lowering_matrix, preferred_element_type=jnp.float32).reshape(batch, rows, width)
    return result.astype(jnp.bfloat16)

def reference(interfaces, doc_ids, w_attn, w_up, w_down, norm_gains, coarse_gain):

    def section(operands):
        states, attn_stack, up_stack, down_stack, gain_stack = operands
        for layer_idx in range(SEC_LAYERS):
            states = one_layer(states, attn_stack[layer_idx], up_stack[layer_idx], down_stack[layer_idx], gain_stack[layer_idx], doc_ids)
        return states

    def relax(starting):
        return lax.map(section, (starting, w_attn, w_up, w_down, norm_gains))
    fine = relax(interfaces)
    following = jnp.concatenate([interfaces[1:], jnp.zeros_like(interfaces[:1])], axis=0)
    mismatch = fine.astype(jnp.float32) - following.astype(jnp.float32)

    def advance(correction, inputs_now):
        multiplier_coefficient, gap = inputs_now
        return (multiplier_coefficient[None, None, :] * correction + gap, correction)
    start_zero = jnp.zeros(interfaces.shape[1:], jnp.float32)
    unused, correction = lax.scan(advance, start_zero, (coarse_gain, mismatch))
    corrected = (interfaces.astype(jnp.float32) + correction).astype(jnp.bfloat16)
    return relax(corrected)
```

```python
import functools

import jax
import jax.numpy as jnp
from jax import lax
from jax.experimental import pallas as pl
from jax.experimental.pallas import tpu as pltpu
from jax.sharding import PartitionSpec as P

HEADS = 16
LANES = 128
BLOCK = 256
VMEM_BYTES = 48 * 1024 * 1024
F32 = jnp.float32
BF16 = jnp.bfloat16


def rms_norm(value, gain):
    return value * lax.rsqrt(jnp.mean(value * value, axis=-1, keepdims=True) + 1e-05) * gain


def dot(a, b):
    return jnp.dot(a, b, preferred_element_type=F32)


def attend(q_ref, k_ref, v_ref, num_ref, den_ref, qcol_ref, krow_ref, qdoc_ref, kdoc_ref, causal):
    rows, width = q_ref.shape
    keys = k_ref.shape[0]
    head_dim = width // HEADS
    q_block, k_block = min(BLOCK, rows), min(BLOCK, keys)
    lane = lax.broadcasted_iota(jnp.int32, (1, LANES), 1)
    members = [lane // head_dim == i for i in range(LANES // head_dim)]
    count_q, count_k = rows // q_block, keys // k_block

    def one(index, carry):
        qi, ki = index // count_k, index % count_k
        q0 = pl.multiple_of(qi * q_block, q_block)
        k0 = pl.multiple_of(ki * k_block, k_block)
        needed = kdoc_ref[0, k0 + k_block - 1] >= qdoc_ref[0, q0]
        if causal:
            needed = (k0 <= q0) & (needed | (k0 == q0))

        @pl.when(needed)
        def _():
            allowed = qcol_ref[pl.ds(q0, q_block), :1] == krow_ref[:, pl.ds(k0, k_block)]
            if causal:
                q_pos = q0 + lax.broadcasted_iota(jnp.int32, (q_block, k_block), 0)
                k_pos = k0 + lax.broadcasted_iota(jnp.int32, (q_block, k_block), 1)
                allowed = allowed & (k_pos <= q_pos)
            ones = jnp.ones((k_block, LANES), BF16)
            for pair in range(width // LANES):
                cols = slice(pair * LANES, (pair + 1) * LANES)
                queries = q_ref[pl.ds(q0, q_block), cols]
                keys_here = k_ref[pl.ds(k0, k_block), cols]
                values = jnp.concatenate([v_ref[pl.ds(k0, k_block), cols], ones], axis=1)
                num, den = None, None
                for member in members:
                    scores = lax.dot_general(
                        jnp.where(member, queries, jnp.zeros_like(queries)),
                        keys_here,
                        (((1,), (1,)), ((), ())),
                        preferred_element_type=F32,
                    )
                    weights = jnp.where(allowed, jnp.exp(scores), 0.0).astype(BF16)
                    out = dot(weights, values)
                    if num is None:
                        num, den = out[:, :LANES], out[:, LANES:]
                    else:
                        num = jnp.where(member, out[:, :LANES], num)
                        den = jnp.where(member, out[:, LANES:], den)
                num_ref[pl.ds(q0, q_block), cols] += num
                den_ref[pl.ds(q0, q_block), cols] += den

        return carry

    lax.fori_loop(0, count_q * count_k, one, 0)


def own_kernel(x_ref, gain_ref, w_ref, qcol_ref, krow_ref, doc_ref, q_ref, num_ref, den_ref, n_ref, k_ref, v_ref):
    step = pl.program_id(0)
    head_dim = x_ref.shape[1] // HEADS

    @pl.when(step == 0)
    def _():
        n_ref[...] = rms_norm(x_ref[...].astype(F32), gain_ref[0:1]).astype(BF16)
        q_ref[...] = dot(n_ref[...], w_ref[...]).astype(BF16) * jnp.asarray(head_dim ** (-0.5), BF16)

    @pl.when(step == 1)
    def _():
        k_ref[...] = dot(n_ref[...], w_ref[...]).astype(BF16)

    @pl.when(step == 2)
    def _():
        v_ref[...] = dot(n_ref[...], w_ref[...]).astype(BF16)
        num_ref[...] = jnp.zeros_like(num_ref)
        den_ref[...] = jnp.zeros_like(den_ref)
        attend(q_ref, k_ref, v_ref, num_ref, den_ref, qcol_ref, krow_ref, doc_ref, doc_ref, True)


def piece_kernel(
    x_ref, gain_ref, w_ref, q_ref, num_in, den_in, qcol_ref, krow_ref, qdoc_ref, kdoc_ref,
    num_ref, den_ref, n_ref, k_ref, v_ref,
):
    step = pl.program_id(0)
    needed = kdoc_ref[0, kdoc_ref.shape[1] - 1] >= qdoc_ref[0, 0]

    @pl.when(needed & (step == 0))
    def _():
        n_ref[...] = rms_norm(x_ref[...].astype(F32), gain_ref[0:1]).astype(BF16)
        k_ref[...] = dot(n_ref[...], w_ref[...]).astype(BF16)

    @pl.when(step == 1)
    def _():
        num_ref[...] = num_in[...]
        den_ref[...] = den_in[...]

    @pl.when(needed & (step == 1))
    def _():
        v_ref[...] = dot(n_ref[...], w_ref[...]).astype(BF16)
        attend(q_ref, k_ref, v_ref, num_ref, den_ref, qcol_ref, krow_ref, qdoc_ref, kdoc_ref, False)


def finish_kernel(x_ref, num_ref, den_ref, wo_ref, gain_ref, up_ref, down_ref, out_ref, acc_ref, n_ref):
    step = pl.program_id(0)

    @pl.when(step == 0)
    def _():
        attended = (num_ref[...] / den_ref[...]).astype(BF16)
        mixed = x_ref[...].astype(F32) + dot(attended, wo_ref[...])
        acc_ref[...] = mixed
        n_ref[...] = rms_norm(mixed, gain_ref[1:2]).astype(BF16)

    expanded = jax.nn.gelu(dot(n_ref[...], up_ref[...])).astype(BF16)
    acc_ref[...] += dot(expanded, down_ref[...])

    @pl.when(step == pl.num_programs(0) - 1)
    def _():
        out_ref[...] = acc_ref[...].astype(BF16)


def whole(shape):
    return pl.BlockSpec(shape, lambda *_: (0,) * len(shape))


def smem():
    return pl.BlockSpec(memory_space=pltpu.SMEM)


def params():
    return pltpu.CompilerParams(vmem_limit_bytes=VMEM_BYTES, dimension_semantics=("arbitrary",))


def own_part(x, gains, w_attn, qcol, doc):
    rows, width = x.shape
    return pl.pallas_call(
        own_kernel,
        grid=(3,),
        in_specs=[
            whole((rows, width)),
            whole(gains.shape),
            pl.BlockSpec((None, width, width), lambda i: (i, 0, 0)),
            whole((rows, LANES)),
            whole((1, rows)),
            smem(),
        ],
        out_specs=[whole((rows, width))] * 3,
        out_shape=[
            jax.ShapeDtypeStruct((rows, width), BF16),
            jax.ShapeDtypeStruct((rows, width), F32),
            jax.ShapeDtypeStruct((rows, width), F32),
        ],
        scratch_shapes=[pltpu.VMEM((rows, width), BF16)] * 3,
        compiler_params=params(),
        cost_estimate=pl.CostEstimate(
            flops=6 * rows * width * width + 16 * rows * rows * width,
            bytes_accessed=6 * width * width + 12 * rows * width,
            transcendentals=HEADS * rows * rows,
        ),
        name="own_part",
    )(x, gains, w_attn, qcol, doc, doc)


def piece_part(x, gains, w_attn, q, num, den, qcol, qdoc, kdoc):
    rows, width = q.shape
    keys = x.shape[0]
    return pl.pallas_call(
        piece_kernel,
        grid=(2,),
        in_specs=[
            whole((keys, width)),
            whole(gains.shape),
            pl.BlockSpec((None, width, width), lambda i: (i + 1, 0, 0)),
            whole((rows, width)),
            whole((rows, width)),
            whole((rows, width)),
            whole((rows, LANES)),
            whole((1, keys)),
            smem(),
            smem(),
        ],
        out_specs=[whole((rows, width))] * 2,
        out_shape=[jax.ShapeDtypeStruct((rows, width), F32)] * 2,
        scratch_shapes=[pltpu.VMEM((keys, width), BF16)] * 3,
        input_output_aliases={4: 0, 5: 1},
        compiler_params=params(),
        cost_estimate=pl.CostEstimate(
            flops=4 * keys * width * width + 16 * rows * keys * width,
            bytes_accessed=4 * width * width + 20 * rows * width,
            transcendentals=HEADS * rows * keys,
        ),
        name="piece_part",
    )(x, gains, w_attn, q, num, den, qcol, kdoc, qdoc, kdoc)


def finish_part(x, num, den, w_attn, gains, w_up, w_down):
    rows, width = x.shape
    hidden = w_up.shape[1]
    tile = min(512, hidden)
    return pl.pallas_call(
        finish_kernel,
        grid=(hidden // tile,),
        in_specs=[
            whole((rows, width)),
            whole((rows, width)),
            whole((rows, width)),
            pl.BlockSpec((None, width, width), lambda i: (3, 0, 0)),
            whole(gains.shape),
            pl.BlockSpec((width, tile), lambda i: (0, i)),
            pl.BlockSpec((tile, width), lambda i: (i, 0)),
        ],
        out_specs=whole((rows, width)),
        out_shape=jax.ShapeDtypeStruct((rows, width), BF16),
        scratch_shapes=[pltpu.VMEM((rows, width), F32), pltpu.VMEM((rows, width), BF16)],
        compiler_params=params(),
        cost_estimate=pl.CostEstimate(
            flops=2 * rows * width * width + 4 * rows * width * hidden,
            bytes_accessed=2 * width * width + 4 * width * hidden + 12 * rows * width,
            transcendentals=rows * hidden,
        ),
        name="finish_part",
    )(x, num, den, w_attn, gains, w_up, w_down)


def shifted(value, axis, steps):
    count = lax.axis_size(axis)
    first, last = max(0, -steps), min(count, count - steps)
    return lax.ppermute(value, axis, [(i, i + steps) for i in range(first, last)])


def swapped(value, axis, bit):
    return lax.ppermute(value, axis, [(i, i ^ bit) for i in range(lax.axis_size(axis))])


def section(x, docs, hops, w_attn, w_up, w_down, gains):
    qcol, doc_pieces = docs
    qdoc = doc_pieces[0]
    piece = shifted(x, "seq", 1) if hops else None
    q, num, den = own_part(x, gains, w_attn, qcol, qdoc)
    for hop in range(1, hops + 1):
        here = piece
        if hop < hops:
            piece = shifted(here, "seq", 1)
        num, den = piece_part(here, gains, w_attn, q, num, den, qcol, qdoc, doc_pieces[hop])
    return finish_part(x, num, den, w_attn, gains, w_up, w_down)


def corrections(fine, following, gain):
    count = lax.axis_size("depth")
    place = lax.axis_index("depth")
    rows = fine.shape[0]
    half = rows // 2
    odd = place % 2 == 1
    mismatch = fine.astype(F32) - following.astype(F32)
    low, high = mismatch[:half], mismatch[half:]
    mine = jnp.where(odd, high, low)
    other = swapped(jnp.where(odd, low, high).astype(BF16), "depth", 1).astype(F32)
    m_even, m_odd = jnp.where(odd, other, mine), jnp.where(odd, mine, other)
    gain_other = swapped(gain, "depth", 1)
    g_even, g_odd = jnp.where(odd, gain_other, gain), jnp.where(odd, gain, gain_other)
    total, factor = g_odd * m_even + m_odd, g_even * g_odd
    before, factor_before = jnp.zeros_like(total), jnp.ones_like(factor)
    bit = 2
    while bit < count:
        upper = (place // bit) % 2 == 1
        if 2 * bit < count:
            theirs = swapped(total.astype(BF16), "depth", bit).astype(F32)
            their_factor = swapped(factor, "depth", bit)
            total_next = jnp.where(upper, factor * theirs + total, their_factor * total + theirs)
            factor_next = factor * their_factor
        else:
            theirs = lax.ppermute(
                total.astype(BF16), "depth", [(i, i + bit) for i in range(count) if not i & bit]
            ).astype(F32)
            their_factor = factor
            total_next, factor_next = total, factor
        before = jnp.where(upper, factor_before * theirs + before, before)
        factor_before = jnp.where(upper, factor_before * their_factor, factor_before)
        total, factor = total_next, factor_next
        bit *= 2
    c_even, c_odd = before, g_even * before + m_even
    mine = jnp.where(odd, c_odd, c_even)
    other = swapped(jnp.where(odd, c_even, c_odd).astype(BF16), "depth", 1).astype(F32)
    return jnp.concatenate([jnp.where(odd, other, mine), jnp.where(odd, mine, other)], axis=0)


def on_device(interfaces, doc_ids, w_attn, w_up, w_down, norm_gains, coarse_gain):
    rows = interfaces.shape[2]
    length = doc_ids.shape[1]
    longest = length // 2
    hops = min(lax.axis_size("seq") - 1, -(-(longest - 1) // rows))
    my_seq = lax.axis_index("seq")
    x = interfaces[0, 0]
    following = shifted(x, "depth", -1)

    def doc_piece(hop):
        start = (my_seq - hop) * rows
        ids = lax.dynamic_slice_in_dim(doc_ids, jnp.maximum(start, 0), rows, 1)
        return jnp.where(start >= 0, ids, -1)

    doc_pieces = [doc_piece(hop) for hop in range(hops + 1)]
    qcol = jnp.broadcast_to(doc_pieces[0].reshape(rows, 1), (rows, LANES))
    layer = functools.partial(
        section,
        docs=(qcol, doc_pieces),
        hops=hops,
        w_attn=w_attn[0, 0],
        w_up=w_up[0, 0],
        w_down=w_down[0, 0],
        gains=norm_gains[0, 0],
    )
    fine = layer(x)
    correction = corrections(fine, following, coarse_gain)
    corrected = (x.astype(F32) + correction).astype(BF16)
    return layer(corrected)[None, None]


def solution(mesh):
    in_specs = (
        P("depth", None, "seq", None),
        P(),
        P("depth", None, None, None, None),
        P("depth", None, None, None),
        P("depth", None, None, None),
        P("depth", None, None, None),
        P("depth", None),
    )
    out_specs = P("depth", None, "seq", None)
    return jax.shard_map(
        on_device, mesh=mesh, in_specs=in_specs, out_specs=out_specs, check_vma=False
    )
```

```python
import jax
import jax.numpy as jnp
from jax import lax
from jax.experimental import pallas as pl
from jax.experimental.pallas import tpu as pltpu
from jax.sharding import PartitionSpec as P

HEADS = 16
LANES = 128
BLOCK = 256
VMEM_BYTES = 48 * 1024 * 1024
COST = pl.CostEstimate(flops=1 << 20, bytes_accessed=1 << 16, transcendentals=0)
F32 = jnp.float32
BF16 = jnp.bfloat16


def rms_norm(value, gain):
    return value * lax.rsqrt(jnp.mean(value * value, axis=-1, keepdims=True) + 1e-05) * gain


def dot(a, b):
    return jnp.dot(a, b, preferred_element_type=F32)


def attend(q_ref, k_ref, v_ref, num_ref, den_ref, qcol_ref, krow_ref, qdoc_ref, kdoc_ref, causal):
    rows, width = q_ref.shape
    keys = k_ref.shape[0]
    head_dim = width // HEADS
    per_tile = LANES // head_dim
    q_block, k_block = min(BLOCK, rows), min(BLOCK, keys)
    lane = lax.broadcasted_iota(jnp.int32, (1, LANES), 1)
    members = [lane // head_dim == i for i in range(per_tile)]
    count_q, count_k = rows // q_block, keys // k_block

    def one(index, carry):
        qi, ki = index // count_k, index % count_k
        q0 = pl.multiple_of(qi * q_block, q_block)
        k0 = pl.multiple_of(ki * k_block, k_block)
        needed = kdoc_ref[0, k0 + k_block - 1] >= qdoc_ref[0, q0]
        if causal:
            needed = (k0 <= q0) & (needed | (k0 == q0))

        @pl.when(needed)
        def _():
            allowed = qcol_ref[pl.ds(q0, q_block), :1] == krow_ref[:, pl.ds(k0, k_block)]
            if causal:
                q_pos = q0 + lax.broadcasted_iota(jnp.int32, (q_block, k_block), 0)
                k_pos = k0 + lax.broadcasted_iota(jnp.int32, (q_block, k_block), 1)
                allowed = allowed & (k_pos <= q_pos)
            ones = jnp.ones((k_block, LANES), BF16)
            den = jnp.zeros((q_block, LANES), F32)
            for tile in range(width // LANES):
                cols = slice(tile * LANES, (tile + 1) * LANES)
                queries = q_ref[pl.ds(q0, q_block), cols]
                keys_here = k_ref[pl.ds(k0, k_block), cols]
                values = jnp.concatenate([v_ref[pl.ds(k0, k_block), cols], ones], axis=1)
                num = None
                for i, member in enumerate(members):
                    scores = lax.dot_general(
                        jnp.where(member, queries, jnp.zeros_like(queries)),
                        keys_here,
                        (((1,), (1,)), ((), ())),
                        preferred_element_type=F32,
                    )
                    weights = jnp.where(allowed, jnp.exp(scores), 0.0).astype(BF16)
                    out = dot(weights, values)
                    num = out[:, :LANES] if num is None else jnp.where(member, out[:, :LANES], num)
                    den = jnp.where(lane == tile * per_tile + i, out[:, LANES:], den)
                num_ref[pl.ds(q0, q_block), cols] += num
            den_ref[pl.ds(q0, q_block), :] += den

        return carry

    lax.fori_loop(0, count_q * count_k, one, 0)


def spread(per_head, width):
    shape = (LANES, width)
    chosen = lax.broadcasted_iota(jnp.int32, shape, 1) // (width // HEADS) == lax.broadcasted_iota(jnp.int32, shape, 0)
    chosen = jnp.where(chosen, 1.0, 0.0).astype(BF16)
    high = per_head.astype(BF16)
    return dot(high, chosen) + dot((per_head - high.astype(F32)).astype(BF16), chosen)


def normed(x_ref, gain_ref):
    return rms_norm(x_ref[...].astype(F32), gain_ref[0:1]).astype(BF16)


def scaled_queries(n, w, head_dim):
    return dot(n, w).astype(BF16) * jnp.asarray(head_dim ** (-0.5), BF16)


def own_kernel(x_ref, gain_ref, w_ref, qcol_ref, krow_ref, doc_ref, q_ref, num_ref, den_ref, n_ref, k_ref, v_ref):
    step = pl.program_id(0)

    @pl.when(step == 0)
    def _():
        n_ref[...] = normed(x_ref, gain_ref)
        q_ref[...] = scaled_queries(n_ref[...], w_ref[...], x_ref.shape[1] // HEADS)

    @pl.when(step == 1)
    def _():
        k_ref[...] = dot(n_ref[...], w_ref[...]).astype(BF16)

    @pl.when(step == 2)
    def _():
        v_ref[...] = dot(n_ref[...], w_ref[...]).astype(BF16)
        num_ref[...] = jnp.zeros_like(num_ref)
        den_ref[...] = jnp.zeros_like(den_ref)
        attend(q_ref, k_ref, v_ref, num_ref, den_ref, qcol_ref, krow_ref, doc_ref, doc_ref, True)


def piece_kernel(
    x_ref, gain_ref, w_ref, q_ref, num_in, den_in, qcol_ref, krow_ref, qdoc_ref, kdoc_ref,
    num_ref, den_ref, n_ref, k_ref, v_ref,
):
    step = pl.program_id(0)
    needed = kdoc_ref[0, kdoc_ref.shape[1] - 1] >= qdoc_ref[0, 0]

    @pl.when(needed & (step == 0))
    def _():
        n_ref[...] = normed(x_ref, gain_ref)
        k_ref[...] = dot(n_ref[...], w_ref[...]).astype(BF16)

    @pl.when(step == 1)
    def _():
        num_ref[...] = num_in[...]
        den_ref[...] = den_in[...]

    @pl.when(needed & (step == 1))
    def _():
        v_ref[...] = dot(n_ref[...], w_ref[...]).astype(BF16)
        attend(q_ref, k_ref, v_ref, num_ref, den_ref, qcol_ref, krow_ref, qdoc_ref, kdoc_ref, False)


def back_kernel(
    x_ref, p0_ref, p1_ref, gain_ref, w_ref, qcol_ref, krow_ref, qdoc_ref, kdoc_ref,
    out_ref, q_ref, n_ref, k_ref, v_ref, num_ref, den_ref,
):
    step = pl.program_id(0)
    half, width = x_ref.shape
    needed = kdoc_ref[0, kdoc_ref.shape[1] - 1] >= qdoc_ref[0, 0]

    @pl.when(needed & (step == 0))
    def _():
        q_ref[...] = scaled_queries(normed(x_ref, gain_ref), w_ref[...], width // HEADS)
        n_ref[:half] = normed(p0_ref, gain_ref)
        n_ref[half:] = normed(p1_ref, gain_ref)

    @pl.when(needed & (step == 1))
    def _():
        k_ref[...] = dot(n_ref[...], w_ref[...]).astype(BF16)

    @pl.when(step == 2)
    def _():
        num_ref[...] = jnp.zeros_like(num_ref)
        den_ref[...] = jnp.zeros_like(den_ref)

        @pl.when(needed)
        def _():
            v_ref[...] = dot(n_ref[...], w_ref[...]).astype(BF16)
            attend(q_ref, k_ref, v_ref, num_ref, den_ref, qcol_ref, krow_ref, qdoc_ref, kdoc_ref, False)

        out_ref[:, :width] = num_ref[...].astype(BF16)
        out_ref[:, width:] = den_ref[...].astype(BF16)


def finish_kernel(x_ref, num_ref, den_ref, wo_ref, gain_ref, up_ref, down_ref, out_ref, acc_ref, n_ref):
    step = pl.program_id(0)

    @pl.when(step == 0)
    def _():
        lane = lax.broadcasted_iota(jnp.int32, den_ref.shape, 1)
        inverse = 1.0 / jnp.where(lane < HEADS, den_ref[...], 1.0)
        attended = (num_ref[...] * spread(inverse, num_ref.shape[1])).astype(BF16)
        mixed = x_ref[...].astype(F32) + dot(attended, wo_ref[...])
        acc_ref[...] = mixed
        n_ref[...] = rms_norm(mixed, gain_ref[1:2]).astype(BF16)

    expanded = jax.nn.gelu(dot(n_ref[...], up_ref[...])).astype(BF16)
    acc_ref[...] += dot(expanded, down_ref[...])

    @pl.when(step == pl.num_programs(0) - 1)
    def _():
        out_ref[...] = acc_ref[...].astype(BF16)


def whole(shape):
    return pl.BlockSpec(shape, lambda *_: (0,) * len(shape))


def smem():
    return pl.BlockSpec(memory_space=pltpu.SMEM)


def params():
    return pltpu.CompilerParams(vmem_limit_bytes=VMEM_BYTES, dimension_semantics=("arbitrary",))


def own_part(x, gains, w_attn, qcol, doc):
    rows, width = x.shape
    return pl.pallas_call(
        own_kernel,
        grid=(3,),
        in_specs=[
            whole((rows, width)),
            whole(gains.shape),
            pl.BlockSpec((None, width, width), lambda i: (i, 0, 0)),
            whole((rows, LANES)),
            whole((1, rows)),
            smem(),
        ],
        out_specs=[whole((rows, width)), whole((rows, width)), whole((rows, LANES))],
        out_shape=[
            jax.ShapeDtypeStruct((rows, width), BF16),
            jax.ShapeDtypeStruct((rows, width), F32),
            jax.ShapeDtypeStruct((rows, LANES), F32),
        ],
        scratch_shapes=[pltpu.VMEM((rows, width), BF16)] * 3,
        compiler_params=params(),
        cost_estimate=COST,
        name="own_part",
    )(x, gains, w_attn, qcol, doc, doc)


def piece_part(x, gains, w_attn, q, num, den, qcol, qdoc, kdoc):
    rows, width = q.shape
    keys = x.shape[0]
    return pl.pallas_call(
        piece_kernel,
        grid=(2,),
        in_specs=[
            whole((keys, width)),
            whole(gains.shape),
            pl.BlockSpec((None, width, width), lambda i: (i + 1, 0, 0)),
            whole((rows, width)),
            whole((rows, width)),
            whole((rows, LANES)),
            whole((rows, LANES)),
            whole((1, keys)),
            smem(),
            smem(),
        ],
        out_specs=[whole((rows, width)), whole((rows, LANES))],
        out_shape=[jax.ShapeDtypeStruct((rows, width), F32), jax.ShapeDtypeStruct((rows, LANES), F32)],
        scratch_shapes=[pltpu.VMEM((keys, width), BF16)] * 3,
        input_output_aliases={4: 0, 5: 1},
        compiler_params=params(),
        cost_estimate=COST,
        name="piece_part",
    )(x, gains, w_attn, q, num, den, qcol, kdoc, qdoc, kdoc)


def back_part(x, pieces, gains, w_attn, qcol, qdoc, kdoc):
    half, width = x.shape
    keys = 2 * half
    return pl.pallas_call(
        back_kernel,
        grid=(3,),
        in_specs=[
            whole((half, width)),
            whole((half, width)),
            whole((half, width)),
            whole(gains.shape),
            pl.BlockSpec((None, width, width), lambda i: (i, 0, 0)),
            whole((half, LANES)),
            whole((1, keys)),
            smem(),
            smem(),
        ],
        out_specs=whole((half, width + LANES)),
        out_shape=jax.ShapeDtypeStruct((half, width + LANES), BF16),
        scratch_shapes=[
            pltpu.VMEM((half, width), BF16),
            pltpu.VMEM((keys, width), BF16),
            pltpu.VMEM((keys, width), BF16),
            pltpu.VMEM((keys, width), BF16),
            pltpu.VMEM((half, width), F32),
            pltpu.VMEM((half, LANES), F32),
        ],
        compiler_params=params(),
        cost_estimate=COST,
        name="back_part",
    )(x, *pieces, gains, w_attn, qcol, kdoc, qdoc, kdoc)


def finish_part(x, num, den, w_attn, gains, w_up, w_down, part, parts):
    width = x.shape[1]
    rows = x.shape[0] // parts
    hidden = w_up.shape[1]
    tile = min(512, hidden)
    return pl.pallas_call(
        finish_kernel,
        grid=(hidden // tile,),
        in_specs=[
            pl.BlockSpec((rows, width), lambda i: (part, 0)),
            pl.BlockSpec((rows, width), lambda i: (part, 0)),
            pl.BlockSpec((rows, LANES), lambda i: (part, 0)),
            pl.BlockSpec((None, width, width), lambda i: (3, 0, 0)),
            whole(gains.shape),
            pl.BlockSpec((width, tile), lambda i: (0, i)),
            pl.BlockSpec((tile, width), lambda i: (i, 0)),
        ],
        out_specs=whole((rows, width)),
        out_shape=jax.ShapeDtypeStruct((rows, width), BF16),
        scratch_shapes=[pltpu.VMEM((rows, width), F32), pltpu.VMEM((rows, width), BF16)],
        compiler_params=params(),
        cost_estimate=COST,
        name="finish_part",
    )(x, num, den, w_attn, gains, w_up, w_down)


def shifted(value, axis, steps):
    count = lax.axis_size(axis)
    first, last = max(0, -steps), min(count, count - steps)
    return lax.ppermute(value, axis, [(i, i + steps) for i in range(first, last)])


def swapped(value, axis, bit):
    return lax.ppermute(value, axis, [(i, i ^ bit) for i in range(lax.axis_size(axis))])


class Documents:
    def __init__(self, doc_ids, rows):
        count = lax.axis_size("seq")
        self.ids, self.rows, self.half = doc_ids, rows, rows // 2
        longest = doc_ids.shape[1] // 2
        self.hops = min(count - 1, -(-(longest - 1) // rows))
        self.short = self.hops == 2 and longest <= 2 * rows and rows % 2 == 0
        self.place = lax.axis_index("seq")
        ids = doc_ids[0]
        if self.short:
            far, near = jnp.asarray(False), jnp.asarray(False)
            for middle in range(1, count - 1):
                start, end = middle * rows, (middle + 1) * rows
                over = ids[start - 1] == ids[end]
                near = near | (over & (ids[start - self.half - 1] != ids[end]))
                far = far | (over & (ids[start - self.half - 1] == ids[end]))
            self.case = jnp.where(far, 2, jnp.where(near, 1, 0)).astype(jnp.int32)

    def piece(self, shift, first, size):
        shard = self.place - shift
        start = jnp.clip(shard * self.rows + first, 0, self.ids.shape[1] - size)
        ids = lax.dynamic_slice_in_dim(self.ids, start, size, 1)
        inside = (shard >= 0) & (shard < lax.axis_size("seq"))
        return jnp.where(inside, ids, -1)

    def column(self, ids):
        return jnp.broadcast_to(ids.reshape(-1, 1), (ids.shape[1], LANES))


def attention(x, halves, first_back, docs, w_attn, gains):
    rows, half = docs.rows, docs.half
    own_ids = docs.piece(0, 0, rows)
    qcol = docs.column(own_ids)
    q, num, den = own_part(x, gains, w_attn, qcol, own_ids)

    def add(piece, shift, first, state):
        ids = docs.piece(shift, first, piece.shape[0])
        return piece_part(piece, gains, w_attn, q, *state, qcol, own_ids, ids)

    state = add(halves[0], 1, 0, (num, den))
    if not docs.short:
        state = add(halves[1], 1, half, state)
        pieces = halves
        for hop in range(2, docs.hops + 1):
            pieces = [shifted(piece, "seq", 1) for piece in pieces]
            for i, piece in enumerate(pieces):
                state = add(piece, hop, i * half, state)
        return state

    def nothing(halves, first_back, state):
        return tuple(add(halves[1], 1, half, state))

    def relay(halves, first_back, state):
        further = shifted(halves[1], "seq", 1)
        state = add(halves[1], 1, half, state)
        return tuple(add(further, 2, half, state))

    def back(halves, first_back, state):
        later_ids = docs.piece(-1, 0, half)
        later_ids = jnp.where(later_ids < 0, jnp.iinfo(jnp.int32).max, later_ids)
        sums = back_part(
            first_back, halves, gains, w_attn, docs.column(later_ids), later_ids, docs.piece(1, 0, rows)
        )
        sums = shifted(sums, "seq", 1).astype(F32)
        num, den = add(halves[1], 1, half, state)
        width = num.shape[1]
        return num.at[:half].add(sums[:, :width]), den.at[:half].add(sums[:, width:])

    return lax.switch(docs.case, [nothing, relay, back], halves, first_back, tuple(state))


def gain_factors(gain):
    count, place = lax.axis_size("depth"), lax.axis_index("depth")
    odd = place % 2 == 1
    other = swapped(gain, "depth", 1)
    even_gain, odd_gain = jnp.where(odd, other, gain), jnp.where(odd, gain, other)
    factor, factor_before, levels, bit = even_gain * odd_gain, jnp.ones_like(gain), [], 2
    while bit < count:
        theirs = swapped(factor, "depth", bit) if 2 * bit < count else factor
        levels.append((bit, factor, theirs, factor_before))
        upper = (place // bit) % 2 == 1
        factor_before = jnp.where(upper, factor_before * theirs, factor_before)
        factor = factor * theirs
        bit *= 2
    return even_gain, odd_gain, levels


def after(value, *earlier):
    return lax.optimization_barrier((value, *earlier))[0]


class Chain:
    def __init__(self, states, following, factors):
        self.states, self.following = states, following
        self.even_gain, self.odd_gain, self.levels = factors
        self.count, self.place = lax.axis_size("depth"), lax.axis_index("depth")
        self.odd = self.place % 2 == 1

    def enter(self, fine, *earlier):
        half = fine.shape[0] // 2
        mismatch = fine.astype(F32) - self.following.astype(F32)
        low, high = mismatch[:half], mismatch[half:]
        mine = jnp.where(self.odd, high, low)
        sent = jnp.where(self.odd, low, high).astype(BF16)
        other = swapped(after(sent, *earlier), "depth", 1).astype(F32)
        self.m_even = jnp.where(self.odd, other, mine)
        self.total = self.odd_gain * self.m_even + jnp.where(self.odd, mine, other)
        self.before = jnp.zeros_like(self.total)
        self.entered = self.total

    def level(self, index, sent_after=(), used_after=()):
        bit, factor, their_factor, factor_before = self.levels[index]
        upper = (self.place // bit) % 2 == 1
        sent = after(self.total.astype(BF16), *sent_after)
        if index + 1 < len(self.levels):
            theirs = after(swapped(sent, "depth", bit), *used_after).astype(F32)
            self.total = jnp.where(upper, factor * theirs + self.total, their_factor * self.total + theirs)
        else:
            pairs = [(i, i + bit) for i in range(self.count) if not i & bit]
            theirs = after(lax.ppermute(sent, "depth", pairs), *used_after).astype(F32)
        self.before = jnp.where(upper, factor_before * theirs + self.before, self.before)

    def leave(self):
        odd, c_even = self.odd, self.before
        c_odd = self.even_gain * c_even + self.m_even
        mine = jnp.where(odd, c_odd, c_even)
        other = swapped(jnp.where(odd, c_even, c_odd).astype(BF16), "depth", 1).astype(F32)
        correction = jnp.concatenate([jnp.where(odd, other, mine), jnp.where(odd, mine, other)], axis=0)
        return (self.states.astype(F32) + correction).astype(BF16)


def on_device(interfaces, doc_ids, w_attn, w_up, w_down, norm_gains, coarse_gain):
    x = interfaces[0, 0]
    rows = x.shape[0]
    half = rows // 2
    w_attn, w_up, w_down, gains = w_attn[0, 0], w_up[0, 0], w_down[0, 0], norm_gains[0, 0]
    docs = Documents(doc_ids, rows)
    parts = [x[:half], x[half:]]
    halves = [shifted(part, "seq", 1) for part in parts]
    first_back = shifted(parts[0], "seq", -1)
    following = [shifted(part, "depth", -1) for part in parts]
    factors = gain_factors(coarse_gain)
    early = after(x, *jax.tree.leaves(factors))
    num, den = attention(early, halves, first_back, docs, w_attn, gains)
    first, second = [Chain(parts[i], following[i], factors) for i in range(2)]
    first.enter(finish_part(x, num, den, w_attn, gains, w_up, w_down, 0, 2))
    fine = finish_part(x, after(num, first.total), den, w_attn, gains, w_up, w_down, 1, 2)
    first.level(0)
    second.enter(fine, first.total)
    for i in range(1, len(first.levels)):
        second.level(i - 1)
        first.level(i, used_after=(second.entered,))
    corrected = [first.leave()]
    second.level(len(first.levels) - 1, sent_after=(corrected[0],))
    corrected.append(second.leave())
    halves = [shifted(part, "seq", 1) for part in corrected]
    first_back = shifted(corrected[0], "seq", -1)
    x = jnp.concatenate(corrected, axis=0)
    num, den = attention(x, halves, first_back, docs, w_attn, gains)
    return finish_part(x, num, den, w_attn, gains, w_up, w_down, 0, 1)[None, None]


def solution(mesh):
    in_specs = (
        P("depth", None, "seq", None),
        P(),
        P("depth", None, None, None, None),
        P("depth", None, None, None),
        P("depth", None, None, None),
        P("depth", None, None, None),
        P("depth", None),
    )
    out_specs = P("depth", None, "seq", None)
    return jax.shard_map(
        on_device, mesh=mesh, in_specs=in_specs, out_specs=out_specs, check_vma=False
    )
```

```python
import functools

import jax
import jax.numpy as jnp
from jax import lax
from jax.experimental import pallas as pl
from jax.experimental.pallas import tpu as pltpu
from jax.sharding import PartitionSpec as P

HEADS = 16
LANES = 128
BLOCK = 256
TILE = 512
VMEM_BYTES = 12 * 1024 * 1024
COST = pl.CostEstimate(flops=1 << 20, bytes_accessed=1 << 16, transcendentals=0)
F32 = jnp.float32
BF16 = jnp.bfloat16


def rms_norm(value, gain):
    return value * lax.rsqrt(jnp.mean(value * value, axis=-1, keepdims=True) + 1e-05) * gain


def dot(a, b):
    return jnp.dot(a, b, preferred_element_type=F32)


def attend(q_ref, k_ref, v_ref, num_ref, den_ref, column_ref, row_ref, doc_ref, q_at, k_at, causal=False):
    rows, width = q_ref.shape
    keys = k_ref.shape[0]
    head_dim = width // HEADS
    per_tile = LANES // head_dim
    q_block, k_block = min(BLOCK, rows), min(BLOCK, keys)
    lane = lax.broadcasted_iota(jnp.int32, (1, LANES), 1)
    members = [lane // head_dim == i for i in range(per_tile)]
    count_q, count_k = rows // q_block, keys // k_block

    def one(index, carry):
        qi, ki = index // count_k, index % count_k
        q0 = pl.multiple_of(qi * q_block, q_block)
        k0 = pl.multiple_of(ki * k_block, k_block)
        needed = doc_ref[0, k_at + k0 + k_block - 1] >= doc_ref[0, q_at + q0]
        if causal:
            needed = (k0 <= q0) & (needed | (k0 == q0))

        @pl.when(needed)
        def _():
            key_docs = row_ref[:, pl.ds(pl.multiple_of(k_at + k0, k_block), k_block)]
            allowed = column_ref[pl.ds(q0, q_block), :1] == key_docs
            if causal:
                q_pos = q0 + lax.broadcasted_iota(jnp.int32, (q_block, k_block), 0)
                k_pos = k0 + lax.broadcasted_iota(jnp.int32, (q_block, k_block), 1)
                allowed = allowed & (k_pos <= q_pos)
            ones = jnp.ones((k_block, LANES), BF16)
            den = jnp.zeros((q_block, LANES), F32)
            for tile in range(width // LANES):
                cols = slice(tile * LANES, (tile + 1) * LANES)
                queries = q_ref[pl.ds(q0, q_block), cols]
                keys_here = k_ref[pl.ds(k0, k_block), cols]
                values = jnp.concatenate([v_ref[pl.ds(k0, k_block), cols], ones], axis=1)
                num = None
                for i, member in enumerate(members):
                    scores = lax.dot_general(
                        jnp.where(member, queries, jnp.zeros_like(queries)),
                        keys_here,
                        (((1,), (1,)), ((), ())),
                        preferred_element_type=F32,
                    )
                    weights = jnp.where(allowed, jnp.exp(scores), 0.0).astype(BF16)
                    out = dot(weights, values)
                    num = out[:, :LANES] if num is None else jnp.where(member, out[:, :LANES], num)
                    den = jnp.where(lane == tile * per_tile + i, out[:, LANES:], den)
                num_ref[pl.ds(q0, q_block), cols] += num
            den_ref[pl.ds(q0, q_block), :] += den

        return carry

    lax.fori_loop(0, count_q * count_k, one, 0)


def spread(per_head, width):
    shape = (LANES, width)
    chosen = lax.broadcasted_iota(jnp.int32, shape, 1) // (width // HEADS) == lax.broadcasted_iota(jnp.int32, shape, 0)
    chosen = jnp.where(chosen, 1.0, 0.0).astype(BF16)
    high = per_head.astype(BF16)
    return dot(high, chosen) + dot((per_head - high.astype(F32)).astype(BF16), chosen)


def normed(x_ref, gain_ref):
    return rms_norm(x_ref[...].astype(F32), gain_ref[0:1]).astype(BF16)


def project(n_ref, w_ref, index, out_ref, scale=None):
    width = w_ref.shape[2]
    tile = min(TILE, width)

    def one(j, carry):
        cols = pl.ds(pl.multiple_of(j * tile, tile), tile)
        out = dot(n_ref[...], w_ref[index, :, cols]).astype(BF16)
        out_ref[:, cols] = out if scale is None else out * jnp.asarray(scale, BF16)
        return carry

    lax.fori_loop(0, width // tile, one, 0)


def own_kernel(
    x_ref, gain_ref, w_ref, column_ref, row_ref, doc_ref, q_ref, num_ref, den_ref, n_ref, k_ref, v_ref
):
    head_dim = x_ref.shape[1] // HEADS
    here = lax.axis_index("seq") * x_ref.shape[0]
    n_ref[...] = normed(x_ref, gain_ref)
    project(n_ref, w_ref, 0, q_ref, head_dim ** (-0.5))
    project(n_ref, w_ref, 1, k_ref)
    project(n_ref, w_ref, 2, v_ref)
    num_ref[...] = jnp.zeros_like(num_ref)
    den_ref[...] = jnp.zeros_like(den_ref)
    attend(q_ref, k_ref, v_ref, num_ref, den_ref, column_ref, row_ref, doc_ref, here, here, True)


def piece_kernel(
    shift, first, x_ref, gain_ref, w_ref, q_ref, num_in, den_in, column_ref, row_ref, doc_ref,
    num_ref, den_ref, n_ref, k_ref, v_ref,
):
    del num_in, den_in
    rows, keys = q_ref.shape[0], x_ref.shape[0]
    shard = lax.axis_index("seq") - shift
    here, there = (shard + shift) * rows, jnp.maximum(shard, 0) * rows + first

    @pl.when((shard >= 0) & (doc_ref[0, there + keys - 1] >= doc_ref[0, here]))
    def _():
        n_ref[...] = normed(x_ref, gain_ref)
        project(n_ref, w_ref, 1, k_ref)
        project(n_ref, w_ref, 2, v_ref)
        attend(q_ref, k_ref, v_ref, num_ref, den_ref, column_ref, row_ref, doc_ref, here, there)


def far_document(doc_ref, rows, count):
    found = False
    for middle in range(1, count - 1):
        over = doc_ref[0, middle * rows - 1] == doc_ref[0, (middle + 1) * rows]
        deep = doc_ref[0, middle * rows - rows // 2 - 1] == doc_ref[0, (middle + 1) * rows]
        found = found | (over & deep)
    return found


def message_kernel(
    x_ref, p0_ref, p1_ref, gain_ref, w_ref, column_ref, row_ref, doc_ref,
    out_ref, q_ref, n_ref, k_ref, v_ref, num_ref, den_ref,
):
    half, width = x_ref.shape
    rows = 2 * half
    count = lax.axis_size("seq")
    place = lax.axis_index("seq")
    inside = (place >= 1) & (place + 1 < count)
    here = jnp.where(inside, place + 1, 0) * rows
    there = jnp.where(inside, place - 1, 0) * rows
    far = far_document(doc_ref, rows, count)

    @pl.when(jnp.logical_not(far))
    def _():
        out_ref[:, :width] = p1_ref[...]

    @pl.when(far)
    def _():
        num_ref[...] = jnp.zeros_like(num_ref)
        den_ref[...] = jnp.zeros_like(den_ref)

        @pl.when(inside & (doc_ref[0, there + rows - 1] >= doc_ref[0, here]))
        def _():
            n_ref[:half] = normed(x_ref, gain_ref)
            project(n_ref.at[:half], w_ref, 0, q_ref, (width // HEADS) ** (-0.5))
            n_ref[:half] = normed(p0_ref, gain_ref)
            n_ref[half:] = normed(p1_ref, gain_ref)
            project(n_ref, w_ref, 1, k_ref)
            project(n_ref, w_ref, 2, v_ref)
            attend(q_ref, k_ref, v_ref, num_ref, den_ref, column_ref, row_ref, doc_ref, here, there)

        out_ref[:, :width] = num_ref[...].astype(BF16)
        out_ref[:, width:] = den_ref[...].astype(BF16)


def reply_kernel(
    message_ref, gain_ref, w_ref, q_ref, num_in, den_in, column_ref, row_ref, doc_ref,
    num_ref, den_ref, n_ref, k_ref, v_ref,
):
    rows, width = q_ref.shape
    half = message_ref.shape[0]
    far = far_document(doc_ref, rows, lax.axis_size("seq"))

    @pl.when(far)
    def _():
        num_ref[:half] += message_ref[:, :width].astype(F32)
        den_ref[:half] += message_ref[:, width:].astype(F32)

    @pl.when(jnp.logical_not(far))
    def _():
        piece_kernel(
            2, half, message_ref.at[:, :width], gain_ref, w_ref, q_ref, num_in, den_in, column_ref, row_ref, doc_ref,
            num_ref, den_ref, n_ref, k_ref, v_ref,
        )


def finish_kernel(
    first, x_ref, num_ref, den_ref, w_ref, gain_ref, up_ref, down_ref, out_ref, acc_ref, n_ref, hidden_ref
):
    rows, width = out_ref.shape
    hidden = up_ref.shape[1]
    tile = min(TILE, hidden)
    here = pl.ds(first, rows)
    lane = lax.broadcasted_iota(jnp.int32, (rows, LANES), 1)
    inverse = 1.0 / jnp.where(lane < HEADS, den_ref[here], 1.0)
    n_ref[...] = (num_ref[here] * spread(inverse, width)).astype(BF16)
    acc_ref[...] = x_ref[here].astype(F32) + dot(n_ref[...], w_ref[3])
    n_ref[...] = rms_norm(acc_ref[...], gain_ref[1:2]).astype(BF16)

    def expand(j):
        cols = pl.ds(pl.multiple_of(j * tile, tile), tile)
        return jax.nn.gelu(dot(n_ref[...], up_ref[:, cols])).astype(BF16)

    def lower(j, expanded):
        return dot(expanded, down_ref[pl.ds(pl.multiple_of(j * tile, tile), tile)])

    hidden_ref[0] = expand(0)

    def one(j, carry):
        acc_ref[...] += lower(j, hidden_ref[j % 2])
        hidden_ref[(j + 1) % 2] = expand(j + 1)
        return carry

    last = hidden // tile - 1
    lax.fori_loop(0, last, one, 0)
    out_ref[...] = (acc_ref[...] + lower(last, hidden_ref[last % 2])).astype(BF16)


def vmem():
    return pl.BlockSpec(memory_space=pltpu.VMEM)


def call(kernel, name, operands, docs, results, scratch, aliases=None, held=True):
    inputs = [pltpu.with_memory_space_constraint(operand, pltpu.VMEM) for operand in operands]
    in_specs = [vmem()] * len(inputs)
    if docs is not None:
        inputs.append(docs)
        in_specs.append(pl.BlockSpec(memory_space=pltpu.SMEM))
    return pl.pallas_call(
        kernel,
        in_specs=in_specs,
        out_specs=[vmem()] * len(results),
        out_shape=[pltpu.VMEM(*one) if held else jax.ShapeDtypeStruct(*one) for one in results],
        scratch_shapes=scratch,
        input_output_aliases=aliases or {},
        compiler_params=pltpu.CompilerParams(vmem_limit_bytes=VMEM_BYTES),
        cost_estimate=COST,
        name=name,
    )(*inputs)


def own_part(x, gains, weights, docs):
    rows, width = x.shape
    results = [((rows, width), BF16), ((rows, width), F32), ((rows, LANES), F32)]
    scratch = [pltpu.VMEM((rows, width), BF16)] * 3
    return call(own_kernel, "own_part", (x, gains, weights[0], docs.column(0), docs.ids), docs.ids, results, scratch)


def piece_part(x, shift, first, gains, w_attn, q, num, den, docs):
    rows, width = q.shape
    return call(
        functools.partial(piece_kernel, shift, first),
        "piece_part",
        (x, gains, w_attn, q, num, den, docs.column(0), docs.ids),
        docs.ids,
        [((rows, width), F32), ((rows, LANES), F32)],
        [pltpu.VMEM((x.shape[0], width), BF16)] * 3,
        aliases={4: 0, 5: 1},
    )


def message_part(x, pieces, gains, w_attn, docs):
    half, width = x.shape
    keys = 2 * half
    return call(
        message_kernel,
        "message_part",
        (x, *pieces, gains, w_attn, docs.column(1, half), docs.ids),
        docs.ids,
        [((half, width + LANES), BF16)],
        [pltpu.VMEM((half, width), BF16)]
        + [pltpu.VMEM((keys, width), BF16)] * 3
        + [pltpu.VMEM((half, width), F32), pltpu.VMEM((half, LANES), F32)],
    )[0]


def reply_part(message, gains, w_attn, q, num, den, docs):
    rows, width = q.shape
    return call(
        reply_kernel,
        "reply_part",
        (message, gains, w_attn, q, num, den, docs.column(0), docs.ids),
        docs.ids,
        [((rows, width), F32), ((rows, LANES), F32)],
        [pltpu.VMEM((message.shape[0], width), BF16)] * 3,
        aliases={4: 0, 5: 1},
    )


def finish_part(x, num, den, weights, gains, part, parts):
    width = x.shape[1]
    rows = x.shape[0] // parts
    w_attn, w_up, w_down = weights
    tile = min(TILE, w_up.shape[1])
    return call(
        functools.partial(finish_kernel, part * rows),
        "finish_part",
        (x, num, den, w_attn, gains, w_up, w_down),
        None,
        [((rows, width), BF16)],
        [pltpu.VMEM((rows, width), F32), pltpu.VMEM((rows, width), BF16), pltpu.VMEM((2, rows, tile), BF16)],
        held=parts > 1,
    )[0]


def shifted(value, axis, steps):
    count = lax.axis_size(axis)
    first, last = max(0, -steps), min(count, count - steps)
    return lax.ppermute(value, axis, [(i, i + steps) for i in range(first, last)])


def swapped(value, axis, bit):
    return lax.ppermute(value, axis, [(i, i ^ bit) for i in range(lax.axis_size(axis))])


class Documents:
    def __init__(self, doc_ids, rows):
        count = lax.axis_size("seq")
        self.ids, self.rows, self.half = doc_ids, rows, rows // 2
        longest = doc_ids.shape[1] // 2
        self.hops = min(count - 1, -(-(longest - 1) // rows))
        self.short = self.hops == 2 and longest <= 2 * rows and rows % 2 == 0
        self.place = lax.axis_index("seq")

    def column(self, later, size=None):
        size = size or self.rows
        start = jnp.minimum((self.place + later) * self.rows, self.ids.shape[1] - size)
        ids = lax.dynamic_slice_in_dim(self.ids, start, size, 1)
        return jnp.broadcast_to(ids.reshape(-1, 1), (size, LANES))


def attention(state, halves, first_back, docs, w_attn, gains):
    half = docs.half
    q, *state = state

    def add(piece, shift, first, state):
        return piece_part(piece, shift, first, gains, w_attn, q, *state, docs)

    if docs.short:
        message = shifted(message_part(first_back, halves, gains, w_attn, docs), "seq", 1)
        num, den = add(halves[1], 1, half, state)
        return reply_part(message, gains, w_attn, q, num, den, docs)
    state = add(halves[1], 1, half, state)
    pieces = halves
    for hop in range(2, docs.hops + 1):
        pieces = [shifted(piece, "seq", 1) for piece in pieces]
        for i, piece in enumerate(pieces):
            state = add(piece, hop, i * half, state)
    return state


def gain_factors(gain):
    count, place = lax.axis_size("depth"), lax.axis_index("depth")
    odd = (place & 1) == 1
    other = swapped(gain, "depth", 1)
    even_gain, odd_gain = jnp.where(odd, other, gain), jnp.where(odd, gain, other)
    factor, factor_before, levels, bit = even_gain * odd_gain, jnp.ones_like(gain), [], 2
    while bit < count:
        theirs = swapped(factor, "depth", bit) if 2 * bit < count else factor
        levels.append((bit, factor, theirs, factor_before))
        upper = (place & bit) != 0
        factor_before = jnp.where(upper, factor_before * theirs, factor_before)
        factor = factor * theirs
        bit *= 2
    return even_gain, odd_gain, levels


def after(value, *earlier):
    return lax.optimization_barrier((value, *earlier))[0]


class Chain:
    def __init__(self, states, following, factors):
        self.states, self.following = states, following
        self.even_gain, self.odd_gain, self.levels = factors
        self.count, self.place = lax.axis_size("depth"), lax.axis_index("depth")
        self.odd = (self.place & 1) == 1

    def enter(self, fine, *earlier):
        half = fine.shape[0] // 2
        mismatch = fine.astype(F32) - self.following.astype(F32)
        low, high = mismatch[:half], mismatch[half:]
        mine = jnp.where(self.odd, high, low)
        sent = jnp.where(self.odd, low, high).astype(BF16)
        other = swapped(after(sent, *earlier), "depth", 1).astype(F32)
        self.m_even = jnp.where(self.odd, other, mine)
        self.total = self.odd_gain * self.m_even + jnp.where(self.odd, mine, other)
        self.before = jnp.zeros_like(self.total)
        self.entered = self.total

    def level(self, index, sent_after=(), used_after=()):
        bit, factor, their_factor, factor_before = self.levels[index]
        upper = (self.place & bit) != 0
        sent = after(self.total.astype(BF16), *sent_after)
        if index + 1 < len(self.levels):
            theirs = after(swapped(sent, "depth", bit), *used_after).astype(F32)
            self.total = jnp.where(upper, factor * theirs + self.total, their_factor * self.total + theirs)
        else:
            pairs = [(i, i + bit) for i in range(self.count) if not i & bit]
            theirs = after(lax.ppermute(sent, "depth", pairs), *used_after).astype(F32)
        self.before = jnp.where(upper, factor_before * theirs + self.before, self.before)

    def leave(self):
        odd, c_even = self.odd, self.before
        c_odd = self.even_gain * c_even + self.m_even
        mine = jnp.where(odd, c_odd, c_even)
        other = swapped(jnp.where(odd, c_even, c_odd).astype(BF16), "depth", 1).astype(F32)
        correction = jnp.concatenate([jnp.where(odd, other, mine), jnp.where(odd, mine, other)], axis=0)
        return (self.states.astype(F32) + correction).astype(BF16)


def on_device(interfaces, doc_ids, w_attn, w_up, w_down, norm_gains, coarse_gain):
    x = interfaces[0, 0]
    rows = x.shape[0]
    half = rows // 2
    gains = norm_gains[0, 0]
    docs = Documents(doc_ids, rows)
    parts = [x[:half], x[half:]]
    halves = [shifted(part, "seq", 1) for part in parts]
    weights = (w_attn[0, 0], w_up[0, 0], w_down[0, 0])
    state = own_part(x, gains, weights, docs)
    state = [state[0], *piece_part(halves[0], 1, 0, gains, weights[0], *state, docs)]
    first_back = shifted(after(parts[0], state[1]), "seq", -1)
    following = [shifted(after(part, state[1]), "depth", -1) for part in parts]
    factors = gain_factors(after(coarse_gain, state[1]))
    num, den = attention(state, halves, first_back, docs, weights[0], gains)
    num = after(num, *jax.tree.leaves(factors))
    first, second = [Chain(parts[i], following[i], factors) for i in range(2)]
    first.enter(finish_part(x, num, den, weights, gains, 0, 2))
    fine = finish_part(x, after(num, first.total), den, weights, gains, 1, 2)
    first.level(0)
    second.enter(fine, first.total)
    for i in range(1, len(first.levels)):
        second.level(i - 1)
        first.level(i, used_after=(second.entered,))
    corrected = [first.leave()]
    second.level(len(first.levels) - 1, sent_after=(corrected[0],))
    corrected.append(second.leave())
    halves = [shifted(part, "seq", 1) for part in corrected]
    first_back = shifted(corrected[0], "seq", -1)
    x = jnp.concatenate(corrected, axis=0)
    state = own_part(x, gains, weights, docs)
    state = [state[0], *piece_part(halves[0], 1, 0, gains, weights[0], *state, docs)]
    num, den = attention(state, halves, first_back, docs, weights[0], gains)
    return finish_part(x, num, den, weights, gains, 0, 1)[None, None]


def solution(mesh):
    in_specs = (
        P("depth", None, "seq", None),
        P(),
        P("depth", None, None, None, None),
        P("depth", None, None, None),
        P("depth", None, None, None),
        P("depth", None, None, None),
        P("depth", None),
    )
    out_specs = P("depth", None, "seq", None)
    return jax.shard_map(
        on_device, mesh=mesh, in_specs=in_specs, out_specs=out_specs, check_vma=False
    )
```

```python
import functools

import jax
import jax.numpy as jnp
from jax import lax
from jax.experimental import pallas as pl
from jax.experimental.pallas import tpu as pltpu
from jax.sharding import PartitionSpec as P

HEADS = 16
LANES = 128
BLOCK = 256
TILE = 512
VMEM_BYTES = 12 * 1024 * 1024
COST = pl.CostEstimate(flops=1 << 20, bytes_accessed=1 << 16, transcendentals=0)
F32 = jnp.float32
BF16 = jnp.bfloat16


def rms_norm(value, gain):
    return value * lax.rsqrt(jnp.mean(value * value, axis=-1, keepdims=True) + 1e-05) * gain


def dot(a, b):
    return jnp.dot(a, b, preferred_element_type=F32)


def attend(q_ref, k_ref, v_ref, num_ref, den_ref, column_ref, row_ref, doc_ref, q_at, k_at, causal=False):
    rows, width = q_ref.shape
    keys = k_ref.shape[0]
    head_dim = width // HEADS
    per_tile = LANES // head_dim
    q_block, k_block = min(BLOCK, rows), min(BLOCK, keys)
    lane = lax.broadcasted_iota(jnp.int32, (1, LANES), 1)
    members = [lane // head_dim == i for i in range(per_tile)]
    count_q, count_k = rows // q_block, keys // k_block

    def one(index, carry):
        qi, ki = index // count_k, index % count_k
        q0 = pl.multiple_of(qi * q_block, q_block)
        k0 = pl.multiple_of(ki * k_block, k_block)
        needed = doc_ref[0, k_at + k0 + k_block - 1] >= doc_ref[0, q_at + q0]
        if causal:
            needed = (k0 <= q0) & (needed | (k0 == q0))

        @pl.when(needed)
        def _():
            key_docs = row_ref[:, pl.ds(pl.multiple_of(k_at + k0, k_block), k_block)]
            allowed = column_ref[pl.ds(q0, q_block), :1] == key_docs
            if causal:
                q_pos = q0 + lax.broadcasted_iota(jnp.int32, (q_block, k_block), 0)
                k_pos = k0 + lax.broadcasted_iota(jnp.int32, (q_block, k_block), 1)
                allowed = allowed & (k_pos <= q_pos)
            ones = jnp.ones((k_block, LANES), BF16)
            den = jnp.zeros((q_block, LANES), F32)
            for tile in range(width // LANES):
                cols = slice(tile * LANES, (tile + 1) * LANES)
                queries = q_ref[pl.ds(q0, q_block), cols]
                keys_here = k_ref[pl.ds(k0, k_block), cols]
                values = jnp.concatenate([v_ref[pl.ds(k0, k_block), cols], ones], axis=1)
                num = None
                for i, member in enumerate(members):
                    scores = lax.dot_general(
                        jnp.where(member, queries, jnp.zeros_like(queries)),
                        keys_here,
                        (((1,), (1,)), ((), ())),
                        preferred_element_type=F32,
                    )
                    weights = jnp.where(allowed, jnp.exp(scores), 0.0).astype(BF16)
                    out = dot(weights, values)
                    num = out[:, :LANES] if num is None else jnp.where(member, out[:, :LANES], num)
                    den = jnp.where(lane == tile * per_tile + i, out[:, LANES:], den)
                num_ref[pl.ds(q0, q_block), cols] += num
            den_ref[pl.ds(q0, q_block), :] += den

        return carry

    lax.fori_loop(0, count_q * count_k, one, 0)


def spread(per_head, width):
    shape = (LANES, width)
    chosen = lax.broadcasted_iota(jnp.int32, shape, 1) // (width // HEADS) == lax.broadcasted_iota(jnp.int32, shape, 0)
    chosen = jnp.where(chosen, 1.0, 0.0).astype(BF16)
    high = per_head.astype(BF16)
    return dot(high, chosen) + dot((per_head - high.astype(F32)).astype(BF16), chosen)


def normed(x_ref, gain_ref):
    return rms_norm(x_ref[...].astype(F32), gain_ref[0:1]).astype(BF16)


def project(n_ref, w_ref, index, out_ref, scale=None):
    width = w_ref.shape[2]
    tile = min(TILE, width)

    def one(j, carry):
        cols = pl.ds(pl.multiple_of(j * tile, tile), tile)
        out = dot(n_ref[...], w_ref[index, :, cols]).astype(BF16)
        out_ref[:, cols] = out if scale is None else out * jnp.asarray(scale, BF16)
        return carry

    lax.fori_loop(0, width // tile, one, 0)


def own_kernel(
    x_ref, gain_ref, w_ref, column_ref, row_ref, doc_ref, q_ref, num_ref, den_ref, n_ref, k_ref, v_ref
):
    head_dim = x_ref.shape[1] // HEADS
    here = lax.axis_index("seq") * x_ref.shape[0]
    n_ref[...] = normed(x_ref, gain_ref)
    project(n_ref, w_ref, 0, q_ref, head_dim ** (-0.5))
    project(n_ref, w_ref, 1, k_ref)
    project(n_ref, w_ref, 2, v_ref)
    num_ref[...] = jnp.zeros_like(num_ref)
    den_ref[...] = jnp.zeros_like(den_ref)
    attend(q_ref, k_ref, v_ref, num_ref, den_ref, column_ref, row_ref, doc_ref, here, here, True)


def piece_kernel(
    shift, first, x_ref, gain_ref, w_ref, q_ref, num_in, den_in, column_ref, row_ref, doc_ref,
    num_ref, den_ref, n_ref, k_ref, v_ref,
):
    del num_in, den_in
    rows, keys = q_ref.shape[0], x_ref.shape[0]
    shard = lax.axis_index("seq") - shift
    here, there = (shard + shift) * rows, jnp.maximum(shard, 0) * rows + first

    @pl.when((shard >= 0) & (doc_ref[0, there + keys - 1] >= doc_ref[0, here]))
    def _():
        n_ref[...] = normed(x_ref, gain_ref)
        project(n_ref, w_ref, 1, k_ref)
        project(n_ref, w_ref, 2, v_ref)
        attend(q_ref, k_ref, v_ref, num_ref, den_ref, column_ref, row_ref, doc_ref, here, there)


def far_document(doc_ref, rows, count):
    found = False
    for middle in range(1, count - 1):
        over = doc_ref[0, middle * rows - 1] == doc_ref[0, (middle + 1) * rows]
        deep = doc_ref[0, middle * rows - rows // 2 - 1] == doc_ref[0, (middle + 1) * rows]
        found = found | (over & deep)
    return found


def message_kernel(
    x_ref, p0_ref, p1_ref, gain_ref, w_ref, column_ref, row_ref, doc_ref,
    out_ref, q_ref, n_ref, k_ref, v_ref, num_ref, den_ref,
):
    half, width = x_ref.shape
    rows = 2 * half
    count = lax.axis_size("seq")
    place = lax.axis_index("seq")
    inside = (place >= 1) & (place + 1 < count)
    here = jnp.where(inside, place + 1, 0) * rows
    there = jnp.where(inside, place - 1, 0) * rows
    far = far_document(doc_ref, rows, count)

    @pl.when(jnp.logical_not(far))
    def _():
        out_ref[:, :width] = p1_ref[...]

    @pl.when(far)
    def _():
        num_ref[...] = jnp.zeros_like(num_ref)
        den_ref[...] = jnp.zeros_like(den_ref)

        @pl.when(inside & (doc_ref[0, there + rows - 1] >= doc_ref[0, here]))
        def _():
            n_ref[:half] = normed(x_ref, gain_ref)
            project(n_ref.at[:half], w_ref, 0, q_ref, (width // HEADS) ** (-0.5))
            n_ref[:half] = normed(p0_ref, gain_ref)
            n_ref[half:] = normed(p1_ref, gain_ref)
            project(n_ref, w_ref, 1, k_ref)
            project(n_ref, w_ref, 2, v_ref)
            attend(q_ref, k_ref, v_ref, num_ref, den_ref, column_ref, row_ref, doc_ref, here, there)

        out_ref[:, :width] = num_ref[...].astype(BF16)
        out_ref[:, width:] = den_ref[...].astype(BF16)


def reply_kernel(
    message_ref, gain_ref, w_ref, q_ref, num_in, den_in, column_ref, row_ref, doc_ref,
    num_ref, den_ref, n_ref, k_ref, v_ref,
):
    rows, width = q_ref.shape
    half = message_ref.shape[0]
    far = far_document(doc_ref, rows, lax.axis_size("seq"))

    @pl.when(far)
    def _():
        num_ref[:half] += message_ref[:, :width].astype(F32)
        den_ref[:half] += message_ref[:, width:].astype(F32)

    @pl.when(jnp.logical_not(far))
    def _():
        piece_kernel(
            2, half, message_ref.at[:, :width], gain_ref, w_ref, q_ref, num_in, den_in, column_ref, row_ref, doc_ref,
            num_ref, den_ref, n_ref, k_ref, v_ref,
        )


def finish_kernel(
    first, x_ref, num_ref, den_ref, w_ref, gain_ref, up_ref, down_ref, out_ref, acc_ref, n_ref, hidden_ref
):
    rows, width = out_ref.shape
    hidden = up_ref.shape[1]
    tile = min(TILE, hidden)
    here = pl.ds(first, rows)
    lane = lax.broadcasted_iota(jnp.int32, (rows, LANES), 1)
    inverse = 1.0 / jnp.where(lane < HEADS, den_ref[here], 1.0)
    n_ref[...] = (num_ref[here] * spread(inverse, width)).astype(BF16)
    acc_ref[...] = x_ref[here].astype(F32) + dot(n_ref[...], w_ref[3])
    n_ref[...] = rms_norm(acc_ref[...], gain_ref[1:2]).astype(BF16)

    def expand(j):
        cols = pl.ds(pl.multiple_of(j * tile, tile), tile)
        return jax.nn.gelu(dot(n_ref[...], up_ref[:, cols])).astype(BF16)

    def lower(j, expanded):
        return dot(expanded, down_ref[pl.ds(pl.multiple_of(j * tile, tile), tile)])

    hidden_ref[0] = expand(0)

    def one(j, carry):
        acc_ref[...] += lower(j, hidden_ref[j % 2])
        hidden_ref[(j + 1) % 2] = expand(j + 1)
        return carry

    last = hidden // tile - 1
    lax.fori_loop(0, last, one, 0)
    out_ref[...] = (acc_ref[...] + lower(last, hidden_ref[last % 2])).astype(BF16)


def vmem():
    return pl.BlockSpec(memory_space=pltpu.VMEM)


def call(kernel, name, operands, docs, results, scratch, aliases=None, held=True):
    inputs = [pltpu.with_memory_space_constraint(operand, pltpu.VMEM) for operand in operands]
    in_specs = [vmem()] * len(inputs)
    if docs is not None:
        inputs.append(docs)
        in_specs.append(pl.BlockSpec(memory_space=pltpu.SMEM))
    return pl.pallas_call(
        kernel,
        in_specs=in_specs,
        out_specs=[vmem()] * len(results),
        out_shape=[pltpu.VMEM(*one) if held else jax.ShapeDtypeStruct(*one) for one in results],
        scratch_shapes=scratch,
        input_output_aliases=aliases or {},
        compiler_params=pltpu.CompilerParams(vmem_limit_bytes=VMEM_BYTES),
        cost_estimate=COST,
        name=name,
    )(*inputs)


def own_part(x, gains, weights, docs):
    rows, width = x.shape
    results = [((rows, width), BF16), ((rows, width), F32), ((rows, LANES), F32)]
    scratch = [pltpu.VMEM((rows, width), BF16)] * 3
    return call(own_kernel, "own_part", (x, gains, weights[0], docs.own_column, docs.ids), docs.ids, results, scratch)


def piece_part(x, shift, first, gains, w_attn, q, num, den, docs):
    rows, width = q.shape
    return call(
        functools.partial(piece_kernel, shift, first),
        "piece_part",
        (x, gains, w_attn, q, num, den, docs.own_column, docs.ids),
        docs.ids,
        [((rows, width), F32), ((rows, LANES), F32)],
        [pltpu.VMEM((x.shape[0], width), BF16)] * 3,
        aliases={4: 0, 5: 1},
    )


def message_part(x, pieces, gains, w_attn, docs):
    half, width = x.shape
    keys = 2 * half
    return call(
        message_kernel,
        "message_part",
        (x, *pieces, gains, w_attn, docs.later_column, docs.ids),
        docs.ids,
        [((half, width + LANES), BF16)],
        [pltpu.VMEM((half, width), BF16)]
        + [pltpu.VMEM((keys, width), BF16)] * 3
        + [pltpu.VMEM((half, width), F32), pltpu.VMEM((half, LANES), F32)],
    )[0]


def reply_part(message, gains, w_attn, q, num, den, docs):
    rows, width = q.shape
    return call(
        reply_kernel,
        "reply_part",
        (message, gains, w_attn, q, num, den, docs.own_column, docs.ids),
        docs.ids,
        [((rows, width), F32), ((rows, LANES), F32)],
        [pltpu.VMEM((message.shape[0], width), BF16)] * 3,
        aliases={4: 0, 5: 1},
    )


def finish_part(x, num, den, weights, gains, part, parts):
    width = x.shape[1]
    rows = x.shape[0] // parts
    w_attn, w_up, w_down = weights
    tile = min(TILE, w_up.shape[1])
    return call(
        functools.partial(finish_kernel, part * rows),
        "finish_part",
        (x, num, den, w_attn, gains, w_up, w_down),
        None,
        [((rows, width), BF16)],
        [pltpu.VMEM((rows, width), F32), pltpu.VMEM((rows, width), BF16), pltpu.VMEM((2, rows, tile), BF16)],
        held=parts > 1,
    )[0]


def shifted(value, axis, steps):
    count = lax.axis_size(axis)
    first, last = max(0, -steps), min(count, count - steps)
    return lax.ppermute(value, axis, [(i, i + steps) for i in range(first, last)])


def swapped(value, axis, bit):
    return lax.ppermute(value, axis, [(i, i ^ bit) for i in range(lax.axis_size(axis))])


class Documents:
    def __init__(self, doc_ids, rows):
        count = lax.axis_size("seq")
        self.ids, self.rows, self.half = doc_ids, rows, rows // 2
        longest = doc_ids.shape[1] // 2
        self.hops = min(count - 1, -(-(longest - 1) // rows))
        self.short = self.hops == 2 and longest <= 2 * rows and rows % 2 == 0
        place = lax.axis_index("seq")

        def column(later, size):
            start = jnp.minimum((place + later) * rows, doc_ids.shape[1] - size)
            ids = lax.dynamic_slice_in_dim(doc_ids, start, size, 1)
            return jnp.broadcast_to(ids.reshape(-1, 1), (size, LANES))

        self.own_column = column(0, rows)
        self.later_column = column(1, self.half) if self.short else self.own_column


def attention(state, halves, first_back, docs, w_attn, gains):
    half = docs.half
    q, *state = state

    def add(piece, shift, first, state):
        return piece_part(piece, shift, first, gains, w_attn, q, *state, docs)

    if docs.short:
        message = shifted(message_part(after(first_back, q), halves, gains, w_attn, docs), "seq", 1)
        num, den = add(halves[1], 1, half, state)
        return reply_part(message, gains, w_attn, q, num, den, docs)
    state = add(halves[1], 1, half, state)
    pieces = halves
    for hop in range(2, docs.hops + 1):
        pieces = [shifted(piece, "seq", 1) for piece in pieces]
        for i, piece in enumerate(pieces):
            state = add(piece, hop, i * half, state)
    return state


def gain_factors(gain, bits):
    count = lax.axis_size("depth")
    all_gains = [gain] + [swapped(gain, "depth", i) for i in range(1, max(2, count // 2))]

    def block(first, size):
        return functools.reduce(jnp.multiply, all_gains[first : first + size])

    even_gain = jnp.where(bits[1], all_gains[1], gain)
    odd_gain = jnp.where(bits[1], gain, all_gains[1])
    factor_before, levels, bit = jnp.ones_like(gain), [], 2
    while bit < count:
        mine = block(0, bit)
        theirs = block(bit, bit) if 2 * bit < count else mine
        levels.append((bit, mine, theirs, factor_before))
        if 2 * bit < count:
            factor_before = jnp.where(bits[bit], factor_before * theirs, factor_before)
        bit *= 2
    return even_gain, odd_gain, levels


def after(value, *earlier):
    return lax.optimization_barrier((value, *earlier))[0]


class Chain:
    def __init__(self, states, following, factors, bits):
        self.states, self.following, self.bits = states, following, bits
        self.even_gain, self.odd_gain, self.levels = factors
        self.count = lax.axis_size("depth")
        self.odd = bits[1]

    def enter(self, fine, *earlier):
        half = fine.shape[0] // 2
        mismatch = after(fine, *earlier).astype(F32) - self.following.astype(F32)
        low, high = mismatch[:half], mismatch[half:]
        mine = jnp.where(self.odd, high, low)
        sent = jnp.where(self.odd, low, high).astype(BF16)
        other = swapped(sent, "depth", 1).astype(F32)
        self.m_even = jnp.where(self.odd, other, mine)
        self.total = self.odd_gain * self.m_even + jnp.where(self.odd, mine, other)
        self.before = jnp.zeros_like(self.total)
        self.entered = self.total

    def level(self, index, sent_after=(), used_after=()):
        bit, factor, their_factor, factor_before = self.levels[index]
        upper = self.bits[bit]
        sent = after(self.total.astype(BF16), *sent_after)
        if index + 1 < len(self.levels):
            theirs = after(swapped(sent, "depth", bit), *used_after).astype(F32)
            self.total = jnp.where(upper, factor * theirs + self.total, their_factor * self.total + theirs)
        else:
            pairs = [(i, i + bit) for i in range(self.count) if not i & bit]
            theirs = after(lax.ppermute(sent, "depth", pairs), *used_after).astype(F32)
        self.before = jnp.where(upper, factor_before * theirs + self.before, self.before)

    def leave(self, used_after=()):
        odd, c_even = self.odd, self.before
        c_odd = self.even_gain * c_even + self.m_even
        mine = jnp.where(odd, c_odd, c_even)
        other = swapped(jnp.where(odd, c_even, c_odd).astype(BF16), "depth", 1)
        other = after(other, *used_after).astype(F32)
        correction = jnp.concatenate([jnp.where(odd, other, mine), jnp.where(odd, mine, other)], axis=0)
        return (self.states.astype(F32) + correction).astype(BF16)


def on_device(interfaces, doc_ids, w_attn, w_up, w_down, norm_gains, coarse_gain):
    x = interfaces[0, 0]
    rows = x.shape[0]
    half = rows // 2
    gains = norm_gains[0, 0]
    weights = (w_attn[0, 0], w_up[0, 0], w_down[0, 0])
    parts = [x[:half], x[half:]]
    halves = [shifted(part, "seq", 1) for part in parts]
    first_back = shifted(parts[0], "seq", -1)
    docs = Documents(doc_ids, rows)
    place, bits, bit = lax.axis_index("depth"), {}, 1
    while bit < lax.axis_size("depth"):
        bits[bit] = (place & bit) != 0
        bit *= 2
    early, bits, docs.own_column, docs.later_column = lax.optimization_barrier(
        (x, bits, docs.own_column, docs.later_column)
    )
    state = own_part(early, gains, weights, docs)
    factors = gain_factors(after(coarse_gain, state[0]), bits)
    following = shifted(after(x, state[0]), "depth", -1)
    state = [state[0], *piece_part(halves[0], 1, 0, gains, weights[0], *state, docs)]
    first_back = after(first_back, *jax.tree.leaves(factors))
    num, den = attention(state, halves, first_back, docs, weights[0], gains)
    following = [following[:half], following[half:]]
    first, second = [Chain(parts[i], following[i], factors, bits) for i in range(2)]
    first.enter(finish_part(x, num, den, weights, gains, 0, 2))
    fine = finish_part(x, after(num, first.total), den, weights, gains, 1, 2)
    first.level(0)
    second.enter(fine, first.total)
    for i in range(1, len(first.levels)):
        second.level(i - 1)
        first.level(i, used_after=(second.entered,))
    corrected = [first.leave()]
    halves = [shifted(corrected[0], "seq", 1)]
    first_back = shifted(corrected[0], "seq", -1)
    second.level(len(first.levels) - 1, sent_after=(corrected[0],))
    corrected.append(second.leave(used_after=(halves[0],)))
    halves.append(shifted(corrected[1], "seq", 1))
    x = jnp.concatenate(corrected, axis=0)
    state = own_part(x, gains, weights, docs)
    state = [state[0], *piece_part(halves[0], 1, 0, gains, weights[0], *state, docs)]
    num, den = attention(state, halves, first_back, docs, weights[0], gains)
    return finish_part(x, num, den, weights, gains, 0, 1)[None, None]


def solution(mesh):
    in_specs = (
        P("depth", None, "seq", None),
        P(),
        P("depth", None, None, None, None),
        P("depth", None, None, None),
        P("depth", None, None, None),
        P("depth", None, None, None),
        P("depth", None),
    )
    out_specs = P("depth", None, "seq", None)
    return jax.shard_map(
        on_device, mesh=mesh, in_specs=in_specs, out_specs=out_specs, check_vma=False
    )
```

```python
import functools

import jax
import jax.numpy as jnp
from jax import lax
from jax.experimental import pallas as pl
from jax.experimental.pallas import tpu as pltpu
from jax.sharding import PartitionSpec as P

HEADS = 16
LANES = 128
BLOCK = 256
TILE = 512
VMEM_BYTES = 12 * 1024 * 1024
COST = pl.CostEstimate(flops=1 << 20, bytes_accessed=1 << 16, transcendentals=0)
F32 = jnp.float32
BF16 = jnp.bfloat16


def rms_norm(value, gain):
    return value * lax.rsqrt(jnp.mean(value * value, axis=-1, keepdims=True) + 1e-05) * gain


def dot(a, b):
    return jnp.dot(a, b, preferred_element_type=F32)


def attend(q_ref, k_ref, v_ref, num_ref, den_ref, column_ref, row_ref, doc_ref, q_at, k_at, causal=False):
    rows, width = q_ref.shape
    keys = k_ref.shape[0]
    head_dim = width // HEADS
    per_tile = LANES // head_dim
    q_block, k_block = min(BLOCK, rows), min(BLOCK, keys)
    lane = lax.broadcasted_iota(jnp.int32, (1, LANES), 1)
    members = [lane // head_dim == i for i in range(per_tile)]
    count_q, count_k = rows // q_block, keys // k_block

    def one(index, carry):
        qi, ki = index // count_k, index % count_k
        q0 = pl.multiple_of(qi * q_block, q_block)
        k0 = pl.multiple_of(ki * k_block, k_block)
        needed = doc_ref[0, k_at + k0 + k_block - 1] >= doc_ref[0, q_at + q0]
        if causal:
            needed = (k0 <= q0) & (needed | (k0 == q0))

        @pl.when(needed)
        def _():
            key_docs = row_ref[:, pl.ds(pl.multiple_of(k_at + k0, k_block), k_block)]
            allowed = column_ref[pl.ds(q0, q_block), :1] == key_docs
            if causal:
                q_pos = q0 + lax.broadcasted_iota(jnp.int32, (q_block, k_block), 0)
                k_pos = k0 + lax.broadcasted_iota(jnp.int32, (q_block, k_block), 1)
                allowed = allowed & (k_pos <= q_pos)
            ones = jnp.ones((k_block, LANES), BF16)
            den = jnp.zeros((q_block, LANES), F32)
            for tile in range(width // LANES):
                cols = slice(tile * LANES, (tile + 1) * LANES)
                queries = q_ref[pl.ds(q0, q_block), cols]
                keys_here = k_ref[pl.ds(k0, k_block), cols]
                values = jnp.concatenate([v_ref[pl.ds(k0, k_block), cols], ones], axis=1)
                num = None
                for i, member in enumerate(members):
                    scores = lax.dot_general(
                        jnp.where(member, queries, jnp.zeros_like(queries)),
                        keys_here,
                        (((1,), (1,)), ((), ())),
                        preferred_element_type=F32,
                    )
                    weights = jnp.where(allowed, jnp.exp(scores), 0.0).astype(BF16)
                    out = dot(weights, values)
                    num = out[:, :LANES] if num is None else jnp.where(member, out[:, :LANES], num)
                    den = jnp.where(lane == tile * per_tile + i, out[:, LANES:], den)
                num_ref[pl.ds(q0, q_block), cols] += num
            den_ref[pl.ds(q0, q_block), :] += den

        return carry

    lax.fori_loop(0, count_q * count_k, one, 0)


def spread(per_head, width):
    shape = (LANES, width)
    chosen = lax.broadcasted_iota(jnp.int32, shape, 1) // (width // HEADS) == lax.broadcasted_iota(jnp.int32, shape, 0)
    chosen = jnp.where(chosen, 1.0, 0.0).astype(BF16)
    high = per_head.astype(BF16)
    return dot(high, chosen) + dot((per_head - high.astype(F32)).astype(BF16), chosen)


def normed(x_ref, gain_ref):
    return rms_norm(x_ref[...].astype(F32), gain_ref[0:1]).astype(BF16)


def project(n_ref, w_ref, index, out_ref, scale=None):
    width = w_ref.shape[2]
    tile = min(TILE, width)

    def one(j, carry):
        cols = pl.ds(pl.multiple_of(j * tile, tile), tile)
        out = dot(n_ref[...], w_ref[index, :, cols]).astype(BF16)
        out_ref[:, cols] = out if scale is None else out * jnp.asarray(scale, BF16)
        return carry

    lax.fori_loop(0, width // tile, one, 0)


def own_kernel(
    x_ref, gain_ref, w_ref, column_ref, row_ref, doc_ref, q_ref, num_ref, den_ref, n_ref, k_ref, v_ref
):
    head_dim = x_ref.shape[1] // HEADS
    here = lax.axis_index("seq") * x_ref.shape[0]
    n_ref[...] = normed(x_ref, gain_ref)
    project(n_ref, w_ref, 0, q_ref, head_dim ** (-0.5))
    project(n_ref, w_ref, 1, k_ref)
    project(n_ref, w_ref, 2, v_ref)
    num_ref[...] = jnp.zeros_like(num_ref)
    den_ref[...] = jnp.zeros_like(den_ref)
    attend(q_ref, k_ref, v_ref, num_ref, den_ref, column_ref, row_ref, doc_ref, here, here, True)


def piece_kernel(
    shift, first, x_ref, gain_ref, w_ref, q_ref, num_in, den_in, column_ref, row_ref, doc_ref,
    num_ref, den_ref, n_ref, k_ref, v_ref,
):
    del num_in, den_in
    rows, keys = q_ref.shape[0], x_ref.shape[0]
    shard = lax.axis_index("seq") - shift
    here, there = (shard + shift) * rows, jnp.maximum(shard, 0) * rows + first

    @pl.when((shard >= 0) & (doc_ref[0, there + keys - 1] >= doc_ref[0, here]))
    def _():
        n_ref[...] = normed(x_ref, gain_ref)
        project(n_ref, w_ref, 1, k_ref)
        project(n_ref, w_ref, 2, v_ref)
        attend(q_ref, k_ref, v_ref, num_ref, den_ref, column_ref, row_ref, doc_ref, here, there)


def far_document(doc_ref, rows, count):
    found = False
    for middle in range(1, count - 1):
        over = doc_ref[0, middle * rows - 1] == doc_ref[0, (middle + 1) * rows]
        deep = doc_ref[0, middle * rows - rows // 2 - 1] == doc_ref[0, (middle + 1) * rows]
        found = found | (over & deep)
    return found


def message_kernel(
    x_ref, p0_ref, p1_ref, gain_ref, w_ref, column_ref, row_ref, doc_ref,
    out_ref, q_ref, n_ref, k_ref, v_ref, num_ref, den_ref,
):
    half, width = x_ref.shape
    rows = 2 * half
    count = lax.axis_size("seq")
    place = lax.axis_index("seq")
    inside = (place >= 1) & (place + 1 < count)
    here = jnp.where(inside, place + 1, 0) * rows
    there = jnp.where(inside, place - 1, 0) * rows
    far = far_document(doc_ref, rows, count)

    @pl.when(jnp.logical_not(far))
    def _():
        out_ref[:, :width] = p1_ref[...]

    @pl.when(far)
    def _():
        num_ref[...] = jnp.zeros_like(num_ref)
        den_ref[...] = jnp.zeros_like(den_ref)

        @pl.when(inside & (doc_ref[0, there + rows - 1] >= doc_ref[0, here]))
        def _():
            n_ref[:half] = normed(x_ref, gain_ref)
            project(n_ref.at[:half], w_ref, 0, q_ref, (width // HEADS) ** (-0.5))
            n_ref[:half] = normed(p0_ref, gain_ref)
            n_ref[half:] = normed(p1_ref, gain_ref)
            project(n_ref, w_ref, 1, k_ref)
            project(n_ref, w_ref, 2, v_ref)
            attend(q_ref, k_ref, v_ref, num_ref, den_ref, column_ref, row_ref, doc_ref, here, there)

        out_ref[:, :width] = num_ref[...].astype(BF16)
        out_ref[:, width:] = den_ref[...].astype(BF16)


def reply_kernel(
    message_ref, gain_ref, w_ref, q_ref, num_in, den_in, column_ref, row_ref, doc_ref,
    num_ref, den_ref, n_ref, k_ref, v_ref,
):
    rows, width = q_ref.shape
    half = message_ref.shape[0]
    far = far_document(doc_ref, rows, lax.axis_size("seq"))

    @pl.when(far)
    def _():
        num_ref[:half] += message_ref[:, :width].astype(F32)
        den_ref[:half] += message_ref[:, width:].astype(F32)

    @pl.when(jnp.logical_not(far))
    def _():
        piece_kernel(
            2, half, message_ref.at[:, :width], gain_ref, w_ref, q_ref, num_in, den_in, column_ref, row_ref, doc_ref,
            num_ref, den_ref, n_ref, k_ref, v_ref,
        )


def finish_kernel(
    first, x_ref, num_ref, den_ref, w_ref, gain_ref, up_ref, down_ref, out_ref, acc_ref, n_ref, hidden_ref
):
    rows, width = out_ref.shape
    hidden = up_ref.shape[1]
    tile = min(TILE, hidden)
    here = pl.ds(first, rows)
    lane = lax.broadcasted_iota(jnp.int32, (rows, LANES), 1)
    inverse = 1.0 / jnp.where(lane < HEADS, den_ref[here], 1.0)
    n_ref[...] = (num_ref[here] * spread(inverse, width)).astype(BF16)
    acc_ref[...] = x_ref[here].astype(F32) + dot(n_ref[...], w_ref[3])
    n_ref[...] = rms_norm(acc_ref[...], gain_ref[1:2]).astype(BF16)

    def expand(j):
        cols = pl.ds(pl.multiple_of(j * tile, tile), tile)
        return jax.nn.gelu(dot(n_ref[...], up_ref[:, cols])).astype(BF16)

    def lower(j, expanded):
        return dot(expanded, down_ref[pl.ds(pl.multiple_of(j * tile, tile), tile)])

    hidden_ref[0] = expand(0)

    def one(j, carry):
        acc_ref[...] += lower(j, hidden_ref[j % 2])
        hidden_ref[(j + 1) % 2] = expand(j + 1)
        return carry

    last = hidden // tile - 1
    lax.fori_loop(0, last, one, 0)
    out_ref[...] = (acc_ref[...] + lower(last, hidden_ref[last % 2])).astype(BF16)


def vmem():
    return pl.BlockSpec(memory_space=pltpu.VMEM)


def call(kernel, name, operands, docs, results, scratch, aliases=None, held=True):
    inputs = [pltpu.with_memory_space_constraint(operand, pltpu.VMEM) for operand in operands]
    in_specs = [vmem()] * len(inputs)
    if docs is not None:
        inputs.append(docs)
        in_specs.append(pl.BlockSpec(memory_space=pltpu.SMEM))
    return pl.pallas_call(
        kernel,
        in_specs=in_specs,
        out_specs=[vmem()] * len(results),
        out_shape=[pltpu.VMEM(*one) if held else jax.ShapeDtypeStruct(*one) for one in results],
        scratch_shapes=scratch,
        input_output_aliases=aliases or {},
        compiler_params=pltpu.CompilerParams(vmem_limit_bytes=VMEM_BYTES),
        cost_estimate=COST,
        name=name,
    )(*inputs)


def own_part(x, gains, weights, docs):
    rows, width = x.shape
    results = [((rows, width), BF16), ((rows, width), F32), ((rows, LANES), F32)]
    scratch = [pltpu.VMEM((rows, width), BF16)] * 3
    return call(own_kernel, "own_part", (x, gains, weights[0], docs.own_column, docs.ids), docs.ids, results, scratch)


def piece_part(x, shift, first, gains, w_attn, q, num, den, docs):
    rows, width = q.shape
    return call(
        functools.partial(piece_kernel, shift, first),
        "piece_part",
        (x, gains, w_attn, q, num, den, docs.own_column, docs.ids),
        docs.ids,
        [((rows, width), F32), ((rows, LANES), F32)],
        [pltpu.VMEM((x.shape[0], width), BF16)] * 3,
        aliases={4: 0, 5: 1},
    )


def message_part(x, pieces, gains, w_attn, docs):
    half, width = x.shape
    keys = 2 * half
    return call(
        message_kernel,
        "message_part",
        (x, *pieces, gains, w_attn, docs.later_column, docs.ids),
        docs.ids,
        [((half, width + LANES), BF16)],
        [pltpu.VMEM((half, width), BF16)]
        + [pltpu.VMEM((keys, width), BF16)] * 3
        + [pltpu.VMEM((half, width), F32), pltpu.VMEM((half, LANES), F32)],
    )[0]


def reply_part(message, gains, w_attn, q, num, den, docs):
    rows, width = q.shape
    return call(
        reply_kernel,
        "reply_part",
        (message, gains, w_attn, q, num, den, docs.own_column, docs.ids),
        docs.ids,
        [((rows, width), F32), ((rows, LANES), F32)],
        [pltpu.VMEM((message.shape[0], width), BF16)] * 3,
        aliases={4: 0, 5: 1},
    )


def finish_part(x, num, den, weights, gains, part, parts):
    width = x.shape[1]
    rows = x.shape[0] // parts
    w_attn, w_up, w_down = weights
    tile = min(TILE, w_up.shape[1])
    return call(
        functools.partial(finish_kernel, part * rows),
        "finish_part",
        (x, num, den, w_attn, gains, w_up, w_down),
        None,
        [((rows, width), BF16)],
        [pltpu.VMEM((rows, width), F32), pltpu.VMEM((rows, width), BF16), pltpu.VMEM((2, rows, tile), BF16)],
        held=parts > 1,
    )[0]


def shifted(value, axis, steps):
    count = lax.axis_size(axis)
    first, last = max(0, -steps), min(count, count - steps)
    return lax.ppermute(value, axis, [(i, i + steps) for i in range(first, last)])


def swapped(value, axis, bit):
    return lax.ppermute(value, axis, [(i, i ^ bit) for i in range(lax.axis_size(axis))])


class Documents:
    def __init__(self, doc_ids, rows):
        count = lax.axis_size("seq")
        self.ids, self.rows, self.half = doc_ids, rows, rows // 2
        longest = doc_ids.shape[1] // 2
        self.hops = min(count - 1, -(-(longest - 1) // rows))
        self.short = self.hops == 2 and longest <= 2 * rows and rows % 2 == 0
        place = lax.axis_index("seq")

        def column(later, size):
            start = jnp.minimum((place + later) * rows, doc_ids.shape[1] - size)
            ids = lax.dynamic_slice_in_dim(doc_ids, start, size, 1)
            return jnp.broadcast_to(ids.reshape(-1, 1), (size, LANES))

        self.own_column = column(0, rows)
        self.later_column = column(1, self.half) if self.short else self.own_column


def attention(state, halves, first_back, docs, w_attn, gains):
    half = docs.half
    q, *state = state

    def add(piece, shift, first, state):
        return piece_part(piece, shift, first, gains, w_attn, q, *state, docs)

    if docs.short:
        message = shifted(message_part(after(first_back, q), halves, gains, w_attn, docs), "seq", 1)
        num, den = add(halves[1], 1, half, state)
        return reply_part(message, gains, w_attn, q, num, den, docs)
    state = add(halves[1], 1, half, state)
    pieces = halves
    for hop in range(2, docs.hops + 1):
        pieces = [shifted(piece, "seq", 1) for piece in pieces]
        for i, piece in enumerate(pieces):
            state = add(piece, hop, i * half, state)
    return state


def gain_factors(gain, bits):
    count = lax.axis_size("depth")
    all_gains = [gain] + [swapped(gain, "depth", i) for i in range(1, max(2, count // 2))]

    def block(first, size):
        return functools.reduce(jnp.multiply, all_gains[first : first + size])

    even_gain = jnp.where(bits[1], all_gains[1], gain)
    odd_gain = jnp.where(bits[1], gain, all_gains[1])
    factor_before, levels, bit = jnp.ones_like(gain), [], 2
    while bit < count:
        mine = block(0, bit)
        theirs = block(bit, bit) if 2 * bit < count else mine
        levels.append((bit, mine, theirs, factor_before))
        if 2 * bit < count:
            factor_before = jnp.where(bits[bit], factor_before * theirs, factor_before)
        bit *= 2
    return even_gain, odd_gain, levels


def after(value, *earlier):
    return lax.optimization_barrier((value, *earlier))[0]


class Chain:
    def __init__(self, states, following, factors, bits):
        self.states, self.following, self.bits = states, following, bits
        self.even_gain, self.odd_gain, self.levels = factors
        self.odd = bits[1]

    def enter(self, fine, *earlier):
        half = fine.shape[0] // 2
        mismatch = after(fine, *earlier).astype(F32) - self.following.astype(F32)
        low, high = mismatch[:half], mismatch[half:]
        mine = jnp.where(self.odd, high, low)
        sent = jnp.where(self.odd, low, high).astype(BF16)
        other = swapped(sent, "depth", 1).astype(F32)
        self.m_even = jnp.where(self.odd, other, mine)
        self.total = self.odd_gain * self.m_even + jnp.where(self.odd, mine, other)
        self.before = jnp.zeros_like(self.total)
        self.entered = self.total

    def level(self, index, sent_after=(), used_after=()):
        bit, factor, their_factor, factor_before = self.levels[index]
        upper = self.bits[bit]
        sent = after(self.total.astype(BF16), *sent_after)
        theirs = after(swapped(sent, "depth", bit), *used_after).astype(F32)
        if index + 1 < len(self.levels):
            self.total = jnp.where(upper, factor * theirs + self.total, their_factor * self.total + theirs)
        self.before = jnp.where(upper, factor_before * theirs + self.before, self.before)

    def leave(self, used_after=()):
        odd, c_even = self.odd, self.before
        c_odd = self.even_gain * c_even + self.m_even
        mine = jnp.where(odd, c_odd, c_even)
        other = swapped(jnp.where(odd, c_even, c_odd).astype(BF16), "depth", 1)
        other = after(other, *used_after).astype(F32)
        correction = jnp.concatenate([jnp.where(odd, other, mine), jnp.where(odd, mine, other)], axis=0)
        return (self.states.astype(F32) + correction).astype(BF16)


def on_device(interfaces, doc_ids, w_attn, w_up, w_down, norm_gains, coarse_gain):
    x = interfaces[0, 0]
    rows = x.shape[0]
    half = rows // 2
    gains = norm_gains[0, 0]
    weights = (w_attn[0, 0], w_up[0, 0], w_down[0, 0])
    parts = [x[:half], x[half:]]
    halves = [shifted(part, "seq", 1) for part in parts]
    first_back = shifted(parts[0], "seq", -1)
    docs = Documents(doc_ids, rows)
    place, bits, bit = lax.axis_index("depth"), {}, 1
    while bit < lax.axis_size("depth"):
        bits[bit] = (place & bit) != 0
        bit *= 2
    early, bits, docs.own_column, docs.later_column = lax.optimization_barrier(
        (x, bits, docs.own_column, docs.later_column)
    )
    state = own_part(early, gains, weights, docs)
    factors = gain_factors(after(coarse_gain, state[0]), bits)
    following = shifted(after(x, *jax.tree.leaves(factors)), "depth", -1)
    state = [state[0], *piece_part(halves[0], 1, 0, gains, weights[0], *state, docs)]
    first_back = after(first_back, *jax.tree.leaves(factors))
    num, den = attention(state, halves, first_back, docs, weights[0], gains)
    following = [following[:half], following[half:]]
    first, second = [Chain(parts[i], following[i], factors, bits) for i in range(2)]
    first.enter(finish_part(x, num, den, weights, gains, 0, 2))
    fine = finish_part(x, after(num, first.total), den, weights, gains, 1, 2)
    first.level(0)
    second.enter(fine, first.total)
    for i in range(1, len(first.levels)):
        second.level(i - 1)
        first.level(i, used_after=(second.entered,))
    corrected = [first.leave()]
    halves = [shifted(corrected[0], "seq", 1)]
    first_back = shifted(corrected[0], "seq", -1)
    second.level(len(first.levels) - 1, sent_after=(corrected[0],))
    corrected.append(second.leave(used_after=(halves[0],)))
    halves.append(shifted(corrected[1], "seq", 1))
    x = jnp.concatenate(corrected, axis=0)
    state = own_part(x, gains, weights, docs)
    state = [state[0], *piece_part(halves[0], 1, 0, gains, weights[0], *state, docs)]
    num, den = attention(state, halves, first_back, docs, weights[0], gains)
    return finish_part(x, num, den, weights, gains, 0, 1)[None, None]


def solution(mesh):
    in_specs = (
        P("depth", None, "seq", None),
        P(),
        P("depth", None, None, None, None),
        P("depth", None, None, None),
        P("depth", None, None, None),
        P("depth", None, None, None),
        P("depth", None),
    )
    out_specs = P("depth", None, "seq", None)
    return jax.shard_map(
        on_device, mesh=mesh, in_specs=in_specs, out_specs=out_specs, check_vma=False
    )
```

```python
import functools

import jax
import jax.numpy as jnp
from jax import lax
from jax.experimental import pallas as pl
from jax.experimental.pallas import tpu as pltpu
from jax.sharding import PartitionSpec as P

HEADS = 16
LANES = 128
BLOCK = 256
TILE = 512
VMEM_BYTES = 12 * 1024 * 1024
COST = pl.CostEstimate(flops=1 << 20, bytes_accessed=1 << 16, transcendentals=0)
F32 = jnp.float32
BF16 = jnp.bfloat16


def rms_norm(value, gain):
    return value * lax.rsqrt(jnp.mean(value * value, axis=-1, keepdims=True) + 1e-05) * gain


def dot(a, b):
    return jnp.dot(a, b, preferred_element_type=F32)


def attend(q_ref, k_ref, v_ref, num_ref, den_ref, column_ref, row_ref, doc_ref, q_at, k_at, causal=False):
    rows, width = q_ref.shape
    keys = k_ref.shape[0]
    head_dim = width // HEADS
    per_tile = LANES // head_dim
    q_block, k_block = min(BLOCK, rows), min(BLOCK, keys)
    lane = lax.broadcasted_iota(jnp.int32, (1, LANES), 1)
    members = [lane // head_dim == i for i in range(per_tile)]
    count_q, count_k = rows // q_block, keys // k_block

    def one(index, carry):
        qi, ki = index // count_k, index % count_k
        q0 = pl.multiple_of(qi * q_block, q_block)
        k0 = pl.multiple_of(ki * k_block, k_block)
        needed = doc_ref[0, k_at + k0 + k_block - 1] >= doc_ref[0, q_at + q0]
        if causal:
            needed = (k0 <= q0) & (needed | (k0 == q0))

        @pl.when(needed)
        def _():
            key_docs = row_ref[:, pl.ds(pl.multiple_of(k_at + k0, k_block), k_block)]
            allowed = column_ref[pl.ds(q0, q_block), :1] == key_docs
            if causal:
                q_pos = q0 + lax.broadcasted_iota(jnp.int32, (q_block, k_block), 0)
                k_pos = k0 + lax.broadcasted_iota(jnp.int32, (q_block, k_block), 1)
                allowed = allowed & (k_pos <= q_pos)
            ones = jnp.ones((k_block, LANES), BF16)
            den = jnp.zeros((q_block, LANES), F32)
            for tile in range(width // LANES):
                cols = slice(tile * LANES, (tile + 1) * LANES)
                queries = q_ref[pl.ds(q0, q_block), cols]
                keys_here = k_ref[pl.ds(k0, k_block), cols]
                values = jnp.concatenate([v_ref[pl.ds(k0, k_block), cols], ones], axis=1)
                num = None
                for i, member in enumerate(members):
                    scores = lax.dot_general(
                        jnp.where(member, queries, jnp.zeros_like(queries)),
                        keys_here,
                        (((1,), (1,)), ((), ())),
                        preferred_element_type=F32,
                    )
                    weights = jnp.where(allowed, jnp.exp(scores), 0.0).astype(BF16)
                    out = dot(weights, values)
                    num = out[:, :LANES] if num is None else jnp.where(member, out[:, :LANES], num)
                    den = jnp.where(lane == tile * per_tile + i, out[:, LANES:], den)
                num_ref[pl.ds(q0, q_block), cols] += num
            den_ref[pl.ds(q0, q_block), :] += den

        return carry

    lax.fori_loop(0, count_q * count_k, one, 0)


def spread(per_head, width):
    shape = (LANES, width)
    chosen = lax.broadcasted_iota(jnp.int32, shape, 1) // (width // HEADS) == lax.broadcasted_iota(jnp.int32, shape, 0)
    chosen = jnp.where(chosen, 1.0, 0.0).astype(BF16)
    high = per_head.astype(BF16)
    return dot(high, chosen) + dot((per_head - high.astype(F32)).astype(BF16), chosen)


def normed(x_ref, gain_ref):
    return rms_norm(x_ref[...].astype(F32), gain_ref[0:1]).astype(BF16)


def project(n_ref, w_ref, index, out_ref, scale=None):
    width = w_ref.shape[2]
    tile = min(TILE, width)

    def one(j, carry):
        cols = pl.ds(pl.multiple_of(j * tile, tile), tile)
        out = dot(n_ref[...], w_ref[index, :, cols]).astype(BF16)
        out_ref[:, cols] = out if scale is None else out * jnp.asarray(scale, BF16)
        return carry

    lax.fori_loop(0, width // tile, one, 0)


def own_kernel(
    x_ref, gain_ref, w_ref, column_ref, row_ref, doc_ref, q_ref, num_ref, den_ref, n_ref, k_ref, v_ref
):
    head_dim = x_ref.shape[1] // HEADS
    here = lax.axis_index("seq") * x_ref.shape[0]
    n_ref[...] = normed(x_ref, gain_ref)
    project(n_ref, w_ref, 0, q_ref, head_dim ** (-0.5))
    project(n_ref, w_ref, 1, k_ref)
    project(n_ref, w_ref, 2, v_ref)
    num_ref[...] = jnp.zeros_like(num_ref)
    den_ref[...] = jnp.zeros_like(den_ref)
    attend(q_ref, k_ref, v_ref, num_ref, den_ref, column_ref, row_ref, doc_ref, here, here, True)


def piece_kernel(
    shift, first, x_ref, gain_ref, w_ref, q_ref, num_in, den_in, column_ref, row_ref, doc_ref,
    num_ref, den_ref, n_ref, k_ref, v_ref,
):
    del num_in, den_in
    rows, keys = q_ref.shape[0], x_ref.shape[0]
    shard = lax.axis_index("seq") - shift
    here, there = (shard + shift) * rows, jnp.maximum(shard, 0) * rows + first

    @pl.when((shard >= 0) & (doc_ref[0, there + keys - 1] >= doc_ref[0, here]))
    def _():
        n_ref[...] = normed(x_ref, gain_ref)
        project(n_ref, w_ref, 1, k_ref)
        project(n_ref, w_ref, 2, v_ref)
        attend(q_ref, k_ref, v_ref, num_ref, den_ref, column_ref, row_ref, doc_ref, here, there)


def far_document(doc_ref, rows, count):
    found = False
    for middle in range(1, count - 1):
        over = doc_ref[0, middle * rows - 1] == doc_ref[0, (middle + 1) * rows]
        deep = doc_ref[0, middle * rows - rows // 2 - 1] == doc_ref[0, (middle + 1) * rows]
        found = found | (over & deep)
    return found


def message_kernel(
    x_ref, p0_ref, p1_ref, gain_ref, w_ref, column_ref, row_ref, doc_ref,
    out_ref, q_ref, n_ref, k_ref, v_ref, num_ref, den_ref,
):
    half, width = x_ref.shape
    rows = 2 * half
    count = lax.axis_size("seq")
    place = lax.axis_index("seq")
    inside = (place >= 1) & (place + 1 < count)
    here = jnp.where(inside, place + 1, 0) * rows
    there = jnp.where(inside, place - 1, 0) * rows
    far = far_document(doc_ref, rows, count)

    @pl.when(jnp.logical_not(far))
    def _():
        out_ref[:, :width] = p1_ref[...]

    @pl.when(far)
    def _():
        num_ref[...] = jnp.zeros_like(num_ref)
        den_ref[...] = jnp.zeros_like(den_ref)

        @pl.when(inside & (doc_ref[0, there + rows - 1] >= doc_ref[0, here]))
        def _():
            n_ref[:half] = normed(x_ref, gain_ref)
            project(n_ref.at[:half], w_ref, 0, q_ref, (width // HEADS) ** (-0.5))
            n_ref[:half] = normed(p0_ref, gain_ref)
            n_ref[half:] = normed(p1_ref, gain_ref)
            project(n_ref, w_ref, 1, k_ref)
            project(n_ref, w_ref, 2, v_ref)
            attend(q_ref, k_ref, v_ref, num_ref, den_ref, column_ref, row_ref, doc_ref, here, there)

        out_ref[:, :width] = num_ref[...].astype(BF16)
        out_ref[:, width:] = den_ref[...].astype(BF16)


def reply_kernel(
    message_ref, gain_ref, w_ref, q_ref, num_in, den_in, column_ref, row_ref, doc_ref,
    num_ref, den_ref, n_ref, k_ref, v_ref,
):
    rows, width = q_ref.shape
    half = message_ref.shape[0]
    far = far_document(doc_ref, rows, lax.axis_size("seq"))

    @pl.when(far)
    def _():
        num_ref[:half] += message_ref[:, :width].astype(F32)
        den_ref[:half] += message_ref[:, width:].astype(F32)

    @pl.when(jnp.logical_not(far))
    def _():
        piece_kernel(
            2, half, message_ref.at[:, :width], gain_ref, w_ref, q_ref, num_in, den_in, column_ref, row_ref, doc_ref,
            num_ref, den_ref, n_ref, k_ref, v_ref,
        )


def finish_kernel(
    first, x_ref, num_ref, den_ref, w_ref, gain_ref, up_ref, down_ref, out_ref, acc_ref, n_ref, hidden_ref
):
    rows, width = out_ref.shape
    hidden = up_ref.shape[1]
    tile = min(TILE, hidden)
    here = pl.ds(first, rows)
    lane = lax.broadcasted_iota(jnp.int32, (rows, LANES), 1)
    inverse = 1.0 / jnp.where(lane < HEADS, den_ref[here], 1.0)
    n_ref[...] = (num_ref[here] * spread(inverse, width)).astype(BF16)
    acc_ref[...] = x_ref[here].astype(F32) + dot(n_ref[...], w_ref[3])
    n_ref[...] = rms_norm(acc_ref[...], gain_ref[1:2]).astype(BF16)

    def expand(j):
        cols = pl.ds(pl.multiple_of(j * tile, tile), tile)
        return jax.nn.gelu(dot(n_ref[...], up_ref[:, cols])).astype(BF16)

    def lower(j, expanded):
        return dot(expanded, down_ref[pl.ds(pl.multiple_of(j * tile, tile), tile)])

    hidden_ref[0] = expand(0)

    def one(j, carry):
        acc_ref[...] += lower(j, hidden_ref[j % 2])
        hidden_ref[(j + 1) % 2] = expand(j + 1)
        return carry

    last = hidden // tile - 1
    lax.fori_loop(0, last, one, 0)
    out_ref[...] = (acc_ref[...] + lower(last, hidden_ref[last % 2])).astype(BF16)


def vmem():
    return pl.BlockSpec(memory_space=pltpu.VMEM)


def call(kernel, name, operands, docs, results, scratch, aliases=None, held=True):
    inputs = [pltpu.with_memory_space_constraint(operand, pltpu.VMEM) for operand in operands]
    in_specs = [vmem()] * len(inputs)
    if docs is not None:
        inputs.append(docs)
        in_specs.append(pl.BlockSpec(memory_space=pltpu.SMEM))
    return pl.pallas_call(
        kernel,
        in_specs=in_specs,
        out_specs=[vmem()] * len(results),
        out_shape=[pltpu.VMEM(*one) if held else jax.ShapeDtypeStruct(*one) for one in results],
        scratch_shapes=scratch,
        input_output_aliases=aliases or {},
        compiler_params=pltpu.CompilerParams(vmem_limit_bytes=VMEM_BYTES),
        cost_estimate=COST,
        name=name,
    )(*inputs)


def own_part(x, gains, weights, docs):
    rows, width = x.shape
    results = [((rows, width), BF16), ((rows, width), F32), ((rows, LANES), F32)]
    scratch = [pltpu.VMEM((rows, width), BF16)] * 3
    return call(own_kernel, "own_part", (x, gains, weights[0], docs.own_column, docs.ids), docs.ids, results, scratch)


def piece_part(x, shift, first, gains, w_attn, q, num, den, docs):
    rows, width = q.shape
    return call(
        functools.partial(piece_kernel, shift, first),
        "piece_part",
        (x, gains, w_attn, q, num, den, docs.own_column, docs.ids),
        docs.ids,
        [((rows, width), F32), ((rows, LANES), F32)],
        [pltpu.VMEM((x.shape[0], width), BF16)] * 3,
        aliases={4: 0, 5: 1},
    )


def message_part(x, pieces, gains, w_attn, docs):
    half, width = x.shape
    keys = 2 * half
    return call(
        message_kernel,
        "message_part",
        (x, *pieces, gains, w_attn, docs.later_column, docs.ids),
        docs.ids,
        [((half, width + LANES), BF16)],
        [pltpu.VMEM((half, width), BF16)]
        + [pltpu.VMEM((keys, width), BF16)] * 3
        + [pltpu.VMEM((half, width), F32), pltpu.VMEM((half, LANES), F32)],
    )[0]


def reply_part(message, gains, w_attn, q, num, den, docs):
    rows, width = q.shape
    return call(
        reply_kernel,
        "reply_part",
        (message, gains, w_attn, q, num, den, docs.own_column, docs.ids),
        docs.ids,
        [((rows, width), F32), ((rows, LANES), F32)],
        [pltpu.VMEM((message.shape[0], width), BF16)] * 3,
        aliases={4: 0, 5: 1},
    )


def finish_part(x, num, den, weights, gains, part, parts):
    width = x.shape[1]
    rows = x.shape[0] // parts
    w_attn, w_up, w_down = weights
    tile = min(TILE, w_up.shape[1])
    return call(
        functools.partial(finish_kernel, part * rows),
        "finish_part",
        (x, num, den, w_attn, gains, w_up, w_down),
        None,
        [((rows, width), BF16)],
        [pltpu.VMEM((rows, width), F32), pltpu.VMEM((rows, width), BF16), pltpu.VMEM((2, rows, tile), BF16)],
        held=parts > 1,
    )[0]


def shifted(value, axis, steps):
    count = lax.axis_size(axis)
    first, last = max(0, -steps), min(count, count - steps)
    return lax.ppermute(value, axis, [(i, i + steps) for i in range(first, last)])


def swapped(value, axis, bit):
    return lax.ppermute(value, axis, [(i, i ^ bit) for i in range(lax.axis_size(axis))])


class Documents:
    def __init__(self, doc_ids, rows):
        count = lax.axis_size("seq")
        self.ids, self.rows, self.half = doc_ids, rows, rows // 2
        longest = doc_ids.shape[1] // 2
        self.hops = min(count - 1, -(-(longest - 1) // rows))
        self.short = self.hops == 2 and longest <= 2 * rows and rows % 2 == 0
        place = lax.axis_index("seq")

        def column(later, size):
            start = jnp.minimum((place + later) * rows, doc_ids.shape[1] - size)
            ids = lax.dynamic_slice_in_dim(doc_ids, start, size, 1)
            return jnp.broadcast_to(ids.reshape(-1, 1), (size, LANES))

        self.own_column = column(0, rows)
        self.later_column = column(1, self.half) if self.short else self.own_column


def attention(state, halves, first_back, docs, w_attn, gains):
    half = docs.half
    q, *state = state

    def add(piece, shift, first, state):
        return piece_part(piece, shift, first, gains, w_attn, q, *state, docs)

    if docs.short:
        message = shifted(message_part(after(first_back, q), halves, gains, w_attn, docs), "seq", 1)
        num, den = add(halves[1], 1, half, state)
        return reply_part(message, gains, w_attn, q, num, den, docs)
    state = add(halves[1], 1, half, state)
    pieces = halves
    for hop in range(2, docs.hops + 1):
        pieces = [shifted(piece, "seq", 1) for piece in pieces]
        for i, piece in enumerate(pieces):
            state = add(piece, hop, i * half, state)
    return state


def gain_factors(gain, bits):
    count = lax.axis_size("depth")
    all_gains = [gain] + [swapped(gain, "depth", i) for i in range(1, max(2, count // 2))]

    def block(first, size):
        return functools.reduce(jnp.multiply, all_gains[first : first + size])

    even_gain = jnp.where(bits[1], all_gains[1], gain)
    odd_gain = jnp.where(bits[1], gain, all_gains[1])
    factor_before, levels, bit = jnp.ones_like(gain), [], 2
    while bit < count:
        mine = block(0, bit)
        theirs = block(bit, bit) if 2 * bit < count else mine
        levels.append((bit, mine, theirs, factor_before))
        if 2 * bit < count:
            factor_before = jnp.where(bits[bit], factor_before * theirs, factor_before)
        bit *= 2
    return even_gain, odd_gain, levels


def after(value, *earlier):
    return lax.optimization_barrier((value, *earlier))[0]


class Chain:
    def __init__(self, states, following, factors, bits):
        self.states, self.following, self.bits = states, following, bits
        self.even_gain, self.odd_gain, self.levels = factors
        self.odd = bits[1]

    def enter(self, fine, *earlier):
        half = fine.shape[0] // 2
        mismatch = after(fine, *earlier).astype(F32) - self.following.astype(F32)
        low, high = mismatch[:half], mismatch[half:]
        mine = jnp.where(self.odd, high, low)
        sent = jnp.where(self.odd, low, high).astype(BF16)
        other = swapped(sent, "depth", 1).astype(F32)
        self.m_even = jnp.where(self.odd, other, mine)
        self.total = self.odd_gain * self.m_even + jnp.where(self.odd, mine, other)
        self.before = jnp.zeros_like(self.total)
        self.entered = self.total

    def level(self, index, sent_after=(), used_after=()):
        bit, factor, their_factor, factor_before = self.levels[index]
        upper = self.bits[bit]
        sent = after(self.total.astype(BF16), *sent_after)
        theirs = after(swapped(sent, "depth", bit), *used_after).astype(F32)
        if index + 1 < len(self.levels):
            self.total = jnp.where(upper, factor * theirs + self.total, their_factor * self.total + theirs)
        self.before = jnp.where(upper, factor_before * theirs + self.before, self.before)

    def leave(self, used_after=()):
        odd, c_even = self.odd, self.before
        c_odd = self.even_gain * c_even + self.m_even
        mine = jnp.where(odd, c_odd, c_even)
        other = swapped(jnp.where(odd, c_even, c_odd).astype(BF16), "depth", 1)
        other = after(other, *used_after).astype(F32)
        correction = jnp.concatenate([jnp.where(odd, other, mine), jnp.where(odd, mine, other)], axis=0)
        return (self.states.astype(F32) + correction).astype(BF16)


def on_device(interfaces, doc_ids, w_attn, w_up, w_down, norm_gains, coarse_gain):
    x = interfaces[0, 0]
    rows = x.shape[0]
    half = rows // 2
    gains = norm_gains[0, 0]
    weights = (w_attn[0, 0], w_up[0, 0], w_down[0, 0])
    parts = [x[:half], x[half:]]
    halves = [shifted(part, "seq", 1) for part in parts]
    first_back = shifted(parts[0], "seq", -1)
    docs = Documents(doc_ids, rows)
    place, bits, bit = lax.axis_index("depth"), {}, 1
    while bit < lax.axis_size("depth"):
        bits[bit] = (place & bit) != 0
        bit *= 2
    early, bits, docs.own_column, docs.later_column = lax.optimization_barrier(
        (x, bits, docs.own_column, docs.later_column)
    )
    factors = gain_factors(coarse_gain, bits)
    state = own_part(after(early, *jax.tree.leaves(factors)), gains, weights, docs)
    following = shifted(after(x, state[0]), "depth", -1)
    state = [state[0], *piece_part(halves[0], 1, 0, gains, weights[0], *state, docs)]
    num, den = attention(state, halves, first_back, docs, weights[0], gains)
    following = [following[:half], following[half:]]
    first, second = [Chain(parts[i], following[i], factors, bits) for i in range(2)]
    first.enter(finish_part(x, num, den, weights, gains, 0, 2))
    fine = finish_part(x, after(num, first.total), den, weights, gains, 1, 2)
    first.level(0)
    second.enter(fine, first.total)
    for i in range(1, len(first.levels)):
        second.level(i - 1)
        first.level(i, used_after=(second.entered,))
    corrected = [first.leave()]
    halves = [shifted(corrected[0], "seq", 1)]
    first_back = shifted(corrected[0], "seq", -1)
    second.level(len(first.levels) - 1, sent_after=(corrected[0],))
    corrected.append(second.leave(used_after=(halves[0],)))
    halves.append(shifted(corrected[1], "seq", 1))
    x = jnp.concatenate(corrected, axis=0)
    state = own_part(x, gains, weights, docs)
    state = [state[0], *piece_part(halves[0], 1, 0, gains, weights[0], *state, docs)]
    num, den = attention(state, halves, first_back, docs, weights[0], gains)
    return finish_part(x, num, den, weights, gains, 0, 1)[None, None]


def solution(mesh):
    in_specs = (
        P("depth", None, "seq", None),
        P(),
        P("depth", None, None, None, None),
        P("depth", None, None, None),
        P("depth", None, None, None),
        P("depth", None, None, None),
        P("depth", None),
    )
    out_specs = P("depth", None, "seq", None)
    return jax.shard_map(
        on_device, mesh=mesh, in_specs=in_specs, out_specs=out_specs, check_vma=False
    )
```

```python
import functools

import jax
import jax.numpy as jnp
from jax import lax
from jax.experimental import pallas as pl
from jax.experimental.pallas import tpu as pltpu
from jax.sharding import PartitionSpec as P

HEADS = 16
LANES = 128
BLOCK = 256
TILE = 512
TILES = 2
VMEM_BYTES = 12 * 1024 * 1024
COST = pl.CostEstimate(flops=1 << 20, bytes_accessed=1 << 16, transcendentals=0)
F32 = jnp.float32
BF16 = jnp.bfloat16


def rms_norm(value, gain):
    return value * lax.rsqrt(jnp.mean(value * value, axis=-1, keepdims=True) + 1e-05) * gain


def dot(a, b):
    return jnp.dot(a, b, preferred_element_type=F32)


def attend(q_ref, k_ref, v_ref, num_ref, den_ref, column_ref, row_ref, doc_ref, q_at, k_at, causal=False):
    rows, width = q_ref.shape
    keys = k_ref.shape[0]
    head_dim = width // HEADS
    per_tile = LANES // head_dim
    q_block, k_block = min(BLOCK, rows), min(BLOCK, keys)
    lane = lax.broadcasted_iota(jnp.int32, (1, LANES), 1)
    members = [lane // head_dim == i for i in range(per_tile)]
    count_q, count_k = rows // q_block, keys // k_block

    def one(index, carry):
        qi, ki = index // count_k, index % count_k
        q0 = pl.multiple_of(qi * q_block, q_block)
        k0 = pl.multiple_of(ki * k_block, k_block)
        needed = doc_ref[0, k_at + k0 + k_block - 1] >= doc_ref[0, q_at + q0]
        if causal:
            needed = (k0 <= q0) & (needed | (k0 == q0))

        @pl.when(needed)
        def _():
            key_docs = row_ref[:, pl.ds(pl.multiple_of(k_at + k0, k_block), k_block)]
            allowed = column_ref[pl.ds(q0, q_block), :1] == key_docs
            if causal:
                q_pos = q0 + lax.broadcasted_iota(jnp.int32, (q_block, k_block), 0)
                k_pos = k0 + lax.broadcasted_iota(jnp.int32, (q_block, k_block), 1)
                allowed = allowed & (k_pos <= q_pos)
            ones = jnp.ones((k_block, LANES), BF16)

            def heads(tile, den):
                cols = pl.ds(pl.multiple_of(tile * LANES, LANES), LANES)
                queries = q_ref[pl.ds(q0, q_block), cols]
                keys_here = k_ref[pl.ds(k0, k_block), cols]
                values = jnp.concatenate([v_ref[pl.ds(k0, k_block), cols], ones], axis=1)
                num = None
                for i, member in enumerate(members):
                    scores = lax.dot_general(
                        jnp.where(member, queries, jnp.zeros_like(queries)),
                        keys_here,
                        (((1,), (1,)), ((), ())),
                        preferred_element_type=F32,
                    )
                    weights = jnp.where(allowed, jnp.exp(scores), 0.0).astype(BF16)
                    out = dot(weights, values)
                    num = out[:, :LANES] if num is None else jnp.where(member, out[:, :LANES], num)
                    den = jnp.where(lane == tile * per_tile + i, out[:, LANES:], den)
                num_ref[pl.ds(q0, q_block), cols] += num
                return den

            def some(step, den):
                for i in range(TILES):
                    den = heads(step * TILES + i, den)
                return den

            den = jnp.zeros((q_block, LANES), F32)
            den_ref[pl.ds(q0, q_block), :] += lax.fori_loop(0, width // LANES // TILES, some, den)

        return carry

    lax.fori_loop(0, count_q * count_k, one, 0)


def spread(per_head, width):
    shape = (LANES, width)
    chosen = lax.broadcasted_iota(jnp.int32, shape, 1) // (width // HEADS) == lax.broadcasted_iota(jnp.int32, shape, 0)
    chosen = jnp.where(chosen, 1.0, 0.0).astype(BF16)
    high = per_head.astype(BF16)
    return dot(high, chosen) + dot((per_head - high.astype(F32)).astype(BF16), chosen)


def normed(x_ref, gain_ref):
    return rms_norm(x_ref[...].astype(F32), gain_ref[0:1]).astype(BF16)


def project(n_ref, w_ref, index, out_ref, scale=None):
    width = w_ref.shape[2]
    tile = min(TILE, width)

    def one(j, carry):
        cols = pl.ds(pl.multiple_of(j * tile, tile), tile)
        out = dot(n_ref[...], w_ref[index, :, cols]).astype(BF16)
        out_ref[:, cols] = out if scale is None else out * jnp.asarray(scale, BF16)
        return carry

    lax.fori_loop(0, width // tile, one, 0)


def own_kernel(
    x_ref, gain_ref, w_ref, column_ref, row_ref, doc_ref, q_ref, num_ref, den_ref, n_ref, k_ref, v_ref
):
    head_dim = x_ref.shape[1] // HEADS
    here = lax.axis_index("seq") * x_ref.shape[0]
    n_ref[...] = normed(x_ref, gain_ref)
    project(n_ref, w_ref, 0, q_ref, head_dim ** (-0.5))
    project(n_ref, w_ref, 1, k_ref)
    project(n_ref, w_ref, 2, v_ref)
    num_ref[...] = jnp.zeros_like(num_ref)
    den_ref[...] = jnp.zeros_like(den_ref)
    attend(q_ref, k_ref, v_ref, num_ref, den_ref, column_ref, row_ref, doc_ref, here, here, True)


def piece_kernel(
    shift, first, x_ref, gain_ref, w_ref, q_ref, num_in, den_in, column_ref, row_ref, doc_ref,
    num_ref, den_ref, n_ref, k_ref, v_ref,
):
    del num_in, den_in
    rows, keys = q_ref.shape[0], x_ref.shape[0]
    shard = lax.axis_index("seq") - shift
    here, there = (shard + shift) * rows, jnp.maximum(shard, 0) * rows + first

    @pl.when((shard >= 0) & (doc_ref[0, there + keys - 1] >= doc_ref[0, here]))
    def _():
        n_ref[...] = normed(x_ref, gain_ref)
        project(n_ref, w_ref, 1, k_ref)
        project(n_ref, w_ref, 2, v_ref)
        attend(q_ref, k_ref, v_ref, num_ref, den_ref, column_ref, row_ref, doc_ref, here, there)


def far_document(doc_ref, rows, count):
    found = False
    for middle in range(1, count - 1):
        over = doc_ref[0, middle * rows - 1] == doc_ref[0, (middle + 1) * rows]
        deep = doc_ref[0, middle * rows - rows // 2 - 1] == doc_ref[0, (middle + 1) * rows]
        found = found | (over & deep)
    return found


def message_kernel(
    x_ref, piece_ref, gain_ref, w_ref, column_ref, row_ref, doc_ref,
    out_ref, q_ref, n_ref, k_ref, v_ref, num_ref, den_ref,
):
    half, width = x_ref.shape
    rows = 2 * half
    count = lax.axis_size("seq")
    place = lax.axis_index("seq")
    inside = (place >= 1) & (place + 1 < count)
    here = jnp.where(inside, place + 1, 0) * rows
    there = jnp.where(inside, place - 1, 0) * rows
    far = far_document(doc_ref, rows, count)

    @pl.when(jnp.logical_not(far))
    def _():
        out_ref[:, :width] = piece_ref[half:]

    @pl.when(far)
    def _():
        num_ref[...] = jnp.zeros_like(num_ref)
        den_ref[...] = jnp.zeros_like(den_ref)

        @pl.when(inside & (doc_ref[0, there + rows - 1] >= doc_ref[0, here]))
        def _():
            n_ref[:half] = normed(x_ref, gain_ref)
            project(n_ref.at[:half], w_ref, 0, q_ref, (width // HEADS) ** (-0.5))
            n_ref[...] = normed(piece_ref, gain_ref)
            project(n_ref, w_ref, 1, k_ref)
            project(n_ref, w_ref, 2, v_ref)
            attend(q_ref, k_ref, v_ref, num_ref, den_ref, column_ref, row_ref, doc_ref, here, there)

        out_ref[:, :width] = num_ref[...].astype(BF16)
        out_ref[:, width:] = den_ref[...].astype(BF16)


def reply_kernel(
    message_ref, gain_ref, w_ref, q_ref, num_in, den_in, column_ref, row_ref, doc_ref,
    num_ref, den_ref, n_ref, k_ref, v_ref,
):
    rows, width = q_ref.shape
    half = message_ref.shape[0]
    far = far_document(doc_ref, rows, lax.axis_size("seq"))

    @pl.when(far)
    def _():
        num_ref[:half] += message_ref[:, :width].astype(F32)
        den_ref[:half] += message_ref[:, width:].astype(F32)

    @pl.when(jnp.logical_not(far))
    def _():
        piece_kernel(
            2, half, message_ref.at[:, :width], gain_ref, w_ref, q_ref, num_in, den_in, column_ref, row_ref, doc_ref,
            num_ref, den_ref, n_ref, k_ref, v_ref,
        )


def finish_kernel(
    first, x_ref, num_ref, den_ref, w_ref, gain_ref, up_ref, down_ref, out_ref, acc_ref, n_ref, hidden_ref
):
    rows, width = out_ref.shape
    hidden = up_ref.shape[1]
    tile = min(TILE, hidden)
    here = pl.ds(first, rows)
    lane = lax.broadcasted_iota(jnp.int32, (rows, LANES), 1)
    inverse = 1.0 / jnp.where(lane < HEADS, den_ref[here], 1.0)
    n_ref[...] = (num_ref[here] * spread(inverse, width)).astype(BF16)
    acc_ref[...] = x_ref[here].astype(F32) + dot(n_ref[...], w_ref[3])
    n_ref[...] = rms_norm(acc_ref[...], gain_ref[1:2]).astype(BF16)

    def expand(j):
        cols = pl.ds(pl.multiple_of(j * tile, tile), tile)
        return jax.nn.gelu(dot(n_ref[...], up_ref[:, cols])).astype(BF16)

    def lower(j, expanded):
        return dot(expanded, down_ref[pl.ds(pl.multiple_of(j * tile, tile), tile)])

    hidden_ref[0] = expand(0)

    def one(j, carry):
        expanded = expand(j + 1)
        acc_ref[...] += lower(j, hidden_ref[j % 2])
        hidden_ref[(j + 1) % 2] = expanded
        return carry

    last = hidden // tile - 1
    lax.fori_loop(0, last, one, 0)
    out_ref[...] = (acc_ref[...] + lower(last, hidden_ref[last % 2])).astype(BF16)


def vmem():
    return pl.BlockSpec(memory_space=pltpu.VMEM)


def call(kernel, name, operands, docs, results, scratch, aliases=None, held=True):
    inputs = [pltpu.with_memory_space_constraint(operand, pltpu.VMEM) for operand in operands]
    in_specs = [vmem()] * len(inputs)
    if docs is not None:
        inputs.append(docs)
        in_specs.append(pl.BlockSpec(memory_space=pltpu.SMEM))
    return pl.pallas_call(
        kernel,
        in_specs=in_specs,
        out_specs=[vmem()] * len(results),
        out_shape=[pltpu.VMEM(*one) if held else jax.ShapeDtypeStruct(*one) for one in results],
        scratch_shapes=scratch,
        input_output_aliases=aliases or {},
        compiler_params=pltpu.CompilerParams(vmem_limit_bytes=VMEM_BYTES),
        cost_estimate=COST,
        name=name,
    )(*inputs)


def own_part(x, gains, weights, docs):
    rows, width = x.shape
    results = [((rows, width), BF16), ((rows, width), F32), ((rows, LANES), F32)]
    scratch = [pltpu.VMEM((rows, width), BF16)] * 3
    return call(own_kernel, "own_part", (x, gains, weights[0], docs.own_column, docs.ids), docs.ids, results, scratch)


def piece_part(x, shift, gains, w_attn, q, num, den, docs):
    rows, width = q.shape
    return call(
        functools.partial(piece_kernel, shift, 0),
        "piece_part",
        (x, gains, w_attn, q, num, den, docs.own_column, docs.ids),
        docs.ids,
        [((rows, width), F32), ((rows, LANES), F32)],
        [pltpu.VMEM((x.shape[0], width), BF16)] * 3,
        aliases={4: 0, 5: 1},
    )


def message_part(x, piece, gains, w_attn, docs):
    half, width = x.shape
    keys = 2 * half
    return call(
        message_kernel,
        "message_part",
        (x, piece, gains, w_attn, docs.later_column, docs.ids),
        docs.ids,
        [((half, width + LANES), BF16)],
        [pltpu.VMEM((half, width), BF16)]
        + [pltpu.VMEM((keys, width), BF16)] * 3
        + [pltpu.VMEM((half, width), F32), pltpu.VMEM((half, LANES), F32)],
    )[0]


def reply_part(message, gains, w_attn, q, num, den, docs):
    rows, width = q.shape
    return call(
        reply_kernel,
        "reply_part",
        (message, gains, w_attn, q, num, den, docs.own_column, docs.ids),
        docs.ids,
        [((rows, width), F32), ((rows, LANES), F32)],
        [pltpu.VMEM((message.shape[0], width), BF16)] * 3,
        aliases={4: 0, 5: 1},
    )


def finish_part(x, num, den, weights, gains, part, parts):
    width = x.shape[1]
    rows = x.shape[0] // parts
    w_attn, w_up, w_down = weights
    tile = min(TILE, w_up.shape[1])
    return call(
        functools.partial(finish_kernel, part * rows),
        "finish_part",
        (x, num, den, w_attn, gains, w_up, w_down),
        None,
        [((rows, width), BF16)],
        [pltpu.VMEM((rows, width), F32), pltpu.VMEM((rows, width), BF16), pltpu.VMEM((2, rows, tile), BF16)],
        held=parts > 1,
    )[0]


def shifted(value, axis, steps):
    count = lax.axis_size(axis)
    first, last = max(0, -steps), min(count, count - steps)
    return lax.ppermute(value, axis, [(i, i + steps) for i in range(first, last)])


def swapped(value, axis, bit):
    return lax.ppermute(value, axis, [(i, i ^ bit) for i in range(lax.axis_size(axis))])


class Documents:
    def __init__(self, doc_ids, rows):
        count = lax.axis_size("seq")
        self.ids, self.rows, self.half = doc_ids, rows, rows // 2
        longest = doc_ids.shape[1] // 2
        self.hops = min(count - 1, -(-(longest - 1) // rows))
        self.short = self.hops == 2 and longest <= 2 * rows and rows % 2 == 0
        place = lax.axis_index("seq")

        def column(later, size):
            start = jnp.minimum((place + later) * rows, doc_ids.shape[1] - size)
            ids = lax.dynamic_slice_in_dim(doc_ids, start, size, 1)
            return jnp.broadcast_to(ids.reshape(-1, 1), (size, LANES))

        self.own_column = column(0, rows)
        self.later_column = column(1, self.half) if self.short else self.own_column


def attention(state, piece, first_back, docs, gains, w_attn):
    q, *state = state
    if docs.short:
        message = shifted(message_part(after(first_back, q), piece, gains, w_attn, docs), "seq", 1)
        num, den = piece_part(piece, 1, gains, w_attn, q, *state, docs)
        return reply_part(message, gains, w_attn, q, num, den, docs)
    state = piece_part(piece, 1, gains, w_attn, q, *state, docs)
    for hop in range(2, docs.hops + 1):
        piece = shifted(piece, "seq", 1)
        state = piece_part(piece, hop, gains, w_attn, q, *state, docs)
    return state


def gain_factors(gain, bits):
    count = lax.axis_size("depth")
    all_gains = [gain] + [swapped(gain, "depth", i) for i in range(1, max(2, count // 2))]

    def block(first, size):
        return functools.reduce(jnp.multiply, all_gains[first : first + size])

    even_gain = jnp.where(bits[1], all_gains[1], gain)
    odd_gain = jnp.where(bits[1], gain, all_gains[1])
    factor_before, levels, bit = jnp.ones_like(gain), [], 2
    while bit < count:
        mine = block(0, bit)
        theirs = block(bit, bit) if 2 * bit < count else mine
        levels.append((bit, mine, theirs, factor_before))
        if 2 * bit < count:
            factor_before = jnp.where(bits[bit], factor_before * theirs, factor_before)
        bit *= 2
    return even_gain, odd_gain, levels


def after(value, *earlier):
    return lax.optimization_barrier((value, *earlier))[0]


class Chain:
    def __init__(self, states, following, factors, bits):
        self.states, self.following, self.bits = states, following, bits
        self.even_gain, self.odd_gain, self.levels = factors
        self.odd = bits[1]

    def enter(self, fine, *earlier):
        half = fine.shape[0] // 2
        mismatch = after(fine, *earlier).astype(F32) - self.following.astype(F32)
        low, high = mismatch[:half], mismatch[half:]
        mine = jnp.where(self.odd, high, low)
        sent = jnp.where(self.odd, low, high).astype(BF16)
        other = swapped(sent, "depth", 1).astype(F32)
        self.m_even = jnp.where(self.odd, other, mine)
        self.total = self.odd_gain * self.m_even + jnp.where(self.odd, mine, other)
        self.before = jnp.zeros_like(self.total)
        self.entered = self.total

    def level(self, index, sent_after=(), used_after=()):
        bit, factor, their_factor, factor_before = self.levels[index]
        upper = self.bits[bit]
        sent = after(self.total.astype(BF16), *sent_after)
        theirs = after(swapped(sent, "depth", bit), *used_after).astype(F32)
        if index + 1 < len(self.levels):
            self.total = jnp.where(upper, factor * theirs + self.total, their_factor * self.total + theirs)
        self.before = jnp.where(upper, factor_before * theirs + self.before, self.before)

    def leave(self, used_after=()):
        odd, c_even = self.odd, self.before
        c_odd = self.even_gain * c_even + self.m_even
        mine = jnp.where(odd, c_odd, c_even)
        other = swapped(jnp.where(odd, c_even, c_odd).astype(BF16), "depth", 1)
        other = after(other, *used_after).astype(F32)
        correction = jnp.concatenate([jnp.where(odd, other, mine), jnp.where(odd, mine, other)], axis=0)
        return (self.states.astype(F32) + correction).astype(BF16)


def on_device(interfaces, doc_ids, w_attn, w_up, w_down, norm_gains, coarse_gain):
    x = interfaces[0, 0]
    rows = x.shape[0]
    half = rows // 2
    gains = norm_gains[0, 0]
    weights = (w_attn[0, 0], w_up[0, 0], w_down[0, 0])
    parts = [x[:half], x[half:]]
    piece = shifted(x, "seq", 1)
    first_back = shifted(parts[0], "seq", -1)
    docs = Documents(doc_ids, rows)
    place, bits, bit = lax.axis_index("depth"), {}, 1
    while bit < lax.axis_size("depth"):
        bits[bit] = (place & bit) != 0
        bit *= 2
    early, bits, docs.own_column, docs.later_column = lax.optimization_barrier(
        (x, bits, docs.own_column, docs.later_column)
    )
    factors = gain_factors(after(coarse_gain, docs.own_column), bits)
    state = own_part(after(early, *jax.tree.leaves(factors)), gains, weights, docs)
    following = shifted(after(x, state[0]), "depth", -1)
    num, den = attention(state, piece, first_back, docs, gains, weights[0])
    following = [following[:half], following[half:]]
    first, second = [Chain(parts[i], following[i], factors, bits) for i in range(2)]
    first.enter(finish_part(x, num, den, weights, gains, 0, 2))
    fine = finish_part(x, after(num, first.total), den, weights, gains, 1, 2)
    first.level(0)
    second.enter(fine, first.total)
    for i in range(1, len(first.levels)):
        second.level(i - 1)
        first.level(i, used_after=(second.entered,))
    corrected = [first.leave()]
    halves = [shifted(corrected[0], "seq", 1)]
    first_back = shifted(corrected[0], "seq", -1)
    second.level(len(first.levels) - 1, sent_after=(corrected[0],))
    corrected.append(second.leave(used_after=(halves[0],)))
    halves.append(shifted(corrected[1], "seq", 1))
    x = jnp.concatenate(corrected, axis=0)
    state = own_part(x, gains, weights, docs)
    piece = jnp.concatenate(halves, axis=0)
    num, den = attention(state, piece, first_back, docs, gains, weights[0])
    return finish_part(x, num, den, weights, gains, 0, 1)[None, None]


def solution(mesh):
    in_specs = (
        P("depth", None, "seq", None),
        P(),
        P("depth", None, None, None, None),
        P("depth", None, None, None),
        P("depth", None, None, None),
        P("depth", None, None, None),
        P("depth", None),
    )
    out_specs = P("depth", None, "seq", None)
    return jax.shard_map(
        on_device, mesh=mesh, in_specs=in_specs, out_specs=out_specs, check_vma=False
    )
```

```python
import functools

import jax
import jax.numpy as jnp
from jax import lax
from jax.experimental import pallas as pl
from jax.experimental.pallas import tpu as pltpu
from jax.sharding import PartitionSpec as P

HEADS = 16
LANES = 128
BLOCK = 256
TILE = 512
TILES = 8
VMEM_BYTES = 12 * 1024 * 1024
COST = pl.CostEstimate(flops=1 << 20, bytes_accessed=1 << 16, transcendentals=0)
F32 = jnp.float32
BF16 = jnp.bfloat16


def rms_norm(value, gain):
    return value * lax.rsqrt(jnp.mean(value * value, axis=-1, keepdims=True) + 1e-05) * gain


def dot(a, b):
    return jnp.dot(a, b, preferred_element_type=F32)


def attend(q_ref, k_ref, v_ref, num_ref, den_ref, column_ref, row_ref, doc_ref, q_at, k_at, causal=False):
    rows, width = q_ref.shape
    keys = k_ref.shape[0]
    head_dim = width // HEADS
    per_tile = LANES // head_dim
    q_block, k_block = min(BLOCK, rows), min(BLOCK, keys)
    lane = lax.broadcasted_iota(jnp.int32, (1, LANES), 1)
    members = [lane // head_dim == i for i in range(per_tile)]
    count_q, count_k = rows // q_block, keys // k_block

    def one(index, carry):
        qi, ki = index // count_k, index % count_k
        q0 = pl.multiple_of(qi * q_block, q_block)
        k0 = pl.multiple_of(ki * k_block, k_block)
        needed = doc_ref[0, k_at + k0 + k_block - 1] >= doc_ref[0, q_at + q0]
        if causal:
            needed = (k0 <= q0) & (needed | (k0 == q0))

        @pl.when(needed)
        def _():
            key_docs = row_ref[:, pl.ds(pl.multiple_of(k_at + k0, k_block), k_block)]
            allowed = column_ref[pl.ds(q0, q_block), :1] == key_docs
            if causal:
                q_pos = q0 + lax.broadcasted_iota(jnp.int32, (q_block, k_block), 0)
                k_pos = k0 + lax.broadcasted_iota(jnp.int32, (q_block, k_block), 1)
                allowed = allowed & (k_pos <= q_pos)
            ones = jnp.ones((k_block, LANES), BF16)

            def heads(tile, den):
                cols = pl.ds(pl.multiple_of(tile * LANES, LANES), LANES)
                queries = q_ref[pl.ds(q0, q_block), cols]
                keys_here = k_ref[pl.ds(k0, k_block), cols]
                values = jnp.concatenate([v_ref[pl.ds(k0, k_block), cols], ones], axis=1)
                num = None
                for i, member in enumerate(members):
                    scores = lax.dot_general(
                        jnp.where(member, queries, jnp.zeros_like(queries)),
                        keys_here,
                        (((1,), (1,)), ((), ())),
                        preferred_element_type=F32,
                    )
                    weights = jnp.where(allowed, jnp.exp(scores), 0.0).astype(BF16)
                    out = dot(weights, values)
                    num = out[:, :LANES] if num is None else jnp.where(member, out[:, :LANES], num)
                    den = jnp.where(lane == tile * per_tile + i, out[:, LANES:], den)
                num_ref[pl.ds(q0, q_block), cols] += num
                return den

            def some(step, den):
                for i in range(TILES):
                    den = heads(step * TILES + i, den)
                return den

            den = jnp.zeros((q_block, LANES), F32)
            den_ref[pl.ds(q0, q_block), :] += lax.fori_loop(0, width // LANES // TILES, some, den, unroll=True)

        return carry

    lax.fori_loop(0, count_q * count_k, one, 0)


def spread(per_head, width):
    shape = (LANES, width)
    chosen = lax.broadcasted_iota(jnp.int32, shape, 1) // (width // HEADS) == lax.broadcasted_iota(jnp.int32, shape, 0)
    chosen = jnp.where(chosen, 1.0, 0.0).astype(BF16)
    high = per_head.astype(BF16)
    return dot(high, chosen) + dot((per_head - high.astype(F32)).astype(BF16), chosen)


def normed(x_ref, gain_ref):
    return rms_norm(x_ref[...].astype(F32), gain_ref[0:1]).astype(BF16)


def project(n_ref, w_ref, first, out_ref):
    count, _, width = out_ref.shape
    tile = min(TILE, width)
    steps = width // tile

    def one(step, carry):
        i, j = step // steps, step % steps
        cols = pl.ds(pl.multiple_of(j * tile, tile), tile)
        out = dot(n_ref[...], w_ref[first + i, :, cols]).astype(BF16)
        if first == 0:
            out *= jnp.where(i == 0, (width // HEADS) ** (-0.5), 1.0).astype(BF16)
        out_ref[i, :, cols] = out
        return carry

    lax.fori_loop(0, count * steps, one, 0)


def own_kernel(x_ref, gain_ref, w_ref, column_ref, row_ref, doc_ref, qkv_ref, num_ref, den_ref, n_ref):
    here = lax.axis_index("seq") * x_ref.shape[0]
    n_ref[...] = normed(x_ref, gain_ref)
    project(n_ref, w_ref, 0, qkv_ref)
    num_ref[...] = jnp.zeros_like(num_ref)
    den_ref[...] = jnp.zeros_like(den_ref)
    q_ref, k_ref, v_ref = [qkv_ref.at[i] for i in range(3)]
    attend(q_ref, k_ref, v_ref, num_ref, den_ref, column_ref, row_ref, doc_ref, here, here, True)


def piece_kernel(
    shift, first, x_ref, gain_ref, w_ref, qkv_ref, num_in, den_in, column_ref, row_ref, doc_ref,
    num_ref, den_ref, n_ref, kv_ref,
):
    del num_in, den_in
    rows, keys = qkv_ref.shape[1], x_ref.shape[0]
    shard = lax.axis_index("seq") - shift
    here, there = (shard + shift) * rows, jnp.maximum(shard, 0) * rows + first

    @pl.when((shard >= 0) & (doc_ref[0, there + keys - 1] >= doc_ref[0, here]))
    def _():
        n_ref[...] = normed(x_ref, gain_ref)
        project(n_ref, w_ref, 1, kv_ref)
        attend(
            qkv_ref.at[0], kv_ref.at[0], kv_ref.at[1], num_ref, den_ref, column_ref, row_ref, doc_ref, here, there
        )


def far_document(doc_ref, rows, count):
    found = False
    for middle in range(1, count - 1):
        over = doc_ref[0, middle * rows - 1] == doc_ref[0, (middle + 1) * rows]
        deep = doc_ref[0, middle * rows - rows // 2 - 1] == doc_ref[0, (middle + 1) * rows]
        found = found | (over & deep)
    return found


def message_kernel(
    x_ref, piece_ref, gain_ref, w_ref, column_ref, row_ref, doc_ref,
    out_ref, q_ref, n_ref, kv_ref, num_ref, den_ref,
):
    half, width = x_ref.shape
    rows = 2 * half
    count = lax.axis_size("seq")
    place = lax.axis_index("seq")
    inside = (place >= 1) & (place + 1 < count)
    here = jnp.where(inside, place + 1, 0) * rows
    there = jnp.where(inside, place - 1, 0) * rows
    far = far_document(doc_ref, rows, count)

    @pl.when(jnp.logical_not(far))
    def _():
        out_ref[:, :width] = piece_ref[half:]

    @pl.when(far)
    def _():
        num_ref[...] = jnp.zeros_like(num_ref)
        den_ref[...] = jnp.zeros_like(den_ref)

        @pl.when(inside & (doc_ref[0, there + rows - 1] >= doc_ref[0, here]))
        def _():
            n_ref[:half] = normed(x_ref, gain_ref)
            project(n_ref.at[:half], w_ref, 0, q_ref)
            n_ref[...] = normed(piece_ref, gain_ref)
            project(n_ref, w_ref, 1, kv_ref)
            attend(
                q_ref.at[0], kv_ref.at[0], kv_ref.at[1], num_ref, den_ref, column_ref, row_ref, doc_ref, here, there
            )

        out_ref[:, :width] = num_ref[...].astype(BF16)
        out_ref[:, width:] = den_ref[...].astype(BF16)


def reply_kernel(
    message_ref, gain_ref, w_ref, qkv_ref, num_in, den_in, column_ref, row_ref, doc_ref,
    num_ref, den_ref, n_ref, kv_ref,
):
    _, rows, width = qkv_ref.shape
    half = message_ref.shape[0]
    far = far_document(doc_ref, rows, lax.axis_size("seq"))

    @pl.when(far)
    def _():
        num_ref[:half] += message_ref[:, :width].astype(F32)
        den_ref[:half] += message_ref[:, width:].astype(F32)

    @pl.when(jnp.logical_not(far))
    def _():
        piece_kernel(
            2, half, message_ref.at[:, :width], gain_ref, w_ref, qkv_ref, num_in, den_in, column_ref, row_ref, doc_ref,
            num_ref, den_ref, n_ref, kv_ref,
        )


def finish_kernel(
    first, x_ref, num_ref, den_ref, w_ref, gain_ref, up_ref, down_ref, out_ref, acc_ref, n_ref, hidden_ref
):
    rows, width = out_ref.shape
    hidden = up_ref.shape[1]
    tile = min(TILE, hidden)
    here = pl.ds(first, rows)
    lane = lax.broadcasted_iota(jnp.int32, (rows, LANES), 1)
    inverse = 1.0 / jnp.where(lane < HEADS, den_ref[here], 1.0)
    n_ref[...] = (num_ref[here] * spread(inverse, width)).astype(BF16)
    acc_ref[...] = x_ref[here].astype(F32) + dot(n_ref[...], w_ref[3])
    n_ref[...] = rms_norm(acc_ref[...], gain_ref[1:2]).astype(BF16)

    def expand(j):
        cols = pl.ds(pl.multiple_of(j * tile, tile), tile)
        return jax.nn.gelu(dot(n_ref[...], up_ref[:, cols])).astype(BF16)

    def lower(j, expanded):
        return dot(expanded, down_ref[pl.ds(pl.multiple_of(j * tile, tile), tile)])

    hidden_ref[0] = expand(0)

    def one(j, carry):
        acc_ref[...] += lower(j, hidden_ref[j % 2])
        hidden_ref[(j + 1) % 2] = expand(j + 1)
        return carry

    last = hidden // tile - 1
    lax.fori_loop(0, last, one, 0)
    out_ref[...] = (acc_ref[...] + lower(last, hidden_ref[last % 2])).astype(BF16)


def vmem():
    return pl.BlockSpec(memory_space=pltpu.VMEM)


def call(kernel, name, operands, docs, results, scratch, aliases=None, held=True):
    inputs = [pltpu.with_memory_space_constraint(operand, pltpu.VMEM) for operand in operands]
    in_specs = [vmem()] * len(inputs)
    if docs is not None:
        inputs.append(docs)
        in_specs.append(pl.BlockSpec(memory_space=pltpu.SMEM))
    return pl.pallas_call(
        kernel,
        in_specs=in_specs,
        out_specs=[vmem()] * len(results),
        out_shape=[pltpu.VMEM(*one) if held else jax.ShapeDtypeStruct(*one) for one in results],
        scratch_shapes=scratch,
        input_output_aliases=aliases or {},
        compiler_params=pltpu.CompilerParams(vmem_limit_bytes=VMEM_BYTES),
        cost_estimate=COST,
        name=name,
    )(*inputs)


def own_part(x, gains, weights, docs):
    rows, width = x.shape
    results = [((3, rows, width), BF16), ((rows, width), F32), ((rows, LANES), F32)]
    scratch = [pltpu.VMEM((rows, width), BF16)]
    return call(own_kernel, "own_part", (x, gains, weights[0], docs.own_column, docs.ids), docs.ids, results, scratch)


def piece_part(x, shift, gains, w_attn, qkv, num, den, docs):
    _, rows, width = qkv.shape
    keys = x.shape[0]
    return call(
        functools.partial(piece_kernel, shift, 0),
        "piece_part",
        (x, gains, w_attn, qkv, num, den, docs.own_column, docs.ids),
        docs.ids,
        [((rows, width), F32), ((rows, LANES), F32)],
        [pltpu.VMEM((keys, width), BF16), pltpu.VMEM((2, keys, width), BF16)],
        aliases={4: 0, 5: 1},
    )


def message_part(x, piece, gains, w_attn, docs):
    half, width = x.shape
    keys = 2 * half
    return call(
        message_kernel,
        "message_part",
        (x, piece, gains, w_attn, docs.later_column, docs.ids),
        docs.ids,
        [((half, width + LANES), BF16)],
        [pltpu.VMEM((1, half, width), BF16), pltpu.VMEM((keys, width), BF16), pltpu.VMEM((2, keys, width), BF16)]
        + [pltpu.VMEM((half, width), F32), pltpu.VMEM((half, LANES), F32)],
    )[0]


def reply_part(message, gains, w_attn, qkv, num, den, docs):
    _, rows, width = qkv.shape
    keys = message.shape[0]
    return call(
        reply_kernel,
        "reply_part",
        (message, gains, w_attn, qkv, num, den, docs.own_column, docs.ids),
        docs.ids,
        [((rows, width), F32), ((rows, LANES), F32)],
        [pltpu.VMEM((keys, width), BF16), pltpu.VMEM((2, keys, width), BF16)],
        aliases={4: 0, 5: 1},
    )


def finish_part(x, num, den, weights, gains, part, parts):
    width = x.shape[1]
    rows = x.shape[0] // parts
    w_attn, w_up, w_down = weights
    tile = min(TILE, w_up.shape[1])
    return call(
        functools.partial(finish_kernel, part * rows),
        "finish_part",
        (x, num, den, w_attn, gains, w_up, w_down),
        None,
        [((rows, width), BF16)],
        [pltpu.VMEM((rows, width), F32), pltpu.VMEM((rows, width), BF16), pltpu.VMEM((2, rows, tile), BF16)],
        held=parts > 1,
    )[0]


def shifted(value, axis, steps):
    count = lax.axis_size(axis)
    return lax.ppermute(value, axis, [(i, (i + steps) % count) for i in range(count)])


def sent_back(value, axis):
    return lax.ppermute(value, axis, [(i, i - 1) for i in range(1, lax.axis_size(axis))])


def swapped(value, axis, bit):
    return lax.ppermute(value, axis, [(i, i ^ bit) for i in range(lax.axis_size(axis))])


class Documents:
    def __init__(self, doc_ids, rows):
        count = lax.axis_size("seq")
        self.ids, self.rows, self.half = doc_ids, rows, rows // 2
        longest = doc_ids.shape[1] // 2
        self.hops = min(count - 1, -(-(longest - 1) // rows))
        self.short = self.hops == 2 and longest <= 2 * rows and rows % 2 == 0
        place = lax.axis_index("seq")

        def column(later, size):
            start = jnp.minimum((place + later) * rows, doc_ids.shape[1] - size)
            ids = lax.dynamic_slice_in_dim(doc_ids, start, size, 1)
            return jnp.broadcast_to(ids.reshape(-1, 1), (size, LANES))

        self.own_column = column(0, rows)
        self.later_column = column(1, self.half) if self.short else self.own_column


def attention(state, piece, first_back, docs, gains, w_attn, meanwhile=lambda token: ()):
    qkv, *state = state
    if docs.short:
        message = message_part(after(first_back, qkv), piece, gains, w_attn, docs)
        message = shifted(message, "seq", 1)
        num, den = piece_part(piece, 1, gains, w_attn, qkv, *state, docs)
        done = meanwhile(den)
        num = after(num, *jax.tree.leaves(done))
        return reply_part(message, gains, w_attn, qkv, num, den, docs), done
    state = piece_part(piece, 1, gains, w_attn, qkv, *state, docs)
    done = meanwhile(state[1])
    for hop in range(2, docs.hops + 1):
        piece = shifted(piece, "seq", 1)
        state = piece_part(piece, hop, gains, w_attn, qkv, *state, docs)
    return state, done


def gain_factors(gain, bits):
    count = lax.axis_size("depth")
    all_gains = [gain] + [swapped(gain, "depth", i) for i in range(1, max(2, count // 2))]

    def block(first, size):
        return functools.reduce(jnp.multiply, all_gains[first : first + size])

    even_gain = jnp.where(bits[1], all_gains[1], gain)
    odd_gain = jnp.where(bits[1], gain, all_gains[1])
    factor_before, levels, bit = jnp.ones_like(gain), [], 2
    while bit < count:
        mine = block(0, bit)
        theirs = block(bit, bit) if 2 * bit < count else mine
        levels.append((bit, mine, theirs, factor_before))
        if 2 * bit < count:
            factor_before = jnp.where(bits[bit], factor_before * theirs, factor_before)
        bit *= 2
    return even_gain, odd_gain, levels


def after(value, *earlier):
    return lax.optimization_barrier((value, *earlier))[0]


class Chain:
    def __init__(self, states, following, factors, bits):
        self.states, self.following, self.bits = states, following, bits
        self.even_gain, self.odd_gain, self.levels = factors
        self.odd = bits[1]

    def enter(self, fine, *earlier):
        half = fine.shape[0] // 2
        mismatch = after(fine, *earlier).astype(F32) - self.following.astype(F32)
        low, high = mismatch[:half], mismatch[half:]
        mine = jnp.where(self.odd, high, low)
        sent = jnp.where(self.odd, low, high).astype(BF16)
        other = swapped(sent, "depth", 1).astype(F32)
        self.m_even = jnp.where(self.odd, other, mine)
        self.total = self.odd_gain * self.m_even + jnp.where(self.odd, mine, other)
        self.before = jnp.zeros_like(self.total)
        self.entered = self.total

    def level(self, index, sent_after=(), used_after=()):
        bit, factor, their_factor, factor_before = self.levels[index]
        upper = self.bits[bit]
        sent = after(self.total.astype(BF16), *sent_after)
        theirs = after(swapped(sent, "depth", bit), *used_after).astype(F32)
        if index + 1 < len(self.levels):
            self.total = jnp.where(upper, factor * theirs + self.total, their_factor * self.total + theirs)
        self.before = jnp.where(upper, factor_before * theirs + self.before, self.before)

    def leave(self, used_after=()):
        odd, c_even = self.odd, self.before
        c_odd = self.even_gain * c_even + self.m_even
        mine = jnp.where(odd, c_odd, c_even)
        other = swapped(jnp.where(odd, c_even, c_odd).astype(BF16), "depth", 1)
        other = after(other, *used_after).astype(F32)
        correction = jnp.concatenate([jnp.where(odd, other, mine), jnp.where(odd, mine, other)], axis=0)
        return (self.states.astype(F32) + correction).astype(BF16)


def on_device(interfaces, doc_ids, w_attn, w_up, w_down, norm_gains, coarse_gain):
    x = interfaces[0, 0]
    rows = x.shape[0]
    half = rows // 2
    gains = norm_gains[0, 0]
    weights = (w_attn[0, 0], w_up[0, 0], w_down[0, 0])
    parts = [x[:half], x[half:]]
    piece = shifted(x, "seq", 1)
    first_back = sent_back(parts[0], "seq")
    docs = Documents(doc_ids, rows)
    place, bits, bit = lax.axis_index("depth"), {}, 1
    while bit < lax.axis_size("depth"):
        bits[bit] = (place & bit) != 0
        bit *= 2
    early, bits, docs.own_column, docs.later_column = lax.optimization_barrier(
        (x, bits, docs.own_column, docs.later_column)
    )
    state = own_part(early, gains, weights, docs)
    following = sent_back(after(x, state[0]), "depth")
    (num, den), factors = attention(
        state, piece, first_back, docs, gains, weights[0], lambda token: gain_factors(after(coarse_gain, token), bits)
    )
    following = [following[:half], following[half:]]
    first, second = [Chain(parts[i], following[i], factors, bits) for i in range(2)]
    first.enter(finish_part(x, num, den, weights, gains, 0, 2))
    fine = finish_part(x, after(num, first.total), den, weights, gains, 1, 2)
    first.level(0)
    second.enter(fine, first.total)
    for i in range(1, len(first.levels)):
        second.level(i - 1)
        first.level(i, used_after=(second.entered,))
    corrected = [first.leave()]
    halves = [shifted(corrected[0], "seq", 1)]
    first_back = sent_back(corrected[0], "seq")
    second.level(len(first.levels) - 1, sent_after=(corrected[0],))
    corrected.append(second.leave(used_after=(halves[0],)))
    halves.append(shifted(corrected[1], "seq", 1))
    x = jnp.concatenate(corrected, axis=0)
    state = own_part(x, gains, weights, docs)
    piece = jnp.concatenate(halves, axis=0)
    (num, den), _ = attention(state, piece, first_back, docs, gains, weights[0])
    return finish_part(x, num, den, weights, gains, 0, 1)[None, None]


def solution(mesh):
    in_specs = (
        P("depth", None, "seq", None),
        P(),
        P("depth", None, None, None, None),
        P("depth", None, None, None),
        P("depth", None, None, None),
        P("depth", None, None, None),
        P("depth", None),
    )
    out_specs = P("depth", None, "seq", None)
    return jax.shard_map(
        on_device, mesh=mesh, in_specs=in_specs, out_specs=out_specs, check_vma=False
    )
```

```python
import functools

import jax
import jax.numpy as jnp
from jax import lax
from jax.experimental import pallas as pl
from jax.experimental.pallas import tpu as pltpu
from jax.sharding import PartitionSpec as P

HEADS = 16
LANES = 128
BLOCK = 256
TILE = 512
TILES = 8
VMEM_BYTES = 12 * 1024 * 1024
COST = pl.CostEstimate(flops=1 << 20, bytes_accessed=1 << 16, transcendentals=0)
F32 = jnp.float32
BF16 = jnp.bfloat16


def rms_norm(value, gain):
    return value * lax.rsqrt(jnp.mean(value * value, axis=-1, keepdims=True) + 1e-05) * gain


def dot(a, b):
    return jnp.dot(a, b, preferred_element_type=F32)


def attend(q_ref, k_ref, v_ref, num_ref, den_ref, column_ref, row_ref, doc_ref, q_at, k_at, causal=False):
    rows, width = q_ref.shape
    keys = k_ref.shape[0]
    head_dim = width // HEADS
    per_tile = LANES // head_dim
    q_block, k_block = min(BLOCK, rows), min(BLOCK, keys)
    lane = lax.broadcasted_iota(jnp.int32, (1, LANES), 1)
    members = [lane // head_dim == i for i in range(per_tile)]
    count_q, count_k = rows // q_block, keys // k_block

    def one(index, carry):
        qi, ki = index // count_k, index % count_k
        q0 = pl.multiple_of(qi * q_block, q_block)
        k0 = pl.multiple_of(ki * k_block, k_block)
        needed = doc_ref[0, k_at + k0 + k_block - 1] >= doc_ref[0, q_at + q0]
        if causal:
            needed = (k0 <= q0) & (needed | (k0 == q0))

        @pl.when(needed)
        def _():
            key_docs = row_ref[:, pl.ds(pl.multiple_of(k_at + k0, k_block), k_block)]
            allowed = column_ref[pl.ds(q0, q_block), :1] == key_docs
            if causal:
                q_pos = q0 + lax.broadcasted_iota(jnp.int32, (q_block, k_block), 0)
                k_pos = k0 + lax.broadcasted_iota(jnp.int32, (q_block, k_block), 1)
                allowed = allowed & (k_pos <= q_pos)
            ones = jnp.ones((k_block, LANES), BF16)

            def heads(tile, den):
                cols = pl.ds(pl.multiple_of(tile * LANES, LANES), LANES)
                queries = q_ref[pl.ds(q0, q_block), cols]
                keys_here = k_ref[pl.ds(k0, k_block), cols]
                values = jnp.concatenate([v_ref[pl.ds(k0, k_block), cols], ones], axis=1)
                num = None
                for i, member in enumerate(members):
                    scores = lax.dot_general(
                        jnp.where(member, queries, jnp.zeros_like(queries)),
                        keys_here,
                        (((1,), (1,)), ((), ())),
                        preferred_element_type=F32,
                    )
                    weights = jnp.where(allowed, jnp.exp(scores), 0.0).astype(BF16)
                    out = dot(weights, values)
                    num = out[:, :LANES] if num is None else jnp.where(member, out[:, :LANES], num)
                    den = jnp.where(lane == tile * per_tile + i, out[:, LANES:], den)
                num_ref[pl.ds(q0, q_block), cols] += num
                return den

            def some(step, den):
                for i in range(TILES):
                    den = heads(step * TILES + i, den)
                return den

            den = jnp.zeros((q_block, LANES), F32)
            den_ref[pl.ds(q0, q_block), :] += lax.fori_loop(0, width // LANES // TILES, some, den, unroll=True)

        return carry

    lax.fori_loop(0, count_q * count_k, one, 0)


def spread(per_head, width):
    shape = (LANES, width)
    chosen = lax.broadcasted_iota(jnp.int32, shape, 1) // (width // HEADS) == lax.broadcasted_iota(jnp.int32, shape, 0)
    chosen = jnp.where(chosen, 1.0, 0.0).astype(BF16)
    high = per_head.astype(BF16)
    return dot(high, chosen) + dot((per_head - high.astype(F32)).astype(BF16), chosen)


def normed(x_ref, gain_ref):
    return rms_norm(x_ref[...].astype(F32), gain_ref[0:1]).astype(BF16)


def project(n_ref, w_ref, first, out_ref):
    count, _, width = out_ref.shape
    tile = min(TILE, width)
    steps = width // tile

    def one(step, carry):
        i, j = step // steps, step % steps
        cols = pl.ds(pl.multiple_of(j * tile, tile), tile)
        out = dot(n_ref[...], w_ref[first + i, :, cols]).astype(BF16)
        if first == 0:
            out *= jnp.where(i == 0, (width // HEADS) ** (-0.5), 1.0).astype(BF16)
        out_ref[i, :, cols] = out
        return carry

    lax.fori_loop(0, count * steps, one, 0)


def own_kernel(x_ref, gain_ref, w_ref, column_ref, row_ref, doc_ref, qkv_ref, num_ref, den_ref, n_ref):
    here = lax.axis_index("seq") * x_ref.shape[0]
    n_ref[...] = normed(x_ref, gain_ref)
    project(n_ref, w_ref, 0, qkv_ref)
    num_ref[...] = jnp.zeros_like(num_ref)
    den_ref[...] = jnp.zeros_like(den_ref)
    q_ref, k_ref, v_ref = [qkv_ref.at[i] for i in range(3)]
    attend(q_ref, k_ref, v_ref, num_ref, den_ref, column_ref, row_ref, doc_ref, here, here, True)


def piece_kernel(
    shift, first, x_ref, gain_ref, w_ref, qkv_ref, num_in, den_in, column_ref, row_ref, doc_ref,
    num_ref, den_ref, n_ref, kv_ref,
):
    del num_in, den_in
    rows, keys = qkv_ref.shape[1], x_ref.shape[0]
    shard = lax.axis_index("seq") - shift
    here, there = (shard + shift) * rows, jnp.maximum(shard, 0) * rows + first

    @pl.when((shard >= 0) & (doc_ref[0, there + keys - 1] >= doc_ref[0, here]))
    def _():
        n_ref[...] = normed(x_ref, gain_ref)
        project(n_ref, w_ref, 1, kv_ref)
        attend(
            qkv_ref.at[0], kv_ref.at[0], kv_ref.at[1], num_ref, den_ref, column_ref, row_ref, doc_ref, here, there
        )


def far_document(doc_ref, rows, count):
    found = False
    for middle in range(1, count - 1):
        over = doc_ref[0, middle * rows - 1] == doc_ref[0, (middle + 1) * rows]
        deep = doc_ref[0, middle * rows - rows // 2 - 1] == doc_ref[0, (middle + 1) * rows]
        found = found | (over & deep)
    return found


def message_kernel(
    x_ref, piece_ref, gain_ref, w_ref, column_ref, row_ref, doc_ref,
    out_ref, q_ref, n_ref, kv_ref, num_ref, den_ref,
):
    half, width = x_ref.shape
    rows = 2 * half
    count = lax.axis_size("seq")
    place = lax.axis_index("seq")
    inside = (place >= 1) & (place + 1 < count)
    here = jnp.where(inside, place + 1, 0) * rows
    there = jnp.where(inside, place - 1, 0) * rows
    far = far_document(doc_ref, rows, count)

    @pl.when(jnp.logical_not(far))
    def _():
        out_ref[:, :width] = piece_ref[half:]

    @pl.when(far)
    def _():
        num_ref[...] = jnp.zeros_like(num_ref)
        den_ref[...] = jnp.zeros_like(den_ref)

        @pl.when(inside & (doc_ref[0, there + rows - 1] >= doc_ref[0, here]))
        def _():
            n_ref[:half] = normed(x_ref, gain_ref)
            project(n_ref.at[:half], w_ref, 0, q_ref)
            n_ref[...] = normed(piece_ref, gain_ref)
            project(n_ref, w_ref, 1, kv_ref)
            attend(
                q_ref.at[0], kv_ref.at[0], kv_ref.at[1], num_ref, den_ref, column_ref, row_ref, doc_ref, here, there
            )

        out_ref[:, :width] = num_ref[...].astype(BF16)
        out_ref[:, width:] = den_ref[...].astype(BF16)


def reply_kernel(
    message_ref, gain_ref, w_ref, qkv_ref, num_in, den_in, column_ref, row_ref, doc_ref,
    num_ref, den_ref, n_ref, kv_ref,
):
    _, rows, width = qkv_ref.shape
    half = message_ref.shape[0]
    far = far_document(doc_ref, rows, lax.axis_size("seq"))

    @pl.when(far)
    def _():
        num_ref[:half] += message_ref[:, :width].astype(F32)
        den_ref[:half] += message_ref[:, width:].astype(F32)

    @pl.when(jnp.logical_not(far))
    def _():
        piece_kernel(
            2, half, message_ref.at[:, :width], gain_ref, w_ref, qkv_ref, num_in, den_in, column_ref, row_ref, doc_ref,
            num_ref, den_ref, n_ref, kv_ref,
        )


def mix(first, x_ref, num_ref, den_ref, w_ref, gain_ref, acc_ref, n_ref):
    rows, width = acc_ref.shape
    here = pl.ds(first, rows)
    lane = lax.broadcasted_iota(jnp.int32, (rows, LANES), 1)
    inverse = 1.0 / jnp.where(lane < HEADS, den_ref[here], 1.0)
    n_ref[...] = (num_ref[here] * spread(inverse, width)).astype(BF16)
    acc_ref[...] = x_ref[here].astype(F32) + dot(n_ref[...], w_ref[3])
    n_ref[...] = rms_norm(acc_ref[...], gain_ref[1:2]).astype(BF16)


def feed_forward(begin, end, n_ref, up_ref, down_ref, acc_ref, hidden_ref):
    tile = hidden_ref.shape[2]

    def expand(j):
        cols = pl.ds(pl.multiple_of(j * tile, tile), tile)
        return jax.nn.gelu(dot(n_ref[...], up_ref[:, cols])).astype(BF16)

    def lower(j):
        return dot(hidden_ref[j % 2], down_ref[pl.ds(pl.multiple_of(j * tile, tile), tile)])

    hidden_ref[begin % 2] = expand(begin)

    def one(j, carry):
        acc_ref[...] += lower(j)
        hidden_ref[(j + 1) % 2] = expand(j + 1)
        return carry

    lax.fori_loop(begin, end - 1, one, 0)
    return lower(end - 1)


def finish_kernel(
    first, x_ref, num_ref, den_ref, w_ref, gain_ref, up_ref, down_ref, out_ref, acc_ref, n_ref, hidden_ref
):
    mix(first, x_ref, num_ref, den_ref, w_ref, gain_ref, acc_ref, n_ref)
    tiles = up_ref.shape[1] // hidden_ref.shape[2]
    last = feed_forward(0, tiles, n_ref, up_ref, down_ref, acc_ref, hidden_ref)
    out_ref[...] = (acc_ref[...] + last).astype(BF16)


def open_kernel(
    first, tiles, x_ref, num_ref, den_ref, w_ref, gain_ref, up_ref, down_ref, acc_ref, n_ref, hidden_ref
):
    mix(first, x_ref, num_ref, den_ref, w_ref, gain_ref, acc_ref, n_ref)
    last = feed_forward(0, tiles, n_ref, up_ref, down_ref, acc_ref, hidden_ref)
    acc_ref[...] += last


def close_kernel(begin, acc_in, n_ref, up_ref, down_ref, out_ref, acc_ref, hidden_ref):
    acc_ref[...] = acc_in[...]
    tiles = up_ref.shape[1] // hidden_ref.shape[2]
    last = feed_forward(begin, tiles, n_ref, up_ref, down_ref, acc_ref, hidden_ref)
    out_ref[...] = (acc_ref[...] + last).astype(BF16)


def vmem():
    return pl.BlockSpec(memory_space=pltpu.VMEM)


def call(kernel, name, operands, docs, results, scratch, aliases=None, held=True):
    inputs = [pltpu.with_memory_space_constraint(operand, pltpu.VMEM) for operand in operands]
    in_specs = [vmem()] * len(inputs)
    if docs is not None:
        inputs.append(docs)
        in_specs.append(pl.BlockSpec(memory_space=pltpu.SMEM))
    return pl.pallas_call(
        kernel,
        in_specs=in_specs,
        out_specs=[vmem()] * len(results),
        out_shape=[pltpu.VMEM(*one) if held else jax.ShapeDtypeStruct(*one) for one in results],
        scratch_shapes=scratch,
        input_output_aliases=aliases or {},
        compiler_params=pltpu.CompilerParams(vmem_limit_bytes=VMEM_BYTES),
        cost_estimate=COST,
        name=name,
    )(*inputs)


def own_part(x, gains, weights, docs):
    rows, width = x.shape
    results = [((3, rows, width), BF16), ((rows, width), F32), ((rows, LANES), F32)]
    scratch = [pltpu.VMEM((rows, width), BF16)]
    return call(own_kernel, "own_part", (x, gains, weights[0], docs.own_column, docs.ids), docs.ids, results, scratch)


def piece_part(x, shift, gains, w_attn, qkv, num, den, docs):
    _, rows, width = qkv.shape
    keys = x.shape[0]
    return call(
        functools.partial(piece_kernel, shift, 0),
        "piece_part",
        (x, gains, w_attn, qkv, num, den, docs.own_column, docs.ids),
        docs.ids,
        [((rows, width), F32), ((rows, LANES), F32)],
        [pltpu.VMEM((keys, width), BF16), pltpu.VMEM((2, keys, width), BF16)],
        aliases={4: 0, 5: 1},
    )


def message_part(x, piece, gains, w_attn, docs):
    half, width = x.shape
    keys = 2 * half
    return call(
        message_kernel,
        "message_part",
        (x, piece, gains, w_attn, docs.later_column, docs.ids),
        docs.ids,
        [((half, width + LANES), BF16)],
        [pltpu.VMEM((1, half, width), BF16), pltpu.VMEM((keys, width), BF16), pltpu.VMEM((2, keys, width), BF16)]
        + [pltpu.VMEM((half, width), F32), pltpu.VMEM((half, LANES), F32)],
    )[0]


def reply_part(message, gains, w_attn, qkv, num, den, docs):
    _, rows, width = qkv.shape
    keys = message.shape[0]
    return call(
        reply_kernel,
        "reply_part",
        (message, gains, w_attn, qkv, num, den, docs.own_column, docs.ids),
        docs.ids,
        [((rows, width), F32), ((rows, LANES), F32)],
        [pltpu.VMEM((keys, width), BF16), pltpu.VMEM((2, keys, width), BF16)],
        aliases={4: 0, 5: 1},
    )


def finish_part(x, num, den, weights, gains, part, parts):
    width = x.shape[1]
    rows = x.shape[0] // parts
    w_attn, w_up, w_down = weights
    tile = min(TILE, w_up.shape[1])
    return call(
        functools.partial(finish_kernel, part * rows),
        "finish_part",
        (x, num, den, w_attn, gains, w_up, w_down),
        None,
        [((rows, width), BF16)],
        [pltpu.VMEM((rows, width), F32), pltpu.VMEM((rows, width), BF16), pltpu.VMEM((2, rows, tile), BF16)],
        held=parts > 1,
    )[0]


def open_part(x, num, den, weights, gains, part, parts, tiles):
    width = x.shape[1]
    rows = x.shape[0] // parts
    return call(
        functools.partial(open_kernel, part * rows, tiles),
        "open_part",
        (x, num, den, weights[0], gains, *weights[1:]),
        None,
        [((rows, width), F32), ((rows, width), BF16)],
        [pltpu.VMEM((2, rows, min(TILE, weights[1].shape[1])), BF16)],
    )


def close_part(acc, n, weights, tiles):
    return call(
        functools.partial(close_kernel, tiles),
        "close_part",
        (acc, n, *weights[1:]),
        None,
        [(acc.shape, BF16)],
        [pltpu.VMEM(acc.shape, F32), pltpu.VMEM((2, acc.shape[0], min(TILE, weights[1].shape[1])), BF16)],
    )[0]


def shifted(value, axis, steps):
    count = lax.axis_size(axis)
    first, last = max(0, -steps), min(count, count - steps)
    return lax.ppermute(value, axis, [(i, i + steps) for i in range(first, last)])


def swapped(value, axis, bit):
    return lax.ppermute(value, axis, [(i, i ^ bit) for i in range(lax.axis_size(axis))])


class Documents:
    def __init__(self, doc_ids, rows):
        count = lax.axis_size("seq")
        self.ids, self.rows, self.half = doc_ids, rows, rows // 2
        longest = doc_ids.shape[1] // 2
        self.hops = min(count - 1, -(-(longest - 1) // rows))
        self.short = self.hops == 2 and longest <= 2 * rows and rows % 2 == 0
        place = lax.axis_index("seq")

        def column(later, size):
            start = jnp.minimum((place + later) * rows, doc_ids.shape[1] - size)
            ids = lax.dynamic_slice_in_dim(doc_ids, start, size, 1)
            return jnp.broadcast_to(ids.reshape(-1, 1), (size, LANES))

        self.own_column = column(0, rows)
        self.later_column = column(1, self.half) if self.short else self.own_column


def attention(state, piece, first_back, docs, gains, w_attn, meanwhile=lambda token: ()):
    qkv, *state = state
    if docs.short:
        message = message_part(after(first_back, qkv), piece, gains, w_attn, docs)
        message = shifted(message, "seq", 1)
        num, den = piece_part(piece, 1, gains, w_attn, qkv, *state, docs)
        done = meanwhile(den)
        num = after(num, *jax.tree.leaves(done))
        return reply_part(message, gains, w_attn, qkv, num, den, docs), done
    state = piece_part(piece, 1, gains, w_attn, qkv, *state, docs)
    done = meanwhile(state[1])
    for hop in range(2, docs.hops + 1):
        piece = shifted(piece, "seq", 1)
        state = piece_part(piece, hop, gains, w_attn, qkv, *state, docs)
    return state, done


def gain_factors(gain, bits):
    count = lax.axis_size("depth")
    all_gains = [gain] + [swapped(gain, "depth", i) for i in range(1, max(2, count // 2))]

    def block(first, size):
        return functools.reduce(jnp.multiply, all_gains[first : first + size])

    even_gain = jnp.where(bits[1], all_gains[1], gain)
    odd_gain = jnp.where(bits[1], gain, all_gains[1])
    factor_before, levels, bit = jnp.ones_like(gain), [], 2
    while bit < count:
        mine = block(0, bit)
        theirs = block(bit, bit) if 2 * bit < count else mine
        levels.append((bit, mine, theirs, factor_before))
        if 2 * bit < count:
            factor_before = jnp.where(bits[bit], factor_before * theirs, factor_before)
        bit *= 2
    return even_gain, odd_gain, levels


def after(value, *earlier):
    return lax.optimization_barrier((value, *earlier))[0]


class Chain:
    def __init__(self, states, following, factors, bits):
        self.states, self.following, self.bits = states, following, bits
        self.even_gain, self.odd_gain, self.levels = factors
        self.odd = bits[1]

    def enter(self, fine, *earlier):
        half = fine.shape[0] // 2
        mismatch = after(fine, *earlier).astype(F32) - self.following.astype(F32)
        low, high = mismatch[:half], mismatch[half:]
        mine = jnp.where(self.odd, high, low)
        sent = jnp.where(self.odd, low, high).astype(BF16)
        other = swapped(sent, "depth", 1).astype(F32)
        self.m_even = jnp.where(self.odd, other, mine)
        self.total = self.odd_gain * self.m_even + jnp.where(self.odd, mine, other)
        self.before = jnp.zeros_like(self.total)
        self.entered = self.total

    def level(self, index, sent_after=(), used_after=()):
        bit, factor, their_factor, factor_before = self.levels[index]
        upper = self.bits[bit]
        sent = after(self.total.astype(BF16), *sent_after)
        theirs = after(swapped(sent, "depth", bit), *used_after).astype(F32)
        if index + 1 < len(self.levels):
            self.total = jnp.where(upper, factor * theirs + self.total, their_factor * self.total + theirs)
        self.before = jnp.where(upper, factor_before * theirs + self.before, self.before)

    def leave(self, used_after=()):
        odd, c_even = self.odd, self.before
        c_odd = self.even_gain * c_even + self.m_even
        mine = jnp.where(odd, c_odd, c_even)
        other = swapped(jnp.where(odd, c_even, c_odd).astype(BF16), "depth", 1)
        other = after(other, *used_after).astype(F32)
        correction = jnp.concatenate([jnp.where(odd, other, mine), jnp.where(odd, mine, other)], axis=0)
        return (self.states.astype(F32) + correction).astype(BF16)


def on_device(interfaces, doc_ids, w_attn, w_up, w_down, norm_gains, coarse_gain):
    x = interfaces[0, 0]
    rows = x.shape[0]
    half = rows // 2
    gains = norm_gains[0, 0]
    weights = (w_attn[0, 0], w_up[0, 0], w_down[0, 0])
    parts = [x[:half], x[half:]]
    piece = shifted(x, "seq", 1)
    first_back = shifted(parts[0], "seq", -1)
    docs = Documents(doc_ids, rows)
    place, bits, bit = lax.axis_index("depth"), {}, 1
    while bit < lax.axis_size("depth"):
        bits[bit] = (place & bit) != 0
        bit *= 2
    early, bits, docs.own_column, docs.later_column = lax.optimization_barrier(
        (x, bits, docs.own_column, docs.later_column)
    )
    state = own_part(early, gains, weights, docs)
    following = shifted(after(x, state[0]), "depth", -1)
    (num, den), factors = attention(
        state, piece, first_back, docs, gains, weights[0], lambda token: gain_factors(after(coarse_gain, token), bits)
    )
    following = [following[:half], following[half:]]
    first, second = [Chain(parts[i], following[i], factors, bits) for i in range(2)]
    first.enter(finish_part(x, num, den, weights, gains, 0, 2))
    tiles = weights[1].shape[1] // TILE // 2
    acc, n = open_part(x, after(num, first.total), den, weights, gains, 1, 2, tiles)
    first.level(0, used_after=(n,))
    fine = close_part(after(acc, first.total), n, weights, tiles)
    first.level(1, used_after=(fine,))
    second.enter(fine, first.before)
    for i in range(2, len(first.levels)):
        second.level(i - 2)
        first.level(i)
    corrected = [first.leave()]
    halves = [shifted(corrected[0], "seq", 1)]
    first_back = shifted(corrected[0], "seq", -1)
    for i in range(max(0, len(first.levels) - 2), len(first.levels)):
        second.level(i, sent_after=(corrected[0],) if i > 0 else ())
    corrected.append(second.leave(used_after=(halves[0],)))
    halves.append(shifted(corrected[1], "seq", 1))
    x = jnp.concatenate(corrected, axis=0)
    state = own_part(x, gains, weights, docs)
    piece = jnp.concatenate(halves, axis=0)
    (num, den), _ = attention(state, piece, first_back, docs, gains, weights[0])
    return finish_part(x, num, den, weights, gains, 0, 1)[None, None]


def solution(mesh):
    in_specs = (
        P("depth", None, "seq", None),
        P(),
        P("depth", None, None, None, None),
        P("depth", None, None, None),
        P("depth", None, None, None),
        P("depth", None, None, None),
        P("depth", None),
    )
    out_specs = P("depth", None, "seq", None)
    return jax.shard_map(
        on_device, mesh=mesh, in_specs=in_specs, out_specs=out_specs, check_vma=False
    )
```

```python
import functools

import jax
import jax.numpy as jnp
from jax import lax
from jax.experimental import pallas as pl
from jax.experimental.pallas import tpu as pltpu
from jax.sharding import PartitionSpec as P

HEADS = 16
LANES = 128
BLOCK = 256
TILE = 512
TILES = 8
VMEM_BYTES = 10 * 1024 * 1024
COST = pl.CostEstimate(flops=1 << 20, bytes_accessed=1 << 16, transcendentals=0)
F32 = jnp.float32
BF16 = jnp.bfloat16


def rms_norm(value, gain):
    return value * lax.rsqrt(jnp.mean(value * value, axis=-1, keepdims=True) + 1e-05) * gain


def dot(a, b):
    return jnp.dot(a, b, preferred_element_type=F32)


def attend(q_ref, k_ref, v_ref, num_ref, den_ref, column_ref, row_ref, doc_ref, q_at, k_at, causal=False):
    rows, width = q_ref.shape
    keys = k_ref.shape[0]
    head_dim = width // HEADS
    per_tile = LANES // head_dim
    q_block, k_block = min(BLOCK, rows), min(BLOCK, keys)
    lane = lax.broadcasted_iota(jnp.int32, (1, LANES), 1)
    members = [lane // head_dim == i for i in range(per_tile)]
    count_q, count_k = rows // q_block, keys // k_block

    def one(index, carry):
        qi, ki = index // count_k, index % count_k
        q0 = pl.multiple_of(qi * q_block, q_block)
        k0 = pl.multiple_of(ki * k_block, k_block)
        needed = doc_ref[0, k_at + k0 + k_block - 1] >= doc_ref[0, q_at + q0]
        if causal:
            needed = (k0 <= q0) & (needed | (k0 == q0))

        @pl.when(needed)
        def _():
            key_docs = row_ref[:, pl.ds(pl.multiple_of(k_at + k0, k_block), k_block)]
            allowed = column_ref[pl.ds(q0, q_block), :1] == key_docs
            if causal:
                q_pos = q0 + lax.broadcasted_iota(jnp.int32, (q_block, k_block), 0)
                k_pos = k0 + lax.broadcasted_iota(jnp.int32, (q_block, k_block), 1)
                allowed = allowed & (k_pos <= q_pos)
            ones = jnp.ones((k_block, LANES), BF16)

            def heads(tile, den):
                cols = pl.ds(pl.multiple_of(tile * LANES, LANES), LANES)
                queries = q_ref[pl.ds(q0, q_block), cols]
                keys_here = k_ref[pl.ds(k0, k_block), cols]
                values = jnp.concatenate([v_ref[pl.ds(k0, k_block), cols], ones], axis=1)
                num = None
                for i, member in enumerate(members):
                    scores = lax.dot_general(
                        jnp.where(member, queries, jnp.zeros_like(queries)),
                        keys_here,
                        (((1,), (1,)), ((), ())),
                        preferred_element_type=F32,
                    )
                    weights = jnp.where(allowed, jnp.exp(scores), 0.0).astype(BF16)
                    out = dot(weights, values)
                    num = out[:, :LANES] if num is None else jnp.where(member, out[:, :LANES], num)
                    den = jnp.where(lane == tile * per_tile + i, out[:, LANES:], den)
                num_ref[pl.ds(q0, q_block), cols] += num
                return den

            def some(step, den):
                for i in range(TILES):
                    den = heads(step * TILES + i, den)
                return den

            den = jnp.zeros((q_block, LANES), F32)
            den_ref[pl.ds(q0, q_block), :] += lax.fori_loop(0, width // LANES // TILES, some, den, unroll=True)

        return carry

    lax.fori_loop(0, count_q * count_k, one, 0)


def spread(per_head, width):
    shape = (LANES, width)
    chosen = lax.broadcasted_iota(jnp.int32, shape, 1) // (width // HEADS) == lax.broadcasted_iota(jnp.int32, shape, 0)
    chosen = jnp.where(chosen, 1.0, 0.0).astype(BF16)
    high = per_head.astype(BF16)
    return dot(high, chosen) + dot((per_head - high.astype(F32)).astype(BF16), chosen)


def normed(x_ref, gain_ref):
    return rms_norm(x_ref[...].astype(F32), gain_ref[0:1]).astype(BF16)


def project(n_ref, w_ref, first, out_ref):
    count, _, width = out_ref.shape
    tile = min(TILE, width)
    steps = width // tile

    def one(step, carry):
        i, j = step // steps, step % steps
        cols = pl.ds(pl.multiple_of(j * tile, tile), tile)
        out = dot(n_ref[...], w_ref[first + i, :, cols]).astype(BF16)
        if first == 0:
            out *= jnp.where(i == 0, (width // HEADS) ** (-0.5), 1.0).astype(BF16)
        out_ref[i, :, cols] = out
        return carry

    lax.fori_loop(0, count * steps, one, 0)


def own_kernel(x_ref, gain_ref, w_ref, column_ref, row_ref, doc_ref, qkv_ref, num_ref, den_ref, n_ref):
    here = lax.axis_index("seq") * x_ref.shape[0]
    n_ref[...] = normed(x_ref, gain_ref)
    project(n_ref, w_ref, 0, qkv_ref)
    num_ref[...] = jnp.zeros_like(num_ref)
    den_ref[...] = jnp.zeros_like(den_ref)
    q_ref, k_ref, v_ref = [qkv_ref.at[i] for i in range(3)]
    attend(q_ref, k_ref, v_ref, num_ref, den_ref, column_ref, row_ref, doc_ref, here, here, True)


def piece_kernel(
    shift, first, x_ref, gain_ref, w_ref, qkv_ref, num_in, den_in, column_ref, row_ref, doc_ref,
    num_ref, den_ref, n_ref, kv_ref,
):
    del num_in, den_in
    rows, keys = qkv_ref.shape[1], x_ref.shape[0]
    shard = lax.axis_index("seq") - shift
    here, there = (shard + shift) * rows, jnp.maximum(shard, 0) * rows + first

    @pl.when((shard >= 0) & (doc_ref[0, there + keys - 1] >= doc_ref[0, here]))
    def _():
        n_ref[...] = normed(x_ref, gain_ref)
        project(n_ref, w_ref, 1, kv_ref)
        attend(
            qkv_ref.at[0], kv_ref.at[0], kv_ref.at[1], num_ref, den_ref, column_ref, row_ref, doc_ref, here, there
        )


def far_document(doc_ref, rows, count):
    found = False
    for middle in range(1, count - 1):
        over = doc_ref[0, middle * rows - 1] == doc_ref[0, (middle + 1) * rows]
        deep = doc_ref[0, middle * rows - rows // 2 - 1] == doc_ref[0, (middle + 1) * rows]
        found = found | (over & deep)
    return found


def message_kernel(
    x_ref, piece_ref, gain_ref, w_ref, column_ref, row_ref, doc_ref,
    out_ref, q_ref, n_ref, kv_ref, num_ref, den_ref,
):
    half, width = x_ref.shape
    rows = 2 * half
    count = lax.axis_size("seq")
    place = lax.axis_index("seq")
    inside = (place >= 1) & (place + 1 < count)
    here = jnp.where(inside, place + 1, 0) * rows
    there = jnp.where(inside, place - 1, 0) * rows
    far = far_document(doc_ref, rows, count)

    @pl.when(jnp.logical_not(far))
    def _():
        out_ref[:, :width] = piece_ref[half:]

    @pl.when(far)
    def _():
        num_ref[...] = jnp.zeros_like(num_ref)
        den_ref[...] = jnp.zeros_like(den_ref)

        @pl.when(inside & (doc_ref[0, there + rows - 1] >= doc_ref[0, here]))
        def _():
            n_ref[:half] = normed(x_ref, gain_ref)
            project(n_ref.at[:half], w_ref, 0, q_ref)
            n_ref[...] = normed(piece_ref, gain_ref)
            project(n_ref, w_ref, 1, kv_ref)
            attend(
                q_ref.at[0], kv_ref.at[0], kv_ref.at[1], num_ref, den_ref, column_ref, row_ref, doc_ref, here, there
            )

        out_ref[:, :width] = num_ref[...].astype(BF16)
        out_ref[:, width:] = den_ref[...].astype(BF16)


def reply_kernel(
    message_ref, gain_ref, w_ref, qkv_ref, num_in, den_in, column_ref, row_ref, doc_ref,
    num_ref, den_ref, n_ref, kv_ref,
):
    _, rows, width = qkv_ref.shape
    half = message_ref.shape[0]
    far = far_document(doc_ref, rows, lax.axis_size("seq"))

    @pl.when(far)
    def _():
        num_ref[:half] += message_ref[:, :width].astype(F32)
        den_ref[:half] += message_ref[:, width:].astype(F32)

    @pl.when(jnp.logical_not(far))
    def _():
        piece_kernel(
            2, half, message_ref.at[:, :width], gain_ref, w_ref, qkv_ref, num_in, den_in, column_ref, row_ref, doc_ref,
            num_ref, den_ref, n_ref, kv_ref,
        )


def mix(first, x_ref, num_ref, den_ref, w_ref, gain_ref, acc_ref, n_ref):
    rows, width = acc_ref.shape
    here = pl.ds(first, rows)
    lane = lax.broadcasted_iota(jnp.int32, (rows, LANES), 1)
    inverse = 1.0 / jnp.where(lane < HEADS, den_ref[here], 1.0)
    n_ref[...] = (num_ref[here] * spread(inverse, width)).astype(BF16)
    acc_ref[...] = x_ref[here].astype(F32) + dot(n_ref[...], w_ref[3])
    n_ref[...] = rms_norm(acc_ref[...], gain_ref[1:2]).astype(BF16)


def feed_forward(begin, end, n_ref, up_ref, down_ref, acc_ref, hidden_ref):
    tile = hidden_ref.shape[2]

    def expand(j):
        cols = pl.ds(pl.multiple_of(j * tile, tile), tile)
        return jax.nn.gelu(dot(n_ref[...], up_ref[:, cols])).astype(BF16)

    def lower(j):
        return dot(hidden_ref[j % 2], down_ref[pl.ds(pl.multiple_of(j * tile, tile), tile)])

    hidden_ref[begin % 2] = expand(begin)

    def one(j, carry):
        acc_ref[...] += lower(j)
        hidden_ref[(j + 1) % 2] = expand(j + 1)
        return carry

    lax.fori_loop(begin, end - 1, one, 0)
    return lower(end - 1)


def finish_kernel(
    first, x_ref, num_ref, den_ref, w_ref, gain_ref, up_ref, down_ref, out_ref, acc_ref, n_ref, hidden_ref
):
    mix(first, x_ref, num_ref, den_ref, w_ref, gain_ref, acc_ref, n_ref)
    tiles = up_ref.shape[1] // hidden_ref.shape[2]
    last = feed_forward(0, tiles, n_ref, up_ref, down_ref, acc_ref, hidden_ref)
    out_ref[...] = (acc_ref[...] + last).astype(BF16)


def open_kernel(
    first, tiles, x_ref, num_ref, den_ref, w_ref, gain_ref, up_ref, down_ref, acc_ref, n_ref, hidden_ref
):
    mix(first, x_ref, num_ref, den_ref, w_ref, gain_ref, acc_ref, n_ref)
    last = feed_forward(0, tiles, n_ref, up_ref, down_ref, acc_ref, hidden_ref)
    acc_ref[...] += last


def close_kernel(begin, acc_in, n_ref, up_ref, down_ref, out_ref, acc_ref, hidden_ref):
    acc_ref[...] = acc_in[...]
    tiles = up_ref.shape[1] // hidden_ref.shape[2]
    last = feed_forward(begin, tiles, n_ref, up_ref, down_ref, acc_ref, hidden_ref)
    out_ref[...] = (acc_ref[...] + last).astype(BF16)


def vmem():
    return pl.BlockSpec(memory_space=pltpu.VMEM)


def call(kernel, name, operands, docs, results, scratch, aliases=None, held=True):
    inputs = [pltpu.with_memory_space_constraint(operand, pltpu.VMEM) for operand in operands]
    in_specs = [vmem()] * len(inputs)
    if docs is not None:
        inputs.append(docs)
        in_specs.append(pl.BlockSpec(memory_space=pltpu.SMEM))
    return pl.pallas_call(
        kernel,
        in_specs=in_specs,
        out_specs=[vmem()] * len(results),
        out_shape=[pltpu.VMEM(*one) if held else jax.ShapeDtypeStruct(*one) for one in results],
        scratch_shapes=scratch,
        input_output_aliases=aliases or {},
        compiler_params=pltpu.CompilerParams(vmem_limit_bytes=VMEM_BYTES),
        cost_estimate=COST,
        name=name,
    )(*inputs)


def own_part(x, gains, weights, docs):
    rows, width = x.shape
    results = [((3, rows, width), BF16), ((rows, width), F32), ((rows, LANES), F32)]
    scratch = [pltpu.VMEM((rows, width), BF16)]
    return call(own_kernel, "own_part", (x, gains, weights[0], docs.own_column, docs.ids), docs.ids, results, scratch)


def piece_part(x, shift, gains, w_attn, qkv, num, den, docs):
    _, rows, width = qkv.shape
    keys = x.shape[0]
    return call(
        functools.partial(piece_kernel, shift, 0),
        "piece_part",
        (x, gains, w_attn, qkv, num, den, docs.own_column, docs.ids),
        docs.ids,
        [((rows, width), F32), ((rows, LANES), F32)],
        [pltpu.VMEM((keys, width), BF16), pltpu.VMEM((2, keys, width), BF16)],
        aliases={4: 0, 5: 1},
    )


def message_part(x, piece, gains, w_attn, docs):
    half, width = x.shape
    keys = 2 * half
    return call(
        message_kernel,
        "message_part",
        (x, piece, gains, w_attn, docs.later_column, docs.ids),
        docs.ids,
        [((half, width + LANES), BF16)],
        [pltpu.VMEM((1, half, width), BF16), pltpu.VMEM((keys, width), BF16), pltpu.VMEM((2, keys, width), BF16)]
        + [pltpu.VMEM((half, width), F32), pltpu.VMEM((half, LANES), F32)],
    )[0]


def reply_part(message, gains, w_attn, qkv, num, den, docs):
    _, rows, width = qkv.shape
    keys = message.shape[0]
    return call(
        reply_kernel,
        "reply_part",
        (message, gains, w_attn, qkv, num, den, docs.own_column, docs.ids),
        docs.ids,
        [((rows, width), F32), ((rows, LANES), F32)],
        [pltpu.VMEM((keys, width), BF16), pltpu.VMEM((2, keys, width), BF16)],
        aliases={4: 0, 5: 1},
    )


def finish_part(x, num, den, weights, gains, part, parts):
    width = x.shape[1]
    rows = x.shape[0] // parts
    w_attn, w_up, w_down = weights
    tile = min(TILE, w_up.shape[1])
    return call(
        functools.partial(finish_kernel, part * rows),
        "finish_part",
        (x, num, den, w_attn, gains, w_up, w_down),
        None,
        [((rows, width), BF16)],
        [pltpu.VMEM((rows, width), F32), pltpu.VMEM((rows, width), BF16), pltpu.VMEM((2, rows, tile), BF16)],
        held=parts > 1,
    )[0]


def open_part(x, num, den, weights, gains, part, parts, tiles):
    width = x.shape[1]
    rows = x.shape[0] // parts
    return call(
        functools.partial(open_kernel, part * rows, tiles),
        "open_part",
        (x, num, den, weights[0], gains, *weights[1:]),
        None,
        [((rows, width), F32), ((rows, width), BF16)],
        [pltpu.VMEM((2, rows, min(TILE, weights[1].shape[1])), BF16)],
    )


def close_part(acc, n, weights, tiles):
    return call(
        functools.partial(close_kernel, tiles),
        "close_part",
        (acc, n, *weights[1:]),
        None,
        [(acc.shape, BF16)],
        [pltpu.VMEM(acc.shape, F32), pltpu.VMEM((2, acc.shape[0], min(TILE, weights[1].shape[1])), BF16)],
    )[0]


def shifted(value, axis, steps):
    count = lax.axis_size(axis)
    first, last = max(0, -steps), min(count, count - steps)
    return lax.ppermute(value, axis, [(i, i + steps) for i in range(first, last)])


def swapped(value, axis, bit):
    return lax.ppermute(value, axis, [(i, i ^ bit) for i in range(lax.axis_size(axis))])


class Documents:
    def __init__(self, doc_ids, rows):
        count = lax.axis_size("seq")
        self.ids, self.rows, self.half = doc_ids, rows, rows // 2
        longest = doc_ids.shape[1] // 2
        self.hops = min(count - 1, -(-(longest - 1) // rows))
        self.short = self.hops == 2 and longest <= 2 * rows and rows % 2 == 0
        place = lax.axis_index("seq")

        def column(later, size):
            start = jnp.minimum((place + later) * rows, doc_ids.shape[1] - size)
            ids = lax.dynamic_slice_in_dim(doc_ids, start, size, 1)
            return jnp.broadcast_to(ids.reshape(-1, 1), (size, LANES))

        self.own_column = column(0, rows)
        self.later_column = column(1, self.half) if self.short else self.own_column


def attention(state, piece, first_back, docs, gains, w_attn, meanwhile=lambda token: ()):
    qkv, *state = state
    if docs.short:
        message = message_part(after(first_back, qkv), piece, gains, w_attn, docs)
        state = after(state[0], message), state[1]
        message = shifted(message, "seq", 1)
        num, den = piece_part(piece, 1, gains, w_attn, qkv, *state, docs)
        done = meanwhile(den)
        num = after(num, *jax.tree.leaves(done))
        return reply_part(message, gains, w_attn, qkv, num, den, docs), done
    state = piece_part(piece, 1, gains, w_attn, qkv, *state, docs)
    done = meanwhile(state[1])
    for hop in range(2, docs.hops + 1):
        piece = shifted(piece, "seq", 1)
        state = piece_part(piece, hop, gains, w_attn, qkv, *state, docs)
    return state, done


def gain_factors(gain, bits):
    count = lax.axis_size("depth")
    all_gains = [gain] + [swapped(gain, "depth", i) for i in range(1, max(2, count // 2))]

    def block(first, size):
        return functools.reduce(jnp.multiply, all_gains[first : first + size])

    even_gain = jnp.where(bits[1], all_gains[1], gain)
    odd_gain = jnp.where(bits[1], gain, all_gains[1])
    factor_before, levels, bit = jnp.ones_like(gain), [], 2
    while bit < count:
        mine = block(0, bit)
        theirs = block(bit, bit) if 2 * bit < count else mine
        levels.append((bit, mine, theirs, factor_before))
        if 2 * bit < count:
            factor_before = jnp.where(bits[bit], factor_before * theirs, factor_before)
        bit *= 2
    return even_gain, odd_gain, levels


def after(value, *earlier):
    return lax.optimization_barrier((value, *earlier))[0]


def own_half(rows, odd):
    half = rows.shape[0] // 2
    return jnp.where(odd, rows[half:], rows[:half]), jnp.where(odd, rows[:half], rows[half:])


class Chain:
    def __init__(self, own_states, other_states, factors, bits):
        self.bits, self.odd = bits, bits[1]
        self.even_gain, self.odd_gain, self.levels = factors
        even, odd = self.sorted(own_states, other_states)
        self.even_states = even
        self.leading = jnp.logical_not(functools.reduce(jnp.logical_or, [bits[b] for b in bits if b > 1], False))
        behind = jnp.where(self.leading, 0.0, self.even_gain * even.astype(F32))
        self.known = self.odd_gain * (behind + odd.astype(F32))

    def sorted(self, mine, other):
        return jnp.where(self.odd, other, mine), jnp.where(self.odd, mine, other)

    def enter(self, fine, *earlier):
        fine = after(fine, *earlier)
        half = fine.shape[0] // 2
        mine, sent = own_half(fine, self.odd)
        other = swapped(sent, "depth", 1)
        self.fine_even, fine_odd = self.sorted(mine, other)
        self.total = self.odd_gain * self.fine_even.astype(F32) + fine_odd.astype(F32) - self.known
        self.before = jnp.zeros_like(self.total)

    def level(self, index, sent_after=(), used_after=()):
        bit, factor, their_factor, factor_before = self.levels[index]
        upper = self.bits[bit]
        sent = after(self.total.astype(BF16), *sent_after)
        theirs = after(swapped(sent, "depth", bit), *used_after).astype(F32)
        if index + 1 < len(self.levels):
            self.total = jnp.where(upper, factor * theirs + self.total, their_factor * self.total + theirs)
        self.before = jnp.where(upper, factor_before * theirs + self.before, self.before)

    def leave(self, sent_after=()):
        even_states = self.even_states.astype(F32)
        even = jnp.where(self.leading, even_states, self.before)
        odd = self.even_gain * (even - even_states) + self.fine_even.astype(F32)
        even, odd = even.astype(BF16), odd.astype(BF16)
        mine, sent = jnp.where(self.odd, odd, even), jnp.where(self.odd, even, odd)
        other = swapped(after(sent, *sent_after), "depth", 1)
        low, high = self.sorted(mine, other)
        return jnp.concatenate([low, high], axis=0)


def on_device(interfaces, doc_ids, w_attn, w_up, w_down, norm_gains, coarse_gain):
    x = interfaces[0, 0]
    rows = x.shape[0]
    half = rows // 2
    gains = norm_gains[0, 0]
    weights = (w_attn[0, 0], w_up[0, 0], w_down[0, 0])
    parts = [x[:half], x[half:]]
    piece = shifted(x, "seq", 1)
    first_back = shifted(parts[0], "seq", -1)
    docs = Documents(doc_ids, rows)
    place, bits, bit = lax.axis_index("depth"), {}, 1
    while bit < lax.axis_size("depth"):
        bits[bit] = (place & bit) != 0
        bit *= 2
    early, bits, docs.own_column, docs.later_column = lax.optimization_barrier(
        (x, bits, docs.own_column, docs.later_column)
    )
    state = own_part(early, gains, weights, docs)
    kept, sent = zip(*[own_half(part, bits[1]) for part in parts])
    other = swapped(after(jnp.concatenate(sent, axis=0), state[0]), "depth", 1)
    other = other[: half // 2], other[half // 2 :]
    (num, den), factors = attention(
        state, piece, first_back, docs, gains, weights[0], lambda token: gain_factors(after(coarse_gain, token), bits)
    )
    first, second = [Chain(kept[i], other[i], factors, bits) for i in range(2)]
    num = after(num, first.known, second.known)
    first.enter(finish_part(x, num, den, weights, gains, 0, 2))
    tiles = weights[1].shape[1] // TILE // 2
    acc, n = open_part(x, after(num, first.total), den, weights, gains, 1, 2, tiles)
    first.level(0, used_after=(n,))
    fine = close_part(after(acc, first.total), n, weights, tiles)
    first.level(1, used_after=(fine,))
    second.enter(fine, first.before)
    for i in range(2, len(first.levels)):
        second.level(i - 2)
        first.level(i)
    corrected = [first.leave()]
    halves = [shifted(corrected[0], "seq", 1)]
    first_back = shifted(corrected[0], "seq", -1)
    for i in range(max(0, len(first.levels) - 2), len(first.levels)):
        second.level(i, sent_after=(corrected[0],) if i > 0 else ())
    corrected.append(second.leave(sent_after=(halves[0],)))
    halves.append(shifted(corrected[1], "seq", 1))
    x = jnp.concatenate(corrected, axis=0)
    state = own_part(x, gains, weights, docs)
    piece = jnp.concatenate(halves, axis=0)
    (num, den), _ = attention(state, piece, first_back, docs, gains, weights[0])
    return finish_part(x, num, den, weights, gains, 0, 1)[None, None]


def solution(mesh):
    in_specs = (
        P("depth", None, "seq", None),
        P(),
        P("depth", None, None, None, None),
        P("depth", None, None, None),
        P("depth", None, None, None),
        P("depth", None, None, None),
        P("depth", None),
    )
    out_specs = P("depth", None, "seq", None)
    return jax.shard_map(
        on_device, mesh=mesh, in_specs=in_specs, out_specs=out_specs, check_vma=False
    )
```

```python
import functools

import jax
import jax.numpy as jnp
from jax import lax
from jax.experimental import pallas as pl
from jax.experimental.pallas import tpu as pltpu
from jax.sharding import PartitionSpec as P

HEADS = 16
LANES = 128
CARRIED = 16
BLOCK = 256
TILE = 512
TILES = 8
VMEM_BYTES = 10 * 1024 * 1024
COST = pl.CostEstimate(flops=1 << 20, bytes_accessed=1 << 16, transcendentals=0)
F32 = jnp.float32
BF16 = jnp.bfloat16


def rms_norm(value, gain):
    return value * lax.rsqrt(jnp.mean(value * value, axis=-1, keepdims=True) + 1e-05) * gain


def dot(a, b):
    return jnp.dot(a, b, preferred_element_type=F32)


def attend(q_ref, k_ref, v_ref, num_ref, den_ref, column_ref, row_ref, doc_ref, q_at, k_at, causal=False):
    rows, width = q_ref.shape
    keys = k_ref.shape[0]
    head_dim = width // HEADS
    per_tile = LANES // head_dim
    q_block, k_block = min(BLOCK, rows), min(BLOCK, keys)
    lane = lax.broadcasted_iota(jnp.int32, (1, LANES), 1)
    members = [lane // head_dim == i for i in range(per_tile)]
    count_q, count_k = rows // q_block, keys // k_block

    def one(index, carry):
        qi, ki = index // count_k, index % count_k
        q0 = pl.multiple_of(qi * q_block, q_block)
        k0 = pl.multiple_of(ki * k_block, k_block)
        needed = doc_ref[0, k_at + k0 + k_block - 1] >= doc_ref[0, q_at + q0]
        if causal:
            needed = (k0 <= q0) & (needed | (k0 == q0))

        @pl.when(needed)
        def _():
            key_docs = row_ref[:, pl.ds(pl.multiple_of(k_at + k0, k_block), k_block)]
            allowed = column_ref[pl.ds(q0, q_block), :1] == key_docs
            if causal:
                q_pos = q0 + lax.broadcasted_iota(jnp.int32, (q_block, k_block), 0)
                k_pos = k0 + lax.broadcasted_iota(jnp.int32, (q_block, k_block), 1)
                allowed = allowed & (k_pos <= q_pos)
            ones = jnp.ones((k_block, LANES), BF16)

            def heads(tile, den):
                cols = pl.ds(pl.multiple_of(tile * LANES, LANES), LANES)
                queries = q_ref[pl.ds(q0, q_block), cols]
                keys_here = k_ref[pl.ds(k0, k_block), cols]
                values = jnp.concatenate([v_ref[pl.ds(k0, k_block), cols], ones], axis=1)
                num = None
                for i, member in enumerate(members):
                    scores = lax.dot_general(
                        jnp.where(member, queries, jnp.zeros_like(queries)),
                        keys_here,
                        (((1,), (1,)), ((), ())),
                        preferred_element_type=F32,
                    )
                    weights = jnp.where(allowed, jnp.exp(scores), 0.0).astype(BF16)
                    out = dot(weights, values)
                    num = out[:, :LANES] if num is None else jnp.where(member, out[:, :LANES], num)
                    den = jnp.where(lane == tile * per_tile + i, out[:, LANES:], den)
                num_ref[pl.ds(q0, q_block), cols] += num
                return den

            def some(step, den):
                for i in range(TILES):
                    den = heads(step * TILES + i, den)
                return den

            den = jnp.zeros((q_block, LANES), F32)
            den_ref[pl.ds(q0, q_block), :] += lax.fori_loop(0, width // LANES // TILES, some, den, unroll=True)

        return carry

    lax.fori_loop(0, count_q * count_k, one, 0)


def spread(per_head, width):
    shape = (LANES, width)
    chosen = lax.broadcasted_iota(jnp.int32, shape, 1) // (width // HEADS) == lax.broadcasted_iota(jnp.int32, shape, 0)
    chosen = jnp.where(chosen, 1.0, 0.0).astype(BF16)
    high = per_head.astype(BF16)
    return dot(high, chosen) + dot((per_head - high.astype(F32)).astype(BF16), chosen)


def normed(x_ref, gain_ref):
    return rms_norm(x_ref[...].astype(F32), gain_ref[0:1]).astype(BF16)


def project(n_ref, w_ref, first, out_ref):
    count, _, width = out_ref.shape
    tile = min(TILE, width)
    steps = width // tile

    def one(step, carry):
        i, j = step // steps, step % steps
        cols = pl.ds(pl.multiple_of(j * tile, tile), tile)
        out = dot(n_ref[...], w_ref[first + i, :, cols]).astype(BF16)
        if first == 0:
            out *= jnp.where(i == 0, (width // HEADS) ** (-0.5), 1.0).astype(BF16)
        out_ref[i, :, cols] = out
        return carry

    lax.fori_loop(0, count * steps, one, 0)


def own_kernel(x_ref, gain_ref, w_ref, column_ref, row_ref, doc_ref, qkv_ref, num_ref, den_ref, n_ref):
    here = lax.axis_index("seq") * x_ref.shape[0]
    n_ref[...] = normed(x_ref, gain_ref)
    project(n_ref, w_ref, 0, qkv_ref)
    num_ref[...] = jnp.zeros_like(num_ref)
    den_ref[...] = jnp.zeros_like(den_ref)
    q_ref, k_ref, v_ref = [qkv_ref.at[i] for i in range(3)]
    attend(q_ref, k_ref, v_ref, num_ref, den_ref, column_ref, row_ref, doc_ref, here, here, True)


def piece_kernel(
    shift, first, x_ref, gain_ref, w_ref, qkv_ref, num_in, den_in, column_ref, row_ref, doc_ref,
    num_ref, den_ref, n_ref, kv_ref,
):
    del num_in, den_in
    rows, keys = qkv_ref.shape[1], x_ref.shape[0]
    shard = lax.axis_index("seq") - shift
    here, there = (shard + shift) * rows, jnp.maximum(shard, 0) * rows + first

    @pl.when((shard >= 0) & (doc_ref[0, there + keys - 1] >= doc_ref[0, here]))
    def _():
        n_ref[...] = normed(x_ref, gain_ref)
        project(n_ref, w_ref, 1, kv_ref)
        attend(
            qkv_ref.at[0], kv_ref.at[0], kv_ref.at[1], num_ref, den_ref, column_ref, row_ref, doc_ref, here, there
        )


def far_document(doc_ref, rows, count):
    found = False
    for middle in range(1, count - 1):
        over = doc_ref[0, middle * rows - 1] == doc_ref[0, (middle + 1) * rows]
        deep = doc_ref[0, middle * rows - rows // 2 - 1] == doc_ref[0, (middle + 1) * rows]
        found = found | (over & deep)
    return found


def message_kernel(
    x_ref, piece_ref, gain_ref, w_ref, column_ref, row_ref, doc_ref,
    out_ref, q_ref, n_ref, kv_ref, num_ref, den_ref,
):
    half, width = x_ref.shape
    rows = 2 * half
    count = lax.axis_size("seq")
    place = lax.axis_index("seq")
    inside = (place >= 1) & (place + 1 < count)
    here = jnp.where(inside, place + 1, 0) * rows
    there = jnp.where(inside, place - 1, 0) * rows
    far = far_document(doc_ref, rows, count)

    @pl.when(jnp.logical_not(far))
    def _():
        out_ref[:, :width] = piece_ref[half:]

    @pl.when(far)
    def _():
        num_ref[...] = jnp.zeros_like(num_ref)
        den_ref[...] = jnp.zeros_like(den_ref)

        @pl.when(inside & (doc_ref[0, there + rows - 1] >= doc_ref[0, here]))
        def _():
            n_ref[:half] = normed(x_ref, gain_ref)
            project(n_ref.at[:half], w_ref, 0, q_ref)
            n_ref[...] = normed(piece_ref, gain_ref)
            project(n_ref, w_ref, 1, kv_ref)
            attend(
                q_ref.at[0], kv_ref.at[0], kv_ref.at[1], num_ref, den_ref, column_ref, row_ref, doc_ref, here, there
            )

        out_ref[:, :width] = num_ref[...].astype(BF16)
        out_ref[:, width:] = den_ref[...].astype(BF16)


def reply_kernel(
    message_ref, gain_ref, w_ref, qkv_ref, num_in, den_in, column_ref, row_ref, doc_ref,
    num_ref, den_ref, n_ref, kv_ref,
):
    _, rows, width = qkv_ref.shape
    half = message_ref.shape[0]
    far = far_document(doc_ref, rows, lax.axis_size("seq"))

    @pl.when(far)
    def _():
        num_ref[:half] += message_ref[:, :width].astype(F32)
        den_ref[:half] += message_ref[:, width:].astype(F32)

    @pl.when(jnp.logical_not(far))
    def _():
        piece_kernel(
            2, half, message_ref.at[:, :width], gain_ref, w_ref, qkv_ref, num_in, den_in, column_ref, row_ref, doc_ref,
            num_ref, den_ref, n_ref, kv_ref,
        )


def mix(first, x_ref, num_ref, den_ref, w_ref, gain_ref, acc_ref, n_ref):
    rows, width = acc_ref.shape
    here = pl.ds(first, rows)
    lane = lax.broadcasted_iota(jnp.int32, (rows, LANES), 1)
    inverse = 1.0 / jnp.where(lane < HEADS, den_ref[here], 1.0)
    n_ref[...] = (num_ref[here] * spread(inverse, width)).astype(BF16)
    acc_ref[...] = x_ref[here].astype(F32) + dot(n_ref[...], w_ref[3])
    n_ref[...] = rms_norm(acc_ref[...], gain_ref[1:2]).astype(BF16)


def feed_forward(begin, end, n_ref, up_ref, down_ref, acc_ref, hidden_ref):
    tile = hidden_ref.shape[2]

    def expand(j):
        cols = pl.ds(pl.multiple_of(j * tile, tile), tile)
        return jax.nn.gelu(dot(n_ref[...], up_ref[:, cols])).astype(BF16)

    def lower(j):
        return dot(hidden_ref[j % 2], down_ref[pl.ds(pl.multiple_of(j * tile, tile), tile)])

    hidden_ref[begin % 2] = expand(begin)

    def one(j, carry):
        acc_ref[...] += lower(j)
        hidden_ref[(j + 1) % 2] = expand(j + 1)
        return carry

    lax.fori_loop(begin, end - 1, one, 0)
    return lower(end - 1)


def finish_kernel(
    first, x_ref, num_ref, den_ref, w_ref, gain_ref, up_ref, down_ref, out_ref, acc_ref, n_ref, hidden_ref
):
    mix(first, x_ref, num_ref, den_ref, w_ref, gain_ref, acc_ref, n_ref)
    tiles = up_ref.shape[1] // hidden_ref.shape[2]
    last = feed_forward(0, tiles, n_ref, up_ref, down_ref, acc_ref, hidden_ref)
    out_ref[...] = (acc_ref[...] + last).astype(BF16)


def open_kernel(
    first, tiles, x_ref, num_ref, den_ref, w_ref, gain_ref, up_ref, down_ref, acc_ref, n_ref, hidden_ref
):
    mix(first, x_ref, num_ref, den_ref, w_ref, gain_ref, acc_ref, n_ref)
    last = feed_forward(0, tiles, n_ref, up_ref, down_ref, acc_ref, hidden_ref)
    acc_ref[...] += last


def close_kernel(begin, acc_in, n_ref, up_ref, down_ref, out_ref, acc_ref, hidden_ref):
    acc_ref[...] = acc_in[...]
    tiles = up_ref.shape[1] // hidden_ref.shape[2]
    last = feed_forward(begin, tiles, n_ref, up_ref, down_ref, acc_ref, hidden_ref)
    out_ref[...] = (acc_ref[...] + last).astype(BF16)


def vmem():
    return pl.BlockSpec(memory_space=pltpu.VMEM)


def call(kernel, name, operands, docs, results, scratch, aliases=None, held=True):
    inputs = [pltpu.with_memory_space_constraint(operand, pltpu.VMEM) for operand in operands]
    in_specs = [vmem()] * len(inputs)
    if docs is not None:
        inputs.append(docs)
        in_specs.append(pl.BlockSpec(memory_space=pltpu.SMEM))
    return pl.pallas_call(
        kernel,
        in_specs=in_specs,
        out_specs=[vmem()] * len(results),
        out_shape=[pltpu.VMEM(*one) if held else jax.ShapeDtypeStruct(*one) for one in results],
        scratch_shapes=scratch,
        input_output_aliases=aliases or {},
        compiler_params=pltpu.CompilerParams(vmem_limit_bytes=VMEM_BYTES),
        cost_estimate=COST,
        name=name,
    )(*inputs)


def own_part(x, gains, weights, docs):
    rows, width = x.shape
    results = [((3, rows, width), BF16), ((rows, width), F32), ((rows, LANES), F32)]
    scratch = [pltpu.VMEM((rows, width), BF16)]
    return call(own_kernel, "own_part", (x, gains, weights[0], docs.own_column, docs.ids), docs.ids, results, scratch)


def piece_part(x, shift, gains, w_attn, qkv, num, den, docs):
    _, rows, width = qkv.shape
    keys = x.shape[0]
    return call(
        functools.partial(piece_kernel, shift, 0),
        "piece_part",
        (x, gains, w_attn, qkv, num, den, docs.own_column, docs.ids),
        docs.ids,
        [((rows, width), F32), ((rows, LANES), F32)],
        [pltpu.VMEM((keys, width), BF16), pltpu.VMEM((2, keys, width), BF16)],
        aliases={4: 0, 5: 1},
    )


def message_part(x, piece, gains, w_attn, docs):
    half, width = x.shape
    keys = 2 * half
    return call(
        message_kernel,
        "message_part",
        (x, piece, gains, w_attn, docs.later_column, docs.ids),
        docs.ids,
        [((half, width + LANES), BF16)],
        [pltpu.VMEM((1, half, width), BF16), pltpu.VMEM((keys, width), BF16), pltpu.VMEM((2, keys, width), BF16)]
        + [pltpu.VMEM((half, width), F32), pltpu.VMEM((half, LANES), F32)],
    )[0]


def reply_part(message, gains, w_attn, qkv, num, den, docs):
    _, rows, width = qkv.shape
    keys = message.shape[0]
    return call(
        reply_kernel,
        "reply_part",
        (message, gains, w_attn, qkv, num, den, docs.own_column, docs.ids),
        docs.ids,
        [((rows, width), F32), ((rows, LANES), F32)],
        [pltpu.VMEM((keys, width), BF16), pltpu.VMEM((2, keys, width), BF16)],
        aliases={4: 0, 5: 1},
    )


def finish_part(x, num, den, weights, gains, part, parts):
    width = x.shape[1]
    rows = x.shape[0] // parts
    w_attn, w_up, w_down = weights
    tile = min(TILE, w_up.shape[1])
    return call(
        functools.partial(finish_kernel, part * rows),
        "finish_part",
        (x, num, den, w_attn, gains, w_up, w_down),
        None,
        [((rows, width), BF16)],
        [pltpu.VMEM((rows, width), F32), pltpu.VMEM((rows, width), BF16), pltpu.VMEM((2, rows, tile), BF16)],
        held=parts > 1,
    )[0]


def open_part(x, num, den, weights, gains, part, parts, tiles):
    width = x.shape[1]
    rows = x.shape[0] // parts
    return call(
        functools.partial(open_kernel, part * rows, tiles),
        "open_part",
        (x, num, den, weights[0], gains, *weights[1:]),
        None,
        [((rows, width), F32), ((rows, width), BF16)],
        [pltpu.VMEM((2, rows, min(TILE, weights[1].shape[1])), BF16)],
    )


def close_part(acc, n, weights, tiles):
    return call(
        functools.partial(close_kernel, tiles),
        "close_part",
        (acc, n, *weights[1:]),
        None,
        [(acc.shape, BF16)],
        [pltpu.VMEM(acc.shape, F32), pltpu.VMEM((2, acc.shape[0], min(TILE, weights[1].shape[1])), BF16)],
    )[0]


def shifted(value, axis, steps):
    count = lax.axis_size(axis)
    first, last = max(0, -steps), min(count, count - steps)
    return lax.ppermute(value, axis, [(i, i + steps) for i in range(first, last)])


def swapped(value, axis, bit):
    return lax.ppermute(value, axis, [(i, i ^ bit) for i in range(lax.axis_size(axis))])


class Documents:
    def __init__(self, doc_ids, rows):
        count = lax.axis_size("seq")
        self.ids, self.rows, self.half = doc_ids, rows, rows // 2
        longest = doc_ids.shape[1] // 2
        self.hops = min(count - 1, -(-(longest - 1) // rows))
        self.short = self.hops == 2 and longest <= 2 * rows and rows % 2 == 0
        place = lax.axis_index("seq")

        def column(later, size):
            start = jnp.minimum((place + later) * rows, doc_ids.shape[1] - size)
            ids = lax.dynamic_slice_in_dim(doc_ids, start, size, 1)
            return jnp.broadcast_to(ids.reshape(-1, 1), (size, LANES))

        self.own_column = column(0, rows)
        self.later_column = column(1, self.half) if self.short else self.own_column


def attention(state, piece, first_back, docs, gains, w_attn, ):
    qkv, *state = state
    if docs.short:
        message = message_part(after(first_back, qkv), piece, gains, w_attn, docs)
        state = after(state[0], message), state[1]
        message = shifted(message, "seq", 1)
        num, den = piece_part(piece, 1, gains, w_attn, qkv, *state, docs)
        return reply_part(message, gains, w_attn, qkv, num, den, docs)
    state = piece_part(piece, 1, gains, w_attn, qkv, *state, docs)
    for hop in range(2, docs.hops + 1):
        piece = shifted(piece, "seq", 1)
        state = piece_part(piece, hop, gains, w_attn, qkv, *state, docs)
    return state


def packed(row):
    high = lax.reduce_precision(row, 8, 7)
    low = lax.reduce_precision(row - high, 8, 7)
    pad = jnp.zeros((CARRIED - 2, row.shape[1]), BF16)
    return jnp.concatenate([high.astype(BF16), low.astype(BF16), pad], axis=0)


def unpacked(rows):
    return rows[:1].astype(F32) + rows[1:2].astype(F32)


def after(value, *earlier):
    return lax.optimization_barrier((value, *earlier))[0]


def own_half(rows, odd):
    half = rows.shape[0] // 2
    return jnp.where(odd, rows[half:], rows[:half]), jnp.where(odd, rows[:half], rows[half:])


class Chain:
    def __init__(self, own_states, other_states, even_gain, odd_gain, bits, before=None):
        self.bits, self.odd, self.leading = bits, bits[1], bits[0]
        self.even_gain, self.odd_gain = even_gain, odd_gain
        self.levels = before.levels if before else []
        self.factor, self.factor_before = even_gain * odd_gain, jnp.ones_like(even_gain)
        even, odd = self.sorted(own_states, other_states)
        self.even_states = even
        behind = jnp.where(self.leading, 0.0, self.even_gain * even.astype(F32))
        self.known = self.odd_gain * (behind + odd.astype(F32))

    def sorted(self, mine, other):
        return jnp.where(self.odd, other, mine), jnp.where(self.odd, mine, other)

    def enter(self, fine, *earlier):
        fine = after(fine, *earlier)
        half = fine.shape[0] // 2
        mine, sent = own_half(fine, self.odd)
        other = swapped(sent, "depth", 1)
        self.fine_even, fine_odd = self.sorted(mine, other)
        self.total = self.odd_gain * self.fine_even.astype(F32) + fine_odd.astype(F32) - self.known
        self.before = jnp.zeros_like(self.total)

    def level(self, index, sent_after=(), used_after=()):
        bit, last = 2 << index, index + 1 == self.steps()
        upper, rows = self.bits[bit], self.total.shape[0]
        sent = self.total.astype(BF16)
        carries = index == len(self.levels) and not last
        if carries:
            sent = jnp.concatenate([sent, packed(self.factor)], axis=0)
        theirs = after(swapped(after(sent, *sent_after), "depth", bit), *used_after)
        if index == len(self.levels):
            their_factor = unpacked(theirs[rows:]) if carries else None
            self.levels.append((self.factor, their_factor, self.factor_before))
            if carries:
                self.factor_before = jnp.where(upper, self.factor_before * their_factor, self.factor_before)
                self.factor = self.factor * their_factor
        factor, their_factor, factor_before = self.levels[index]
        theirs = theirs[:rows].astype(F32)
        if not last:
            self.total = jnp.where(upper, factor * theirs + self.total, their_factor * self.total + theirs)
        self.before = jnp.where(upper, factor_before * theirs + self.before, self.before)

    def steps(self):
        return len(self.bits) - 2

    def leave(self, sent_after=()):
        even_states = self.even_states.astype(F32)
        even = jnp.where(self.leading, even_states, self.before)
        odd = self.even_gain * (even - even_states) + self.fine_even.astype(F32)
        even, odd = even.astype(BF16), odd.astype(BF16)
        mine, sent = jnp.where(self.odd, odd, even), jnp.where(self.odd, even, odd)
        other = swapped(after(sent, *sent_after), "depth", 1)
        low, high = self.sorted(mine, other)
        return jnp.concatenate([low, high], axis=0)


def on_device(interfaces, doc_ids, w_attn, w_up, w_down, norm_gains, coarse_gain):
    x = interfaces[0, 0]
    rows = x.shape[0]
    half = rows // 2
    gains = norm_gains[0, 0]
    weights = (w_attn[0, 0], w_up[0, 0], w_down[0, 0])
    parts = [x[:half], x[half:]]
    piece = shifted(x, "seq", 1)
    first_back = shifted(parts[0], "seq", -1)
    docs = Documents(doc_ids, rows)
    place, bits, bit = lax.axis_index("depth"), {}, 1
    while bit < lax.axis_size("depth"):
        bits[bit] = (place & bit) != 0
        bit *= 2
    bits[0] = place < 2
    early, bits, docs.own_column, docs.later_column = lax.optimization_barrier(
        (x, bits, docs.own_column, docs.later_column)
    )
    state = own_part(early, gains, weights, docs)
    kept, sent = zip(*[own_half(part, bits[1]) for part in parts])
    sent = jnp.concatenate([*sent, packed(coarse_gain)], axis=0)
    other = swapped(after(sent, state[0], first_back), "depth", 1)
    first_back = after(first_back, other)
    num, den = attention(state, piece, first_back, docs, gains, weights[0])
    other_gain = unpacked(other[half:])
    pair = jnp.where(bits[1], other_gain, coarse_gain), jnp.where(bits[1], coarse_gain, other_gain)
    first = Chain(kept[0], other[: half // 2], *pair, bits)
    second = Chain(kept[1], other[half // 2 : half], *pair, bits, first)
    num = after(num, first.known, second.known)
    first.enter(finish_part(x, num, den, weights, gains, 0, 2))
    tiles = weights[1].shape[1] // TILE // 2
    acc, n = open_part(x, after(num, first.total), den, weights, gains, 1, 2, tiles)
    first.level(0, used_after=(n,))
    fine = close_part(after(acc, first.total), n, weights, tiles)
    first.level(1, used_after=(fine,))
    second.enter(fine, first.before)
    for i in range(2, first.steps()):
        second.level(i - 2)
        first.level(i)
    corrected = [first.leave()]
    halves = [shifted(corrected[0], "seq", 1)]
    first_back = shifted(corrected[0], "seq", -1)
    for i in range(max(0, first.steps() - 2), first.steps()):
        second.level(i, sent_after=(corrected[0],) if i > 0 else ())
    corrected.append(second.leave(sent_after=(halves[0],)))
    halves.append(shifted(corrected[1], "seq", 1))
    x = jnp.concatenate(corrected, axis=0)
    state = own_part(x, gains, weights, docs)
    piece = jnp.concatenate(halves, axis=0)
    num, den = attention(state, piece, first_back, docs, gains, weights[0])
    return finish_part(x, num, den, weights, gains, 0, 1)[None, None]


def solution(mesh):
    in_specs = (
        P("depth", None, "seq", None),
        P(),
        P("depth", None, None, None, None),
        P("depth", None, None, None),
        P("depth", None, None, None),
        P("depth", None, None, None),
        P("depth", None),
    )
    out_specs = P("depth", None, "seq", None)
    return jax.shard_map(
        on_device, mesh=mesh, in_specs=in_specs, out_specs=out_specs, check_vma=False
    )
```

```python
import functools

import jax
import jax.numpy as jnp
from jax import lax
from jax.experimental import pallas as pl
from jax.experimental.pallas import tpu as pltpu
from jax.sharding import PartitionSpec as P

HEADS = 16
LANES = 128
CARRIED = 16
BLOCK = 256
TILE = 512
TILES = 8
VMEM_BYTES = 10 * 1024 * 1024
COST = pl.CostEstimate(flops=1 << 20, bytes_accessed=1 << 16, transcendentals=0)
F32 = jnp.float32
BF16 = jnp.bfloat16


def rms_norm(value, gain):
    return value * lax.rsqrt(jnp.mean(value * value, axis=-1, keepdims=True) + 1e-05) * gain


def dot(a, b):
    return jnp.dot(a, b, preferred_element_type=F32)


def attend(q_ref, k_ref, v_ref, num_ref, den_ref, column_ref, row_ref, doc_ref, q_at, k_at, causal=False):
    rows, width = q_ref.shape
    keys = k_ref.shape[0]
    head_dim = width // HEADS
    per_tile = LANES // head_dim
    q_block, k_block = min(BLOCK, rows), min(BLOCK, keys)
    lane = lax.broadcasted_iota(jnp.int32, (1, LANES), 1)
    members = [lane // head_dim == i for i in range(per_tile)]
    count_q, count_k = rows // q_block, keys // k_block

    def one(index, carry):
        qi, ki = index // count_k, index % count_k
        q0 = pl.multiple_of(qi * q_block, q_block)
        k0 = pl.multiple_of(ki * k_block, k_block)
        needed = doc_ref[0, k_at + k0 + k_block - 1] >= doc_ref[0, q_at + q0]
        if causal:
            needed = (k0 <= q0) & (needed | (k0 == q0))

        @pl.when(needed)
        def _():
            key_docs = row_ref[:, pl.ds(pl.multiple_of(k_at + k0, k_block), k_block)]
            allowed = column_ref[pl.ds(q0, q_block), :1] == key_docs
            if causal:
                q_pos = q0 + lax.broadcasted_iota(jnp.int32, (q_block, k_block), 0)
                k_pos = k0 + lax.broadcasted_iota(jnp.int32, (q_block, k_block), 1)
                allowed = allowed & (k_pos <= q_pos)
            ones = jnp.ones((k_block, LANES), BF16)

            def heads(tile, den):
                cols = pl.ds(pl.multiple_of(tile * LANES, LANES), LANES)
                queries = q_ref[pl.ds(q0, q_block), cols]
                keys_here = k_ref[pl.ds(k0, k_block), cols]
                values = jnp.concatenate([v_ref[pl.ds(k0, k_block), cols], ones], axis=1)
                num = None
                for i, member in enumerate(members):
                    scores = lax.dot_general(
                        jnp.where(member, queries, jnp.zeros_like(queries)),
                        keys_here,
                        (((1,), (1,)), ((), ())),
                        preferred_element_type=F32,
                    )
                    weights = jnp.where(allowed, jnp.exp(scores), 0.0).astype(BF16)
                    out = dot(weights, values)
                    num = out[:, :LANES] if num is None else jnp.where(member, out[:, :LANES], num)
                    den = jnp.where(lane == tile * per_tile + i, out[:, LANES:], den)
                num_ref[pl.ds(q0, q_block), cols] += num
                return den

            def some(step, den):
                for i in range(TILES):
                    den = heads(step * TILES + i, den)
                return den

            den = jnp.zeros((q_block, LANES), F32)
            den_ref[pl.ds(q0, q_block), :] += lax.fori_loop(0, width // LANES // TILES, some, den, unroll=True)

        return carry

    lax.fori_loop(0, count_q * count_k, one, 0)


def spread(per_head, width):
    shape = (LANES, width)
    chosen = lax.broadcasted_iota(jnp.int32, shape, 1) // (width // HEADS) == lax.broadcasted_iota(jnp.int32, shape, 0)
    chosen = jnp.where(chosen, 1.0, 0.0).astype(BF16)
    high = per_head.astype(BF16)
    return dot(high, chosen) + dot((per_head - high.astype(F32)).astype(BF16), chosen)


def normed(x_ref, gain_ref):
    return rms_norm(x_ref[...].astype(F32), gain_ref[0:1]).astype(BF16)


def project(n_ref, w_ref, first, out_ref):
    count, _, width = out_ref.shape
    tile = min(TILE, width)
    steps = width // tile

    def one(step, carry):
        i, j = step // steps, step % steps
        cols = pl.ds(pl.multiple_of(j * tile, tile), tile)
        out = dot(n_ref[...], w_ref[first + i, :, cols]).astype(BF16)
        if first == 0:
            out *= jnp.where(i == 0, (width // HEADS) ** (-0.5), 1.0).astype(BF16)
        out_ref[i, :, cols] = out
        return carry

    lax.fori_loop(0, count * steps, one, 0)


def own_kernel(x_ref, gain_ref, w_ref, column_ref, row_ref, doc_ref, qkv_ref, num_ref, den_ref, n_ref):
    here = lax.axis_index("seq") * x_ref.shape[0]
    n_ref[...] = normed(x_ref, gain_ref)
    project(n_ref, w_ref, 0, qkv_ref)
    num_ref[...] = jnp.zeros_like(num_ref)
    den_ref[...] = jnp.zeros_like(den_ref)
    q_ref, k_ref, v_ref = [qkv_ref.at[i] for i in range(3)]
    attend(q_ref, k_ref, v_ref, num_ref, den_ref, column_ref, row_ref, doc_ref, here, here, True)


def piece_kernel(
    shift, first, x_ref, gain_ref, w_ref, qkv_ref, num_in, den_in, column_ref, row_ref, doc_ref,
    num_ref, den_ref, n_ref, kv_ref,
):
    del num_in, den_in
    rows, keys = qkv_ref.shape[1], x_ref.shape[0]
    shard = lax.axis_index("seq") - shift
    here, there = (shard + shift) * rows, jnp.maximum(shard, 0) * rows + first

    @pl.when((shard >= 0) & (doc_ref[0, there + keys - 1] >= doc_ref[0, here]))
    def _():
        n_ref[...] = normed(x_ref, gain_ref)
        project(n_ref, w_ref, 1, kv_ref)
        attend(
            qkv_ref.at[0], kv_ref.at[0], kv_ref.at[1], num_ref, den_ref, column_ref, row_ref, doc_ref, here, there
        )


def far_document(doc_ref, rows, count):
    found = False
    for middle in range(1, count - 1):
        over = doc_ref[0, middle * rows - 1] == doc_ref[0, (middle + 1) * rows]
        deep = doc_ref[0, middle * rows - rows // 2 - 1] == doc_ref[0, (middle + 1) * rows]
        found = found | (over & deep)
    return found


def message_kernel(
    x_ref, piece_ref, gain_ref, w_ref, column_ref, row_ref, doc_ref,
    out_ref, q_ref, n_ref, kv_ref, num_ref, den_ref,
):
    half, width = x_ref.shape
    rows = 2 * half
    count = lax.axis_size("seq")
    place = lax.axis_index("seq")
    inside = (place >= 1) & (place + 1 < count)
    here = jnp.where(inside, place + 1, 0) * rows
    there = jnp.where(inside, place - 1, 0) * rows
    far = far_document(doc_ref, rows, count)

    @pl.when(jnp.logical_not(far))
    def _():
        out_ref[:, :width] = piece_ref[half:]

    @pl.when(far)
    def _():
        num_ref[...] = jnp.zeros_like(num_ref)
        den_ref[...] = jnp.zeros_like(den_ref)

        @pl.when(inside & (doc_ref[0, there + rows - 1] >= doc_ref[0, here]))
        def _():
            n_ref[:half] = normed(x_ref, gain_ref)
            project(n_ref.at[:half], w_ref, 0, q_ref)
            n_ref[...] = normed(piece_ref, gain_ref)
            project(n_ref, w_ref, 1, kv_ref)
            attend(
                q_ref.at[0], kv_ref.at[0], kv_ref.at[1], num_ref, den_ref, column_ref, row_ref, doc_ref, here, there
            )

        out_ref[:, :width] = num_ref[...].astype(BF16)
        out_ref[:, width:] = den_ref[...].astype(BF16)


def reply_kernel(
    message_ref, gain_ref, w_ref, qkv_ref, num_in, den_in, column_ref, row_ref, doc_ref,
    num_ref, den_ref, n_ref, kv_ref,
):
    _, rows, width = qkv_ref.shape
    half = message_ref.shape[0]
    far = far_document(doc_ref, rows, lax.axis_size("seq"))

    @pl.when(far)
    def _():
        num_ref[:half] += message_ref[:, :width].astype(F32)
        den_ref[:half] += message_ref[:, width:].astype(F32)

    @pl.when(jnp.logical_not(far))
    def _():
        piece_kernel(
            2, half, message_ref.at[:, :width], gain_ref, w_ref, qkv_ref, num_in, den_in, column_ref, row_ref, doc_ref,
            num_ref, den_ref, n_ref, kv_ref,
        )


def mix(first, x_ref, num_ref, den_ref, w_ref, gain_ref, acc_ref, n_ref):
    rows, width = acc_ref.shape
    here = pl.ds(first, rows)
    lane = lax.broadcasted_iota(jnp.int32, (rows, LANES), 1)
    inverse = 1.0 / jnp.where(lane < HEADS, den_ref[here], 1.0)
    n_ref[...] = (num_ref[here] * spread(inverse, width)).astype(BF16)
    acc_ref[...] = x_ref[here].astype(F32) + dot(n_ref[...], w_ref[3])
    n_ref[...] = rms_norm(acc_ref[...], gain_ref[1:2]).astype(BF16)


def feed_forward(begin, end, n_ref, up_ref, down_ref, acc_ref, hidden_ref):
    tile = hidden_ref.shape[2]

    def expand(j):
        cols = pl.ds(pl.multiple_of(j * tile, tile), tile)
        return jax.nn.gelu(dot(n_ref[...], up_ref[:, cols])).astype(BF16)

    def lower(j):
        return dot(hidden_ref[j % 2], down_ref[pl.ds(pl.multiple_of(j * tile, tile), tile)])

    hidden_ref[begin % 2] = expand(begin)

    def one(j, carry):
        acc_ref[...] += lower(j)
        hidden_ref[(j + 1) % 2] = expand(j + 1)
        return carry

    lax.fori_loop(begin, end - 1, one, 0)
    return lower(end - 1)


def finish_kernel(
    first, x_ref, num_ref, den_ref, w_ref, gain_ref, up_ref, down_ref, out_ref, acc_ref, n_ref, hidden_ref
):
    mix(first, x_ref, num_ref, den_ref, w_ref, gain_ref, acc_ref, n_ref)
    tiles = up_ref.shape[1] // hidden_ref.shape[2]
    last = feed_forward(0, tiles, n_ref, up_ref, down_ref, acc_ref, hidden_ref)
    out_ref[...] = (acc_ref[...] + last).astype(BF16)


def open_kernel(
    first, tiles, x_ref, num_ref, den_ref, w_ref, gain_ref, up_ref, down_ref, acc_ref, n_ref, hidden_ref
):
    mix(first, x_ref, num_ref, den_ref, w_ref, gain_ref, acc_ref, n_ref)
    last = feed_forward(0, tiles, n_ref, up_ref, down_ref, acc_ref, hidden_ref)
    acc_ref[...] += last


def close_kernel(begin, acc_in, n_ref, up_ref, down_ref, out_ref, acc_ref, hidden_ref):
    acc_ref[...] = acc_in[...]
    tiles = up_ref.shape[1] // hidden_ref.shape[2]
    last = feed_forward(begin, tiles, n_ref, up_ref, down_ref, acc_ref, hidden_ref)
    out_ref[...] = (acc_ref[...] + last).astype(BF16)


def vmem():
    return pl.BlockSpec(memory_space=pltpu.VMEM)


def call(kernel, name, operands, docs, results, scratch, aliases=None, held=True):
    inputs = [pltpu.with_memory_space_constraint(operand, pltpu.VMEM) for operand in operands]
    in_specs = [vmem()] * len(inputs)
    if docs is not None:
        inputs.append(docs)
        in_specs.append(pl.BlockSpec(memory_space=pltpu.SMEM))
    return pl.pallas_call(
        kernel,
        in_specs=in_specs,
        out_specs=[vmem()] * len(results),
        out_shape=[pltpu.VMEM(*one) if held else jax.ShapeDtypeStruct(*one) for one in results],
        scratch_shapes=scratch,
        input_output_aliases=aliases or {},
        compiler_params=pltpu.CompilerParams(vmem_limit_bytes=VMEM_BYTES),
        cost_estimate=COST,
        name=name,
    )(*inputs)


def own_part(x, gains, weights, docs):
    rows, width = x.shape
    results = [((3, rows, width), BF16), ((rows, width), F32), ((rows, LANES), F32)]
    scratch = [pltpu.VMEM((rows, width), BF16)]
    return call(own_kernel, "own_part", (x, gains, weights[0], docs.own_column, docs.ids), docs.ids, results, scratch)


def piece_part(x, shift, gains, w_attn, qkv, num, den, docs):
    _, rows, width = qkv.shape
    keys = x.shape[0]
    return call(
        functools.partial(piece_kernel, shift, 0),
        "piece_part",
        (x, gains, w_attn, qkv, num, den, docs.own_column, docs.ids),
        docs.ids,
        [((rows, width), F32), ((rows, LANES), F32)],
        [pltpu.VMEM((keys, width), BF16), pltpu.VMEM((2, keys, width), BF16)],
        aliases={4: 0, 5: 1},
    )


def message_part(x, piece, gains, w_attn, docs):
    half, width = x.shape
    keys = 2 * half
    return call(
        message_kernel,
        "message_part",
        (x, piece, gains, w_attn, docs.later_column, docs.ids),
        docs.ids,
        [((half, width + LANES), BF16)],
        [pltpu.VMEM((1, half, width), BF16), pltpu.VMEM((keys, width), BF16), pltpu.VMEM((2, keys, width), BF16)]
        + [pltpu.VMEM((half, width), F32), pltpu.VMEM((half, LANES), F32)],
    )[0]


def reply_part(message, gains, w_attn, qkv, num, den, docs):
    _, rows, width = qkv.shape
    keys = message.shape[0]
    return call(
        reply_kernel,
        "reply_part",
        (message, gains, w_attn, qkv, num, den, docs.own_column, docs.ids),
        docs.ids,
        [((rows, width), F32), ((rows, LANES), F32)],
        [pltpu.VMEM((keys, width), BF16), pltpu.VMEM((2, keys, width), BF16)],
        aliases={4: 0, 5: 1},
    )


def finish_part(x, num, den, weights, gains, part, parts):
    width = x.shape[1]
    rows = x.shape[0] // parts
    w_attn, w_up, w_down = weights
    tile = min(TILE, w_up.shape[1])
    return call(
        functools.partial(finish_kernel, part * rows),
        "finish_part",
        (x, num, den, w_attn, gains, w_up, w_down),
        None,
        [((rows, width), BF16)],
        [pltpu.VMEM((rows, width), F32), pltpu.VMEM((rows, width), BF16), pltpu.VMEM((2, rows, tile), BF16)],
        held=parts > 1,
    )[0]


def open_part(x, num, den, weights, gains, part, parts, tiles):
    width = x.shape[1]
    rows = x.shape[0] // parts
    return call(
        functools.partial(open_kernel, part * rows, tiles),
        "open_part",
        (x, num, den, weights[0], gains, *weights[1:]),
        None,
        [((rows, width), F32), ((rows, width), BF16)],
        [pltpu.VMEM((2, rows, min(TILE, weights[1].shape[1])), BF16)],
    )


def close_part(acc, n, weights, tiles):
    return call(
        functools.partial(close_kernel, tiles),
        "close_part",
        (acc, n, *weights[1:]),
        None,
        [(acc.shape, BF16)],
        [pltpu.VMEM(acc.shape, F32), pltpu.VMEM((2, acc.shape[0], min(TILE, weights[1].shape[1])), BF16)],
    )[0]


def shifted(value, axis, steps):
    count = lax.axis_size(axis)
    first, last = max(0, -steps), min(count, count - steps)
    return lax.ppermute(value, axis, [(i, i + steps) for i in range(first, last)])


def swapped(value, axis, bit):
    return lax.ppermute(value, axis, [(i, i ^ bit) for i in range(lax.axis_size(axis))])


class Documents:
    def __init__(self, doc_ids, rows):
        count = lax.axis_size("seq")
        self.ids, self.rows, self.half = doc_ids, rows, rows // 2
        longest = doc_ids.shape[1] // 2
        self.hops = min(count - 1, -(-(longest - 1) // rows))
        self.short = self.hops == 2 and longest <= 2 * rows and rows % 2 == 0
        place = lax.axis_index("seq")

        def column(later, size):
            start = jnp.minimum((place + later) * rows, doc_ids.shape[1] - size)
            ids = lax.dynamic_slice_in_dim(doc_ids, start, size, 1)
            return jnp.broadcast_to(ids.reshape(-1, 1), (size, LANES))

        self.own_column = column(0, rows)
        self.later_column = column(1, self.half) if self.short else self.own_column


def attention(state, piece, first_back, docs, gains, w_attn, ):
    qkv, *state = state
    if docs.short:
        message = message_part(after(first_back, qkv), piece, gains, w_attn, docs)
        state = after(state[0], message), state[1]
        message = shifted(message, "seq", 1)
        num, den = piece_part(piece, 1, gains, w_attn, qkv, *state, docs)
        return reply_part(message, gains, w_attn, qkv, num, den, docs)
    state = piece_part(piece, 1, gains, w_attn, qkv, *state, docs)
    for hop in range(2, docs.hops + 1):
        piece = shifted(piece, "seq", 1)
        state = piece_part(piece, hop, gains, w_attn, qkv, *state, docs)
    return state


def packed(row):
    high = lax.reduce_precision(row, 8, 7)
    low = lax.reduce_precision(row - high, 8, 7)
    place = lax.broadcasted_iota(jnp.int32, (CARRIED, row.shape[1]), 0)
    return jnp.where(place == 0, high, jnp.where(place == 1, low, 0.0)).astype(BF16)


def unpacked(rows):
    return rows[:1].astype(F32) + rows[1:2].astype(F32)


def after(value, *earlier):
    return lax.optimization_barrier((value, *earlier))[0]


def own_half(rows, odd):
    half = rows.shape[0] // 2
    return jnp.where(odd, rows[half:], rows[:half]), jnp.where(odd, rows[:half], rows[half:])


class Chain:
    def __init__(self, own_states, other_states, even_gain, odd_gain, bits, before=None):
        self.bits, self.odd, self.leading = bits, bits[1], bits[0]
        self.even_gain, self.odd_gain = even_gain, odd_gain
        self.levels = before.levels if before else []
        self.factor, self.factor_before = even_gain * odd_gain, jnp.ones_like(even_gain)
        even, odd = self.sorted(own_states, other_states)
        self.even_states = even
        behind = jnp.where(self.leading, 0.0, self.even_gain * even.astype(F32))
        self.known = self.odd_gain * (behind + odd.astype(F32))

    def sorted(self, mine, other):
        return jnp.where(self.odd, other, mine), jnp.where(self.odd, mine, other)

    def enter(self, fine, *earlier):
        fine = after(fine, *earlier)
        half = fine.shape[0] // 2
        mine, sent = own_half(fine, self.odd)
        other = swapped(sent, "depth", 1)
        self.fine_even, fine_odd = self.sorted(mine, other)
        self.total = self.odd_gain * self.fine_even.astype(F32) + fine_odd.astype(F32) - self.known
        self.before = jnp.zeros_like(self.total)

    def level(self, index, sent_after=(), used_after=()):
        bit, last = 2 << index, index + 1 == self.steps()
        upper, rows = self.bits[bit], self.total.shape[0]
        sent = self.total.astype(BF16)
        carries = index == len(self.levels) and not last
        if carries:
            sent = jnp.concatenate([sent, packed(self.factor)], axis=0)
        theirs = after(swapped(after(sent, *sent_after), "depth", bit), *used_after)
        if index == len(self.levels):
            their_factor = unpacked(theirs[rows:]) if carries else None
            self.levels.append((self.factor, their_factor, self.factor_before))
            if carries:
                self.factor_before = jnp.where(upper, self.factor_before * their_factor, self.factor_before)
                self.factor = self.factor * their_factor
        factor, their_factor, factor_before = self.levels[index]
        theirs = theirs[:rows].astype(F32)
        if not last:
            self.total = jnp.where(upper, factor * theirs + self.total, their_factor * self.total + theirs)
        self.before = jnp.where(upper, factor_before * theirs + self.before, self.before)

    def steps(self):
        return len(self.bits) - 2

    def leave(self, used_after=()):
        even_states = self.even_states.astype(F32)
        even = jnp.where(self.leading, even_states, self.before)
        odd = self.even_gain * (even - even_states) + self.fine_even.astype(F32)
        even, odd = even.astype(BF16), odd.astype(BF16)
        mine, sent = jnp.where(self.odd, odd, even), jnp.where(self.odd, even, odd)
        other = after(swapped(sent, "depth", 1), *used_after)
        low, high = self.sorted(mine, other)
        return jnp.concatenate([low, high], axis=0)


def on_device(interfaces, doc_ids, w_attn, w_up, w_down, norm_gains, coarse_gain):
    x = interfaces[0, 0]
    rows = x.shape[0]
    half = rows // 2
    gains = norm_gains[0, 0]
    weights = (w_attn[0, 0], w_up[0, 0], w_down[0, 0])
    parts = [x[:half], x[half:]]
    piece = shifted(x, "seq", 1)
    docs = Documents(doc_ids, rows)
    place, bits, bit = lax.axis_index("depth"), {}, 1
    while bit < lax.axis_size("depth"):
        bits[bit] = (place & bit) != 0
        bit *= 2
    bits[0] = place < 2
    early, bits, docs.own_column, docs.later_column = lax.optimization_barrier(
        (x, bits, docs.own_column, docs.later_column)
    )
    first_back = shifted(after(parts[0], docs.own_column), "seq", -1)
    state = own_part(early, gains, weights, docs)
    kept, sent = zip(*[own_half(part, bits[1]) for part in parts])
    sent = jnp.concatenate([*after(sent, state[0]), packed(coarse_gain)], axis=0)
    other = swapped(sent, "depth", 1)
    num, den = attention(state, piece, first_back, docs, gains, weights[0])
    other_gain = unpacked(other[half:])
    pair = jnp.where(bits[1], other_gain, coarse_gain), jnp.where(bits[1], coarse_gain, other_gain)
    first = Chain(kept[0], other[: half // 2], *pair, bits)
    second = Chain(kept[1], other[half // 2 : half], *pair, bits, first)
    num = after(num, first.known, second.known)
    first.enter(finish_part(x, num, den, weights, gains, 0, 2))
    tiles = weights[1].shape[1] // TILE // 2
    acc, n = open_part(x, after(num, first.total), den, weights, gains, 1, 2, tiles)
    first.level(0, used_after=(n,))
    fine = close_part(after(acc, first.total), n, weights, tiles)
    first.level(1, used_after=(fine,))
    second.enter(fine, first.before)
    for i in range(2, first.steps()):
        second.level(i - 2)
        first.level(i)
    corrected = [first.leave()]
    halves = [shifted(corrected[0], "seq", 1)]
    first_back = shifted(corrected[0], "seq", -1)
    for i in range(max(0, first.steps() - 2), first.steps()):
        last = i + 1 == first.steps()
        second.level(i, (corrected[0],) if i > 0 else (), (halves[0],) if last else ())
    corrected.append(second.leave())
    halves.append(shifted(corrected[1], "seq", 1))
    x = jnp.concatenate(corrected, axis=0)
    state = own_part(x, gains, weights, docs)
    piece = jnp.concatenate(halves, axis=0)
    num, den = attention(state, piece, first_back, docs, gains, weights[0])
    return finish_part(x, num, den, weights, gains, 0, 1)[None, None]


def solution(mesh):
    in_specs = (
        P("depth", None, "seq", None),
        P(),
        P("depth", None, None, None, None),
        P("depth", None, None, None),
        P("depth", None, None, None),
        P("depth", None, None, None),
        P("depth", None),
    )
    out_specs = P("depth", None, "seq", None)
    return jax.shard_map(
        on_device, mesh=mesh, in_specs=in_specs, out_specs=out_specs, check_vma=False
    )
```

```python
import functools

import jax
import jax.numpy as jnp
from jax import lax
from jax.experimental import pallas as pl
from jax.experimental.pallas import tpu as pltpu
from jax.sharding import PartitionSpec as P

HEADS = 16
LANES = 128
CARRIED = 16
BLOCK = 256
TILE = 512
TILES = 8
VMEM_BYTES = 10 * 1024 * 1024
COST = pl.CostEstimate(flops=1 << 20, bytes_accessed=1 << 16, transcendentals=0)
F32 = jnp.float32
BF16 = jnp.bfloat16


def rms_norm(value, gain):
    return value * lax.rsqrt(jnp.mean(value * value, axis=-1, keepdims=True) + 1e-05) * gain


def dot(a, b):
    return jnp.dot(a, b, preferred_element_type=F32)


def attend(q_ref, k_ref, v_ref, num_ref, den_ref, column_ref, row_ref, doc_ref, q_at, k_at, causal=False):
    rows, width = q_ref.shape
    keys = k_ref.shape[0]
    head_dim = width // HEADS
    per_tile = LANES // head_dim
    q_block, k_block = min(BLOCK, rows), min(BLOCK, keys)
    lane = lax.broadcasted_iota(jnp.int32, (1, LANES), 1)
    members = [lane // head_dim == i for i in range(per_tile)]
    count_q, count_k = rows // q_block, keys // k_block

    def one(index, carry):
        qi, ki = index // count_k, index % count_k
        q0 = pl.multiple_of(qi * q_block, q_block)
        k0 = pl.multiple_of(ki * k_block, k_block)
        needed = doc_ref[0, k_at + k0 + k_block - 1] >= doc_ref[0, q_at + q0]
        if causal:
            needed = (k0 <= q0) & (needed | (k0 == q0))

        @pl.when(needed)
        def _():
            key_docs = row_ref[:, pl.ds(pl.multiple_of(k_at + k0, k_block), k_block)]
            allowed = column_ref[pl.ds(q0, q_block), :1] == key_docs
            if causal:
                q_pos = q0 + lax.broadcasted_iota(jnp.int32, (q_block, k_block), 0)
                k_pos = k0 + lax.broadcasted_iota(jnp.int32, (q_block, k_block), 1)
                allowed = allowed & (k_pos <= q_pos)
            ones = jnp.ones((k_block, LANES), BF16)

            def heads(tile, den):
                cols = pl.ds(pl.multiple_of(tile * LANES, LANES), LANES)
                queries = q_ref[pl.ds(q0, q_block), cols]
                keys_here = k_ref[pl.ds(k0, k_block), cols]
                values = jnp.concatenate([v_ref[pl.ds(k0, k_block), cols], ones], axis=1)
                num = None
                for i, member in enumerate(members):
                    scores = lax.dot_general(
                        jnp.where(member, queries, jnp.zeros_like(queries)),
                        keys_here,
                        (((1,), (1,)), ((), ())),
                        preferred_element_type=F32,
                    )
                    weights = jnp.where(allowed, jnp.exp(scores), 0.0).astype(BF16)
                    out = dot(weights, values)
                    num = out[:, :LANES] if num is None else jnp.where(member, out[:, :LANES], num)
                    den = jnp.where(lane == tile * per_tile + i, out[:, LANES:], den)
                num_ref[pl.ds(q0, q_block), cols] += num
                return den

            def some(step, den):
                for i in range(TILES):
                    den = heads(step * TILES + i, den)
                return den

            den = jnp.zeros((q_block, LANES), F32)
            den_ref[pl.ds(q0, q_block), :] += lax.fori_loop(0, width // LANES // TILES, some, den, unroll=True)

        return carry

    lax.fori_loop(0, count_q * count_k, one, 0)


def spread(per_head, width):
    shape = (LANES, width)
    chosen = lax.broadcasted_iota(jnp.int32, shape, 1) // (width // HEADS) == lax.broadcasted_iota(jnp.int32, shape, 0)
    chosen = jnp.where(chosen, 1.0, 0.0).astype(BF16)
    high = per_head.astype(BF16)
    return dot(high, chosen) + dot((per_head - high.astype(F32)).astype(BF16), chosen)


def normed(x_ref, gain_ref):
    return rms_norm(x_ref[...].astype(F32), gain_ref[0:1]).astype(BF16)


def project(n_ref, w_ref, first, out_ref):
    count, _, width = out_ref.shape
    tile = min(TILE, width)
    steps = width // tile

    def one(step, carry):
        i, j = step // steps, step % steps
        cols = pl.ds(pl.multiple_of(j * tile, tile), tile)
        out = dot(n_ref[...], w_ref[first + i, :, cols]).astype(BF16)
        if first == 0:
            out *= jnp.where(i == 0, (width // HEADS) ** (-0.5), 1.0).astype(BF16)
        out_ref[i, :, cols] = out
        return carry

    lax.fori_loop(0, count * steps, one, 0)


def own_kernel(x_ref, gain_ref, w_ref, column_ref, row_ref, doc_ref, qkv_ref, num_ref, den_ref, n_ref):
    here = lax.axis_index("seq") * x_ref.shape[0]
    n_ref[...] = normed(x_ref, gain_ref)
    project(n_ref, w_ref, 0, qkv_ref)
    num_ref[...] = jnp.zeros_like(num_ref)
    den_ref[...] = jnp.zeros_like(den_ref)
    q_ref, k_ref, v_ref = [qkv_ref.at[i] for i in range(3)]
    attend(q_ref, k_ref, v_ref, num_ref, den_ref, column_ref, row_ref, doc_ref, here, here, True)


def piece_kernel(
    shift, first, x_ref, gain_ref, w_ref, qkv_ref, num_in, den_in, column_ref, row_ref, doc_ref,
    num_ref, den_ref, n_ref, kv_ref,
):
    del num_in, den_in
    rows, keys = qkv_ref.shape[1], x_ref.shape[0]
    shard = lax.axis_index("seq") - shift
    here, there = (shard + shift) * rows, jnp.maximum(shard, 0) * rows + first

    @pl.when((shard >= 0) & (doc_ref[0, there + keys - 1] >= doc_ref[0, here]))
    def _():
        n_ref[...] = normed(x_ref, gain_ref)
        project(n_ref, w_ref, 1, kv_ref)
        attend(
            qkv_ref.at[0], kv_ref.at[0], kv_ref.at[1], num_ref, den_ref, column_ref, row_ref, doc_ref, here, there
        )


def far_document(doc_ref, rows, count):
    found = False
    for middle in range(1, count - 1):
        over = doc_ref[0, middle * rows - 1] == doc_ref[0, (middle + 1) * rows]
        deep = doc_ref[0, middle * rows - rows // 2 - 1] == doc_ref[0, (middle + 1) * rows]
        found = found | (over & deep)
    return found


def message_kernel(
    x_ref, piece_ref, gain_ref, w_ref, column_ref, row_ref, doc_ref,
    out_ref, q_ref, n_ref, kv_ref, num_ref, den_ref,
):
    half, width = x_ref.shape
    rows = 2 * half
    count = lax.axis_size("seq")
    place = lax.axis_index("seq")
    inside = (place >= 1) & (place + 1 < count)
    here = jnp.where(inside, place + 1, 0) * rows
    there = jnp.where(inside, place - 1, 0) * rows
    far = far_document(doc_ref, rows, count)

    @pl.when(jnp.logical_not(far))
    def _():
        out_ref[:, :width] = piece_ref[half:]

    @pl.when(far)
    def _():
        num_ref[...] = jnp.zeros_like(num_ref)
        den_ref[...] = jnp.zeros_like(den_ref)

        @pl.when(inside & (doc_ref[0, there + rows - 1] >= doc_ref[0, here]))
        def _():
            n_ref[:half] = normed(x_ref, gain_ref)
            project(n_ref.at[:half], w_ref, 0, q_ref)
            n_ref[...] = normed(piece_ref, gain_ref)
            project(n_ref, w_ref, 1, kv_ref)
            attend(
                q_ref.at[0], kv_ref.at[0], kv_ref.at[1], num_ref, den_ref, column_ref, row_ref, doc_ref, here, there
            )

        out_ref[:, :width] = num_ref[...].astype(BF16)
        out_ref[:, width:] = den_ref[...].astype(BF16)


def reply_kernel(
    message_ref, gain_ref, w_ref, qkv_ref, num_in, den_in, column_ref, row_ref, doc_ref,
    num_ref, den_ref, n_ref, kv_ref,
):
    _, rows, width = qkv_ref.shape
    half = message_ref.shape[0]
    far = far_document(doc_ref, rows, lax.axis_size("seq"))

    @pl.when(far)
    def _():
        num_ref[:half] += message_ref[:, :width].astype(F32)
        den_ref[:half] += message_ref[:, width:].astype(F32)

    @pl.when(jnp.logical_not(far))
    def _():
        piece_kernel(
            2, half, message_ref.at[:, :width], gain_ref, w_ref, qkv_ref, num_in, den_in, column_ref, row_ref, doc_ref,
            num_ref, den_ref, n_ref, kv_ref,
        )


def mix(first, x_ref, num_ref, den_ref, w_ref, gain_ref, acc_ref, n_ref):
    rows, width = acc_ref.shape
    here = pl.ds(first, rows)
    lane = lax.broadcasted_iota(jnp.int32, (rows, LANES), 1)
    inverse = 1.0 / jnp.where(lane < HEADS, den_ref[here], 1.0)
    n_ref[...] = (num_ref[here] * spread(inverse, width)).astype(BF16)
    tile = min(TILE, width)

    def one(j, carry):
        cols = pl.ds(pl.multiple_of(j * tile, tile), tile)
        acc_ref[:, cols] = x_ref[here, cols].astype(F32) + dot(n_ref[...], w_ref[3, :, cols])
        return carry

    lax.fori_loop(0, width // tile, one, 0)
    n_ref[...] = rms_norm(acc_ref[...], gain_ref[1:2]).astype(BF16)


def feed_forward(begin, end, n_ref, up_ref, down_ref, acc_ref, hidden_ref):
    tile = hidden_ref.shape[2]

    def lower(j, slot):
        return dot(hidden_ref[slot], down_ref[pl.ds(pl.multiple_of(j * tile, tile), tile)])

    def one(j, carry):
        acc_ref[...] += lower(jnp.maximum(j - 1, begin), (j + 1) % 2)
        cols = pl.ds(pl.multiple_of(j * tile, tile), tile)
        hidden_ref[j % 2] = jax.nn.gelu(dot(n_ref[...], up_ref[:, cols])).astype(BF16)
        return carry

    hidden_ref[(begin + 1) % 2] = jnp.zeros(hidden_ref.shape[1:], BF16)
    lax.fori_loop(begin, end, one, 0)
    acc_ref[...] += lower(end - 1, (end - 1) % 2)


def finish_kernel(
    first, x_ref, num_ref, den_ref, w_ref, gain_ref, up_ref, down_ref, out_ref, acc_ref, n_ref, hidden_ref
):
    mix(first, x_ref, num_ref, den_ref, w_ref, gain_ref, acc_ref, n_ref)
    tiles = up_ref.shape[1] // hidden_ref.shape[2]
    feed_forward(0, tiles, n_ref, up_ref, down_ref, acc_ref, hidden_ref)
    out_ref[...] = acc_ref[...].astype(BF16)


def seen_by_second_half(doc_ref, rows):
    place = lax.axis_index("seq")
    before = jnp.maximum((place - 1) * rows - 1, 0)
    return (place >= 2) & (doc_ref[0, before] == doc_ref[0, place * rows + rows // 2])


def again_kernel(
    first, done_ref, x_ref, num_ref, den_ref, w_ref, gain_ref, up_ref, down_ref, doc_ref,
    out_ref, acc_ref, n_ref, hidden_ref,
):
    del done_ref

    @pl.when(seen_by_second_half(doc_ref, x_ref.shape[0]))
    def _():
        finish_kernel(
            first, x_ref, num_ref, den_ref, w_ref, gain_ref, up_ref, down_ref, out_ref, acc_ref, n_ref, hidden_ref
        )


def last_kernel(
    done_ref, x_ref, num_ref, den_ref, w_ref, gain_ref, up_ref, down_ref, doc_ref,
    out_ref, acc_ref, n_ref, hidden_ref,
):
    half = done_ref.shape[0]
    out_ref[half:] = done_ref[...]
    again = seen_by_second_half(doc_ref, x_ref.shape[0])

    def one(part, carry):
        @pl.when((part == 0) | again)
        def _():
            first = pl.multiple_of(part * half, half)
            finish_kernel(
                first, x_ref, num_ref, den_ref, w_ref, gain_ref, up_ref, down_ref, out_ref.at[pl.ds(first, half)],
                acc_ref, n_ref, hidden_ref,
            )

        return carry

    lax.fori_loop(0, 2, one, 0)


def open_kernel(
    first, tiles, x_ref, num_ref, den_ref, w_ref, gain_ref, up_ref, down_ref, acc_ref, n_ref, hidden_ref
):
    mix(first, x_ref, num_ref, den_ref, w_ref, gain_ref, acc_ref, n_ref)
    feed_forward(0, tiles, n_ref, up_ref, down_ref, acc_ref, hidden_ref)


def close_kernel(begin, acc_in, n_ref, up_ref, down_ref, out_ref, acc_ref, hidden_ref):
    acc_ref[...] = acc_in[...]
    tiles = up_ref.shape[1] // hidden_ref.shape[2]
    feed_forward(begin, tiles, n_ref, up_ref, down_ref, acc_ref, hidden_ref)
    out_ref[...] = acc_ref[...].astype(BF16)


def vmem():
    return pl.BlockSpec(memory_space=pltpu.VMEM)


def call(kernel, name, operands, docs, results, scratch, aliases=None, held=True):
    inputs = [pltpu.with_memory_space_constraint(operand, pltpu.VMEM) for operand in operands]
    in_specs = [vmem()] * len(inputs)
    if docs is not None:
        inputs.append(docs)
        in_specs.append(pl.BlockSpec(memory_space=pltpu.SMEM))
    return pl.pallas_call(
        kernel,
        in_specs=in_specs,
        out_specs=[vmem()] * len(results),
        out_shape=[pltpu.VMEM(*one) if held else jax.ShapeDtypeStruct(*one) for one in results],
        scratch_shapes=scratch,
        input_output_aliases=aliases or {},
        compiler_params=pltpu.CompilerParams(vmem_limit_bytes=VMEM_BYTES),
        cost_estimate=COST,
        name=name,
    )(*inputs)


def own_part(x, gains, weights, docs):
    rows, width = x.shape
    results = [((3, rows, width), BF16), ((rows, width), F32), ((rows, LANES), F32)]
    scratch = [pltpu.VMEM((rows, width), BF16)]
    return call(own_kernel, "own_part", (x, gains, weights[0], docs.own_column, docs.ids), docs.ids, results, scratch)


def piece_part(x, shift, gains, w_attn, qkv, num, den, docs):
    _, rows, width = qkv.shape
    keys = x.shape[0]
    return call(
        functools.partial(piece_kernel, shift, 0),
        "piece_part",
        (x, gains, w_attn, qkv, num, den, docs.own_column, docs.ids),
        docs.ids,
        [((rows, width), F32), ((rows, LANES), F32)],
        [pltpu.VMEM((keys, width), BF16), pltpu.VMEM((2, keys, width), BF16)],
        aliases={4: 0, 5: 1},
    )


def message_part(x, piece, gains, w_attn, docs):
    half, width = x.shape
    keys = 2 * half
    return call(
        message_kernel,
        "message_part",
        (x, piece, gains, w_attn, docs.later_column, docs.ids),
        docs.ids,
        [((half, width + LANES), BF16)],
        [pltpu.VMEM((1, half, width), BF16), pltpu.VMEM((keys, width), BF16), pltpu.VMEM((2, keys, width), BF16)]
        + [pltpu.VMEM((half, width), F32), pltpu.VMEM((half, LANES), F32)],
    )[0]


def reply_part(message, gains, w_attn, qkv, num, den, docs):
    _, rows, width = qkv.shape
    keys = message.shape[0]
    return call(
        reply_kernel,
        "reply_part",
        (message, gains, w_attn, qkv, num, den, docs.own_column, docs.ids),
        docs.ids,
        [((rows, width), F32), ((rows, LANES), F32)],
        [pltpu.VMEM((keys, width), BF16), pltpu.VMEM((2, keys, width), BF16)],
        aliases={4: 0, 5: 1},
    )


def finish_scratch(rows, width, weights):
    tile = min(TILE, weights[1].shape[1])
    return [pltpu.VMEM((rows, width), F32), pltpu.VMEM((rows, width), BF16), pltpu.VMEM((2, rows, tile), BF16)]


def finish_part(x, num, den, weights, gains, part):
    half, width = x.shape[0] // 2, x.shape[1]
    return call(
        functools.partial(finish_kernel, part * half),
        "finish_part",
        (x, num, den, weights[0], gains, *weights[1:]),
        None,
        [((half, width), BF16)],
        finish_scratch(half, width, weights),
    )[0]


def again_part(done, x, num, den, weights, gains, docs):
    half, width = done.shape
    return call(
        functools.partial(again_kernel, half),
        "again_part",
        (done, x, num, den, weights[0], gains, *weights[1:]),
        docs.ids,
        [((half, width), BF16)],
        finish_scratch(half, width, weights),
        aliases={0: 0},
    )[0]


def last_part(done, x, num, den, weights, gains, docs):
    half, width = done.shape
    return call(
        last_kernel,
        "last_part",
        (done, x, num, den, weights[0], gains, *weights[1:]),
        docs.ids,
        [(x.shape, BF16)],
        finish_scratch(half, width, weights),
        held=False,
    )[0]


def open_part(x, num, den, weights, gains, part, tiles):
    width = x.shape[1]
    rows = x.shape[0] // 2
    return call(
        functools.partial(open_kernel, part * rows, tiles),
        "open_part",
        (x, num, den, weights[0], gains, *weights[1:]),
        None,
        [((rows, width), F32), ((rows, width), BF16)],
        [pltpu.VMEM((2, rows, min(TILE, weights[1].shape[1])), BF16)],
    )


def close_part(acc, n, weights, tiles):
    return call(
        functools.partial(close_kernel, tiles),
        "close_part",
        (acc, n, *weights[1:]),
        None,
        [(acc.shape, BF16)],
        [pltpu.VMEM(acc.shape, F32), pltpu.VMEM((2, acc.shape[0], min(TILE, weights[1].shape[1])), BF16)],
    )[0]


def shifted(value, axis, steps):
    count = lax.axis_size(axis)
    first, last = max(0, -steps), min(count, count - steps)
    return lax.ppermute(value, axis, [(i, i + steps) for i in range(first, last)])


def swapped(value, axis, bit):
    return lax.ppermute(value, axis, [(i, i ^ bit) for i in range(lax.axis_size(axis))])


class Documents:
    def __init__(self, doc_ids, rows):
        count = lax.axis_size("seq")
        self.ids, self.rows, self.half = doc_ids, rows, rows // 2
        longest = doc_ids.shape[1] // 2
        self.hops = min(count - 1, -(-(longest - 1) // rows))
        self.short = self.hops == 2 and longest <= 2 * rows and rows % 2 == 0
        place = lax.axis_index("seq")

        def column(later, size):
            start = jnp.minimum((place + later) * rows, doc_ids.shape[1] - size)
            ids = lax.dynamic_slice_in_dim(doc_ids, start, size, 1)
            return jnp.broadcast_to(ids.reshape(-1, 1), (size, LANES))

        self.own_column = column(0, rows)
        self.later_column = column(1, self.half) if self.short else self.own_column


def attention(x, state, piece, first_back, docs, gains, weights):
    qkv, *state = state
    w_attn = weights[0]
    if docs.short:
        message = message_part(after(first_back, qkv), piece, gains, w_attn, docs)
        state = after(state[0], message), state[1]
        message = shifted(message, "seq", 1)
        num, den = piece_part(piece, 1, gains, w_attn, qkv, *state, docs)
        done = finish_part(x, num, den, weights, gains, 1)
        return *reply_part(message, gains, w_attn, qkv, after(num, done), den, docs), done
    state = piece_part(piece, 1, gains, w_attn, qkv, *state, docs)
    for hop in range(2, docs.hops + 1):
        piece = shifted(piece, "seq", 1)
        state = piece_part(piece, hop, gains, w_attn, qkv, *state, docs)
    return *state, finish_part(x, *state, weights, gains, 1)


def packed(row):
    high = lax.reduce_precision(row, 8, 7)
    low = lax.reduce_precision(row - high, 8, 7)
    place = lax.broadcasted_iota(jnp.int32, (CARRIED, row.shape[1]), 0)
    return jnp.where(place == 0, high, jnp.where(place == 1, low, 0.0)).astype(BF16)


def unpacked(rows):
    return rows[:1].astype(F32) + rows[1:2].astype(F32)


def after(value, *earlier):
    return lax.optimization_barrier((value, *earlier))[0]


def own_half(rows, odd):
    half = rows.shape[0] // 2
    return jnp.where(odd, rows[half:], rows[:half]), jnp.where(odd, rows[:half], rows[half:])


class Chain:
    def __init__(self, own_states, other_states, even_gain, odd_gain, bits, before=None):
        self.bits, self.odd, self.leading = bits, bits[1], bits[0]
        self.even_gain, self.odd_gain = even_gain, odd_gain
        self.levels = before.levels if before else []
        self.factor, self.factor_before = even_gain * odd_gain, jnp.ones_like(even_gain)
        even, odd = self.sorted(own_states, other_states)
        self.even_states = even
        behind = jnp.where(self.leading, 0.0, self.even_gain * even.astype(F32))
        self.known = self.odd_gain * (behind + odd.astype(F32))

    def sorted(self, mine, other):
        return jnp.where(self.odd, other, mine), jnp.where(self.odd, mine, other)

    def enter(self, fine, *earlier):
        fine = after(fine, *earlier)
        half = fine.shape[0] // 2
        mine, sent = own_half(fine, self.odd)
        other = swapped(sent, "depth", 1)
        self.fine_even, fine_odd = self.sorted(mine, other)
        self.total = self.odd_gain * self.fine_even.astype(F32) + fine_odd.astype(F32) - self.known
        self.before = jnp.zeros_like(self.total)

    def level(self, index, sent_after=(), used_after=()):
        bit, last = 2 << index, index + 1 == self.steps()
        upper, rows = self.bits[bit], self.total.shape[0]
        sent = self.total.astype(BF16)
        carries = index == len(self.levels) and not last
        if carries:
            sent = jnp.concatenate([sent, packed(self.factor)], axis=0)
        theirs = after(swapped(after(sent, *sent_after), "depth", bit), *used_after)
        if index == len(self.levels):
            their_factor = unpacked(theirs[rows:]) if carries else None
            self.levels.append((self.factor, their_factor, self.factor_before))
            if carries:
                self.factor_before = jnp.where(upper, self.factor_before * their_factor, self.factor_before)
                self.factor = self.factor * their_factor
        factor, their_factor, factor_before = self.levels[index]
        theirs = theirs[:rows].astype(F32)
        if not last:
            self.total = jnp.where(upper, factor * theirs + self.total, their_factor * self.total + theirs)
        self.before = jnp.where(upper, factor_before * theirs + self.before, self.before)

    def steps(self):
        return len(self.bits) - 2

    def leave(self, used_after=()):
        even_states = self.even_states.astype(F32)
        even = jnp.where(self.leading, even_states, self.before)
        odd = self.even_gain * (even - even_states) + self.fine_even.astype(F32)
        even, odd = even.astype(BF16), odd.astype(BF16)
        mine, sent = jnp.where(self.odd, odd, even), jnp.where(self.odd, even, odd)
        other = after(swapped(sent, "depth", 1), *used_after)
        low, high = self.sorted(mine, other)
        return jnp.concatenate([low, high], axis=0)


def on_device(interfaces, doc_ids, w_attn, w_up, w_down, norm_gains, coarse_gain):
    x = interfaces[0, 0]
    rows = x.shape[0]
    half = rows // 2
    gains = norm_gains[0, 0]
    weights = (w_attn[0, 0], w_up[0, 0], w_down[0, 0])
    parts = [x[:half], x[half:]]
    piece = shifted(x, "seq", 1)
    docs = Documents(doc_ids, rows)
    place, bits, bit = lax.axis_index("depth"), {}, 1
    while bit < lax.axis_size("depth"):
        bits[bit] = (place & bit) != 0
        bit *= 2
    bits[0] = place < 2
    early, bits, docs.own_column, docs.later_column = lax.optimization_barrier(
        (x, bits, docs.own_column, docs.later_column)
    )
    first_back = shifted(after(parts[0], docs.own_column), "seq", -1)
    state = own_part(early, gains, weights, docs)
    kept, sent = zip(*[own_half(part, bits[1]) for part in parts])
    sent = jnp.concatenate([*after(sent, state[0]), packed(coarse_gain)], axis=0)
    other = swapped(sent, "depth", 1)
    num, den, done = attention(early, state, piece, first_back, docs, gains, weights)
    other_gain = unpacked(other[half:])
    pair = jnp.where(bits[1], other_gain, coarse_gain), jnp.where(bits[1], coarse_gain, other_gain)
    first = Chain(kept[1], other[half // 2 : half], *pair, bits)
    second = Chain(kept[0], other[: half // 2], *pair, bits, first)
    num = after(num, first.known, second.known)
    first.enter(again_part(done, early, num, den, weights, gains, docs) if docs.short else done)
    tiles = weights[1].shape[1] // TILE // 2
    acc, n = open_part(early, after(num, first.total), den, weights, gains, 0, tiles)
    first.level(0, used_after=(n,))
    fine = close_part(after(acc, first.total), n, weights, tiles)
    first.level(1, used_after=(fine,))
    second.enter(fine, first.before)
    for i in range(2, first.steps()):
        second.level(i - 2)
        first.level(i)
    late = first.leave()
    late_piece = shifted(late, "seq", 1)
    for i in range(max(0, first.steps() - 2), first.steps()):
        last = i + 1 == first.steps()
        second.level(i, (late,) if i > 0 else (), (late_piece,) if last else ())
    soon = second.leave()
    piece = jnp.concatenate([shifted(soon, "seq", 1), late_piece], axis=0)
    x = jnp.concatenate([soon, late], axis=0)
    first_back = shifted(after(soon, x), "seq", -1)
    state = own_part(x, gains, weights, docs)
    num, den, done = attention(x, state, piece, first_back, docs, gains, weights)
    return last_part(done, x, num, den, weights, gains, docs)[None, None]


def solution(mesh):
    in_specs = (
        P("depth", None, "seq", None),
        P(),
        P("depth", None, None, None, None),
        P("depth", None, None, None),
        P("depth", None, None, None),
        P("depth", None, None, None),
        P("depth", None),
    )
    out_specs = P("depth", None, "seq", None)
    return jax.shard_map(
        on_device, mesh=mesh, in_specs=in_specs, out_specs=out_specs, check_vma=False
    )
```

```python
import functools

import jax
import jax.numpy as jnp
from jax import lax
from jax.experimental import pallas as pl
from jax.experimental.pallas import tpu as pltpu
from jax.sharding import PartitionSpec as P

HEADS = 16
LANES = 128
CARRIED = 16
BLOCK = 256
TILE = 512
TILES = 8
VMEM_BYTES = 10 * 1024 * 1024
COST = pl.CostEstimate(flops=1 << 20, bytes_accessed=1 << 16, transcendentals=0)
F32 = jnp.float32
BF16 = jnp.bfloat16


def rms_norm(value, gain):
    return value * lax.rsqrt(jnp.mean(value * value, axis=-1, keepdims=True) + 1e-05) * gain


def dot(a, b):
    return jnp.dot(a, b, preferred_element_type=F32)


def attend(q_ref, k_ref, v_ref, num_ref, den_ref, column_ref, row_ref, doc_ref, q_at, k_at, causal=False):
    rows, width = q_ref.shape
    keys = k_ref.shape[0]
    head_dim = width // HEADS
    per_tile = LANES // head_dim
    q_block, k_block = min(BLOCK, rows), min(BLOCK, keys)
    lane = lax.broadcasted_iota(jnp.int32, (1, LANES), 1)
    members = [lane // head_dim == i for i in range(per_tile)]
    count_q, count_k = rows // q_block, keys // k_block

    def one(index, carry):
        qi, ki = index // count_k, index % count_k
        q0 = pl.multiple_of(qi * q_block, q_block)
        k0 = pl.multiple_of(ki * k_block, k_block)
        needed = doc_ref[0, k_at + k0 + k_block - 1] >= doc_ref[0, q_at + q0]
        if causal:
            needed = (k0 <= q0) & (needed | (k0 == q0))

        @pl.when(needed)
        def _():
            key_docs = row_ref[:, pl.ds(pl.multiple_of(k_at + k0, k_block), k_block)]
            allowed = column_ref[pl.ds(q0, q_block), :1] == key_docs
            if causal:
                q_pos = q0 + lax.broadcasted_iota(jnp.int32, (q_block, k_block), 0)
                k_pos = k0 + lax.broadcasted_iota(jnp.int32, (q_block, k_block), 1)
                allowed = allowed & (k_pos <= q_pos)
            ones = jnp.ones((k_block, LANES), BF16)

            def heads(tile, den):
                cols = pl.ds(pl.multiple_of(tile * LANES, LANES), LANES)
                queries = q_ref[pl.ds(q0, q_block), cols]
                keys_here = k_ref[pl.ds(k0, k_block), cols]
                values = jnp.concatenate([v_ref[pl.ds(k0, k_block), cols], ones], axis=1)
                num = None
                for i, member in enumerate(members):
                    scores = lax.dot_general(
                        jnp.where(member, queries, jnp.zeros_like(queries)),
                        keys_here,
                        (((1,), (1,)), ((), ())),
                        preferred_element_type=F32,
                    )
                    weights = jnp.where(allowed, jnp.exp(scores), 0.0).astype(BF16)
                    out = dot(weights, values)
                    num = out[:, :LANES] if num is None else jnp.where(member, out[:, :LANES], num)
                    den = jnp.where(lane == tile * per_tile + i, out[:, LANES:], den)
                num_ref[pl.ds(q0, q_block), cols] += num
                return den

            def some(step, den):
                for i in range(TILES):
                    den = heads(step * TILES + i, den)
                return den

            den = jnp.zeros((q_block, LANES), F32)
            den_ref[pl.ds(q0, q_block), :] += lax.fori_loop(0, width // LANES // TILES, some, den, unroll=True)

        return carry

    lax.fori_loop(0, count_q * count_k, one, 0)


def spread(per_head, width):
    shape = (LANES, width)
    chosen = lax.broadcasted_iota(jnp.int32, shape, 1) // (width // HEADS) == lax.broadcasted_iota(jnp.int32, shape, 0)
    chosen = jnp.where(chosen, 1.0, 0.0).astype(BF16)
    high = per_head.astype(BF16)
    return dot(high, chosen) + dot((per_head - high.astype(F32)).astype(BF16), chosen)


def normed(x_ref, gain_ref):
    return rms_norm(x_ref[...].astype(F32), gain_ref[0:1]).astype(BF16)


def project(n_ref, w_ref, first, out_ref):
    count, _, width = out_ref.shape
    tile = min(TILE, width)
    steps = width // tile

    def one(step, carry):
        i, j = step // steps, step % steps
        cols = pl.ds(pl.multiple_of(j * tile, tile), tile)
        out = dot(n_ref[...], w_ref[first + i, :, cols]).astype(BF16)
        if first == 0:
            out *= jnp.where(i == 0, (width // HEADS) ** (-0.5), 1.0).astype(BF16)
        out_ref[i, :, cols] = out
        return carry

    lax.fori_loop(0, count * steps, one, 0)


def own_kernel(x_ref, gain_ref, w_ref, column_ref, row_ref, doc_ref, qkv_ref, num_ref, den_ref, n_ref):
    here = lax.axis_index("seq") * x_ref.shape[0]
    n_ref[...] = normed(x_ref, gain_ref)
    project(n_ref, w_ref, 0, qkv_ref)
    num_ref[...] = jnp.zeros_like(num_ref)
    den_ref[...] = jnp.zeros_like(den_ref)
    q_ref, k_ref, v_ref = [qkv_ref.at[i] for i in range(3)]
    attend(q_ref, k_ref, v_ref, num_ref, den_ref, column_ref, row_ref, doc_ref, here, here, True)


def piece_kernel(
    shift, first, x_ref, gain_ref, w_ref, qkv_ref, num_in, den_in, column_ref, row_ref, doc_ref,
    num_ref, den_ref, n_ref, kv_ref,
):
    del num_in, den_in
    rows, keys = qkv_ref.shape[1], x_ref.shape[0]
    shard = lax.axis_index("seq") - shift
    here, there = (shard + shift) * rows, jnp.maximum(shard, 0) * rows + first

    @pl.when((shard >= 0) & (doc_ref[0, there + keys - 1] >= doc_ref[0, here]))
    def _():
        n_ref[...] = normed(x_ref, gain_ref)
        project(n_ref, w_ref, 1, kv_ref)
        attend(
            qkv_ref.at[0], kv_ref.at[0], kv_ref.at[1], num_ref, den_ref, column_ref, row_ref, doc_ref, here, there
        )


def far_document(doc_ref, rows, count):
    found = False
    for middle in range(1, count - 1):
        over = doc_ref[0, middle * rows - 1] == doc_ref[0, (middle + 1) * rows]
        deep = doc_ref[0, middle * rows - rows // 2 - 1] == doc_ref[0, (middle + 1) * rows]
        found = found | (over & deep)
    return found


def message_kernel(
    x_ref, piece_ref, gain_ref, w_ref, column_ref, row_ref, doc_ref,
    out_ref, q_ref, n_ref, kv_ref, num_ref, den_ref,
):
    half, width = x_ref.shape
    rows = 2 * half
    count = lax.axis_size("seq")
    place = lax.axis_index("seq")
    inside = (place >= 1) & (place + 1 < count)
    here = jnp.where(inside, place + 1, 0) * rows
    there = jnp.where(inside, place - 1, 0) * rows
    far = far_document(doc_ref, rows, count)

    @pl.when(jnp.logical_not(far))
    def _():
        out_ref[:, :width] = piece_ref[half:]

    @pl.when(far)
    def _():
        num_ref[...] = jnp.zeros_like(num_ref)
        den_ref[...] = jnp.zeros_like(den_ref)

        @pl.when(inside & (doc_ref[0, there + rows - 1] >= doc_ref[0, here]))
        def _():
            n_ref[:half] = normed(x_ref, gain_ref)
            project(n_ref.at[:half], w_ref, 0, q_ref)
            n_ref[...] = normed(piece_ref, gain_ref)
            project(n_ref, w_ref, 1, kv_ref)
            attend(
                q_ref.at[0], kv_ref.at[0], kv_ref.at[1], num_ref, den_ref, column_ref, row_ref, doc_ref, here, there
            )

        out_ref[:, :width] = num_ref[...].astype(BF16)
        out_ref[:, width:] = den_ref[...].astype(BF16)


def reply_kernel(
    message_ref, gain_ref, w_ref, qkv_ref, num_in, den_in, column_ref, row_ref, doc_ref,
    num_ref, den_ref, n_ref, kv_ref,
):
    _, rows, width = qkv_ref.shape
    half = message_ref.shape[0]
    far = far_document(doc_ref, rows, lax.axis_size("seq"))

    @pl.when(far)
    def _():
        num_ref[:half] += message_ref[:, :width].astype(F32)
        den_ref[:half] += message_ref[:, width:].astype(F32)

    @pl.when(jnp.logical_not(far))
    def _():
        piece_kernel(
            2, half, message_ref.at[:, :width], gain_ref, w_ref, qkv_ref, num_in, den_in, column_ref, row_ref, doc_ref,
            num_ref, den_ref, n_ref, kv_ref,
        )


def mix(first, x_ref, num_ref, den_ref, w_ref, gain_ref, acc_ref, n_ref):
    rows, width = acc_ref.shape
    here = pl.ds(first, rows)
    lane = lax.broadcasted_iota(jnp.int32, (rows, LANES), 1)
    inverse = 1.0 / jnp.where(lane < HEADS, den_ref[here], 1.0)
    n_ref[...] = (num_ref[here] * spread(inverse, width)).astype(BF16)
    tile = min(TILE, width)

    def one(j, carry):
        cols = pl.ds(pl.multiple_of(j * tile, tile), tile)
        acc_ref[:, cols] = x_ref[here, cols].astype(F32) + dot(n_ref[...], w_ref[3, :, cols])
        return carry

    lax.fori_loop(0, width // tile, one, 0)
    n_ref[...] = rms_norm(acc_ref[...], gain_ref[1:2]).astype(BF16)


def feed_forward(begin, end, n_ref, up_ref, down_ref, acc_ref):
    tile = min(TILE, up_ref.shape[1])

    def one(j, carry):
        units = pl.ds(pl.multiple_of(j * tile, tile), tile)
        expanded = jax.nn.gelu(dot(n_ref[...], up_ref[:, units])).astype(BF16)
        acc_ref[...] += dot(expanded, down_ref[units])
        return carry

    lax.fori_loop(begin, end, one, 0)


def tiles_of(up_ref):
    return up_ref.shape[1] // min(TILE, up_ref.shape[1])


def finish_kernel(first, x_ref, num_ref, den_ref, w_ref, gain_ref, up_ref, down_ref, out_ref, acc_ref, n_ref):
    mix(first, x_ref, num_ref, den_ref, w_ref, gain_ref, acc_ref, n_ref)
    feed_forward(0, tiles_of(up_ref), n_ref, up_ref, down_ref, acc_ref)
    out_ref[...] = acc_ref[...].astype(BF16)


def seen_by_second_half(doc_ref, rows):
    place = lax.axis_index("seq")
    before = jnp.maximum((place - 1) * rows - 1, 0)
    return (place >= 2) & (doc_ref[0, before] == doc_ref[0, place * rows + rows // 2])


def again_kernel(
    message_ref, gain_ref, w_ref, qkv_ref, num_in, den_in, done_in, x_ref, up_ref, down_ref, column_ref, row_ref, doc_ref,
    num_ref, den_ref, done_ref, n_ref, kv_ref, acc_ref,
):
    del done_in
    half = done_ref.shape[0]
    reply_kernel(
        message_ref, gain_ref, w_ref, qkv_ref, num_in, den_in, column_ref, row_ref, doc_ref,
        num_ref, den_ref, n_ref, kv_ref,
    )

    @pl.when(seen_by_second_half(doc_ref, 2 * half))
    def _():
        finish_kernel(half, x_ref, num_ref, den_ref, w_ref, gain_ref, up_ref, down_ref, done_ref, acc_ref, n_ref)


def last_kernel(
    message_ref, gain_ref, w_ref, qkv_ref, num_in, den_in, done_ref, x_ref, up_ref, down_ref, column_ref, row_ref, doc_ref,
    num_ref, den_ref, out_ref, n_ref, kv_ref, acc_ref, result_ref, sems,
):
    half = done_ref.shape[0]
    again = seen_by_second_half(doc_ref, 2 * half) if message_ref is not None else False
    halves = [out_ref.at[:half], out_ref.at[half:]]
    as_it_was = pltpu.make_async_copy(done_ref, halves[1], sems.at[1])
    copies = [pltpu.make_async_copy(result_ref.at[i], halves[i], sems.at[i]) for i in range(2)]

    @pl.when(jnp.logical_not(again))
    def _():
        as_it_was.start()

    if message_ref is not None:
        reply_kernel(
            message_ref, gain_ref, w_ref, qkv_ref, num_in, den_in, column_ref, row_ref, doc_ref,
            num_ref, den_ref, n_ref, kv_ref,
        )

    def one(part, carry):
        @pl.when((part == 0) | again)
        def _():
            first = pl.multiple_of(part * half, half)
            finish_kernel(
                first, x_ref, num_ref, den_ref, w_ref, gain_ref, up_ref, down_ref, result_ref.at[part], acc_ref, n_ref
            )

        return carry

    lax.fori_loop(0, 2, one, 0)
    copies[0].start()

    @pl.when(again)
    def _():
        copies[1].start()
        copies[1].wait()

    @pl.when(jnp.logical_not(again))
    def _():
        as_it_was.wait()

    copies[0].wait()


def open_kernel(first, tiles, x_ref, num_ref, den_ref, w_ref, gain_ref, up_ref, down_ref, acc_ref, n_ref):
    mix(first, x_ref, num_ref, den_ref, w_ref, gain_ref, acc_ref, n_ref)
    feed_forward(0, tiles, n_ref, up_ref, down_ref, acc_ref)


def close_kernel(begin, acc_in, n_ref, up_ref, down_ref, out_ref, acc_ref):
    acc_ref[...] = acc_in[...]
    feed_forward(begin, tiles_of(up_ref), n_ref, up_ref, down_ref, acc_ref)
    out_ref[...] = acc_ref[...].astype(BF16)


def vmem():
    return pl.BlockSpec(memory_space=pltpu.VMEM)


def call(kernel, name, operands, docs, results, scratch, aliases=None, sent=()):
    inputs = [pltpu.with_memory_space_constraint(operand, pltpu.VMEM) for operand in operands]
    in_specs = [vmem()] * len(inputs)
    if docs is not None:
        inputs.append(docs)
        in_specs.append(pl.BlockSpec(memory_space=pltpu.SMEM))
    return pl.pallas_call(
        kernel,
        in_specs=in_specs,
        out_specs=[pl.BlockSpec(memory_space=pl.ANY) if i in sent else vmem() for i in range(len(results))],
        out_shape=[
            jax.ShapeDtypeStruct(*one) if i in sent else pltpu.VMEM(*one) for i, one in enumerate(results)
        ],
        scratch_shapes=scratch,
        input_output_aliases=aliases or {},
        compiler_params=pltpu.CompilerParams(vmem_limit_bytes=VMEM_BYTES),
        cost_estimate=COST,
        name=name,
    )(*inputs)


def own_part(x, gains, weights, docs):
    rows, width = x.shape
    results = [((3, rows, width), BF16), ((rows, width), F32), ((rows, LANES), F32)]
    scratch = [pltpu.VMEM((rows, width), BF16)]
    return call(own_kernel, "own_part", (x, gains, weights[0], docs.own_column, docs.ids), docs.ids, results, scratch)


def piece_part(x, shift, gains, w_attn, qkv, num, den, docs):
    _, rows, width = qkv.shape
    keys = x.shape[0]
    return call(
        functools.partial(piece_kernel, shift, 0),
        "piece_part",
        (x, gains, w_attn, qkv, num, den, docs.own_column, docs.ids),
        docs.ids,
        [((rows, width), F32), ((rows, LANES), F32)],
        [pltpu.VMEM((keys, width), BF16), pltpu.VMEM((2, keys, width), BF16)],
        aliases={4: 0, 5: 1},
    )


def message_part(x, piece, gains, w_attn, docs):
    half, width = x.shape
    keys = 2 * half
    return call(
        message_kernel,
        "message_part",
        (x, piece, gains, w_attn, docs.later_column, docs.ids),
        docs.ids,
        [((half, width + LANES), BF16)],
        [pltpu.VMEM((1, half, width), BF16), pltpu.VMEM((keys, width), BF16), pltpu.VMEM((2, keys, width), BF16)]
        + [pltpu.VMEM((half, width), F32), pltpu.VMEM((half, LANES), F32)],
    )[0]


def finish_part(x, num, den, weights, gains, part):
    half, width = x.shape[0] // 2, x.shape[1]
    return call(
        functools.partial(finish_kernel, part * half),
        "finish_part",
        (x, num, den, weights[0], gains, *weights[1:]),
        None,
        [((half, width), BF16)],
        [pltpu.VMEM((half, width), F32), pltpu.VMEM((half, width), BF16)],
    )[0]


def reply_scratch(half, width):
    return [
        pltpu.VMEM((half, width), BF16),
        pltpu.VMEM((2, half, width), BF16),
        pltpu.VMEM((half, width), F32),
    ]


def again_part(message, state, done, x, weights, gains, docs):
    qkv, num, den = state
    half, width = done.shape
    return call(
        again_kernel,
        "again_part",
        (message, gains, weights[0], qkv, num, den, done, x, *weights[1:], docs.own_column, docs.ids),
        docs.ids,
        [(num.shape, F32), (den.shape, F32), ((half, width), BF16)],
        reply_scratch(half, width),
        aliases={4: 0, 5: 1, 6: 2},
    )


def last_part(message, state, done, x, weights, gains, docs):
    qkv, num, den = state
    half, width = done.shape
    operands = (message, gains, weights[0], qkv, num, den, done, x, *weights[1:], docs.own_column, docs.ids)
    kernel, aliases = last_kernel, {4: 0, 5: 1}
    if message is None:
        kernel, operands, aliases = functools.partial(last_kernel, None), operands[1:], {3: 0, 4: 1}
    return call(
        kernel,
        "last_part",
        operands,
        docs.ids,
        [(num.shape, F32), (den.shape, F32), (x.shape, BF16)],
        reply_scratch(half, width) + [pltpu.VMEM((2, half, width), BF16), pltpu.SemaphoreType.DMA((2,))],
        aliases=aliases,
        sent=(2,),
    )[2]


def open_part(x, num, den, weights, gains, part, tiles):
    width = x.shape[1]
    rows = x.shape[0] // 2
    return call(
        functools.partial(open_kernel, part * rows, tiles),
        "open_part",
        (x, num, den, weights[0], gains, *weights[1:]),
        None,
        [((rows, width), F32), ((rows, width), BF16)],
        [],
    )


def close_part(acc, n, weights, tiles):
    return call(
        functools.partial(close_kernel, tiles),
        "close_part",
        (acc, n, *weights[1:]),
        None,
        [(acc.shape, BF16)],
        [pltpu.VMEM(acc.shape, F32)],
    )[0]


def shifted(value, axis, steps):
    count = lax.axis_size(axis)
    first, last = max(0, -steps), min(count, count - steps)
    return lax.ppermute(value, axis, [(i, i + steps) for i in range(first, last)])


def swapped(value, axis, bit):
    return lax.ppermute(value, axis, [(i, i ^ bit) for i in range(lax.axis_size(axis))])


class Documents:
    def __init__(self, doc_ids, rows):
        count = lax.axis_size("seq")
        self.ids, self.rows, self.half = doc_ids, rows, rows // 2
        longest = doc_ids.shape[1] // 2
        self.hops = min(count - 1, -(-(longest - 1) // rows))
        self.short = self.hops == 2 and longest <= 2 * rows and rows % 2 == 0
        place = lax.axis_index("seq")

        def column(later, size):
            start = jnp.minimum((place + later) * rows, doc_ids.shape[1] - size)
            ids = lax.dynamic_slice_in_dim(doc_ids, start, size, 1)
            return jnp.broadcast_to(ids.reshape(-1, 1), (size, LANES))

        self.own_column = column(0, rows)
        self.later_column = column(1, self.half) if self.short else self.own_column


def attention(x, state, piece, first_back, docs, gains, weights):
    qkv, *state = state
    w_attn = weights[0]
    if docs.short:
        message = message_part(after(first_back, qkv), piece, gains, w_attn, docs)
        state = after(state[0], message), state[1]
        message = shifted(message, "seq", 1)
        num, den = piece_part(piece, 1, gains, w_attn, qkv, *state, docs)
        done = finish_part(x, num, den, weights, gains, 1)
        return after(message, done), (qkv, num, den), done
    state = piece_part(piece, 1, gains, w_attn, qkv, *state, docs)
    for hop in range(2, docs.hops + 1):
        piece = shifted(piece, "seq", 1)
        state = piece_part(piece, hop, gains, w_attn, qkv, *state, docs)
    return None, (qkv, *state), finish_part(x, *state, weights, gains, 1)


def packed(row):
    high = lax.reduce_precision(row, 8, 7)
    low = lax.reduce_precision(row - high, 8, 7)
    place = lax.broadcasted_iota(jnp.int32, (CARRIED, row.shape[1]), 0)
    return jnp.where(place == 0, high, jnp.where(place == 1, low, 0.0)).astype(BF16)


def unpacked(rows):
    return rows[:1].astype(F32) + rows[1:2].astype(F32)


def after(value, *earlier):
    return lax.optimization_barrier((value, *earlier))[0]


def own_half(rows, odd):
    half = rows.shape[0] // 2
    return jnp.where(odd, rows[half:], rows[:half]), jnp.where(odd, rows[:half], rows[half:])


class Chain:
    def __init__(self, own_states, other_states, even_gain, odd_gain, bits, before=None):
        self.bits, self.odd, self.leading = bits, bits[1], bits[0]
        self.even_gain, self.odd_gain = even_gain, odd_gain
        self.levels = before.levels if before else []
        self.factor, self.factor_before = even_gain * odd_gain, jnp.ones_like(even_gain)
        even, odd = self.sorted(own_states, other_states)
        self.even_states = even
        behind = jnp.where(self.leading, 0.0, self.even_gain * even.astype(F32))
        self.known = self.odd_gain * (behind + odd.astype(F32))

    def sorted(self, mine, other):
        return jnp.where(self.odd, other, mine), jnp.where(self.odd, mine, other)

    def enter(self, fine, *earlier):
        fine = after(fine, *earlier)
        half = fine.shape[0] // 2
        mine, sent = own_half(fine, self.odd)
        other = swapped(sent, "depth", 1)
        self.fine_even, fine_odd = self.sorted(mine, other)
        self.total = self.odd_gain * self.fine_even.astype(F32) + fine_odd.astype(F32) - self.known
        self.before = jnp.zeros_like(self.total)

    def level(self, index, sent_after=(), used_after=()):
        bit, last = 2 << index, index + 1 == self.steps()
        upper, rows = self.bits[bit], self.total.shape[0]
        sent = self.total.astype(BF16)
        carries = index == len(self.levels) and not last
        if carries:
            sent = jnp.concatenate([sent, packed(self.factor)], axis=0)
        theirs = after(swapped(after(sent, *sent_after), "depth", bit), *used_after)
        if index == len(self.levels):
            their_factor = unpacked(theirs[rows:]) if carries else None
            self.levels.append((self.factor, their_factor, self.factor_before))
            if carries:
                self.factor_before = jnp.where(upper, self.factor_before * their_factor, self.factor_before)
                self.factor = self.factor * their_factor
        factor, their_factor, factor_before = self.levels[index]
        theirs = theirs[:rows].astype(F32)
        if not last:
            self.total = jnp.where(upper, factor * theirs + self.total, their_factor * self.total + theirs)
        self.before = jnp.where(upper, factor_before * theirs + self.before, self.before)

    def steps(self):
        return len(self.bits) - 2

    def leave(self, used_after=()):
        even_states = self.even_states.astype(F32)
        even = jnp.where(self.leading, even_states, self.before)
        odd = self.even_gain * (even - even_states) + self.fine_even.astype(F32)
        even, odd = even.astype(BF16), odd.astype(BF16)
        mine, sent = jnp.where(self.odd, odd, even), jnp.where(self.odd, even, odd)
        other = after(swapped(sent, "depth", 1), *used_after)
        low, high = self.sorted(mine, other)
        return jnp.concatenate([low, high], axis=0)


def on_device(interfaces, doc_ids, w_attn, w_up, w_down, norm_gains, coarse_gain):
    x = interfaces[0, 0]
    rows = x.shape[0]
    half = rows // 2
    gains = norm_gains[0, 0]
    weights = (w_attn[0, 0], w_up[0, 0], w_down[0, 0])
    parts = [x[:half], x[half:]]
    piece = shifted(x, "seq", 1)
    docs = Documents(doc_ids, rows)
    place, bits, bit = lax.axis_index("depth"), {}, 1
    while bit < lax.axis_size("depth"):
        bits[bit] = (place & bit) != 0
        bit *= 2
    bits[0] = place < 2
    early, bits, docs.own_column, docs.later_column = lax.optimization_barrier(
        (x, bits, docs.own_column, docs.later_column)
    )
    first_back = shifted(after(parts[0], docs.own_column), "seq", -1)
    state = own_part(early, gains, weights, docs)
    kept, sent = zip(*[own_half(part, bits[1]) for part in parts])
    sent = jnp.concatenate([*after(sent, state[0]), packed(coarse_gain)], axis=0)
    other = swapped(sent, "depth", 1)
    message, state, done = attention(early, state, piece, first_back, docs, gains, weights)
    other_gain = unpacked(other[half:])
    pair = jnp.where(bits[1], other_gain, coarse_gain), jnp.where(bits[1], coarse_gain, other_gain)
    first = Chain(kept[1], other[half // 2 : half], *pair, bits)
    second = Chain(kept[0], other[: half // 2], *pair, bits, first)
    _, num, den = state
    if message is not None:
        message = after(message, first.known, second.known)
        num, den, done = again_part(message, state, done, early, weights, gains, docs)
    first.enter(done)
    tiles = weights[1].shape[1] // TILE // 2
    acc, n = open_part(early, after(num, first.total), den, weights, gains, 0, tiles)
    first.level(0, used_after=(n,))
    fine = close_part(after(acc, first.total), n, weights, tiles)
    first.level(1, used_after=(fine,))
    second.enter(fine, first.before)
    for i in range(2, first.steps()):
        second.level(i - 2)
        first.level(i)
    late = first.leave()
    late_piece = shifted(late, "seq", 1)
    for i in range(max(0, first.steps() - 2), first.steps()):
        last = i + 1 == first.steps()
        second.level(i, (late,) if i > 0 else (), (late_piece,) if last else ())
    soon = second.leave()
    piece = jnp.concatenate([shifted(soon, "seq", 1), late_piece], axis=0)
    x = jnp.concatenate([soon, late], axis=0)
    first_back = shifted(after(soon, x), "seq", -1)
    state = own_part(x, gains, weights, docs)
    message, state, done = attention(x, state, piece, first_back, docs, gains, weights)
    return last_part(message, state, done, x, weights, gains, docs)[None, None]


def solution(mesh):
    in_specs = (
        P("depth", None, "seq", None),
        P(),
        P("depth", None, None, None, None),
        P("depth", None, None, None),
        P("depth", None, None, None),
        P("depth", None, None, None),
        P("depth", None),
    )
    out_specs = P("depth", None, "seq", None)
    return jax.shard_map(
        on_device, mesh=mesh, in_specs=in_specs, out_specs=out_specs, check_vma=False
    )
```

```python
import functools

import jax
import jax.numpy as jnp
from jax import lax
from jax.experimental import pallas as pl
from jax.experimental.pallas import tpu as pltpu
from jax.sharding import PartitionSpec as P

HEADS = 16
LANES = 128
CARRIED = 16
BLOCK = 256
TILE = 512
TILES = 8
VMEM_BYTES = 8 * 1024 * 1024
COST = pl.CostEstimate(flops=1 << 20, bytes_accessed=1 << 16, transcendentals=0)
F32 = jnp.float32
BF16 = jnp.bfloat16


def rms_norm(value, gain):
    return value * lax.rsqrt(jnp.mean(value * value, axis=-1, keepdims=True) + 1e-05) * gain


def dot(a, b):
    return jnp.dot(a, b, preferred_element_type=F32)


def attend(q_ref, k_ref, v_ref, num_ref, den_ref, column_ref, row_ref, doc_ref, q_at, k_at, causal=False):
    rows, width = q_ref.shape
    keys = k_ref.shape[0]
    head_dim = width // HEADS
    per_tile = LANES // head_dim
    q_block, k_block = min(BLOCK, rows), min(BLOCK, keys)
    lane = lax.broadcasted_iota(jnp.int32, (1, LANES), 1)
    members = [lane // head_dim == i for i in range(per_tile)]
    count_q, count_k = rows // q_block, keys // k_block

    def one(index, carry):
        qi, ki = index // count_k, index % count_k
        q0 = pl.multiple_of(qi * q_block, q_block)
        k0 = pl.multiple_of(ki * k_block, k_block)
        needed = doc_ref[0, k_at + k0 + k_block - 1] >= doc_ref[0, q_at + q0]
        if causal:
            needed = (k0 <= q0) & (needed | (k0 == q0))

        @pl.when(needed)
        def _():
            key_docs = row_ref[:, pl.ds(pl.multiple_of(k_at + k0, k_block), k_block)]
            allowed = column_ref[pl.ds(q0, q_block), :1] == key_docs
            if causal:
                q_pos = q0 + lax.broadcasted_iota(jnp.int32, (q_block, k_block), 0)
                k_pos = k0 + lax.broadcasted_iota(jnp.int32, (q_block, k_block), 1)
                allowed = allowed & (k_pos <= q_pos)
            ones = jnp.ones((k_block, LANES), BF16)

            def heads(tile, den):
                cols = pl.ds(pl.multiple_of(tile * LANES, LANES), LANES)
                queries = q_ref[pl.ds(q0, q_block), cols]
                keys_here = k_ref[pl.ds(k0, k_block), cols]
                values = jnp.concatenate([v_ref[pl.ds(k0, k_block), cols], ones], axis=1)
                num = None
                for i, member in enumerate(members):
                    scores = lax.dot_general(
                        jnp.where(member, queries, jnp.zeros_like(queries)),
                        keys_here,
                        (((1,), (1,)), ((), ())),
                        preferred_element_type=F32,
                    )
                    weights = jnp.where(allowed, jnp.exp(scores), 0.0).astype(BF16)
                    out = dot(weights, values)
                    num = out[:, :LANES] if num is None else jnp.where(member, out[:, :LANES], num)
                    den = jnp.where(lane == tile * per_tile + i, out[:, LANES:], den)
                num_ref[pl.ds(q0, q_block), cols] += num
                return den

            def some(step, den):
                for i in range(TILES):
                    den = heads(step * TILES + i, den)
                return den

            den = jnp.zeros((q_block, LANES), F32)
            den_ref[pl.ds(q0, q_block), :] += lax.fori_loop(0, width // LANES // TILES, some, den, unroll=True)

        return carry

    lax.fori_loop(0, count_q * count_k, one, 0)


def spread(per_head, width):
    shape = (LANES, width)
    chosen = lax.broadcasted_iota(jnp.int32, shape, 1) // (width // HEADS) == lax.broadcasted_iota(jnp.int32, shape, 0)
    chosen = jnp.where(chosen, 1.0, 0.0).astype(BF16)
    high = per_head.astype(BF16)
    return dot(high, chosen) + dot((per_head - high.astype(F32)).astype(BF16), chosen)


def normed(x_ref, gain_ref):
    return rms_norm(x_ref[...].astype(F32), gain_ref[0:1]).astype(BF16)


def project(n_ref, w_ref, first, out_ref):
    count, _, width = out_ref.shape
    tile = min(TILE, width)
    steps = width // tile

    def one(step, carry):
        i, j = step // steps, step % steps
        cols = pl.ds(pl.multiple_of(j * tile, tile), tile)
        out = dot(n_ref[...], w_ref[first + i, :, cols]).astype(BF16)
        if first == 0:
            out *= jnp.where(i == 0, (width // HEADS) ** (-0.5), 1.0).astype(BF16)
        out_ref[i, :, cols] = out
        return carry

    lax.fori_loop(0, count * steps, one, 0)


def own_kernel(x_ref, gain_ref, w_ref, column_ref, row_ref, doc_ref, q_ref, num_ref, den_ref, n_ref, qkv_ref):
    here = lax.axis_index("seq") * x_ref.shape[0]
    n_ref[...] = normed(x_ref, gain_ref)
    project(n_ref, w_ref, 0, qkv_ref)
    q_ref[...] = qkv_ref[0]
    num_ref[...] = jnp.zeros_like(num_ref)
    den_ref[...] = jnp.zeros_like(den_ref)
    k_ref, v_ref = qkv_ref.at[1], qkv_ref.at[2]
    attend(q_ref, k_ref, v_ref, num_ref, den_ref, column_ref, row_ref, doc_ref, here, here, True)


def piece_kernel(
    shift, first, x_ref, gain_ref, w_ref, q_ref, num_in, den_in, column_ref, row_ref, doc_ref,
    num_ref, den_ref, n_ref, kv_ref,
):
    del num_in, den_in
    rows, keys = q_ref.shape[0], x_ref.shape[0]
    shard = lax.axis_index("seq") - shift
    here, there = (shard + shift) * rows, jnp.maximum(shard, 0) * rows + first

    @pl.when((shard >= 0) & (doc_ref[0, there + keys - 1] >= doc_ref[0, here]))
    def _():
        n_ref[...] = normed(x_ref, gain_ref)
        project(n_ref, w_ref, 1, kv_ref)
        attend(
            q_ref, kv_ref.at[0], kv_ref.at[1], num_ref, den_ref, column_ref, row_ref, doc_ref, here, there
        )


def far_document(doc_ref, rows, count):
    found = False
    for middle in range(1, count - 1):
        over = doc_ref[0, middle * rows - 1] == doc_ref[0, (middle + 1) * rows]
        deep = doc_ref[0, middle * rows - rows // 2 - 1] == doc_ref[0, (middle + 1) * rows]
        found = found | (over & deep)
    return found


def message_kernel(
    x_ref, piece_ref, gain_ref, w_ref, column_ref, row_ref, doc_ref,
    out_ref, q_ref, n_ref, kv_ref, num_ref, den_ref,
):
    half, width = x_ref.shape
    rows = 2 * half
    count = lax.axis_size("seq")
    place = lax.axis_index("seq")
    inside = (place >= 1) & (place + 1 < count)
    here = jnp.where(inside, place + 1, 0) * rows
    there = jnp.where(inside, place - 1, 0) * rows
    far = far_document(doc_ref, rows, count)

    @pl.when(jnp.logical_not(far))
    def _():
        out_ref[:, :width] = piece_ref[half:]

    @pl.when(far)
    def _():
        num_ref[...] = jnp.zeros_like(num_ref)
        den_ref[...] = jnp.zeros_like(den_ref)

        @pl.when(inside & (doc_ref[0, there + rows - 1] >= doc_ref[0, here]))
        def _():
            n_ref[:half] = normed(x_ref, gain_ref)
            project(n_ref.at[:half], w_ref, 0, q_ref)
            n_ref[...] = normed(piece_ref, gain_ref)
            project(n_ref, w_ref, 1, kv_ref)
            attend(
                q_ref.at[0], kv_ref.at[0], kv_ref.at[1], num_ref, den_ref, column_ref, row_ref, doc_ref, here, there
            )

        out_ref[:, :width] = num_ref[...].astype(BF16)
        out_ref[:, width:] = den_ref[...].astype(BF16)


def reply_kernel(
    message_ref, gain_ref, w_ref, q_ref, num_in, den_in, column_ref, row_ref, doc_ref,
    num_ref, den_ref, n_ref, kv_ref,
):
    rows, width = q_ref.shape
    half = message_ref.shape[0]
    far = far_document(doc_ref, rows, lax.axis_size("seq"))

    @pl.when(far)
    def _():
        num_ref[:half] += message_ref[:, :width].astype(F32)
        den_ref[:half] += message_ref[:, width:].astype(F32)

    @pl.when(jnp.logical_not(far))
    def _():
        piece_kernel(
            2, half, message_ref.at[:, :width], gain_ref, w_ref, q_ref, num_in, den_in, column_ref, row_ref, doc_ref,
            num_ref, den_ref, n_ref, kv_ref,
        )


def mix(first, x_ref, num_ref, den_ref, w_ref, gain_ref, acc_ref, n_ref):
    rows, width = acc_ref.shape
    here = pl.ds(first, rows)
    lane = lax.broadcasted_iota(jnp.int32, (rows, LANES), 1)
    inverse = 1.0 / jnp.where(lane < HEADS, den_ref[here], 1.0)
    n_ref[...] = (num_ref[here] * spread(inverse, width)).astype(BF16)
    tile = min(TILE, width)

    def one(j, carry):
        cols = pl.ds(pl.multiple_of(j * tile, tile), tile)
        acc_ref[:, cols] = x_ref[here, cols].astype(F32) + dot(n_ref[...], w_ref[3, :, cols])
        return carry

    lax.fori_loop(0, width // tile, one, 0)
    n_ref[...] = rms_norm(acc_ref[...], gain_ref[1:2]).astype(BF16)


def feed_forward(begin, end, n_ref, up_ref, down_ref, acc_ref):
    tile = min(TILE, up_ref.shape[1])

    def one(j, carry):
        units = pl.ds(pl.multiple_of(j * tile, tile), tile)
        expanded = jax.nn.gelu(dot(n_ref[...], up_ref[:, units])).astype(BF16)
        acc_ref[...] += dot(expanded, down_ref[units])
        return carry

    lax.fori_loop(begin, end, one, 0)


def feed_forward_ahead(n_ref, up_ref, down_ref, acc_ref, hidden_ref):
    tile = hidden_ref.shape[2]
    last = up_ref.shape[1] // tile - 1

    def expand(j):
        units = pl.ds(pl.multiple_of(j * tile, tile), tile)
        hidden_ref[j % 2] = jax.nn.gelu(dot(n_ref[...], up_ref[:, units])).astype(BF16)

    def lower(j):
        acc_ref[...] += dot(hidden_ref[j % 2], down_ref[pl.ds(pl.multiple_of(j * tile, tile), tile)])

    def one(j, carry):
        lower(j)
        expand(j + 1)
        return carry

    expand(0)
    lax.fori_loop(0, last, one, 0)
    lower(last)


def tiles_of(up_ref):
    return up_ref.shape[1] // min(TILE, up_ref.shape[1])


def finish_kernel(
    first, x_ref, num_ref, den_ref, w_ref, gain_ref, up_ref, down_ref, out_ref, acc_ref, n_ref, hidden_ref=None
):
    mix(first, x_ref, num_ref, den_ref, w_ref, gain_ref, acc_ref, n_ref)
    if hidden_ref is None:
        feed_forward(0, tiles_of(up_ref), n_ref, up_ref, down_ref, acc_ref)
    else:
        feed_forward_ahead(n_ref, up_ref, down_ref, acc_ref, hidden_ref)
    out_ref[...] = acc_ref[...].astype(BF16)


def seen_by_second_half(doc_ref, rows):
    place = lax.axis_index("seq")
    before = jnp.maximum((place - 1) * rows - 1, 0)
    return (place >= 2) & (doc_ref[0, before] == doc_ref[0, place * rows + rows // 2])


def again_kernel(
    message_ref, gain_ref, w_ref, q_ref, num_in, den_in, done_in, x_ref, up_ref, down_ref, column_ref, row_ref, doc_ref,
    num_ref, den_ref, done_ref, n_ref, kv_ref, acc_ref,
):
    del done_in
    half = done_ref.shape[0]
    reply_kernel(
        message_ref, gain_ref, w_ref, q_ref, num_in, den_in, column_ref, row_ref, doc_ref,
        num_ref, den_ref, n_ref, kv_ref,
    )

    @pl.when(seen_by_second_half(doc_ref, 2 * half))
    def _():
        finish_kernel(half, x_ref, num_ref, den_ref, w_ref, gain_ref, up_ref, down_ref, done_ref, acc_ref, n_ref)


def last_kernel(
    message_ref, gain_ref, w_ref, q_ref, num_in, den_in, done_ref, x_ref, up_ref, down_ref, column_ref, row_ref, doc_ref,
    num_ref, den_ref, out_ref, n_ref, kv_ref, acc_ref, result_ref, hidden_ref, sems,
):
    half = done_ref.shape[0]
    again = seen_by_second_half(doc_ref, 2 * half) if message_ref is not None else False
    halves = [out_ref.at[:half], out_ref.at[half:]]
    as_it_was = pltpu.make_async_copy(done_ref, halves[1], sems.at[1])
    copies = [pltpu.make_async_copy(result_ref.at[i], halves[i], sems.at[i]) for i in range(2)]

    @pl.when(jnp.logical_not(again))
    def _():
        as_it_was.start()

    if message_ref is not None:
        reply_kernel(
            message_ref, gain_ref, w_ref, q_ref, num_in, den_in, column_ref, row_ref, doc_ref,
            num_ref, den_ref, n_ref, kv_ref,
        )

    def one(part, carry):
        @pl.when((part == 0) | again)
        def _():
            first = pl.multiple_of(part * half, half)
            finish_kernel(
                first, x_ref, num_ref, den_ref, w_ref, gain_ref, up_ref, down_ref, result_ref.at[part], acc_ref, n_ref,
                hidden_ref,
            )

        return carry

    lax.fori_loop(0, 2, one, 0)
    copies[0].start()

    @pl.when(again)
    def _():
        copies[1].start()
        copies[1].wait()

    @pl.when(jnp.logical_not(again))
    def _():
        as_it_was.wait()

    copies[0].wait()


def open_kernel(first, tiles, x_ref, num_ref, den_ref, w_ref, gain_ref, up_ref, down_ref, acc_ref, n_ref):
    mix(first, x_ref, num_ref, den_ref, w_ref, gain_ref, acc_ref, n_ref)
    feed_forward(0, tiles, n_ref, up_ref, down_ref, acc_ref)


def close_kernel(begin, acc_in, n_ref, up_ref, down_ref, out_ref, acc_ref):
    acc_ref[...] = acc_in[...]
    feed_forward(begin, tiles_of(up_ref), n_ref, up_ref, down_ref, acc_ref)
    out_ref[...] = acc_ref[...].astype(BF16)


def vmem():
    return pl.BlockSpec(memory_space=pltpu.VMEM)


def call(kernel, name, operands, docs, results, scratch, aliases=None, sent=()):
    inputs = [pltpu.with_memory_space_constraint(operand, pltpu.VMEM) for operand in operands]
    in_specs = [vmem()] * len(inputs)
    if docs is not None:
        inputs.append(docs)
        in_specs.append(pl.BlockSpec(memory_space=pltpu.SMEM))
    return pl.pallas_call(
        kernel,
        in_specs=in_specs,
        out_specs=[pl.BlockSpec(memory_space=pl.ANY) if i in sent else vmem() for i in range(len(results))],
        out_shape=[
            jax.ShapeDtypeStruct(*one) if i in sent else pltpu.VMEM(*one) for i, one in enumerate(results)
        ],
        scratch_shapes=scratch,
        input_output_aliases=aliases or {},
        compiler_params=pltpu.CompilerParams(vmem_limit_bytes=VMEM_BYTES),
        cost_estimate=COST,
        name=name,
    )(*inputs)


def own_part(x, gains, weights, docs):
    rows, width = x.shape
    results = [((rows, width), BF16), ((rows, width), F32), ((rows, LANES), F32)]
    scratch = [pltpu.VMEM((rows, width), BF16), pltpu.VMEM((3, rows, width), BF16)]
    return call(own_kernel, "own_part", (x, gains, weights[0], docs.own_column, docs.ids), docs.ids, results, scratch)


def piece_part(x, shift, gains, w_attn, q, num, den, docs):
    rows, width = q.shape
    keys = x.shape[0]
    return call(
        functools.partial(piece_kernel, shift, 0),
        "piece_part",
        (x, gains, w_attn, q, num, den, docs.own_column, docs.ids),
        docs.ids,
        [((rows, width), F32), ((rows, LANES), F32)],
        [pltpu.VMEM((keys, width), BF16), pltpu.VMEM((2, keys, width), BF16)],
        aliases={4: 0, 5: 1},
    )


def message_part(x, piece, gains, w_attn, docs):
    half, width = x.shape
    keys = 2 * half
    return call(
        message_kernel,
        "message_part",
        (x, piece, gains, w_attn, docs.later_column, docs.ids),
        docs.ids,
        [((half, width + LANES), BF16)],
        [pltpu.VMEM((1, half, width), BF16), pltpu.VMEM((keys, width), BF16), pltpu.VMEM((2, keys, width), BF16)]
        + [pltpu.VMEM((half, width), F32), pltpu.VMEM((half, LANES), F32)],
    )[0]


def finish_part(x, num, den, weights, gains, part):
    half, width = x.shape[0] // 2, x.shape[1]
    return call(
        functools.partial(finish_kernel, part * half),
        "finish_part",
        (x, num, den, weights[0], gains, *weights[1:]),
        None,
        [((half, width), BF16)],
        [pltpu.VMEM((half, width), F32), pltpu.VMEM((half, width), BF16), hidden_scratch(half, weights)],
    )[0]


def hidden_scratch(rows, weights):
    return pltpu.VMEM((2, rows, min(TILE, weights[1].shape[1])), BF16)


def reply_scratch(half, width):
    return [
        pltpu.VMEM((half, width), BF16),
        pltpu.VMEM((2, half, width), BF16),
        pltpu.VMEM((half, width), F32),
    ]


def again_part(message, state, done, x, weights, gains, docs):
    q, num, den = state
    half, width = done.shape
    return call(
        again_kernel,
        "again_part",
        (message, gains, weights[0], q, num, den, done, x, *weights[1:], docs.own_column, docs.ids),
        docs.ids,
        [(num.shape, F32), (den.shape, F32), ((half, width), BF16)],
        reply_scratch(half, width),
        aliases={4: 0, 5: 1, 6: 2},
    )


def last_part(message, state, done, x, weights, gains, docs):
    q, num, den = state
    half, width = done.shape
    operands = (message, gains, weights[0], q, num, den, done, x, *weights[1:], docs.own_column, docs.ids)
    kernel, aliases = last_kernel, {4: 0, 5: 1}
    if message is None:
        kernel, operands, aliases = functools.partial(last_kernel, None), operands[1:], {3: 0, 4: 1}
    return call(
        kernel,
        "last_part",
        operands,
        docs.ids,
        [(num.shape, F32), (den.shape, F32), (x.shape, BF16)],
        reply_scratch(half, width) + [
            pltpu.VMEM((2, half, width), BF16),
            hidden_scratch(half, weights),
            pltpu.SemaphoreType.DMA((2,)),
        ],
        aliases=aliases,
        sent=(2,),
    )[2]


def open_part(x, num, den, weights, gains, part, tiles):
    width = x.shape[1]
    rows = x.shape[0] // 2
    return call(
        functools.partial(open_kernel, part * rows, tiles),
        "open_part",
        (x, num, den, weights[0], gains, *weights[1:]),
        None,
        [((rows, width), F32), ((rows, width), BF16)],
        [],
    )


def close_part(acc, n, weights, tiles):
    return call(
        functools.partial(close_kernel, tiles),
        "close_part",
        (acc, n, *weights[1:]),
        None,
        [(acc.shape, BF16)],
        [pltpu.VMEM(acc.shape, F32)],
    )[0]


def shifted(value, axis, steps):
    count = lax.axis_size(axis)
    first, last = max(0, -steps), min(count, count - steps)
    return lax.ppermute(value, axis, [(i, i + steps) for i in range(first, last)])


def swapped(value, axis, bit):
    return lax.ppermute(value, axis, [(i, i ^ bit) for i in range(lax.axis_size(axis))])


class Documents:
    def __init__(self, doc_ids, rows):
        count = lax.axis_size("seq")
        self.ids, self.rows, self.half = doc_ids, rows, rows // 2
        longest = doc_ids.shape[1] // 2
        self.hops = min(count - 1, -(-(longest - 1) // rows))
        self.short = self.hops == 2 and longest <= 2 * rows and rows % 2 == 0
        place = lax.axis_index("seq")

        def column(later, size):
            start = jnp.minimum((place + later) * rows, doc_ids.shape[1] - size)
            ids = lax.dynamic_slice_in_dim(doc_ids, start, size, 1)
            return jnp.broadcast_to(ids.reshape(-1, 1), (size, LANES))

        self.own_column = column(0, rows)
        self.later_column = column(1, self.half) if self.short else self.own_column


def attention(x, state, piece, first_back, docs, gains, weights):
    q, *state = state
    w_attn = weights[0]
    if docs.short:
        message = message_part(after(first_back, q), piece, gains, w_attn, docs)
        state = after(state[0], message), state[1]
        message = shifted(message, "seq", 1)
        num, den = piece_part(piece, 1, gains, w_attn, q, *state, docs)
        done = finish_part(x, num, den, weights, gains, 1)
        return after(message, done), (q, num, den), done
    state = piece_part(piece, 1, gains, w_attn, q, *state, docs)
    for hop in range(2, docs.hops + 1):
        piece = shifted(piece, "seq", 1)
        state = piece_part(piece, hop, gains, w_attn, q, *state, docs)
    return None, (q, *state), finish_part(x, *state, weights, gains, 1)


def packed(row):
    high = lax.reduce_precision(row, 8, 7)
    low = lax.reduce_precision(row - high, 8, 7)
    place = lax.broadcasted_iota(jnp.int32, (CARRIED, row.shape[1]), 0)
    return jnp.where(place == 0, high, jnp.where(place == 1, low, 0.0)).astype(BF16)


def unpacked(rows):
    return rows[:1].astype(F32) + rows[1:2].astype(F32)


def after(value, *earlier):
    return lax.optimization_barrier((value, *earlier))[0]


def own_half(rows, odd):
    half = rows.shape[0] // 2
    return jnp.where(odd, rows[half:], rows[:half]), jnp.where(odd, rows[:half], rows[half:])


class Chain:
    def __init__(self, own_states, other_states, even_gain, odd_gain, bits, before=None):
        self.bits, self.odd, self.leading = bits, bits[1], bits[0]
        self.even_gain, self.odd_gain = even_gain, odd_gain
        self.levels = before.levels if before else []
        self.factor, self.factor_before = even_gain * odd_gain, jnp.ones_like(even_gain)
        even, odd = self.sorted(own_states, other_states)
        self.even_states = even
        behind = jnp.where(self.leading, 0.0, self.even_gain * even.astype(F32))
        self.known = self.odd_gain * (behind + odd.astype(F32))

    def sorted(self, mine, other):
        return jnp.where(self.odd, other, mine), jnp.where(self.odd, mine, other)

    def enter(self, fine, *earlier):
        fine = after(fine, *earlier)
        half = fine.shape[0] // 2
        mine, sent = own_half(fine, self.odd)
        other = swapped(sent, "depth", 1)
        self.fine_even, fine_odd = self.sorted(mine, other)
        self.total = self.odd_gain * self.fine_even.astype(F32) + fine_odd.astype(F32) - self.known
        self.before = jnp.zeros_like(self.total)

    def level(self, index, sent_after=(), used_after=()):
        bit, last = 2 << index, index + 1 == self.steps()
        upper, rows = self.bits[bit], self.total.shape[0]
        sent = self.total.astype(BF16)
        carries = index == len(self.levels) and not last
        if carries:
            sent = jnp.concatenate([sent, packed(self.factor)], axis=0)
        theirs = after(swapped(after(sent, *sent_after), "depth", bit), *used_after)
        if index == len(self.levels):
            their_factor = unpacked(theirs[rows:]) if carries else None
            self.levels.append((self.factor, their_factor, self.factor_before))
            if carries:
                self.factor_before = jnp.where(upper, self.factor_before * their_factor, self.factor_before)
                self.factor = self.factor * their_factor
        factor, their_factor, factor_before = self.levels[index]
        theirs = theirs[:rows].astype(F32)
        if not last:
            self.total = jnp.where(upper, factor * theirs + self.total, their_factor * self.total + theirs)
        self.before = jnp.where(upper, factor_before * theirs + self.before, self.before)

    def steps(self):
        return len(self.bits) - 2

    def leave(self, used_after=()):
        even_states = self.even_states.astype(F32)
        even = jnp.where(self.leading, even_states, self.before)
        odd = self.even_gain * (even - even_states) + self.fine_even.astype(F32)
        even, odd = even.astype(BF16), odd.astype(BF16)
        mine, sent = jnp.where(self.odd, odd, even), jnp.where(self.odd, even, odd)
        other = after(swapped(sent, "depth", 1), *used_after)
        low, high = self.sorted(mine, other)
        return jnp.concatenate([low, high], axis=0)


def on_device(interfaces, doc_ids, w_attn, w_up, w_down, norm_gains, coarse_gain):
    x = interfaces[0, 0]
    rows = x.shape[0]
    half = rows // 2
    gains = norm_gains[0, 0]
    weights = (w_attn[0, 0], w_up[0, 0], w_down[0, 0])
    parts = [x[:half], x[half:]]
    piece = shifted(x, "seq", 1)
    docs = Documents(doc_ids, rows)
    place, bits, bit = lax.axis_index("depth"), {}, 1
    while bit < lax.axis_size("depth"):
        bits[bit] = (place & bit) != 0
        bit *= 2
    bits[0] = place < 2
    early, bits, docs.own_column, docs.later_column = lax.optimization_barrier(
        (x, bits, docs.own_column, docs.later_column)
    )
    first_back = shifted(after(parts[0], docs.own_column), "seq", -1)
    state = own_part(early, gains, weights, docs)
    kept, sent = zip(*[own_half(part, bits[1]) for part in parts])
    sent = jnp.concatenate([*after(sent, state[0]), packed(coarse_gain)], axis=0)
    other = swapped(sent, "depth", 1)
    message, state, done = attention(early, state, piece, first_back, docs, gains, weights)
    other_gain = unpacked(other[half:])
    pair = jnp.where(bits[1], other_gain, coarse_gain), jnp.where(bits[1], coarse_gain, other_gain)
    first = Chain(kept[1], other[half // 2 : half], *pair, bits)
    second = Chain(kept[0], other[: half // 2], *pair, bits, first)
    _, num, den = state
    if message is not None:
        message = after(message, first.known, second.known)
        num, den, done = again_part(message, state, done, early, weights, gains, docs)
    first.enter(done)
    tiles = weights[1].shape[1] // TILE // 2
    acc, n = open_part(early, after(num, first.total), den, weights, gains, 0, tiles)
    first.level(0, used_after=(n,))
    fine = close_part(after(acc, first.total), n, weights, tiles)
    first.level(1, used_after=(fine,))
    second.enter(fine, first.before)
    for i in range(2, first.steps()):
        second.level(i - 2)
        first.level(i)
    late = first.leave()
    late_piece = shifted(late, "seq", 1)
    for i in range(max(0, first.steps() - 2), first.steps()):
        last = i + 1 == first.steps()
        second.level(i, (late,) if i > 0 else (), (late_piece,) if last else ())
    soon = second.leave()
    piece = jnp.concatenate([shifted(soon, "seq", 1), late_piece], axis=0)
    x = jnp.concatenate([soon, late], axis=0)
    first_back = shifted(after(soon, x), "seq", -1)
    state = own_part(x, gains, weights, docs)
    message, state, done = attention(x, state, piece, first_back, docs, gains, weights)
    return last_part(message, state, done, x, weights, gains, docs)[None, None]


def solution(mesh):
    in_specs = (
        P("depth", None, "seq", None),
        P(),
        P("depth", None, None, None, None),
        P("depth", None, None, None),
        P("depth", None, None, None),
        P("depth", None, None, None),
        P("depth", None),
    )
    out_specs = P("depth", None, "seq", None)
    return jax.shard_map(
        on_device, mesh=mesh, in_specs=in_specs, out_specs=out_specs, check_vma=False
    )
```

```python
import functools

import jax
import jax.numpy as jnp
from jax import lax
from jax.experimental import pallas as pl
from jax.experimental.pallas import tpu as pltpu
from jax.sharding import PartitionSpec as P

HEADS = 16
LANES = 128
CARRIED = 16
BLOCK = 256
TILE = 512
TILES = 8
VMEM_BYTES = 8 * 1024 * 1024
COST = pl.CostEstimate(flops=1 << 20, bytes_accessed=1 << 16, transcendentals=0)
F32 = jnp.float32
BF16 = jnp.bfloat16


def rms_norm(value, gain):
    return value * lax.rsqrt(jnp.mean(value * value, axis=-1, keepdims=True) + 1e-05) * gain


def dot(a, b):
    return jnp.dot(a, b, preferred_element_type=F32)


def attend(q_ref, k_ref, v_ref, num_ref, den_ref, column_ref, row_ref, doc_ref, q_at, k_at, causal=False):
    rows, width = q_ref.shape
    keys = k_ref.shape[0]
    head_dim = width // HEADS
    per_tile = LANES // head_dim
    q_block, k_block = min(BLOCK, rows), min(BLOCK, keys)
    lane = lax.broadcasted_iota(jnp.int32, (1, LANES), 1)
    members = [lane // head_dim == i for i in range(per_tile)]
    count_q, count_k = rows // q_block, keys // k_block

    def one(index, carry):
        qi, ki = index // count_k, index % count_k
        q0 = pl.multiple_of(qi * q_block, q_block)
        k0 = pl.multiple_of(ki * k_block, k_block)
        needed = doc_ref[0, k_at + k0 + k_block - 1] >= doc_ref[0, q_at + q0]
        if causal:
            needed = (k0 <= q0) & (needed | (k0 == q0))

        @pl.when(needed)
        def _():
            key_docs = row_ref[:, pl.ds(pl.multiple_of(k_at + k0, k_block), k_block)]
            allowed = column_ref[pl.ds(q0, q_block), :1] == key_docs
            if causal:
                q_pos = q0 + lax.broadcasted_iota(jnp.int32, (q_block, k_block), 0)
                k_pos = k0 + lax.broadcasted_iota(jnp.int32, (q_block, k_block), 1)
                allowed = allowed & (k_pos <= q_pos)
            ones = jnp.ones((k_block, LANES), BF16)

            def heads(tile, den):
                cols = pl.ds(pl.multiple_of(tile * LANES, LANES), LANES)
                queries = q_ref[pl.ds(q0, q_block), cols]
                keys_here = k_ref[pl.ds(k0, k_block), cols]
                values = jnp.concatenate([v_ref[pl.ds(k0, k_block), cols], ones], axis=1)
                num = None
                for i, member in enumerate(members):
                    scores = lax.dot_general(
                        jnp.where(member, queries, jnp.zeros_like(queries)),
                        keys_here,
                        (((1,), (1,)), ((), ())),
                        preferred_element_type=F32,
                    )
                    weights = jnp.where(allowed, jnp.exp(scores), 0.0).astype(BF16)
                    out = dot(weights, values)
                    num = out[:, :LANES] if num is None else jnp.where(member, out[:, :LANES], num)
                    den = jnp.where(lane == tile * per_tile + i, out[:, LANES:], den)
                num_ref[pl.ds(q0, q_block), cols] += num
                return den

            def some(step, den):
                for i in range(TILES):
                    den = heads(step * TILES + i, den)
                return den

            den = jnp.zeros((q_block, LANES), F32)
            den_ref[pl.ds(q0, q_block), :] += lax.fori_loop(0, width // LANES // TILES, some, den, unroll=True)

        return carry

    lax.fori_loop(0, count_q * count_k, one, 0)


def spread(per_head, width):
    shape = (LANES, width)
    chosen = lax.broadcasted_iota(jnp.int32, shape, 1) // (width // HEADS) == lax.broadcasted_iota(jnp.int32, shape, 0)
    chosen = jnp.where(chosen, 1.0, 0.0).astype(BF16)
    high = per_head.astype(BF16)
    return dot(high, chosen) + dot((per_head - high.astype(F32)).astype(BF16), chosen)


def normed(x_ref, gain_ref):
    return rms_norm(x_ref[...].astype(F32), gain_ref[0:1]).astype(BF16)


def project(n_ref, w_ref, first, out_ref):
    count, _, width = out_ref.shape
    tile = min(TILE, width)
    steps = width // tile

    def one(step, carry):
        i, j = step // steps, step % steps
        cols = pl.ds(pl.multiple_of(j * tile, tile), tile)
        out = dot(n_ref[...], w_ref[first + i, :, cols]).astype(BF16)
        if first == 0:
            out *= jnp.where(i == 0, (width // HEADS) ** (-0.5), 1.0).astype(BF16)
        out_ref[i, :, cols] = out
        return carry

    lax.fori_loop(0, count * steps, one, 0)


def own_kernel(x_ref, gain_ref, w_ref, column_ref, row_ref, doc_ref, q_ref, num_ref, den_ref, n_ref, qkv_ref):
    here = lax.axis_index("seq") * x_ref.shape[0]
    n_ref[...] = normed(x_ref, gain_ref)
    project(n_ref, w_ref, 0, qkv_ref)
    q_ref[...] = qkv_ref[0]
    num_ref[...] = jnp.zeros_like(num_ref)
    den_ref[...] = jnp.zeros_like(den_ref)
    k_ref, v_ref = qkv_ref.at[1], qkv_ref.at[2]
    attend(q_ref, k_ref, v_ref, num_ref, den_ref, column_ref, row_ref, doc_ref, here, here, True)


def keys_kernel(x_ref, gain_ref, w_ref, doc_ref, kv_ref, n_ref):
    half = x_ref.shape[0]
    here = lax.axis_index("seq") * 2 * half

    @pl.when((here > 0) & (doc_ref[0, jnp.maximum(here - 1, 0)] >= doc_ref[0, here]))
    def _():
        n_ref[...] = normed(x_ref, gain_ref)
        project(n_ref, w_ref, 1, kv_ref.at[:, half:])


def fill_keys(ready, x_ref, gain_ref, w_ref, n_ref, kv_ref):
    rows = x_ref.shape[0] // 2 if ready else x_ref.shape[0]
    n_ref[:rows] = rms_norm(x_ref[:rows].astype(F32), gain_ref[0:1]).astype(BF16)
    project(n_ref.at[:rows], w_ref, 1, kv_ref.at[:, :rows])


def message_place(doc_ref, rows):
    place, count = lax.axis_index("seq"), lax.axis_size("seq")
    inside = (place >= 1) & (place + 1 < count)
    here = jnp.where(inside, place + 1, 0) * rows
    there = jnp.where(inside, place - 1, 0) * rows
    return here, there, inside & (doc_ref[0, there + rows - 1] >= doc_ref[0, here])


def piece_kernel(
    ready, shift, x_ref, gain_ref, w_ref, q_ref, num_in, den_in, kv_in, column_ref, row_ref, doc_ref,
    num_ref, den_ref, kv_ref, n_ref,
):
    del num_in, den_in, kv_in
    rows, keys = q_ref.shape[0], x_ref.shape[0]
    shard = lax.axis_index("seq") - shift
    here, there = (shard + shift) * rows, jnp.maximum(shard, 0) * rows + rows - keys

    @pl.when((shard >= 0) & (doc_ref[0, there + keys - 1] >= doc_ref[0, here]))
    def _():
        if ready is None:
            fill_keys(False, x_ref, gain_ref, w_ref, n_ref, kv_ref)
        else:
            far = far_document(doc_ref, rows, lax.axis_size("seq"))

            @pl.when(jnp.logical_not(far & message_place(doc_ref, rows)[2]))
            def _():
                fill_keys(ready, x_ref, gain_ref, w_ref, n_ref, kv_ref)

        attend(q_ref, kv_ref.at[0], kv_ref.at[1], num_ref, den_ref, column_ref, row_ref, doc_ref, here, there)


def far_document(doc_ref, rows, count):
    found = False
    for middle in range(1, count - 1):
        over = doc_ref[0, middle * rows - 1] == doc_ref[0, (middle + 1) * rows]
        deep = doc_ref[0, middle * rows - rows // 2 - 1] == doc_ref[0, (middle + 1) * rows]
        found = found | (over & deep)
    return found


def message_kernel(
    ready, x_ref, piece_ref, gain_ref, w_ref, kv_in, column_ref, row_ref, doc_ref,
    out_ref, kv_ref, q_ref, n_ref, num_ref, den_ref,
):
    del kv_in
    half, width = x_ref.shape
    here, there, needed = message_place(doc_ref, 2 * half)
    far = far_document(doc_ref, 2 * half, lax.axis_size("seq"))

    @pl.when(jnp.logical_not(far))
    def _():
        out_ref[:, :width] = piece_ref[half:]

    @pl.when(far)
    def _():
        num_ref[...] = jnp.zeros_like(num_ref)
        den_ref[...] = jnp.zeros_like(den_ref)

        @pl.when(needed)
        def _():
            n_ref[:half] = normed(x_ref, gain_ref)
            project(n_ref.at[:half], w_ref, 0, q_ref)
            fill_keys(ready, piece_ref, gain_ref, w_ref, n_ref, kv_ref)
            attend(
                q_ref.at[0], kv_ref.at[0], kv_ref.at[1], num_ref, den_ref, column_ref, row_ref, doc_ref, here, there
            )

        out_ref[:, :width] = num_ref[...].astype(BF16)
        out_ref[:, width:] = den_ref[...].astype(BF16)


def reply_kernel(
    message_ref, gain_ref, w_ref, q_ref, num_in, den_in, column_ref, row_ref, doc_ref,
    num_ref, den_ref, n_ref, kv_ref,
):
    rows, width = q_ref.shape
    half = message_ref.shape[0]
    far = far_document(doc_ref, rows, lax.axis_size("seq"))

    @pl.when(far)
    def _():
        num_ref[:half] += message_ref[:, :width].astype(F32)
        den_ref[:half] += message_ref[:, width:].astype(F32)

    @pl.when(jnp.logical_not(far))
    def _():
        piece_kernel(
            None, 2, message_ref.at[:, :width], gain_ref, w_ref, q_ref, num_in, den_in, None, column_ref, row_ref, doc_ref,
            num_ref, den_ref, kv_ref, n_ref,
        )


def mix(first, x_ref, num_ref, den_ref, w_ref, gain_ref, acc_ref, n_ref):
    rows, width = acc_ref.shape
    here = pl.ds(first, rows)
    lane = lax.broadcasted_iota(jnp.int32, (rows, LANES), 1)
    inverse = 1.0 / jnp.where(lane < HEADS, den_ref[here], 1.0)
    n_ref[...] = (num_ref[here] * spread(inverse, width)).astype(BF16)
    tile = min(TILE, width)

    def one(j, carry):
        cols = pl.ds(pl.multiple_of(j * tile, tile), tile)
        acc_ref[:, cols] = x_ref[here, cols].astype(F32) + dot(n_ref[...], w_ref[3, :, cols])
        return carry

    lax.fori_loop(0, width // tile, one, 0)
    n_ref[...] = rms_norm(acc_ref[...], gain_ref[1:2]).astype(BF16)


def feed_forward(begin, end, n_ref, up_ref, down_ref, acc_ref):
    tile = min(TILE, up_ref.shape[1])

    def one(j, carry):
        units = pl.ds(pl.multiple_of(j * tile, tile), tile)
        expanded = jax.nn.gelu(dot(n_ref[...], up_ref[:, units])).astype(BF16)
        acc_ref[...] += dot(expanded, down_ref[units])
        return carry

    lax.fori_loop(begin, end, one, 0)


def feed_forward_ahead(n_ref, up_ref, down_ref, acc_ref, hidden_ref):
    tile = hidden_ref.shape[2]
    last = up_ref.shape[1] // tile - 1

    def expand(j):
        units = pl.ds(pl.multiple_of(j * tile, tile), tile)
        hidden_ref[j % 2] = jax.nn.gelu(dot(n_ref[...], up_ref[:, units])).astype(BF16)

    def lower(j):
        acc_ref[...] += dot(hidden_ref[j % 2], down_ref[pl.ds(pl.multiple_of(j * tile, tile), tile)])

    def one(j, carry):
        lower(j)
        expand(j + 1)
        return carry

    expand(0)
    lax.fori_loop(0, last, one, 0)
    lower(last)


def tiles_of(up_ref):
    return up_ref.shape[1] // min(TILE, up_ref.shape[1])


def finish_kernel(
    first, x_ref, num_ref, den_ref, w_ref, gain_ref, up_ref, down_ref, out_ref, acc_ref, n_ref, hidden_ref=None
):
    mix(first, x_ref, num_ref, den_ref, w_ref, gain_ref, acc_ref, n_ref)
    if hidden_ref is None:
        feed_forward(0, tiles_of(up_ref), n_ref, up_ref, down_ref, acc_ref)
    else:
        feed_forward_ahead(n_ref, up_ref, down_ref, acc_ref, hidden_ref)
    out_ref[...] = acc_ref[...].astype(BF16)


def seen_by_second_half(doc_ref, rows):
    place = lax.axis_index("seq")
    before = jnp.maximum((place - 1) * rows - 1, 0)
    return (place >= 2) & (doc_ref[0, before] == doc_ref[0, place * rows + rows // 2])


def again_kernel(
    message_ref, gain_ref, w_ref, q_ref, num_in, den_in, done_in, x_ref, up_ref, down_ref, column_ref, row_ref, doc_ref,
    num_ref, den_ref, done_ref, n_ref, kv_ref, acc_ref,
):
    del done_in
    half = done_ref.shape[0]
    reply_kernel(
        message_ref, gain_ref, w_ref, q_ref, num_in, den_in, column_ref, row_ref, doc_ref,
        num_ref, den_ref, n_ref, kv_ref,
    )

    @pl.when(seen_by_second_half(doc_ref, 2 * half))
    def _():
        finish_kernel(half, x_ref, num_ref, den_ref, w_ref, gain_ref, up_ref, down_ref, done_ref, acc_ref, n_ref)


def last_kernel(
    message_ref, gain_ref, w_ref, q_ref, num_in, den_in, done_ref, x_ref, up_ref, down_ref, column_ref, row_ref, doc_ref,
    num_ref, den_ref, out_ref, n_ref, kv_ref, acc_ref, result_ref, hidden_ref, sems,
):
    half = done_ref.shape[0]
    again = seen_by_second_half(doc_ref, 2 * half) if message_ref is not None else False
    halves = [out_ref.at[:half], out_ref.at[half:]]
    as_it_was = pltpu.make_async_copy(done_ref, halves[1], sems.at[1])
    copies = [pltpu.make_async_copy(result_ref.at[i], halves[i], sems.at[i]) for i in range(2)]

    @pl.when(jnp.logical_not(again))
    def _():
        as_it_was.start()

    if message_ref is not None:
        reply_kernel(
            message_ref, gain_ref, w_ref, q_ref, num_in, den_in, column_ref, row_ref, doc_ref,
            num_ref, den_ref, n_ref, kv_ref,
        )

    def one(part, carry):
        @pl.when((part == 0) | again)
        def _():
            first = pl.multiple_of(part * half, half)
            finish_kernel(
                first, x_ref, num_ref, den_ref, w_ref, gain_ref, up_ref, down_ref, result_ref.at[part], acc_ref, n_ref,
                hidden_ref,
            )

        return carry

    lax.fori_loop(0, 2, one, 0)
    copies[0].start()

    @pl.when(again)
    def _():
        copies[1].start()
        copies[1].wait()

    @pl.when(jnp.logical_not(again))
    def _():
        as_it_was.wait()

    copies[0].wait()


def open_kernel(first, tiles, x_ref, num_ref, den_ref, w_ref, gain_ref, up_ref, down_ref, acc_ref, n_ref):
    mix(first, x_ref, num_ref, den_ref, w_ref, gain_ref, acc_ref, n_ref)
    feed_forward(0, tiles, n_ref, up_ref, down_ref, acc_ref)


def close_kernel(begin, acc_in, n_ref, up_ref, down_ref, out_ref, acc_ref):
    acc_ref[...] = acc_in[...]
    feed_forward(begin, tiles_of(up_ref), n_ref, up_ref, down_ref, acc_ref)
    out_ref[...] = acc_ref[...].astype(BF16)


def vmem():
    return pl.BlockSpec(memory_space=pltpu.VMEM)


def call(kernel, name, operands, docs, results, scratch, aliases=None, sent=()):
    inputs = [pltpu.with_memory_space_constraint(operand, pltpu.VMEM) for operand in operands]
    in_specs = [vmem()] * len(inputs)
    if docs is not None:
        inputs.append(docs)
        in_specs.append(pl.BlockSpec(memory_space=pltpu.SMEM))
    return pl.pallas_call(
        kernel,
        in_specs=in_specs,
        out_specs=[pl.BlockSpec(memory_space=pl.ANY) if i in sent else vmem() for i in range(len(results))],
        out_shape=[
            jax.ShapeDtypeStruct(*one) if i in sent else pltpu.VMEM(*one) for i, one in enumerate(results)
        ],
        scratch_shapes=scratch,
        input_output_aliases=aliases or {},
        compiler_params=pltpu.CompilerParams(vmem_limit_bytes=VMEM_BYTES),
        cost_estimate=COST,
        name=name,
    )(*inputs)


def own_part(x, gains, weights, docs):
    rows, width = x.shape
    results = [((rows, width), BF16), ((rows, width), F32), ((rows, LANES), F32)]
    scratch = [pltpu.VMEM((rows, width), BF16), pltpu.VMEM((3, rows, width), BF16)]
    return call(own_kernel, "own_part", (x, gains, weights[0], docs.own_column, docs.ids), docs.ids, results, scratch)


def keys_part(x, gains, w_attn, docs):
    half, width = x.shape
    return call(
        keys_kernel,
        "keys_part",
        (x, gains, w_attn),
        docs.ids,
        [((2, 2 * half, width), BF16)],
        [pltpu.VMEM((half, width), BF16)],
    )[0]


def piece_part(x, shift, ready, gains, w_attn, q, num, den, kv, docs):
    rows, width = q.shape
    return call(
        functools.partial(piece_kernel, ready, shift),
        "piece_part",
        (x, gains, w_attn, q, num, den, kv, docs.own_column, docs.ids),
        docs.ids,
        [((rows, width), F32), ((rows, LANES), F32), (kv.shape, BF16)],
        [pltpu.VMEM(x.shape, BF16)],
        aliases={4: 0, 5: 1, 6: 2},
    )


def message_part(x, piece, ready, gains, w_attn, kv, docs):
    half, width = x.shape
    return call(
        functools.partial(message_kernel, ready),
        "message_part",
        (x, piece, gains, w_attn, kv, docs.later_column, docs.ids),
        docs.ids,
        [((half, width + LANES), BF16), (kv.shape, BF16)],
        [
            pltpu.VMEM((1, half, width), BF16),
            pltpu.VMEM(piece.shape, BF16),
            pltpu.VMEM((half, width), F32),
            pltpu.VMEM((half, LANES), F32),
        ],
        aliases={4: 1},
    )


def finish_part(x, num, den, weights, gains, part):
    half, width = x.shape[0] // 2, x.shape[1]
    return call(
        functools.partial(finish_kernel, part * half),
        "finish_part",
        (x, num, den, weights[0], gains, *weights[1:]),
        None,
        [((half, width), BF16)],
        [pltpu.VMEM((half, width), F32), pltpu.VMEM((half, width), BF16), hidden_scratch(half, weights)],
    )[0]


def hidden_scratch(rows, weights):
    return pltpu.VMEM((2, rows, min(TILE, weights[1].shape[1])), BF16)


def reply_scratch(half, width):
    return [
        pltpu.VMEM((half, width), BF16),
        pltpu.VMEM((2, half, width), BF16),
        pltpu.VMEM((half, width), F32),
    ]


def again_part(message, state, done, x, weights, gains, docs):
    q, num, den = state
    half, width = done.shape
    return call(
        again_kernel,
        "again_part",
        (message, gains, weights[0], q, num, den, done, x, *weights[1:], docs.own_column, docs.ids),
        docs.ids,
        [(num.shape, F32), (den.shape, F32), ((half, width), BF16)],
        reply_scratch(half, width),
        aliases={4: 0, 5: 1, 6: 2},
    )


def last_part(message, state, done, x, weights, gains, docs):
    q, num, den = state
    half, width = done.shape
    operands = (message, gains, weights[0], q, num, den, done, x, *weights[1:], docs.own_column, docs.ids)
    kernel, aliases = last_kernel, {4: 0, 5: 1}
    if message is None:
        kernel, operands, aliases = functools.partial(last_kernel, None), operands[1:], {3: 0, 4: 1}
    return call(
        kernel,
        "last_part",
        operands,
        docs.ids,
        [(num.shape, F32), (den.shape, F32), (x.shape, BF16)],
        reply_scratch(half, width) + [
            pltpu.VMEM((2, half, width), BF16),
            hidden_scratch(half, weights),
            pltpu.SemaphoreType.DMA((2,)),
        ],
        aliases=aliases,
        sent=(2,),
    )[2]


def open_part(x, num, den, weights, gains, part, tiles):
    width = x.shape[1]
    rows = x.shape[0] // 2
    return call(
        functools.partial(open_kernel, part * rows, tiles),
        "open_part",
        (x, num, den, weights[0], gains, *weights[1:]),
        None,
        [((rows, width), F32), ((rows, width), BF16)],
        [],
    )


def close_part(acc, n, weights, tiles):
    return call(
        functools.partial(close_kernel, tiles),
        "close_part",
        (acc, n, *weights[1:]),
        None,
        [(acc.shape, BF16)],
        [pltpu.VMEM(acc.shape, F32)],
    )[0]


def shifted(value, axis, steps):
    count = lax.axis_size(axis)
    first, last = max(0, -steps), min(count, count - steps)
    return lax.ppermute(value, axis, [(i, i + steps) for i in range(first, last)])


def swapped(value, axis, bit):
    return lax.ppermute(value, axis, [(i, i ^ bit) for i in range(lax.axis_size(axis))])


class Documents:
    def __init__(self, doc_ids, rows):
        count = lax.axis_size("seq")
        self.ids, self.rows, self.half = doc_ids, rows, rows // 2
        longest = doc_ids.shape[1] // 2
        self.hops = min(count - 1, -(-(longest - 1) // rows))
        self.short = self.hops == 2 and longest <= 2 * rows and rows % 2 == 0
        place = lax.axis_index("seq")

        def column(later, size):
            start = jnp.minimum((place + later) * rows, doc_ids.shape[1] - size)
            ids = lax.dynamic_slice_in_dim(doc_ids, start, size, 1)
            return jnp.broadcast_to(ids.reshape(-1, 1), (size, LANES))

        self.own_column = column(0, rows)
        self.later_column = column(1, self.half) if self.short else self.own_column


def attention(x, state, piece, first_back, docs, gains, weights, kv=None):
    q, num, den = state
    w_attn = weights[0]
    ready = kv is not None
    if not ready:
        kv = jnp.zeros((2, *piece.shape), BF16)
    if docs.short:
        message, kv = message_part(after(first_back, q), piece, ready, gains, w_attn, kv, docs)
        num = after(num, message)
        message = shifted(message, "seq", 1)
        num, den, _ = piece_part(piece, 1, ready, gains, w_attn, q, num, den, kv, docs)
        done = finish_part(x, num, den, weights, gains, 1)
        return after(message, done), (q, num, den), done
    for hop in range(1, docs.hops + 1):
        num, den, kv = piece_part(piece, hop, None, gains, w_attn, q, num, den, kv, docs)
        piece = shifted(piece, "seq", 1)
    return None, (q, num, den), finish_part(x, num, den, weights, gains, 1)


def packed(row):
    high = lax.reduce_precision(row, 8, 7)
    low = lax.reduce_precision(row - high, 8, 7)
    place = lax.broadcasted_iota(jnp.int32, (CARRIED, row.shape[1]), 0)
    return jnp.where(place == 0, high, jnp.where(place == 1, low, 0.0)).astype(BF16)


def unpacked(rows):
    return rows[:1].astype(F32) + rows[1:2].astype(F32)


def after(value, *earlier):
    return lax.optimization_barrier((value, *earlier))[0]


def own_half(rows, odd):
    half = rows.shape[0] // 2
    return jnp.where(odd, rows[half:], rows[:half]), jnp.where(odd, rows[:half], rows[half:])


class Chain:
    def __init__(self, own_states, other_states, even_gain, odd_gain, bits, before=None):
        self.bits, self.odd, self.leading = bits, bits[1], bits[0]
        self.even_gain, self.odd_gain = even_gain, odd_gain
        self.levels = before.levels if before else []
        self.factor, self.factor_before = even_gain * odd_gain, jnp.ones_like(even_gain)
        even, odd = self.sorted(own_states, other_states)
        self.even_states = even
        behind = jnp.where(self.leading, 0.0, self.even_gain * even.astype(F32))
        self.known = self.odd_gain * (behind + odd.astype(F32))

    def sorted(self, mine, other):
        return jnp.where(self.odd, other, mine), jnp.where(self.odd, mine, other)

    def enter(self, fine, *earlier):
        fine = after(fine, *earlier)
        half = fine.shape[0] // 2
        mine, sent = own_half(fine, self.odd)
        other = swapped(sent, "depth", 1)
        self.fine_even, fine_odd = self.sorted(mine, other)
        self.total = self.odd_gain * self.fine_even.astype(F32) + fine_odd.astype(F32) - self.known
        self.before = jnp.zeros_like(self.total)

    def level(self, index, sent_after=(), used_after=()):
        bit, last = 2 << index, index + 1 == self.steps()
        upper, rows = self.bits[bit], self.total.shape[0]
        sent = self.total.astype(BF16)
        carries = index == len(self.levels) and not last
        if carries:
            sent = jnp.concatenate([sent, packed(self.factor)], axis=0)
        theirs = after(swapped(after(sent, *sent_after), "depth", bit), *used_after)
        if index == len(self.levels):
            their_factor = unpacked(theirs[rows:]) if carries else None
            self.levels.append((self.factor, their_factor, self.factor_before))
            if carries:
                self.factor_before = jnp.where(upper, self.factor_before * their_factor, self.factor_before)
                self.factor = self.factor * their_factor
        factor, their_factor, factor_before = self.levels[index]
        theirs = theirs[:rows].astype(F32)
        if not last:
            self.total = jnp.where(upper, factor * theirs + self.total, their_factor * self.total + theirs)
        self.before = jnp.where(upper, factor_before * theirs + self.before, self.before)

    def steps(self):
        return len(self.bits) - 2

    def leave(self, used_after=()):
        even_states = self.even_states.astype(F32)
        even = jnp.where(self.leading, even_states, self.before)
        odd = self.even_gain * (even - even_states) + self.fine_even.astype(F32)
        even, odd = even.astype(BF16), odd.astype(BF16)
        mine, sent = jnp.where(self.odd, odd, even), jnp.where(self.odd, even, odd)
        other = after(swapped(sent, "depth", 1), *used_after)
        low, high = self.sorted(mine, other)
        return jnp.concatenate([low, high], axis=0)


def on_device(interfaces, doc_ids, w_attn, w_up, w_down, norm_gains, coarse_gain):
    x = interfaces[0, 0]
    rows = x.shape[0]
    half = rows // 2
    gains = norm_gains[0, 0]
    weights = (w_attn[0, 0], w_up[0, 0], w_down[0, 0])
    parts = [x[:half], x[half:]]
    piece = shifted(x, "seq", 1)
    docs = Documents(doc_ids, rows)
    place, bits, bit = lax.axis_index("depth"), {}, 1
    while bit < lax.axis_size("depth"):
        bits[bit] = (place & bit) != 0
        bit *= 2
    bits[0] = place < 2
    early, bits, docs.own_column, docs.later_column = lax.optimization_barrier(
        (x, bits, docs.own_column, docs.later_column)
    )
    first_back = shifted(after(parts[0], docs.own_column), "seq", -1)
    state = own_part(early, gains, weights, docs)
    kept, sent = zip(*[own_half(part, bits[1]) for part in parts])
    sent = jnp.concatenate([*after(sent, state[0]), packed(coarse_gain)], axis=0)
    other = swapped(sent, "depth", 1)
    message, state, done = attention(early, state, piece, first_back, docs, gains, weights)
    other_gain = unpacked(other[half:])
    pair = jnp.where(bits[1], other_gain, coarse_gain), jnp.where(bits[1], coarse_gain, other_gain)
    first = Chain(kept[1], other[half // 2 : half], *pair, bits)
    second = Chain(kept[0], other[: half // 2], *pair, bits, first)
    _, num, den = state
    if message is not None:
        message = after(message, first.known, second.known)
        num, den, done = again_part(message, state, done, early, weights, gains, docs)
    first.enter(done)
    tiles = weights[1].shape[1] // TILE // 2
    acc, n = open_part(early, after(num, first.total), den, weights, gains, 0, tiles)
    first.level(0, used_after=(n,))
    fine = close_part(after(acc, first.total), n, weights, tiles)
    first.level(1, used_after=(fine,))
    second.enter(fine, first.before)
    for i in range(2, first.steps()):
        second.level(i - 2)
        first.level(i)
    late = first.leave()
    late_piece = shifted(late, "seq", 1)
    for i in range(max(0, first.steps() - 2), first.steps()):
        last = i + 1 == first.steps()
        second.level(i, (late,) if i > 0 else (), (late_piece,) if last else ())
    soon = second.leave()
    piece = jnp.concatenate([shifted(soon, "seq", 1), late_piece], axis=0)
    x = jnp.concatenate([soon, late], axis=0)
    first_back = shifted(after(soon, x), "seq", -1)
    state = own_part(x, gains, weights, docs)
    kv = keys_part(after(late_piece, state[0]), gains, weights[0], docs) if docs.short else None
    message, state, done = attention(x, state, piece, first_back, docs, gains, weights, kv)
    return last_part(message, state, done, x, weights, gains, docs)[None, None]


def solution(mesh):
    in_specs = (
        P("depth", None, "seq", None),
        P(),
        P("depth", None, None, None, None),
        P("depth", None, None, None),
        P("depth", None, None, None),
        P("depth", None, None, None),
        P("depth", None),
    )
    out_specs = P("depth", None, "seq", None)
    return jax.shard_map(
        on_device, mesh=mesh, in_specs=in_specs, out_specs=out_specs, check_vma=False
    )
```

```python
import functools

import jax
import jax.numpy as jnp
from jax import lax
from jax.experimental import pallas as pl
from jax.experimental.pallas import tpu as pltpu
from jax.sharding import PartitionSpec as P

HEADS = 16
LANES = 128
CARRIED = 16
BLOCK = 256
TILE = 512
TILES = 8
VMEM_BYTES = 8 * 1024 * 1024
COST = pl.CostEstimate(flops=1 << 20, bytes_accessed=1 << 16, transcendentals=0)
F32 = jnp.float32
BF16 = jnp.bfloat16


def rms_norm(value, gain):
    return value * lax.rsqrt(jnp.mean(value * value, axis=-1, keepdims=True) + 1e-05) * gain


def dot(a, b):
    return jnp.dot(a, b, preferred_element_type=F32)


def attend(q_ref, k_ref, v_ref, num_ref, den_ref, column_ref, row_ref, doc_ref, q_at, k_at, causal=False):
    rows, width = q_ref.shape
    keys = k_ref.shape[0]
    head_dim = width // HEADS
    per_tile = LANES // head_dim
    q_block, k_block = min(BLOCK, rows), min(BLOCK, keys)
    lane = lax.broadcasted_iota(jnp.int32, (1, LANES), 1)
    members = [lane // head_dim == i for i in range(per_tile)]
    count_q, count_k = rows // q_block, keys // k_block

    def one(index, carry):
        qi, ki = index // count_k, index % count_k
        q0 = pl.multiple_of(qi * q_block, q_block)
        k0 = pl.multiple_of(ki * k_block, k_block)
        needed = doc_ref[0, k_at + k0 + k_block - 1] >= doc_ref[0, q_at + q0]
        if causal:
            needed = (k0 <= q0) & (needed | (k0 == q0))

        @pl.when(needed)
        def _():
            key_docs = row_ref[:, pl.ds(pl.multiple_of(k_at + k0, k_block), k_block)]
            allowed = column_ref[pl.ds(q0, q_block), :1] == key_docs
            if causal:
                q_pos = q0 + lax.broadcasted_iota(jnp.int32, (q_block, k_block), 0)
                k_pos = k0 + lax.broadcasted_iota(jnp.int32, (q_block, k_block), 1)
                allowed = allowed & (k_pos <= q_pos)
            ones = jnp.ones((k_block, LANES), BF16)

            def heads(tile, den):
                cols = pl.ds(pl.multiple_of(tile * LANES, LANES), LANES)
                queries = q_ref[pl.ds(q0, q_block), cols]
                keys_here = k_ref[pl.ds(k0, k_block), cols]
                values = jnp.concatenate([v_ref[pl.ds(k0, k_block), cols], ones], axis=1)
                num = None
                for i, member in enumerate(members):
                    scores = lax.dot_general(
                        jnp.where(member, queries, jnp.zeros_like(queries)),
                        keys_here,
                        (((1,), (1,)), ((), ())),
                        preferred_element_type=F32,
                    )
                    weights = jnp.where(allowed, jnp.exp(scores), 0.0).astype(BF16)
                    out = dot(weights, values)
                    num = out[:, :LANES] if num is None else jnp.where(member, out[:, :LANES], num)
                    den = jnp.where(lane == tile * per_tile + i, out[:, LANES:], den)
                num_ref[pl.ds(q0, q_block), cols] += num
                return den

            def some(step, den):
                for i in range(TILES):
                    den = heads(step * TILES + i, den)
                return den

            den = jnp.zeros((q_block, LANES), F32)
            den_ref[pl.ds(q0, q_block), :] += lax.fori_loop(0, width // LANES // TILES, some, den, unroll=True)

        return carry

    lax.fori_loop(0, count_q * count_k, one, 0)


def spread(per_head, width):
    shape = (LANES, width)
    chosen = lax.broadcasted_iota(jnp.int32, shape, 1) // (width // HEADS) == lax.broadcasted_iota(jnp.int32, shape, 0)
    chosen = jnp.where(chosen, 1.0, 0.0).astype(BF16)
    high = per_head.astype(BF16)
    return dot(high, chosen) + dot((per_head - high.astype(F32)).astype(BF16), chosen)


def normed(x_ref, gain_ref):
    return rms_norm(x_ref[...].astype(F32), gain_ref[0:1]).astype(BF16)


def project(n_ref, w_ref, first, out_ref):
    count, _, width = out_ref.shape
    tile = min(TILE, width)
    steps = width // tile

    def one(step, carry):
        i, j = step // steps, step % steps
        cols = pl.ds(pl.multiple_of(j * tile, tile), tile)
        out = dot(n_ref[...], w_ref[first + i, :, cols]).astype(BF16)
        if first == 0:
            out *= jnp.where(i == 0, (width // HEADS) ** (-0.5), 1.0).astype(BF16)
        out_ref[i, :, cols] = out
        return carry

    lax.fori_loop(0, count * steps, one, 0)


def own_kernel(x_ref, gain_ref, w_ref, column_ref, row_ref, doc_ref, q_ref, num_ref, den_ref, n_ref, qkv_ref):
    here = lax.axis_index("seq") * x_ref.shape[0]
    n_ref[...] = normed(x_ref, gain_ref)
    project(n_ref, w_ref, 0, qkv_ref)
    q_ref[...] = qkv_ref[0]
    num_ref[...] = jnp.zeros_like(num_ref)
    den_ref[...] = jnp.zeros_like(den_ref)
    k_ref, v_ref = qkv_ref.at[1], qkv_ref.at[2]
    attend(q_ref, k_ref, v_ref, num_ref, den_ref, column_ref, row_ref, doc_ref, here, here, True)


def keys_kernel(x_ref, gain_ref, w_ref, doc_ref, kv_ref, n_ref):
    half = x_ref.shape[0]
    here = lax.axis_index("seq") * 2 * half

    @pl.when((here > 0) & (doc_ref[0, jnp.maximum(here - 1, 0)] >= doc_ref[0, here]))
    def _():
        n_ref[...] = normed(x_ref, gain_ref)
        project(n_ref, w_ref, 1, kv_ref.at[:, half:])


def fill_keys(ready, x_ref, gain_ref, w_ref, n_ref, kv_ref):
    rows = x_ref.shape[0] // 2 if ready else x_ref.shape[0]
    n_ref[:rows] = rms_norm(x_ref[:rows].astype(F32), gain_ref[0:1]).astype(BF16)
    project(n_ref.at[:rows], w_ref, 1, kv_ref.at[:, :rows])


def message_place(doc_ref, rows):
    place, count = lax.axis_index("seq"), lax.axis_size("seq")
    inside = (place >= 1) & (place + 1 < count)
    here = jnp.where(inside, place + 1, 0) * rows
    there = jnp.where(inside, place - 1, 0) * rows
    return here, there, inside & (doc_ref[0, there + rows - 1] >= doc_ref[0, here])


def piece_kernel(
    ready, shift, x_ref, gain_ref, w_ref, q_ref, num_in, den_in, kv_in, column_ref, row_ref, doc_ref,
    num_ref, den_ref, kv_ref, n_ref,
):
    del num_in, den_in, kv_in
    rows, keys = q_ref.shape[0], x_ref.shape[0]
    shard = lax.axis_index("seq") - shift
    here, there = (shard + shift) * rows, jnp.maximum(shard, 0) * rows + rows - keys

    @pl.when((shard >= 0) & (doc_ref[0, there + keys - 1] >= doc_ref[0, here]))
    def _():
        if ready is None:
            fill_keys(False, x_ref, gain_ref, w_ref, n_ref, kv_ref)
        else:
            far = far_document(doc_ref, rows, lax.axis_size("seq"))

            @pl.when(jnp.logical_not(far & message_place(doc_ref, rows)[2]))
            def _():
                fill_keys(ready, x_ref, gain_ref, w_ref, n_ref, kv_ref)

        attend(q_ref, kv_ref.at[0], kv_ref.at[1], num_ref, den_ref, column_ref, row_ref, doc_ref, here, there)


def far_document(doc_ref, rows, count):
    found = False
    for middle in range(1, count - 1):
        over = doc_ref[0, middle * rows - 1] == doc_ref[0, (middle + 1) * rows]
        deep = doc_ref[0, middle * rows - rows // 2 - 1] == doc_ref[0, (middle + 1) * rows]
        found = found | (over & deep)
    return found


def message_kernel(
    ready, x_ref, piece_ref, gain_ref, w_ref, kv_in, column_ref, row_ref, doc_ref,
    out_ref, kv_ref, q_ref, n_ref, num_ref, den_ref,
):
    del kv_in
    half, width = x_ref.shape
    here, there, needed = message_place(doc_ref, 2 * half)
    far = far_document(doc_ref, 2 * half, lax.axis_size("seq"))

    @pl.when(jnp.logical_not(far))
    def _():
        out_ref[:, :width] = piece_ref[half:]

    @pl.when(far)
    def _():
        num_ref[...] = jnp.zeros_like(num_ref)
        den_ref[...] = jnp.zeros_like(den_ref)

        @pl.when(needed)
        def _():
            n_ref[:half] = normed(x_ref, gain_ref)
            project(n_ref.at[:half], w_ref, 0, q_ref)
            fill_keys(ready, piece_ref, gain_ref, w_ref, n_ref, kv_ref)
            attend(
                q_ref.at[0], kv_ref.at[0], kv_ref.at[1], num_ref, den_ref, column_ref, row_ref, doc_ref, here, there
            )

        out_ref[:, :width] = num_ref[...].astype(BF16)
        out_ref[:, width:] = den_ref[...].astype(BF16)


def reply_kernel(
    message_ref, gain_ref, w_ref, q_ref, num_in, den_in, column_ref, row_ref, doc_ref,
    num_ref, den_ref, n_ref, kv_ref,
):
    rows, width = q_ref.shape
    half = message_ref.shape[0]
    far = far_document(doc_ref, rows, lax.axis_size("seq"))

    @pl.when(far)
    def _():
        num_ref[:half] += message_ref[:, :width].astype(F32)
        den_ref[:half] += message_ref[:, width:].astype(F32)

    @pl.when(jnp.logical_not(far))
    def _():
        piece_kernel(
            None, 2, message_ref.at[:, :width], gain_ref, w_ref, q_ref, num_in, den_in, None, column_ref, row_ref, doc_ref,
            num_ref, den_ref, kv_ref, n_ref,
        )


def mix(first, x_ref, num_ref, den_ref, w_ref, gain_ref, acc_ref, n_ref):
    rows, width = acc_ref.shape
    here = pl.ds(first, rows)
    lane = lax.broadcasted_iota(jnp.int32, (rows, LANES), 1)
    inverse = 1.0 / jnp.where(lane < HEADS, den_ref[here], 1.0)
    n_ref[...] = (num_ref[here] * spread(inverse, width)).astype(BF16)
    tile = min(TILE, width)

    def one(j, carry):
        cols = pl.ds(pl.multiple_of(j * tile, tile), tile)
        acc_ref[:, cols] = x_ref[here, cols].astype(F32) + dot(n_ref[...], w_ref[3, :, cols])
        return carry

    lax.fori_loop(0, width // tile, one, 0)
    n_ref[...] = rms_norm(acc_ref[...], gain_ref[1:2]).astype(BF16)


def feed_forward(begin, end, n_ref, up_ref, down_ref, acc_ref):
    tile = min(TILE, up_ref.shape[1])

    def one(j, carry):
        units = pl.ds(pl.multiple_of(j * tile, tile), tile)
        expanded = jax.nn.gelu(dot(n_ref[...], up_ref[:, units])).astype(BF16)
        acc_ref[...] += dot(expanded, down_ref[units])
        return carry

    lax.fori_loop(begin, end, one, 0)


def feed_forward_ahead(n_ref, up_ref, down_ref, acc_ref, hidden_ref):
    tile = hidden_ref.shape[2]
    last = up_ref.shape[1] // tile - 1

    def expand(j):
        units = pl.ds(pl.multiple_of(j * tile, tile), tile)
        hidden_ref[j % 2] = jax.nn.gelu(dot(n_ref[...], up_ref[:, units])).astype(BF16)

    def lower(j):
        acc_ref[...] += dot(hidden_ref[j % 2], down_ref[pl.ds(pl.multiple_of(j * tile, tile), tile)])

    def one(j, carry):
        lower(j)
        expand(j + 1)
        return carry

    expand(0)
    lax.fori_loop(0, last, one, 0)
    lower(last)


def tiles_of(up_ref):
    return up_ref.shape[1] // min(TILE, up_ref.shape[1])


def finish_kernel(
    first, x_ref, num_ref, den_ref, w_ref, gain_ref, up_ref, down_ref, out_ref, acc_ref, n_ref, hidden_ref=None
):
    mix(first, x_ref, num_ref, den_ref, w_ref, gain_ref, acc_ref, n_ref)
    if hidden_ref is None:
        feed_forward(0, tiles_of(up_ref), n_ref, up_ref, down_ref, acc_ref)
    else:
        feed_forward_ahead(n_ref, up_ref, down_ref, acc_ref, hidden_ref)
    out_ref[...] = acc_ref[...].astype(BF16)


def seen_by_second_half(doc_ref, rows):
    place = lax.axis_index("seq")
    before = jnp.maximum((place - 1) * rows - 1, 0)
    return (place >= 2) & (doc_ref[0, before] == doc_ref[0, place * rows + rows // 2])


def early_kernel(
    first, x_ref, num_ref, den_ref, w_ref, gain_ref, up_ref, down_ref, doc_ref, out_ref, acc_ref, n_ref, hidden_ref
):
    @pl.when(jnp.logical_not(seen_by_second_half(doc_ref, x_ref.shape[0])))
    def _():
        finish_kernel(
            first, x_ref, num_ref, den_ref, w_ref, gain_ref, up_ref, down_ref, out_ref, acc_ref, n_ref, hidden_ref
        )


def again_kernel(
    message_ref, gain_ref, w_ref, q_ref, num_in, den_in, done_in, x_ref, up_ref, down_ref, column_ref, row_ref, doc_ref,
    num_ref, den_ref, done_ref, n_ref, kv_ref, acc_ref,
):
    del done_in
    half = done_ref.shape[0]
    reply_kernel(
        message_ref, gain_ref, w_ref, q_ref, num_in, den_in, column_ref, row_ref, doc_ref,
        num_ref, den_ref, n_ref, kv_ref,
    )

    @pl.when(seen_by_second_half(doc_ref, 2 * half))
    def _():
        finish_kernel(half, x_ref, num_ref, den_ref, w_ref, gain_ref, up_ref, down_ref, done_ref, acc_ref, n_ref)


def last_kernel(
    message_ref, gain_ref, w_ref, q_ref, num_in, den_in, done_ref, x_ref, up_ref, down_ref, column_ref, row_ref, doc_ref,
    num_ref, den_ref, out_ref, n_ref, kv_ref, acc_ref, result_ref, hidden_ref, sems,
):
    half = done_ref.shape[0]
    again = seen_by_second_half(doc_ref, 2 * half) if message_ref is not None else False
    halves = [out_ref.at[:half], out_ref.at[half:]]
    as_it_was = pltpu.make_async_copy(done_ref, halves[1], sems.at[1])
    copies = [pltpu.make_async_copy(result_ref.at[i], halves[i], sems.at[i]) for i in range(2)]

    @pl.when(jnp.logical_not(again))
    def _():
        as_it_was.start()

    if message_ref is not None:
        reply_kernel(
            message_ref, gain_ref, w_ref, q_ref, num_in, den_in, column_ref, row_ref, doc_ref,
            num_ref, den_ref, n_ref, kv_ref,
        )

    def one(part, carry):
        @pl.when((part == 0) | again)
        def _():
            first = pl.multiple_of(part * half, half)
            finish_kernel(
                first, x_ref, num_ref, den_ref, w_ref, gain_ref, up_ref, down_ref, result_ref.at[part], acc_ref, n_ref,
                hidden_ref,
            )

        return carry

    lax.fori_loop(0, 2, one, 0)
    copies[0].start()

    @pl.when(again)
    def _():
        copies[1].start()
        copies[1].wait()

    @pl.when(jnp.logical_not(again))
    def _():
        as_it_was.wait()

    copies[0].wait()


def open_kernel(first, tiles, x_ref, num_ref, den_ref, w_ref, gain_ref, up_ref, down_ref, acc_ref, n_ref):
    mix(first, x_ref, num_ref, den_ref, w_ref, gain_ref, acc_ref, n_ref)
    feed_forward(0, tiles, n_ref, up_ref, down_ref, acc_ref)


def close_kernel(begin, acc_in, n_ref, up_ref, down_ref, out_ref, acc_ref):
    acc_ref[...] = acc_in[...]
    feed_forward(begin, tiles_of(up_ref), n_ref, up_ref, down_ref, acc_ref)
    out_ref[...] = acc_ref[...].astype(BF16)


def vmem():
    return pl.BlockSpec(memory_space=pltpu.VMEM)


def call(kernel, name, operands, docs, results, scratch, aliases=None, sent=()):
    inputs = [pltpu.with_memory_space_constraint(operand, pltpu.VMEM) for operand in operands]
    in_specs = [vmem()] * len(inputs)
    if docs is not None:
        inputs.append(docs)
        in_specs.append(pl.BlockSpec(memory_space=pltpu.SMEM))
    return pl.pallas_call(
        kernel,
        in_specs=in_specs,
        out_specs=[pl.BlockSpec(memory_space=pl.ANY) if i in sent else vmem() for i in range(len(results))],
        out_shape=[
            jax.ShapeDtypeStruct(*one) if i in sent else pltpu.VMEM(*one) for i, one in enumerate(results)
        ],
        scratch_shapes=scratch,
        input_output_aliases=aliases or {},
        compiler_params=pltpu.CompilerParams(vmem_limit_bytes=VMEM_BYTES),
        cost_estimate=COST,
        name=name,
    )(*inputs)


def own_part(x, gains, weights, docs):
    rows, width = x.shape
    results = [((rows, width), BF16), ((rows, width), F32), ((rows, LANES), F32)]
    scratch = [pltpu.VMEM((rows, width), BF16), pltpu.VMEM((3, rows, width), BF16)]
    return call(own_kernel, "own_part", (x, gains, weights[0], docs.own_column, docs.ids), docs.ids, results, scratch)


def keys_part(x, gains, w_attn, docs):
    half, width = x.shape
    return call(
        keys_kernel,
        "keys_part",
        (x, gains, w_attn),
        docs.ids,
        [((2, 2 * half, width), BF16)],
        [pltpu.VMEM((half, width), BF16)],
    )[0]


def piece_part(x, shift, ready, gains, w_attn, q, num, den, kv, docs):
    rows, width = q.shape
    return call(
        functools.partial(piece_kernel, ready, shift),
        "piece_part",
        (x, gains, w_attn, q, num, den, kv, docs.own_column, docs.ids),
        docs.ids,
        [((rows, width), F32), ((rows, LANES), F32), (kv.shape, BF16)],
        [pltpu.VMEM(x.shape, BF16)],
        aliases={4: 0, 5: 1, 6: 2},
    )


def message_part(x, piece, ready, gains, w_attn, kv, docs):
    half, width = x.shape
    return call(
        functools.partial(message_kernel, ready),
        "message_part",
        (x, piece, gains, w_attn, kv, docs.later_column, docs.ids),
        docs.ids,
        [((half, width + LANES), BF16), (kv.shape, BF16)],
        [
            pltpu.VMEM((1, half, width), BF16),
            pltpu.VMEM(piece.shape, BF16),
            pltpu.VMEM((half, width), F32),
            pltpu.VMEM((half, LANES), F32),
        ],
        aliases={4: 1},
    )


def finish_part(x, num, den, weights, gains, docs):
    half, width = x.shape[0] // 2, x.shape[1]
    return call(
        functools.partial(early_kernel if docs.short else finish_kernel, half),
        "finish_part",
        (x, num, den, weights[0], gains, *weights[1:]),
        docs.ids if docs.short else None,
        [((half, width), BF16)],
        [pltpu.VMEM((half, width), F32), pltpu.VMEM((half, width), BF16), hidden_scratch(half, weights)],
    )[0]


def hidden_scratch(rows, weights):
    return pltpu.VMEM((2, rows, min(TILE, weights[1].shape[1])), BF16)


def reply_scratch(half, width):
    return [
        pltpu.VMEM((half, width), BF16),
        pltpu.VMEM((2, half, width), BF16),
        pltpu.VMEM((half, width), F32),
    ]


def again_part(message, state, done, x, weights, gains, docs):
    q, num, den = state
    half, width = done.shape
    return call(
        again_kernel,
        "again_part",
        (message, gains, weights[0], q, num, den, done, x, *weights[1:], docs.own_column, docs.ids),
        docs.ids,
        [(num.shape, F32), (den.shape, F32), ((half, width), BF16)],
        reply_scratch(half, width),
        aliases={4: 0, 5: 1, 6: 2},
    )


def last_part(message, state, done, x, weights, gains, docs):
    q, num, den = state
    half, width = done.shape
    operands = (message, gains, weights[0], q, num, den, done, x, *weights[1:], docs.own_column, docs.ids)
    kernel, aliases = last_kernel, {4: 0, 5: 1}
    if message is None:
        kernel, operands, aliases = functools.partial(last_kernel, None), operands[1:], {3: 0, 4: 1}
    return call(
        kernel,
        "last_part",
        operands,
        docs.ids,
        [(num.shape, F32), (den.shape, F32), (x.shape, BF16)],
        reply_scratch(half, width) + [
            pltpu.VMEM((2, half, width), BF16),
            hidden_scratch(half, weights),
            pltpu.SemaphoreType.DMA((2,)),
        ],
        aliases=aliases,
        sent=(2,),
    )[2]


def open_part(x, num, den, weights, gains, part, tiles):
    width = x.shape[1]
    rows = x.shape[0] // 2
    return call(
        functools.partial(open_kernel, part * rows, tiles),
        "open_part",
        (x, num, den, weights[0], gains, *weights[1:]),
        None,
        [((rows, width), F32), ((rows, width), BF16)],
        [],
    )


def close_part(acc, n, weights, tiles):
    return call(
        functools.partial(close_kernel, tiles),
        "close_part",
        (acc, n, *weights[1:]),
        None,
        [(acc.shape, BF16)],
        [pltpu.VMEM(acc.shape, F32)],
    )[0]


def shifted(value, axis, steps):
    count = lax.axis_size(axis)
    first, last = max(0, -steps), min(count, count - steps)
    return lax.ppermute(value, axis, [(i, i + steps) for i in range(first, last)])


def swapped(value, axis, bit):
    return lax.ppermute(value, axis, [(i, i ^ bit) for i in range(lax.axis_size(axis))])


class Documents:
    def __init__(self, doc_ids, rows):
        count = lax.axis_size("seq")
        self.ids, self.rows, self.half = doc_ids, rows, rows // 2
        longest = doc_ids.shape[1] // 2
        self.hops = min(count - 1, -(-(longest - 1) // rows))
        self.short = self.hops == 2 and longest <= 2 * rows and rows % 2 == 0
        place = lax.axis_index("seq")

        def column(later, size):
            start = jnp.minimum((place + later) * rows, doc_ids.shape[1] - size)
            ids = lax.dynamic_slice_in_dim(doc_ids, start, size, 1)
            return jnp.broadcast_to(ids.reshape(-1, 1), (size, LANES))

        self.own_column = column(0, rows)
        self.later_column = column(1, self.half) if self.short else self.own_column


def attention(x, state, piece, first_back, docs, gains, weights, kv=None):
    q, num, den = state
    w_attn = weights[0]
    ready = kv is not None
    if not ready:
        kv = jnp.zeros((2, *piece.shape), BF16)
    if docs.short:
        message, kv = message_part(after(first_back, q), piece, ready, gains, w_attn, kv, docs)
        num = after(num, message)
        message = shifted(message, "seq", 1)
        num, den, _ = piece_part(piece, 1, ready, gains, w_attn, q, num, den, kv, docs)
        done = finish_part(x, num, den, weights, gains, docs)
        return after(message, done), (q, num, den), done
    for hop in range(1, docs.hops + 1):
        num, den, kv = piece_part(piece, hop, None, gains, w_attn, q, num, den, kv, docs)
        piece = shifted(piece, "seq", 1)
    return None, (q, num, den), finish_part(x, num, den, weights, gains, docs)


def packed(row):
    high = lax.reduce_precision(row, 8, 7)
    low = lax.reduce_precision(row - high, 8, 7)
    place = lax.broadcasted_iota(jnp.int32, (CARRIED, row.shape[1]), 0)
    return jnp.where(place == 0, high, jnp.where(place == 1, low, 0.0)).astype(BF16)


def unpacked(rows):
    return rows[:1].astype(F32) + rows[1:2].astype(F32)


def after(value, *earlier):
    return lax.optimization_barrier((value, *earlier))[0]


def own_half(rows, odd):
    half = rows.shape[0] // 2
    return jnp.where(odd, rows[half:], rows[:half]), jnp.where(odd, rows[:half], rows[half:])


class Chain:
    def __init__(self, own_states, other_states, even_gain, odd_gain, bits, before=None):
        self.bits, self.odd, self.leading = bits, bits[1], bits[0]
        self.even_gain, self.odd_gain = even_gain, odd_gain
        self.levels = before.levels if before else []
        self.factor, self.factor_before = even_gain * odd_gain, jnp.ones_like(even_gain)
        even, odd = self.sorted(own_states, other_states)
        self.even_states = even
        behind = jnp.where(self.leading, 0.0, self.even_gain * even.astype(F32))
        self.known = self.odd_gain * (behind + odd.astype(F32))

    def sorted(self, mine, other):
        return jnp.where(self.odd, other, mine), jnp.where(self.odd, mine, other)

    def enter(self, fine, *earlier):
        fine = after(fine, *earlier)
        half = fine.shape[0] // 2
        mine, sent = own_half(fine, self.odd)
        other = swapped(sent, "depth", 1)
        self.fine_even, fine_odd = self.sorted(mine, other)
        self.total = self.odd_gain * self.fine_even.astype(F32) + fine_odd.astype(F32) - self.known
        self.before = jnp.zeros_like(self.total)

    def level(self, index, sent_after=(), used_after=()):
        bit, last = 2 << index, index + 1 == self.steps()
        upper, rows = self.bits[bit], self.total.shape[0]
        sent = self.total.astype(BF16)
        carries = index == len(self.levels) and not last
        if carries:
            sent = jnp.concatenate([sent, packed(self.factor)], axis=0)
        theirs = after(swapped(after(sent, *sent_after), "depth", bit), *used_after)
        if index == len(self.levels):
            their_factor = unpacked(theirs[rows:]) if carries else None
            self.levels.append((self.factor, their_factor, self.factor_before))
            if carries:
                self.factor_before = jnp.where(upper, self.factor_before * their_factor, self.factor_before)
                self.factor = self.factor * their_factor
        factor, their_factor, factor_before = self.levels[index]
        theirs = theirs[:rows].astype(F32)
        if not last:
            self.total = jnp.where(upper, factor * theirs + self.total, their_factor * self.total + theirs)
        self.before = jnp.where(upper, factor_before * theirs + self.before, self.before)

    def steps(self):
        return len(self.bits) - 2

    def leave(self, used_after=()):
        even_states = self.even_states.astype(F32)
        even = jnp.where(self.leading, even_states, self.before)
        odd = self.even_gain * (even - even_states) + self.fine_even.astype(F32)
        even, odd = even.astype(BF16), odd.astype(BF16)
        mine, sent = jnp.where(self.odd, odd, even), jnp.where(self.odd, even, odd)
        other = after(swapped(sent, "depth", 1), *used_after)
        low, high = self.sorted(mine, other)
        return jnp.concatenate([low, high], axis=0)


def on_device(interfaces, doc_ids, w_attn, w_up, w_down, norm_gains, coarse_gain):
    x = interfaces[0, 0]
    rows = x.shape[0]
    half = rows // 2
    gains = norm_gains[0, 0]
    weights = (w_attn[0, 0], w_up[0, 0], w_down[0, 0])
    parts = [x[:half], x[half:]]
    piece = shifted(x, "seq", 1)
    docs = Documents(doc_ids, rows)
    place, bits, bit = lax.axis_index("depth"), {}, 1
    while bit < lax.axis_size("depth"):
        bits[bit] = (place & bit) != 0
        bit *= 2
    bits[0] = place < 2
    early, bits, docs.own_column, docs.later_column = lax.optimization_barrier(
        (x, bits, docs.own_column, docs.later_column)
    )
    first_back = shifted(after(parts[0], docs.own_column), "seq", -1)
    state = own_part(early, gains, weights, docs)
    kept, sent = zip(*[own_half(part, bits[1]) for part in parts])
    sent = jnp.concatenate([*after(sent, state[0]), packed(coarse_gain)], axis=0)
    other = swapped(sent, "depth", 1)
    message, state, done = attention(early, state, piece, first_back, docs, gains, weights)
    other_gain = unpacked(other[half:])
    pair = jnp.where(bits[1], other_gain, coarse_gain), jnp.where(bits[1], coarse_gain, other_gain)
    first = Chain(kept[1], other[half // 2 : half], *pair, bits)
    second = Chain(kept[0], other[: half // 2], *pair, bits, first)
    _, num, den = state
    if message is not None:
        message = after(message, first.known, second.known)
        num, den, done = again_part(message, state, done, early, weights, gains, docs)
    first.enter(done)
    tiles = weights[1].shape[1] // TILE // 2
    acc, n = open_part(early, after(num, first.total), den, weights, gains, 0, tiles)
    first.level(0, used_after=(n,))
    fine = close_part(after(acc, first.total), n, weights, tiles)
    first.level(1, used_after=(fine,))
    second.enter(fine, first.before)
    for i in range(2, first.steps()):
        second.level(i - 2)
        first.level(i)
    late = first.leave()
    late_piece = shifted(late, "seq", 1)
    for i in range(max(0, first.steps() - 2), first.steps()):
        last = i + 1 == first.steps()
        second.level(i, (late,) if i > 0 else (), (late_piece,) if last else ())
    soon = second.leave()
    piece = jnp.concatenate([shifted(soon, "seq", 1), late_piece], axis=0)
    x = jnp.concatenate([soon, late], axis=0)
    first_back = shifted(after(soon, x), "seq", -1)
    state = own_part(x, gains, weights, docs)
    kv = keys_part(after(late_piece, state[0]), gains, weights[0], docs) if docs.short else None
    message, state, done = attention(x, state, piece, first_back, docs, gains, weights, kv)
    return last_part(message, state, done, x, weights, gains, docs)[None, None]


def solution(mesh):
    in_specs = (
        P("depth", None, "seq", None),
        P(),
        P("depth", None, None, None, None),
        P("depth", None, None, None),
        P("depth", None, None, None),
        P("depth", None, None, None),
        P("depth", None),
    )
    out_specs = P("depth", None, "seq", None)
    return jax.shard_map(
        on_device, mesh=mesh, in_specs=in_specs, out_specs=out_specs, check_vma=False
    )
```

```python
import functools

import jax
import jax.numpy as jnp
from jax import lax
from jax.experimental import pallas as pl
from jax.experimental.pallas import tpu as pltpu
from jax.sharding import PartitionSpec as P

HEADS = 16
LANES = 128
CARRIED = 16
BLOCK = 256
TILE = 512
TILES = 8
VMEM_BYTES = 8 * 1024 * 1024
COST = pl.CostEstimate(flops=1 << 20, bytes_accessed=1 << 16, transcendentals=0)
F32 = jnp.float32
BF16 = jnp.bfloat16


def rms_norm(value, gain):
    return value * lax.rsqrt(jnp.mean(value * value, axis=-1, keepdims=True) + 1e-05) * gain


def dot(a, b):
    return jnp.dot(a, b, preferred_element_type=F32)


def first_id(marks_ref, position, grain):
    return marks_ref[0, lax.div(position, grain)]


def last_id(marks_ref, end, grain):
    return marks_ref[1, jnp.maximum(lax.div(end, grain) - 1, 0)]


def grain_of(marks_ref, rows):
    return rows * lax.axis_size("seq") // marks_ref.shape[1]


def attend(q_ref, k_ref, v_ref, num_ref, den_ref, column_ref, row_ref, doc_ref, q_at, k_at, causal=False):
    rows, width = q_ref.shape
    keys = k_ref.shape[0]
    head_dim = width // HEADS
    per_tile = LANES // head_dim
    q_block, k_block = min(BLOCK, rows), min(BLOCK, keys)
    lane = lax.broadcasted_iota(jnp.int32, (1, LANES), 1)
    members = [lane // head_dim == i for i in range(per_tile)]
    count_q, count_k = rows // q_block, keys // k_block
    grain = row_ref.shape[1] // doc_ref.shape[1]

    def one(index, carry):
        qi, ki = index // count_k, index % count_k
        q0 = pl.multiple_of(qi * q_block, q_block)
        k0 = pl.multiple_of(ki * k_block, k_block)
        needed = last_id(doc_ref, k_at + k0 + k_block, grain) >= first_id(doc_ref, q_at + q0, grain)
        if causal:
            needed = (k0 <= q0) & (needed | (k0 == q0))

        @pl.when(needed)
        def _():
            key_docs = row_ref[:, pl.ds(pl.multiple_of(k_at + k0, k_block), k_block)]
            allowed = column_ref[pl.ds(q0, q_block), :1] == key_docs
            if causal:
                q_pos = q0 + lax.broadcasted_iota(jnp.int32, (q_block, k_block), 0)
                k_pos = k0 + lax.broadcasted_iota(jnp.int32, (q_block, k_block), 1)
                allowed = allowed & (k_pos <= q_pos)
            ones = jnp.ones((k_block, LANES), BF16)

            def heads(tile, den):
                cols = pl.ds(pl.multiple_of(tile * LANES, LANES), LANES)
                queries = q_ref[pl.ds(q0, q_block), cols]
                keys_here = k_ref[pl.ds(k0, k_block), cols]
                values = jnp.concatenate([v_ref[pl.ds(k0, k_block), cols], ones], axis=1)
                num = None
                for i, member in enumerate(members):
                    scores = lax.dot_general(
                        jnp.where(member, queries, jnp.zeros_like(queries)),
                        keys_here,
                        (((1,), (1,)), ((), ())),
                        preferred_element_type=F32,
                    )
                    weights = jnp.where(allowed, jnp.exp(scores), 0.0).astype(BF16)
                    out = dot(weights, values)
                    num = out[:, :LANES] if num is None else jnp.where(member, out[:, :LANES], num)
                    den = jnp.where(lane == tile * per_tile + i, out[:, LANES:], den)
                num_ref[pl.ds(q0, q_block), cols] += num
                return den

            def some(step, den):
                for i in range(TILES):
                    den = heads(step * TILES + i, den)
                return den

            den = jnp.zeros((q_block, LANES), F32)
            den_ref[pl.ds(q0, q_block), :] += lax.fori_loop(0, width // LANES // TILES, some, den, unroll=True)

        return carry

    lax.fori_loop(0, count_q * count_k, one, 0)


def spread(per_head, width):
    shape = (LANES, width)
    chosen = lax.broadcasted_iota(jnp.int32, shape, 1) // (width // HEADS) == lax.broadcasted_iota(jnp.int32, shape, 0)
    chosen = jnp.where(chosen, 1.0, 0.0).astype(BF16)
    high = per_head.astype(BF16)
    return dot(high, chosen) + dot((per_head - high.astype(F32)).astype(BF16), chosen)


def normed(x_ref, gain_ref):
    return rms_norm(x_ref[...].astype(F32), gain_ref[0:1]).astype(BF16)


def project(n_ref, w_ref, first, out_ref):
    count, _, width = out_ref.shape
    tile = min(TILE, width)
    steps = width // tile

    def one(step, carry):
        i, j = step // steps, step % steps
        cols = pl.ds(pl.multiple_of(j * tile, tile), tile)
        out = dot(n_ref[...], w_ref[first + i, :, cols]).astype(BF16)
        if first == 0:
            out *= jnp.where(i == 0, (width // HEADS) ** (-0.5), 1.0).astype(BF16)
        out_ref[i, :, cols] = out
        return carry

    lax.fori_loop(0, count * steps, one, 0)


def own_kernel(x_ref, gain_ref, w_ref, column_ref, row_ref, doc_ref, q_ref, num_ref, den_ref, n_ref, qkv_ref):
    here = lax.axis_index("seq") * x_ref.shape[0]
    n_ref[...] = normed(x_ref, gain_ref)
    project(n_ref, w_ref, 0, qkv_ref)
    q_ref[...] = qkv_ref[0]
    num_ref[...] = jnp.zeros_like(num_ref)
    den_ref[...] = jnp.zeros_like(den_ref)
    k_ref, v_ref = qkv_ref.at[1], qkv_ref.at[2]
    attend(q_ref, k_ref, v_ref, num_ref, den_ref, column_ref, row_ref, doc_ref, here, here, True)


def keys_kernel(x_ref, gain_ref, w_ref, doc_ref, kv_ref, n_ref):
    half = x_ref.shape[0]
    here = lax.axis_index("seq") * 2 * half

    grain = grain_of(doc_ref, 2 * half)

    @pl.when((here > 0) & (last_id(doc_ref, here, grain) >= first_id(doc_ref, here, grain)))
    def _():
        n_ref[...] = normed(x_ref, gain_ref)
        project(n_ref, w_ref, 1, kv_ref.at[:, half:])


def fill_keys(ready, x_ref, gain_ref, w_ref, n_ref, kv_ref):
    rows = x_ref.shape[0] // 2 if ready else x_ref.shape[0]
    n_ref[:rows] = rms_norm(x_ref[:rows].astype(F32), gain_ref[0:1]).astype(BF16)
    project(n_ref.at[:rows], w_ref, 1, kv_ref.at[:, :rows])


def message_place(doc_ref, rows):
    place, count = lax.axis_index("seq"), lax.axis_size("seq")
    inside = (place >= 1) & (place + 1 < count)
    here = jnp.where(inside, place + 1, 0) * rows
    there = jnp.where(inside, place - 1, 0) * rows
    grain = grain_of(doc_ref, rows)
    return here, there, inside & (last_id(doc_ref, there + rows, grain) >= first_id(doc_ref, here, grain))


def piece_kernel(
    ready, shift, x_ref, gain_ref, w_ref, q_ref, num_in, den_in, kv_in, column_ref, row_ref, doc_ref,
    num_ref, den_ref, kv_ref, n_ref,
):
    del num_in, den_in, kv_in
    rows, keys = q_ref.shape[0], x_ref.shape[0]
    shard = lax.axis_index("seq") - shift
    here, there = (shard + shift) * rows, jnp.maximum(shard, 0) * rows + rows - keys

    grain = grain_of(doc_ref, rows)

    @pl.when((shard >= 0) & (last_id(doc_ref, there + keys, grain) >= first_id(doc_ref, here, grain)))
    def _():
        if ready is None:
            fill_keys(False, x_ref, gain_ref, w_ref, n_ref, kv_ref)
        else:
            far = far_document(doc_ref, rows, lax.axis_size("seq"))

            @pl.when(jnp.logical_not(far & message_place(doc_ref, rows)[2]))
            def _():
                fill_keys(ready, x_ref, gain_ref, w_ref, n_ref, kv_ref)

        attend(q_ref, kv_ref.at[0], kv_ref.at[1], num_ref, den_ref, column_ref, row_ref, doc_ref, here, there)


def far_document(doc_ref, rows, count):
    found, grain = False, grain_of(doc_ref, rows)
    for middle in range(1, count - 1):
        start, behind = middle * rows, first_id(doc_ref, (middle + 1) * rows, grain)
        over = last_id(doc_ref, start, grain) == behind
        deep = last_id(doc_ref, start - rows // 2, grain) == behind
        found = found | (over & deep)
    return found


def message_kernel(
    ready, x_ref, piece_ref, gain_ref, w_ref, kv_in, column_ref, row_ref, doc_ref,
    out_ref, kv_ref, q_ref, n_ref, num_ref, den_ref,
):
    del kv_in
    half, width = x_ref.shape
    here, there, needed = message_place(doc_ref, 2 * half)
    far = far_document(doc_ref, 2 * half, lax.axis_size("seq"))

    @pl.when(jnp.logical_not(far))
    def _():
        out_ref[:, :width] = piece_ref[half:]

    @pl.when(far)
    def _():
        num_ref[...] = jnp.zeros_like(num_ref)
        den_ref[...] = jnp.zeros_like(den_ref)

        @pl.when(needed)
        def _():
            n_ref[:half] = normed(x_ref, gain_ref)
            project(n_ref.at[:half], w_ref, 0, q_ref)
            fill_keys(ready, piece_ref, gain_ref, w_ref, n_ref, kv_ref)
            attend(
                q_ref.at[0], kv_ref.at[0], kv_ref.at[1], num_ref, den_ref, column_ref, row_ref, doc_ref, here, there
            )

        out_ref[:, :width] = num_ref[...].astype(BF16)
        out_ref[:, width:] = den_ref[...].astype(BF16)


def reply_kernel(
    message_ref, gain_ref, w_ref, q_ref, num_in, den_in, column_ref, row_ref, doc_ref,
    num_ref, den_ref, n_ref, kv_ref,
):
    rows, width = q_ref.shape
    half = message_ref.shape[0]
    far = far_document(doc_ref, rows, lax.axis_size("seq"))

    @pl.when(far)
    def _():
        num_ref[:half] += message_ref[:, :width].astype(F32)
        den_ref[:half] += message_ref[:, width:].astype(F32)

    @pl.when(jnp.logical_not(far))
    def _():
        piece_kernel(
            None, 2, message_ref.at[:, :width], gain_ref, w_ref, q_ref, num_in, den_in, None, column_ref, row_ref, doc_ref,
            num_ref, den_ref, kv_ref, n_ref,
        )


def mix(first, x_ref, num_ref, den_ref, w_ref, gain_ref, acc_ref, n_ref):
    rows, width = acc_ref.shape
    here = pl.ds(first, rows)
    lane = lax.broadcasted_iota(jnp.int32, (rows, LANES), 1)
    inverse = 1.0 / jnp.where(lane < HEADS, den_ref[here], 1.0)
    n_ref[...] = (num_ref[here] * spread(inverse, width)).astype(BF16)
    tile = min(TILE, width)

    def one(j, carry):
        cols = pl.ds(pl.multiple_of(j * tile, tile), tile)
        acc_ref[:, cols] = x_ref[here, cols].astype(F32) + dot(n_ref[...], w_ref[3, :, cols])
        return carry

    lax.fori_loop(0, width // tile, one, 0)
    n_ref[...] = rms_norm(acc_ref[...], gain_ref[1:2]).astype(BF16)


def feed_forward(begin, end, n_ref, up_ref, down_ref, acc_ref):
    tile = min(TILE, up_ref.shape[1])

    def one(j, carry):
        units = pl.ds(pl.multiple_of(j * tile, tile), tile)
        expanded = jax.nn.gelu(dot(n_ref[...], up_ref[:, units])).astype(BF16)
        acc_ref[...] += dot(expanded, down_ref[units])
        return carry

    lax.fori_loop(begin, end, one, 0)


def feed_forward_ahead(n_ref, up_ref, down_ref, acc_ref, hidden_ref):
    tile = hidden_ref.shape[2]
    last = up_ref.shape[1] // tile - 1

    def expand(j):
        units = pl.ds(pl.multiple_of(j * tile, tile), tile)
        hidden_ref[j % 2] = jax.nn.gelu(dot(n_ref[...], up_ref[:, units])).astype(BF16)

    def lower(j):
        acc_ref[...] += dot(hidden_ref[j % 2], down_ref[pl.ds(pl.multiple_of(j * tile, tile), tile)])

    def one(j, carry):
        lower(j)
        expand(j + 1)
        return carry

    expand(0)
    lax.fori_loop(0, last, one, 0)
    lower(last)


def tiles_of(up_ref):
    return up_ref.shape[1] // min(TILE, up_ref.shape[1])


def finish_kernel(
    first, x_ref, num_ref, den_ref, w_ref, gain_ref, up_ref, down_ref, out_ref, acc_ref, n_ref, hidden_ref=None
):
    mix(first, x_ref, num_ref, den_ref, w_ref, gain_ref, acc_ref, n_ref)
    if hidden_ref is None:
        feed_forward(0, tiles_of(up_ref), n_ref, up_ref, down_ref, acc_ref)
    else:
        feed_forward_ahead(n_ref, up_ref, down_ref, acc_ref, hidden_ref)
    out_ref[...] = acc_ref[...].astype(BF16)


def seen_by_second_half(doc_ref, rows):
    place = lax.axis_index("seq")
    grain = grain_of(doc_ref, rows)
    before = last_id(doc_ref, jnp.maximum(place - 1, 0) * rows, grain)
    return (place >= 2) & (before == first_id(doc_ref, place * rows + rows // 2, grain))


def early_kernel(
    first, x_ref, num_ref, den_ref, w_ref, gain_ref, up_ref, down_ref, doc_ref, out_ref, acc_ref, n_ref, hidden_ref
):
    @pl.when(jnp.logical_not(seen_by_second_half(doc_ref, x_ref.shape[0])))
    def _():
        finish_kernel(
            first, x_ref, num_ref, den_ref, w_ref, gain_ref, up_ref, down_ref, out_ref, acc_ref, n_ref, hidden_ref
        )


def again_kernel(
    message_ref, gain_ref, w_ref, q_ref, num_in, den_in, done_in, x_ref, up_ref, down_ref, column_ref, row_ref, doc_ref,
    num_ref, den_ref, done_ref, n_ref, kv_ref, acc_ref,
):
    del done_in
    half = done_ref.shape[0]
    reply_kernel(
        message_ref, gain_ref, w_ref, q_ref, num_in, den_in, column_ref, row_ref, doc_ref,
        num_ref, den_ref, n_ref, kv_ref,
    )

    @pl.when(seen_by_second_half(doc_ref, 2 * half))
    def _():
        finish_kernel(half, x_ref, num_ref, den_ref, w_ref, gain_ref, up_ref, down_ref, done_ref, acc_ref, n_ref)


def last_kernel(
    message_ref, gain_ref, w_ref, q_ref, num_in, den_in, done_ref, x_ref, up_ref, down_ref, column_ref, row_ref, doc_ref,
    num_ref, den_ref, out_ref, n_ref, kv_ref, acc_ref, result_ref, hidden_ref, sems,
):
    half = done_ref.shape[0]
    again = seen_by_second_half(doc_ref, 2 * half) if message_ref is not None else False
    halves = [out_ref.at[:half], out_ref.at[half:]]
    as_it_was = pltpu.make_async_copy(done_ref, halves[1], sems.at[1])
    copies = [pltpu.make_async_copy(result_ref.at[i], halves[i], sems.at[i]) for i in range(2)]

    @pl.when(jnp.logical_not(again))
    def _():
        as_it_was.start()

    if message_ref is not None:
        reply_kernel(
            message_ref, gain_ref, w_ref, q_ref, num_in, den_in, column_ref, row_ref, doc_ref,
            num_ref, den_ref, n_ref, kv_ref,
        )

    def one(part, carry):
        @pl.when((part == 0) | again)
        def _():
            first = pl.multiple_of(part * half, half)
            finish_kernel(
                first, x_ref, num_ref, den_ref, w_ref, gain_ref, up_ref, down_ref, result_ref.at[part], acc_ref, n_ref,
                hidden_ref,
            )

        return carry

    lax.fori_loop(0, 2, one, 0)
    copies[0].start()

    @pl.when(again)
    def _():
        copies[1].start()
        copies[1].wait()

    @pl.when(jnp.logical_not(again))
    def _():
        as_it_was.wait()

    copies[0].wait()


def open_kernel(first, tiles, x_ref, num_ref, den_ref, w_ref, gain_ref, up_ref, down_ref, acc_ref, n_ref):
    mix(first, x_ref, num_ref, den_ref, w_ref, gain_ref, acc_ref, n_ref)
    feed_forward(0, tiles, n_ref, up_ref, down_ref, acc_ref)


def close_kernel(begin, acc_in, n_ref, up_ref, down_ref, out_ref, acc_ref):
    acc_ref[...] = acc_in[...]
    feed_forward(begin, tiles_of(up_ref), n_ref, up_ref, down_ref, acc_ref)
    out_ref[...] = acc_ref[...].astype(BF16)


def vmem():
    return pl.BlockSpec(memory_space=pltpu.VMEM)


def call(kernel, name, operands, docs, results, scratch, aliases=None, sent=()):
    inputs = [pltpu.with_memory_space_constraint(operand, pltpu.VMEM) for operand in operands]
    in_specs = [vmem()] * len(inputs)
    if docs is not None:
        inputs.append(docs)
        in_specs.append(pl.BlockSpec(memory_space=pltpu.SMEM))
    return pl.pallas_call(
        kernel,
        in_specs=in_specs,
        out_specs=[pl.BlockSpec(memory_space=pl.ANY) if i in sent else vmem() for i in range(len(results))],
        out_shape=[
            jax.ShapeDtypeStruct(*one) if i in sent else pltpu.VMEM(*one) for i, one in enumerate(results)
        ],
        scratch_shapes=scratch,
        input_output_aliases=aliases or {},
        compiler_params=pltpu.CompilerParams(vmem_limit_bytes=VMEM_BYTES),
        cost_estimate=COST,
        name=name,
    )(*inputs)


def own_part(x, gains, weights, docs):
    rows, width = x.shape
    results = [((rows, width), BF16), ((rows, width), F32), ((rows, LANES), F32)]
    scratch = [pltpu.VMEM((rows, width), BF16), pltpu.VMEM((3, rows, width), BF16)]
    return call(own_kernel, "own_part", (x, gains, weights[0], docs.own_column, docs.ids), docs.marks, results, scratch)


def keys_part(x, gains, w_attn, docs):
    half, width = x.shape
    return call(
        keys_kernel,
        "keys_part",
        (x, gains, w_attn),
        docs.marks,
        [((2, 2 * half, width), BF16)],
        [pltpu.VMEM((half, width), BF16)],
    )[0]


def piece_part(x, shift, ready, gains, w_attn, q, num, den, kv, docs):
    rows, width = q.shape
    return call(
        functools.partial(piece_kernel, ready, shift),
        "piece_part",
        (x, gains, w_attn, q, num, den, kv, docs.own_column, docs.ids),
        docs.marks,
        [((rows, width), F32), ((rows, LANES), F32), (kv.shape, BF16)],
        [pltpu.VMEM(x.shape, BF16)],
        aliases={4: 0, 5: 1, 6: 2},
    )


def message_part(x, piece, ready, gains, w_attn, kv, docs):
    half, width = x.shape
    return call(
        functools.partial(message_kernel, ready),
        "message_part",
        (x, piece, gains, w_attn, kv, docs.later_column, docs.ids),
        docs.marks,
        [((half, width + LANES), BF16), (kv.shape, BF16)],
        [
            pltpu.VMEM((1, half, width), BF16),
            pltpu.VMEM(piece.shape, BF16),
            pltpu.VMEM((half, width), F32),
            pltpu.VMEM((half, LANES), F32),
        ],
        aliases={4: 1},
    )


def finish_part(x, num, den, weights, gains, docs):
    half, width = x.shape[0] // 2, x.shape[1]
    return call(
        functools.partial(early_kernel if docs.short else finish_kernel, half),
        "finish_part",
        (x, num, den, weights[0], gains, *weights[1:]),
        docs.marks if docs.short else None,
        [((half, width), BF16)],
        [pltpu.VMEM((half, width), F32), pltpu.VMEM((half, width), BF16), hidden_scratch(half, weights)],
    )[0]


def hidden_scratch(rows, weights):
    return pltpu.VMEM((2, rows, min(TILE, weights[1].shape[1])), BF16)


def reply_scratch(half, width):
    return [
        pltpu.VMEM((half, width), BF16),
        pltpu.VMEM((2, half, width), BF16),
        pltpu.VMEM((half, width), F32),
    ]


def again_part(message, state, done, x, weights, gains, docs):
    q, num, den = state
    half, width = done.shape
    return call(
        again_kernel,
        "again_part",
        (message, gains, weights[0], q, num, den, done, x, *weights[1:], docs.own_column, docs.ids),
        docs.marks,
        [(num.shape, F32), (den.shape, F32), ((half, width), BF16)],
        reply_scratch(half, width),
        aliases={4: 0, 5: 1, 6: 2},
    )


def last_part(message, state, done, x, weights, gains, docs):
    q, num, den = state
    half, width = done.shape
    operands = (message, gains, weights[0], q, num, den, done, x, *weights[1:], docs.own_column, docs.ids)
    kernel, aliases = last_kernel, {4: 0, 5: 1}
    if message is None:
        kernel, operands, aliases = functools.partial(last_kernel, None), operands[1:], {3: 0, 4: 1}
    return call(
        kernel,
        "last_part",
        operands,
        docs.marks,
        [(num.shape, F32), (den.shape, F32), (x.shape, BF16)],
        reply_scratch(half, width) + [
            pltpu.VMEM((2, half, width), BF16),
            hidden_scratch(half, weights),
            pltpu.SemaphoreType.DMA((2,)),
        ],
        aliases=aliases,
        sent=(2,),
    )[2]


def open_part(x, num, den, weights, gains, part, tiles):
    width = x.shape[1]
    rows = x.shape[0] // 2
    return call(
        functools.partial(open_kernel, part * rows, tiles),
        "open_part",
        (x, num, den, weights[0], gains, *weights[1:]),
        None,
        [((rows, width), F32), ((rows, width), BF16)],
        [],
    )


def close_part(acc, n, weights, tiles):
    return call(
        functools.partial(close_kernel, tiles),
        "close_part",
        (acc, n, *weights[1:]),
        None,
        [(acc.shape, BF16)],
        [pltpu.VMEM(acc.shape, F32)],
    )[0]


def shifted(value, axis, steps):
    count = lax.axis_size(axis)
    first, last = max(0, -steps), min(count, count - steps)
    return lax.ppermute(value, axis, [(i, i + steps) for i in range(first, last)])


def swapped(value, axis, bit):
    return lax.ppermute(value, axis, [(i, i ^ bit) for i in range(lax.axis_size(axis))])


class Documents:
    def __init__(self, doc_ids, rows):
        count = lax.axis_size("seq")
        self.ids, self.rows, self.half = doc_ids, rows, rows // 2
        longest = doc_ids.shape[1] // 2
        self.hops = min(count - 1, -(-(longest - 1) // rows))
        self.short = self.hops == 2 and longest <= 2 * rows and rows % 2 == 0
        place = lax.axis_index("seq")

        def column(later, size):
            start = jnp.minimum((place + later) * rows, doc_ids.shape[1] - size)
            ids = lax.dynamic_slice_in_dim(doc_ids, start, size, 1)
            return jnp.broadcast_to(ids.reshape(-1, 1), (size, LANES))

        grain = min(BLOCK, self.half)
        self.marks = jnp.stack([doc_ids[0, ::grain], doc_ids[0, grain - 1 :: grain]])
        self.own_column = column(0, rows)
        self.later_column = column(1, self.half) if self.short else self.own_column


def attention(x, state, piece, first_back, docs, gains, weights, kv=None):
    q, num, den = state
    w_attn = weights[0]
    ready = kv is not None
    if not ready:
        kv = jnp.zeros((2, *piece.shape), BF16)
    if docs.short:
        message, kv = message_part(after(first_back, q), piece, ready, gains, w_attn, kv, docs)
        num = after(num, message)
        message = shifted(message, "seq", 1)
        num, den, _ = piece_part(piece, 1, ready, gains, w_attn, q, num, den, kv, docs)
        done = finish_part(x, num, den, weights, gains, docs)
        return after(message, done), (q, num, den), done
    for hop in range(1, docs.hops + 1):
        num, den, kv = piece_part(piece, hop, None, gains, w_attn, q, num, den, kv, docs)
        piece = shifted(piece, "seq", 1)
    return None, (q, num, den), finish_part(x, num, den, weights, gains, docs)


def packed(row):
    high = lax.reduce_precision(row, 8, 7)
    low = lax.reduce_precision(row - high, 8, 7)
    place = lax.broadcasted_iota(jnp.int32, (CARRIED, row.shape[1]), 0)
    return jnp.where(place == 0, high, jnp.where(place == 1, low, 0.0)).astype(BF16)


def unpacked(rows):
    return rows[:1].astype(F32) + rows[1:2].astype(F32)


def after(value, *earlier):
    return lax.optimization_barrier((value, *earlier))[0]


def own_half(rows, odd):
    half = rows.shape[0] // 2
    return jnp.where(odd, rows[half:], rows[:half]), jnp.where(odd, rows[:half], rows[half:])


class Chain:
    def __init__(self, own_states, other_states, even_gain, odd_gain, bits, before=None):
        self.bits, self.odd, self.leading = bits, bits[1], bits[0]
        self.even_gain, self.odd_gain = even_gain, odd_gain
        self.levels = before.levels if before else []
        self.factor, self.factor_before = even_gain * odd_gain, jnp.ones_like(even_gain)
        even, odd = self.sorted(own_states, other_states)
        self.even_states = even
        behind = jnp.where(self.leading, 0.0, self.even_gain * even.astype(F32))
        self.known = self.odd_gain * (behind + odd.astype(F32))

    def sorted(self, mine, other):
        return jnp.where(self.odd, other, mine), jnp.where(self.odd, mine, other)

    def enter(self, fine, *earlier):
        fine = after(fine, *earlier)
        half = fine.shape[0] // 2
        mine, sent = own_half(fine, self.odd)
        other = swapped(sent, "depth", 1)
        self.fine_even, fine_odd = self.sorted(mine, other)
        self.total = self.odd_gain * self.fine_even.astype(F32) + fine_odd.astype(F32) - self.known
        self.before = jnp.zeros_like(self.total)

    def level(self, index, sent_after=(), used_after=()):
        bit, last = 2 << index, index + 1 == self.steps()
        upper, rows = self.bits[bit], self.total.shape[0]
        sent = self.total.astype(BF16)
        carries = index == len(self.levels) and not last
        if carries:
            sent = jnp.concatenate([sent, packed(self.factor)], axis=0)
        theirs = after(swapped(after(sent, *sent_after), "depth", bit), *used_after)
        if index == len(self.levels):
            their_factor = unpacked(theirs[rows:]) if carries else None
            self.levels.append((self.factor, their_factor, self.factor_before))
            if carries:
                self.factor_before = jnp.where(upper, self.factor_before * their_factor, self.factor_before)
                self.factor = self.factor * their_factor
        factor, their_factor, factor_before = self.levels[index]
        theirs = theirs[:rows].astype(F32)
        if not last:
            self.total = jnp.where(upper, factor * theirs + self.total, their_factor * self.total + theirs)
        self.before = jnp.where(upper, factor_before * theirs + self.before, self.before)

    def steps(self):
        return len(self.bits) - 2

    def leave(self, used_after=()):
        even_states = self.even_states.astype(F32)
        even = jnp.where(self.leading, even_states, self.before)
        odd = self.even_gain * (even - even_states) + self.fine_even.astype(F32)
        even, odd = even.astype(BF16), odd.astype(BF16)
        mine, sent = jnp.where(self.odd, odd, even), jnp.where(self.odd, even, odd)
        other = after(swapped(sent, "depth", 1), *used_after)
        low, high = self.sorted(mine, other)
        return jnp.concatenate([low, high], axis=0)


def on_device(interfaces, doc_ids, w_attn, w_up, w_down, norm_gains, coarse_gain):
    x = interfaces[0, 0]
    rows = x.shape[0]
    half = rows // 2
    gains = norm_gains[0, 0]
    weights = (w_attn[0, 0], w_up[0, 0], w_down[0, 0])
    parts = [x[:half], x[half:]]
    piece = shifted(x, "seq", 1)
    docs = Documents(doc_ids, rows)
    place, bits, bit = lax.axis_index("depth"), {}, 1
    while bit < lax.axis_size("depth"):
        bits[bit] = (place & bit) != 0
        bit *= 2
    bits[0] = place < 2
    early, bits, docs.own_column, docs.later_column, docs.marks = lax.optimization_barrier(
        (x, bits, docs.own_column, docs.later_column, docs.marks)
    )
    first_back = shifted(after(parts[0], docs.own_column), "seq", -1)
    state = own_part(early, gains, weights, docs)
    kept, sent = zip(*[own_half(part, bits[1]) for part in parts])
    sent = jnp.concatenate([*after(sent, state[0]), packed(coarse_gain)], axis=0)
    other = swapped(sent, "depth", 1)
    message, state, done = attention(early, state, piece, first_back, docs, gains, weights)
    other_gain = unpacked(other[half:])
    pair = jnp.where(bits[1], other_gain, coarse_gain), jnp.where(bits[1], coarse_gain, other_gain)
    first = Chain(kept[1], other[half // 2 : half], *pair, bits)
    second = Chain(kept[0], other[: half // 2], *pair, bits, first)
    _, num, den = state
    if message is not None:
        message = after(message, first.known, second.known)
        num, den, done = again_part(message, state, done, early, weights, gains, docs)
    first.enter(done)
    tiles = weights[1].shape[1] // TILE // 2
    acc, n = open_part(early, after(num, first.total), den, weights, gains, 0, tiles)
    first.level(0, used_after=(n,))
    fine = close_part(after(acc, first.total), n, weights, tiles)
    first.level(1, used_after=(fine,))
    second.enter(fine, first.before)
    for i in range(2, first.steps()):
        second.level(i - 2)
        first.level(i)
    late = first.leave()
    late_piece = shifted(late, "seq", 1)
    for i in range(max(0, first.steps() - 2), first.steps()):
        last = i + 1 == first.steps()
        second.level(i, (late,) if i > 0 else (), (late_piece,) if last else ())
    soon = second.leave()
    piece = jnp.concatenate([shifted(soon, "seq", 1), late_piece], axis=0)
    x = jnp.concatenate([soon, late], axis=0)
    first_back = shifted(after(soon, x), "seq", -1)
    state = own_part(x, gains, weights, docs)
    kv = keys_part(after(late_piece, state[0]), gains, weights[0], docs) if docs.short else None
    message, state, done = attention(x, state, piece, first_back, docs, gains, weights, kv)
    return last_part(message, state, done, x, weights, gains, docs)[None, None]


def solution(mesh):
    in_specs = (
        P("depth", None, "seq", None),
        P(),
        P("depth", None, None, None, None),
        P("depth", None, None, None),
        P("depth", None, None, None),
        P("depth", None, None, None),
        P("depth", None),
    )
    out_specs = P("depth", None, "seq", None)
    return jax.shard_map(
        on_device, mesh=mesh, in_specs=in_specs, out_specs=out_specs, check_vma=False
    )
```

```python
import functools

import jax
import jax.numpy as jnp
from jax import lax
from jax.experimental import pallas as pl
from jax.experimental.pallas import tpu as pltpu
from jax.sharding import PartitionSpec as P

HEADS = 16
LANES = 128
CARRIED = 16
BLOCK = 256
TILE = 512
TILES = 8
VMEM_BYTES = 8 * 1024 * 1024
COST = pl.CostEstimate(flops=1 << 20, bytes_accessed=1 << 16, transcendentals=0)
F32 = jnp.float32
BF16 = jnp.bfloat16


def rms_norm(value, gain):
    return value * lax.rsqrt(jnp.mean(value * value, axis=-1, keepdims=True) + 1e-05) * gain


def dot(a, b):
    return jnp.dot(a, b, preferred_element_type=F32)


def first_id(marks_ref, position, grain):
    return marks_ref[0, lax.div(position, grain)]


def last_id(marks_ref, end, grain):
    return marks_ref[1, jnp.maximum(lax.div(end, grain) - 1, 0)]


def grain_of(marks_ref, rows):
    return rows * lax.axis_size("seq") // marks_ref.shape[1]


def attend(q_ref, k_ref, v_ref, num_ref, den_ref, column_ref, row_ref, doc_ref, q_at, k_at, causal=False):
    rows, width = q_ref.shape
    keys = k_ref.shape[0]
    head_dim = width // HEADS
    per_tile = LANES // head_dim
    q_block, k_block = min(BLOCK, rows), min(BLOCK, keys)
    lane = lax.broadcasted_iota(jnp.int32, (1, LANES), 1)
    members = [lane // head_dim == i for i in range(per_tile)]
    count_q, count_k = rows // q_block, keys // k_block
    grain = row_ref.shape[1] // doc_ref.shape[1]

    def one(index, carry):
        qi, ki = index // count_k, index % count_k
        q0 = pl.multiple_of(qi * q_block, q_block)
        k0 = pl.multiple_of(ki * k_block, k_block)
        needed = last_id(doc_ref, k_at + k0 + k_block, grain) >= first_id(doc_ref, q_at + q0, grain)
        if causal:
            needed = (k0 <= q0) & (needed | (k0 == q0))

        @pl.when(needed)
        def _():
            key_docs = row_ref[:, pl.ds(pl.multiple_of(k_at + k0, k_block), k_block)]
            allowed = column_ref[pl.ds(q0, q_block), :1] == key_docs
            if causal:
                q_pos = q0 + lax.broadcasted_iota(jnp.int32, (q_block, k_block), 0)
                k_pos = k0 + lax.broadcasted_iota(jnp.int32, (q_block, k_block), 1)
                allowed = allowed & (k_pos <= q_pos)
            ones = jnp.ones((k_block, LANES), BF16)

            def heads(tile, den):
                cols = pl.ds(pl.multiple_of(tile * LANES, LANES), LANES)
                queries = q_ref[pl.ds(q0, q_block), cols]
                keys_here = k_ref[pl.ds(k0, k_block), cols]
                values = jnp.concatenate([v_ref[pl.ds(k0, k_block), cols], ones], axis=1)
                num = None
                for i, member in enumerate(members):
                    scores = lax.dot_general(
                        jnp.where(member, queries, jnp.zeros_like(queries)),
                        keys_here,
                        (((1,), (1,)), ((), ())),
                        preferred_element_type=F32,
                    )
                    weights = jnp.where(allowed, jnp.exp(scores), 0.0).astype(BF16)
                    out = dot(weights, values)
                    num = out[:, :LANES] if num is None else jnp.where(member, out[:, :LANES], num)
                    den = jnp.where(lane == tile * per_tile + i, out[:, LANES:], den)
                num_ref[pl.ds(q0, q_block), cols] += num
                return den

            def some(step, den):
                for i in range(TILES):
                    den = heads(step * TILES + i, den)
                return den

            den = jnp.zeros((q_block, LANES), F32)
            den_ref[pl.ds(q0, q_block), :] += lax.fori_loop(0, width // LANES // TILES, some, den, unroll=True)

        return carry

    lax.fori_loop(0, count_q * count_k, one, 0)


def spread(per_head, width):
    shape = (LANES, width)
    chosen = lax.broadcasted_iota(jnp.int32, shape, 1) // (width // HEADS) == lax.broadcasted_iota(jnp.int32, shape, 0)
    chosen = jnp.where(chosen, 1.0, 0.0).astype(BF16)
    high = per_head.astype(BF16)
    return dot(high, chosen) + dot((per_head - high.astype(F32)).astype(BF16), chosen)


def normed(x_ref, gain_ref):
    return rms_norm(x_ref[...].astype(F32), gain_ref[0:1]).astype(BF16)


def project(n_ref, w_ref, first, out_ref):
    count, _, width = out_ref.shape
    tile = min(TILE, width)
    steps = width // tile

    def one(step, carry):
        i, j = step // steps, step % steps
        cols = pl.ds(pl.multiple_of(j * tile, tile), tile)
        out = dot(n_ref[...], w_ref[first + i, :, cols]).astype(BF16)
        if first == 0:
            out *= jnp.where(i == 0, (width // HEADS) ** (-0.5), 1.0).astype(BF16)
        out_ref[i, :, cols] = out
        return carry

    lax.fori_loop(0, count * steps, one, 0)


def own_kernel(x_ref, gain_ref, w_ref, column_ref, row_ref, doc_ref, q_ref, num_ref, den_ref, n_ref, qkv_ref):
    here = lax.axis_index("seq") * x_ref.shape[0]
    n_ref[...] = normed(x_ref, gain_ref)
    project(n_ref, w_ref, 0, qkv_ref)
    q_ref[...] = qkv_ref[0]
    num_ref[...] = jnp.zeros_like(num_ref)
    den_ref[...] = jnp.zeros_like(den_ref)
    k_ref, v_ref = qkv_ref.at[1], qkv_ref.at[2]
    attend(q_ref, k_ref, v_ref, num_ref, den_ref, column_ref, row_ref, doc_ref, here, here, True)


def keys_kernel(x_ref, gain_ref, w_ref, doc_ref, kv_ref, n_ref):
    half = x_ref.shape[0]
    here = lax.axis_index("seq") * 2 * half

    grain = grain_of(doc_ref, 2 * half)

    @pl.when((here > 0) & (last_id(doc_ref, here, grain) >= first_id(doc_ref, here, grain)))
    def _():
        n_ref[...] = normed(x_ref, gain_ref)
        project(n_ref, w_ref, 1, kv_ref.at[:, half:])


def fill_keys(ready, x_ref, gain_ref, w_ref, n_ref, kv_ref):
    rows = x_ref.shape[0] // 2 if ready else x_ref.shape[0]
    n_ref[:rows] = rms_norm(x_ref[:rows].astype(F32), gain_ref[0:1]).astype(BF16)
    project(n_ref.at[:rows], w_ref, 1, kv_ref.at[:, :rows])


def message_place(doc_ref, rows):
    place, count = lax.axis_index("seq"), lax.axis_size("seq")
    inside = (place >= 1) & (place + 1 < count)
    here = jnp.where(inside, place + 1, 0) * rows
    there = jnp.where(inside, place - 1, 0) * rows
    grain = grain_of(doc_ref, rows)
    return here, there, inside & (last_id(doc_ref, there + rows, grain) >= first_id(doc_ref, here, grain))


def piece_kernel(
    ready, shift, x_ref, gain_ref, w_ref, q_ref, num_in, den_in, kv_in, column_ref, row_ref, doc_ref,
    num_ref, den_ref, kv_ref, n_ref,
):
    del num_in, den_in, kv_in
    rows, keys = q_ref.shape[0], x_ref.shape[0]
    shard = lax.axis_index("seq") - shift
    here, there = (shard + shift) * rows, jnp.maximum(shard, 0) * rows + rows - keys

    grain = grain_of(doc_ref, rows)

    @pl.when((shard >= 0) & (last_id(doc_ref, there + keys, grain) >= first_id(doc_ref, here, grain)))
    def _():
        if ready is None:
            fill_keys(False, x_ref, gain_ref, w_ref, n_ref, kv_ref)
        else:
            far = far_document(doc_ref, rows, lax.axis_size("seq"))

            @pl.when(jnp.logical_not(far & message_place(doc_ref, rows)[2]))
            def _():
                fill_keys(ready, x_ref, gain_ref, w_ref, n_ref, kv_ref)

        attend(q_ref, kv_ref.at[0], kv_ref.at[1], num_ref, den_ref, column_ref, row_ref, doc_ref, here, there)


def far_document(doc_ref, rows, count):
    found, grain = False, grain_of(doc_ref, rows)
    for middle in range(1, count - 1):
        start, behind = middle * rows, first_id(doc_ref, (middle + 1) * rows, grain)
        over = last_id(doc_ref, start, grain) == behind
        deep = last_id(doc_ref, start - rows // 2, grain) == behind
        found = found | (over & deep)
    return found


def message_kernel(
    ready, x_ref, piece_ref, gain_ref, w_ref, kv_in, column_ref, row_ref, doc_ref,
    out_ref, kv_ref, q_ref, n_ref, num_ref, den_ref,
):
    del kv_in
    half, width = x_ref.shape
    here, there, needed = message_place(doc_ref, 2 * half)
    far = far_document(doc_ref, 2 * half, lax.axis_size("seq"))

    @pl.when(jnp.logical_not(far))
    def _():
        out_ref[:, :width] = piece_ref[half:]

    @pl.when(far)
    def _():
        num_ref[...] = jnp.zeros_like(num_ref)
        den_ref[...] = jnp.zeros_like(den_ref)

        @pl.when(needed)
        def _():
            n_ref[:half] = normed(x_ref, gain_ref)
            project(n_ref.at[:half], w_ref, 0, q_ref)
            fill_keys(ready, piece_ref, gain_ref, w_ref, n_ref, kv_ref)
            attend(
                q_ref.at[0], kv_ref.at[0], kv_ref.at[1], num_ref, den_ref, column_ref, row_ref, doc_ref, here, there
            )

        out_ref[:, :width] = num_ref[...].astype(BF16)
        out_ref[:, width:] = den_ref[...].astype(BF16)


def reply_kernel(
    message_ref, gain_ref, w_ref, q_ref, num_in, den_in, column_ref, row_ref, doc_ref,
    num_ref, den_ref, n_ref, kv_ref,
):
    rows, width = q_ref.shape
    half = message_ref.shape[0]
    far = far_document(doc_ref, rows, lax.axis_size("seq"))

    @pl.when(far)
    def _():
        num_ref[:half] += message_ref[:, :width].astype(F32)
        den_ref[:half] += message_ref[:, width:].astype(F32)

    @pl.when(jnp.logical_not(far))
    def _():
        piece_kernel(
            None, 2, message_ref.at[:, :width], gain_ref, w_ref, q_ref, num_in, den_in, None, column_ref, row_ref, doc_ref,
            num_ref, den_ref, kv_ref, n_ref,
        )


def mix(first, x_ref, num_ref, den_ref, w_ref, gain_ref, acc_ref, n_ref):
    rows, width = acc_ref.shape
    here = pl.ds(first, rows)
    lane = lax.broadcasted_iota(jnp.int32, (rows, LANES), 1)
    inverse = 1.0 / jnp.where(lane < HEADS, den_ref[here], 1.0)
    n_ref[...] = (num_ref[here] * spread(inverse, width)).astype(BF16)
    tile = min(TILE, width)

    def one(j, carry):
        cols = pl.ds(pl.multiple_of(j * tile, tile), tile)
        acc_ref[:, cols] = x_ref[here, cols].astype(F32) + dot(n_ref[...], w_ref[3, :, cols])
        return carry

    lax.fori_loop(0, width // tile, one, 0)
    n_ref[...] = rms_norm(acc_ref[...], gain_ref[1:2]).astype(BF16)


def feed_forward(begin, end, n_ref, up_ref, down_ref, acc_ref):
    tile = min(TILE, up_ref.shape[1])

    def one(j, carry):
        units = pl.ds(pl.multiple_of(j * tile, tile), tile)
        expanded = jax.nn.gelu(dot(n_ref[...], up_ref[:, units])).astype(BF16)
        acc_ref[...] += dot(expanded, down_ref[units])
        return carry

    lax.fori_loop(begin, end, one, 0)


def feed_forward_ahead(n_ref, up_ref, down_ref, acc_ref, hidden_ref):
    tile = hidden_ref.shape[2]
    last = up_ref.shape[1] // tile - 1

    def expand(j):
        units = pl.ds(pl.multiple_of(j * tile, tile), tile)
        hidden_ref[j % 2] = jax.nn.gelu(dot(n_ref[...], up_ref[:, units])).astype(BF16)

    def lower(j):
        acc_ref[...] += dot(hidden_ref[j % 2], down_ref[pl.ds(pl.multiple_of(j * tile, tile), tile)])

    def one(j, carry):
        lower(j)
        expand(j + 1)
        return carry

    expand(0)
    lax.fori_loop(0, last, one, 0)
    lower(last)


def tiles_of(up_ref):
    return up_ref.shape[1] // min(TILE, up_ref.shape[1])


def finish_kernel(
    first, x_ref, num_ref, den_ref, w_ref, gain_ref, up_ref, down_ref, out_ref, acc_ref, n_ref, hidden_ref=None
):
    mix(first, x_ref, num_ref, den_ref, w_ref, gain_ref, acc_ref, n_ref)
    if hidden_ref is None:
        feed_forward(0, tiles_of(up_ref), n_ref, up_ref, down_ref, acc_ref)
    else:
        feed_forward_ahead(n_ref, up_ref, down_ref, acc_ref, hidden_ref)
    out_ref[...] = acc_ref[...].astype(BF16)


def seen_by_second_half(doc_ref, rows):
    place = lax.axis_index("seq")
    grain = grain_of(doc_ref, rows)
    before = last_id(doc_ref, jnp.maximum(place - 1, 0) * rows, grain)
    return (place >= 2) & (before == first_id(doc_ref, place * rows + rows // 2, grain))


def early_kernel(
    first, x_ref, num_ref, den_ref, w_ref, gain_ref, up_ref, down_ref, doc_ref, out_ref, acc_ref, n_ref, hidden_ref
):
    @pl.when(jnp.logical_not(seen_by_second_half(doc_ref, x_ref.shape[0])))
    def _():
        finish_kernel(
            first, x_ref, num_ref, den_ref, w_ref, gain_ref, up_ref, down_ref, out_ref, acc_ref, n_ref, hidden_ref
        )


def again_kernel(
    message_ref, gain_ref, w_ref, q_ref, num_in, den_in, done_in, x_ref, up_ref, down_ref, column_ref, row_ref, doc_ref,
    num_ref, den_ref, done_ref, n_ref, kv_ref, acc_ref,
):
    del done_in
    half = done_ref.shape[0]
    reply_kernel(
        message_ref, gain_ref, w_ref, q_ref, num_in, den_in, column_ref, row_ref, doc_ref,
        num_ref, den_ref, n_ref, kv_ref,
    )

    @pl.when(seen_by_second_half(doc_ref, 2 * half))
    def _():
        finish_kernel(half, x_ref, num_ref, den_ref, w_ref, gain_ref, up_ref, down_ref, done_ref, acc_ref, n_ref)


def last_kernel(
    message_ref, gain_ref, w_ref, q_ref, num_in, den_in, done_ref, x_ref, up_ref, down_ref, column_ref, row_ref, doc_ref,
    num_ref, den_ref, out_ref, n_ref, kv_ref, acc_ref, result_ref, hidden_ref, sems,
):
    half = done_ref.shape[0]
    again = seen_by_second_half(doc_ref, 2 * half) if message_ref is not None else False
    halves = [out_ref.at[:half], out_ref.at[half:]]
    as_it_was = pltpu.make_async_copy(done_ref, halves[1], sems.at[1])
    copies = [pltpu.make_async_copy(result_ref.at[i], halves[i], sems.at[i]) for i in range(2)]

    @pl.when(jnp.logical_not(again))
    def _():
        as_it_was.start()

    if message_ref is not None:
        reply_kernel(
            message_ref, gain_ref, w_ref, q_ref, num_in, den_in, column_ref, row_ref, doc_ref,
            num_ref, den_ref, n_ref, kv_ref,
        )

    def one(part, carry):
        @pl.when((part == 0) | again)
        def _():
            first = pl.multiple_of(part * half, half)
            finish_kernel(
                first, x_ref, num_ref, den_ref, w_ref, gain_ref, up_ref, down_ref, result_ref.at[part], acc_ref, n_ref,
                hidden_ref,
            )

        return carry

    lax.fori_loop(0, 2, one, 0)
    copies[0].start()

    @pl.when(again)
    def _():
        copies[1].start()
        copies[1].wait()

    @pl.when(jnp.logical_not(again))
    def _():
        as_it_was.wait()

    copies[0].wait()


def open_kernel(first, tiles, x_ref, num_ref, den_ref, w_ref, gain_ref, up_ref, down_ref, acc_ref, n_ref):
    mix(first, x_ref, num_ref, den_ref, w_ref, gain_ref, acc_ref, n_ref)
    feed_forward(0, tiles, n_ref, up_ref, down_ref, acc_ref)


def close_kernel(begin, acc_in, n_ref, up_ref, down_ref, out_ref, acc_ref):
    acc_ref[...] = acc_in[...]
    feed_forward(begin, tiles_of(up_ref), n_ref, up_ref, down_ref, acc_ref)
    out_ref[...] = acc_ref[...].astype(BF16)


def vmem():
    return pl.BlockSpec(memory_space=pltpu.VMEM)


def call(kernel, name, operands, docs, results, scratch, aliases=None, sent=()):
    inputs = [pltpu.with_memory_space_constraint(operand, pltpu.VMEM) for operand in operands]
    in_specs = [vmem()] * len(inputs)
    if docs is not None:
        inputs.append(docs)
        in_specs.append(pl.BlockSpec(memory_space=pltpu.SMEM))
    return pl.pallas_call(
        kernel,
        in_specs=in_specs,
        out_specs=[pl.BlockSpec(memory_space=pl.ANY) if i in sent else vmem() for i in range(len(results))],
        out_shape=[
            jax.ShapeDtypeStruct(*one) if i in sent else pltpu.VMEM(*one) for i, one in enumerate(results)
        ],
        scratch_shapes=scratch,
        input_output_aliases=aliases or {},
        compiler_params=pltpu.CompilerParams(vmem_limit_bytes=VMEM_BYTES),
        cost_estimate=COST,
        name=name,
    )(*inputs)


def own_part(x, gains, weights, docs):
    rows, width = x.shape
    results = [((rows, width), BF16), ((rows, width), F32), ((rows, LANES), F32)]
    scratch = [pltpu.VMEM((rows, width), BF16), pltpu.VMEM((3, rows, width), BF16)]
    return call(own_kernel, "own_part", (x, gains, weights[0], docs.own_column, docs.ids), docs.marks, results, scratch)


def keys_part(x, gains, w_attn, docs):
    half, width = x.shape
    return call(
        keys_kernel,
        "keys_part",
        (x, gains, w_attn),
        docs.marks,
        [((2, 2 * half, width), BF16)],
        [pltpu.VMEM((half, width), BF16)],
    )[0]


def piece_part(x, shift, ready, gains, w_attn, q, num, den, kv, docs):
    rows, width = q.shape
    return call(
        functools.partial(piece_kernel, ready, shift),
        "piece_part",
        (x, gains, w_attn, q, num, den, kv, docs.own_column, docs.ids),
        docs.marks,
        [((rows, width), F32), ((rows, LANES), F32), (kv.shape, BF16)],
        [pltpu.VMEM(x.shape, BF16)],
        aliases={4: 0, 5: 1, 6: 2},
    )


def message_part(x, piece, ready, gains, w_attn, kv, docs):
    half, width = x.shape
    return call(
        functools.partial(message_kernel, ready),
        "message_part",
        (x, piece, gains, w_attn, kv, docs.later_column, docs.ids),
        docs.marks,
        [((half, width + LANES), BF16), (kv.shape, BF16)],
        [
            pltpu.VMEM((1, half, width), BF16),
            pltpu.VMEM(piece.shape, BF16),
            pltpu.VMEM((half, width), F32),
            pltpu.VMEM((half, LANES), F32),
        ],
        aliases={4: 1},
    )


def finish_part(x, num, den, weights, gains, docs):
    half, width = x.shape[0] // 2, x.shape[1]
    return call(
        functools.partial(early_kernel if docs.short else finish_kernel, half),
        "finish_part",
        (x, num, den, weights[0], gains, *weights[1:]),
        docs.marks if docs.short else None,
        [((half, width), BF16)],
        [pltpu.VMEM((half, width), F32), pltpu.VMEM((half, width), BF16), hidden_scratch(half, weights)],
    )[0]


def hidden_scratch(rows, weights):
    return pltpu.VMEM((2, rows, min(TILE, weights[1].shape[1])), BF16)


def reply_scratch(half, width):
    return [
        pltpu.VMEM((half, width), BF16),
        pltpu.VMEM((2, half, width), BF16),
        pltpu.VMEM((half, width), F32),
    ]


def again_part(message, state, done, x, weights, gains, docs):
    q, num, den = state
    half, width = done.shape
    return call(
        again_kernel,
        "again_part",
        (message, gains, weights[0], q, num, den, done, x, *weights[1:], docs.own_column, docs.ids),
        docs.marks,
        [(num.shape, F32), (den.shape, F32), ((half, width), BF16)],
        reply_scratch(half, width),
        aliases={4: 0, 5: 1, 6: 2},
    )


def last_part(message, state, done, x, weights, gains, docs):
    q, num, den = state
    half, width = done.shape
    operands = (message, gains, weights[0], q, num, den, done, x, *weights[1:], docs.own_column, docs.ids)
    kernel, aliases = last_kernel, {4: 0, 5: 1}
    if message is None:
        kernel, operands, aliases = functools.partial(last_kernel, None), operands[1:], {3: 0, 4: 1}
    return call(
        kernel,
        "last_part",
        operands,
        docs.marks,
        [(num.shape, F32), (den.shape, F32), (x.shape, BF16)],
        reply_scratch(half, width) + [
            pltpu.VMEM((2, half, width), BF16),
            hidden_scratch(half, weights),
            pltpu.SemaphoreType.DMA((2,)),
        ],
        aliases=aliases,
        sent=(2,),
    )[2]


def open_part(x, num, den, weights, gains, part, tiles):
    width = x.shape[1]
    rows = x.shape[0] // 2
    return call(
        functools.partial(open_kernel, part * rows, tiles),
        "open_part",
        (x, num, den, weights[0], gains, *weights[1:]),
        None,
        [((rows, width), F32), ((rows, width), BF16)],
        [],
    )


def close_part(acc, n, weights, tiles):
    return call(
        functools.partial(close_kernel, tiles),
        "close_part",
        (acc, n, *weights[1:]),
        None,
        [(acc.shape, BF16)],
        [pltpu.VMEM(acc.shape, F32)],
    )[0]


def shifted(value, axis, steps):
    count = lax.axis_size(axis)
    first, last = max(0, -steps), min(count, count - steps)
    return lax.ppermute(value, axis, [(i, i + steps) for i in range(first, last)])


def swapped(value, axis, bit):
    return lax.ppermute(value, axis, [(i, i ^ bit) for i in range(lax.axis_size(axis))])


class Documents:
    def __init__(self, doc_ids, rows):
        count = lax.axis_size("seq")
        self.ids, self.rows, self.half = doc_ids, rows, rows // 2
        longest = doc_ids.shape[1] // 2
        self.hops = min(count - 1, -(-(longest - 1) // rows))
        self.short = self.hops == 2 and longest <= 2 * rows and rows % 2 == 0
        place = lax.axis_index("seq")

        def column(later, size):
            start = jnp.minimum((place + later) * rows, doc_ids.shape[1] - size)
            ids = lax.dynamic_slice_in_dim(doc_ids, start, size, 1)
            return jnp.broadcast_to(ids.reshape(-1, 1), (size, LANES))

        grain = min(BLOCK, self.half)
        self.marks = jnp.stack([doc_ids[0, ::grain], doc_ids[0, grain - 1 :: grain]])
        self.own_column = column(0, rows)
        self.later_column = column(1, self.half) if self.short else self.own_column


def attention(x, state, piece, first_back, docs, gains, weights, kv=None):
    q, num, den = state
    w_attn = weights[0]
    ready = kv is not None
    if not ready:
        kv = jnp.zeros((2, *piece.shape), BF16)
    if docs.short:
        message, kv = message_part(after(first_back, q), piece, ready, gains, w_attn, kv, docs)
        num = after(num, message)
        message = shifted(message, "seq", 1)
        num, den, _ = piece_part(piece, 1, ready, gains, w_attn, q, num, den, kv, docs)
        done = finish_part(x, num, den, weights, gains, docs)
        return after(message, done), (q, num, den), done
    for hop in range(1, docs.hops + 1):
        num, den, kv = piece_part(piece, hop, None, gains, w_attn, q, num, den, kv, docs)
        piece = shifted(piece, "seq", 1)
    return None, (q, num, den), finish_part(x, num, den, weights, gains, docs)


def packed(row):
    high = lax.reduce_precision(row, 8, 7)
    low = lax.reduce_precision(row - high, 8, 7)
    place = lax.broadcasted_iota(jnp.int32, (CARRIED, row.shape[1]), 0)
    return jnp.where(place == 0, high, jnp.where(place == 1, low, 0.0)).astype(BF16)


def unpacked(rows):
    return rows[:1].astype(F32) + rows[1:2].astype(F32)


def after(value, *earlier):
    return lax.optimization_barrier((value, *earlier))[0]


def own_half(rows, odd):
    half = rows.shape[0] // 2
    return jnp.where(odd, rows[half:], rows[:half]), jnp.where(odd, rows[:half], rows[half:])


class Chain:
    def __init__(self, own_states, other_states, even_gain, odd_gain, bits, before=None):
        self.bits, self.odd, self.leading = bits, bits[1], bits[0]
        self.even_gain, self.odd_gain = even_gain, odd_gain
        self.levels = before.levels if before else []
        self.factor, self.factor_before = even_gain * odd_gain, jnp.ones_like(even_gain)
        even, odd = self.sorted(own_states, other_states)
        self.even_states = even
        behind = jnp.where(self.leading, 0.0, self.even_gain * even.astype(F32))
        self.known = self.odd_gain * (behind + odd.astype(F32))

    def sorted(self, mine, other):
        return jnp.where(self.odd, other, mine), jnp.where(self.odd, mine, other)

    def enter(self, fine, *earlier):
        fine = after(fine, *earlier)
        half = fine.shape[0] // 2
        mine, sent = own_half(fine, self.odd)
        other = swapped(sent, "depth", 1)
        self.fine_even, fine_odd = self.sorted(mine, other)
        self.total = self.odd_gain * self.fine_even.astype(F32) + fine_odd.astype(F32) - self.known
        self.before = jnp.zeros_like(self.total)

    def level(self, index, sent_after=(), used_after=()):
        bit, last = 2 << index, index + 1 == self.steps()
        upper, rows = self.bits[bit], self.total.shape[0]
        sent = self.total.astype(BF16)
        carries = index == len(self.levels) and not last
        if carries:
            sent = jnp.concatenate([sent, packed(self.factor)], axis=0)
        theirs = after(swapped(after(sent, *sent_after), "depth", bit), *used_after)
        if index == len(self.levels):
            their_factor = unpacked(theirs[rows:]) if carries else None
            self.levels.append((self.factor, their_factor, self.factor_before))
            if carries:
                self.factor_before = jnp.where(upper, self.factor_before * their_factor, self.factor_before)
                self.factor = self.factor * their_factor
        factor, their_factor, factor_before = self.levels[index]
        theirs = theirs[:rows].astype(F32)
        if not last:
            self.total = jnp.where(upper, factor * theirs + self.total, their_factor * self.total + theirs)
        self.before = jnp.where(upper, factor_before * theirs + self.before, self.before)

    def steps(self):
        return len(self.bits) - 2

    def leave(self, used_after=()):
        even_states = self.even_states.astype(F32)
        even = jnp.where(self.leading, even_states, self.before)
        odd = self.even_gain * (even - even_states) + self.fine_even.astype(F32)
        even, odd = even.astype(BF16), odd.astype(BF16)
        mine, sent = jnp.where(self.odd, odd, even), jnp.where(self.odd, even, odd)
        other = after(swapped(sent, "depth", 1), *used_after)
        low, high = self.sorted(mine, other)
        return jnp.concatenate([low, high], axis=0)


def on_device(interfaces, doc_ids, w_attn, w_up, w_down, norm_gains, coarse_gain):
    x = interfaces[0, 0]
    rows = x.shape[0]
    half = rows // 2
    gains = norm_gains[0, 0]
    weights = (w_attn[0, 0], w_up[0, 0], w_down[0, 0])
    parts = [x[:half], x[half:]]
    piece = shifted(x, "seq", 1)
    docs = Documents(doc_ids, rows)
    place, bits, bit = lax.axis_index("depth"), {}, 1
    while bit < lax.axis_size("depth"):
        bits[bit] = (place & bit) != 0
        bit *= 2
    bits[0] = place < 2
    early, bits, docs.own_column, docs.later_column, docs.marks = lax.optimization_barrier(
        (x, bits, docs.own_column, docs.later_column, docs.marks)
    )
    first_back = shifted(after(parts[0], docs.own_column), "seq", -1)
    state = own_part(early, gains, weights, docs)
    kept, sent = zip(*[own_half(part, bits[1]) for part in parts])
    sent = jnp.concatenate([*after(sent, state[0]), packed(coarse_gain)], axis=0)
    other = swapped(sent, "depth", 1)
    message, state, done = attention(early, state, piece, first_back, docs, gains, weights)
    other_gain = unpacked(other[half:])
    pair = jnp.where(bits[1], other_gain, coarse_gain), jnp.where(bits[1], coarse_gain, other_gain)
    first = Chain(kept[1], other[half // 2 : half], *pair, bits)
    second = Chain(kept[0], other[: half // 2], *pair, bits, first)
    _, num, den = state
    if message is not None:
        message = after(message, first.known, second.known)
        num, den, done = again_part(message, state, done, early, weights, gains, docs)
    first.enter(done)
    tiles = weights[1].shape[1] // TILE // 2
    acc, n = open_part(early, after(num, first.total), den, weights, gains, 0, tiles)
    first.level(0, used_after=(n,))
    fine = close_part(after(acc, first.total), n, weights, tiles)
    first.level(1, used_after=(fine,))
    second.enter(fine, first.before)
    for i in range(2, first.steps()):
        second.level(i - 2)
        first.level(i)
    late = first.leave()
    late_piece = shifted(late, "seq", 1)
    for i in range(max(0, first.steps() - 2), first.steps()):
        last = i + 1 == first.steps()
        second.level(i, (late,) if i > 0 else (), (late_piece,) if last else ())
    soon = second.leave()
    piece = jnp.concatenate([shifted(soon, "seq", 1), late_piece], axis=0)
    x = jnp.concatenate([soon, late], axis=0)
    first_back = shifted(after(soon, x), "seq", -1)
    state = own_part(x, gains, weights, docs)
    kv = keys_part(after(late_piece, state[0]), gains, weights[0], docs) if docs.short else None
    first_back = after(first_back, piece)
    message, state, done = attention(x, state, piece, first_back, docs, gains, weights, kv)
    return last_part(message, state, done, x, weights, gains, docs)[None, None]


def solution(mesh):
    in_specs = (
        P("depth", None, "seq", None),
        P(),
        P("depth", None, None, None, None),
        P("depth", None, None, None),
        P("depth", None, None, None),
        P("depth", None, None, None),
        P("depth", None),
    )
    out_specs = P("depth", None, "seq", None)
    return jax.shard_map(
        on_device, mesh=mesh, in_specs=in_specs, out_specs=out_specs, check_vma=False
    )
```
